32 devices in a mesh: dp: 8 (over z, core), seq: 4 (over y, x).
Axes of the slice: x: 2, y: 2, z: 4, core: 2. Of those that a mesh axis runs over, the one named last changes fastest.
Arguments:
- inputs: bfloat16 [16, 1024, 768], P('dp', 'seq'), may hold values from -6 to 6
- w_query: bfloat16 [768, 768], P('seq'), may hold values from -0.109375 to 0.109375
- w_key: bfloat16 [768, 768], P('seq'), may hold values from -0.109375 to 0.109375
- w_value: bfloat16 [768, 768], P('seq'), may hold values from -0.21875 to 0.21875
- w_out: bfloat16 [768, 768], P('seq'), may hold values from -0.875 to 0.875
- w_ffn_in: bfloat16 [768, 3072], P('seq'), may hold values from -0.21875 to 0.21875
- w_ffn_out: bfloat16 [3072, 768], P('seq'), may hold values from -0.15625 to 0.15625
- attn_gain: bfloat16 [768], P('seq'), may hold values from 0.099609375 to 1.8984375
- ffn_gain: bfloat16 [768], P('seq'), may hold values from 0.099609375 to 1.8984375
- rel_bias: bfloat16 [32, 12], P('seq'), may hold values from -3 to 3
- doc_lengths: int32 [16], P('dp'), may hold values from 64 to 1024, as said below
- cotangent: bfloat16 [16, 1024, 768], P('dp', 'seq'), may hold values from -6 to 6
Outputs:
- pooled: float32 [16, 768], P('dp')
- grad_input: float32 [16, 1024, 768], P('dp', 'seq')
- grad_query: float32 [768, 768], P('seq')
- grad_key: float32 [768, 768], P('seq')
- grad_value: float32 [768, 768], P('seq')
- grad_out_proj: float32 [768, 768], P('seq')
- grad_ffn_in: float32 [768, 3072], P('seq')
- grad_ffn_out: float32 [3072, 768], P('seq')
- grad_attn_gain: float32 [768], P('seq')
- grad_ffn_gain: float32 [768], P('seq')
- grad_rel_bias: float32 [32, 12], P('seq')
The draws below stay inside these ranges and needn't reach their ends.
Inputs may be any that keep to these rules, and one draw needn't show every extreme that they name: `doc_lengths`: each length is one of 64, 128, 256, 512 and 1024; some document has length 1024.
All inputs are finite; a program needn't handle non-finite values.
Results may differ from the reference program's by a relative error of at most 0.028.
Values may be sent and summed in bfloat16 or wider, within the bound.
A program may use at most 256 MiB of HBM per device.

```python
import math
import jax
import jax.numpy as jnp
from jax import lax

D = 768
HEADS = 12
HEAD_DIM = 64
FF = 3072
NBUCKET = 32
DOC_LEN = 1024
NDOCS = 16


def draw_doc_lengths(key, part):
    first, second = jax.random.split(jax.random.fold_in(key, 11))
    levels = jax.random.randint(first, (NDOCS,), 0, 7)
    table = jnp.array([DOC_LEN // 16, DOC_LEN // 8, DOC_LEN // 4, DOC_LEN // 2, DOC_LEN, DOC_LEN, DOC_LEN], jnp.int32)
    lengths = table[levels]
    longest = jax.random.randint(second, (), 0, NDOCS)
    return lengths.at[longest].set(DOC_LEN).astype(jnp.int32)


def block_scale(stream_key, dims, cuts, low, high):
    factor_of = 1.0
    for dim, shards_of in cuts:
        draws = jax.random.uniform(jax.random.fold_in(jax.random.fold_in(stream_key, 6), dim), (shards_of,), jnp.float32, low / len(cuts), high / len(cuts))
        factor_of = factor_of * jnp.repeat(jnp.exp(draws), dims[dim] // shards_of).reshape((-1,) + (1,) * (len(dims) - 1 - dim))
    return factor_of


def normal_values(stream_key, extent, width, most, cuts=(), held_as=jnp.bfloat16):
    factor_of = block_scale(stream_key, extent, cuts, -0.22, 0.18) if cuts else 1.0
    values = jax.random.normal(stream_key, extent, jnp.float32) * width * factor_of
    return jnp.minimum(jnp.maximum(values, -most), most).astype(held_as)


def setup_inputs(seed: int = 0) -> dict:
    seeds = jax.random.split(jax.random.key(seed), 13)
    inputs = normal_values(seeds[0], (NDOCS, DOC_LEN, D), 1.0, 6.0, ((0, 8), (1, 4)))
    w_query = normal_values(seeds[1], (D, D), (4 * D) ** -0.5, 0.109375, ((0, 4),))
    w_key = normal_values(seeds[2], (D, D), (4 * D) ** -0.5, 0.109375, ((0, 4),))
    w_value = normal_values(seeds[3], (D, D), D ** -0.5, 0.21875, ((0, 4),))
    w_out = normal_values(seeds[4], (D, D), (D // 16) ** -0.5, 0.875, ((0, 4),))
    w_ffn_in = normal_values(seeds[5], (D, FF), D ** -0.5, 0.21875, ((0, 4),))
    w_ffn_out = normal_values(seeds[6], (FF, D), (FF // 2) ** -0.5, 0.15625, ((0, 4),))
    attn_gain = jnp.clip(1.0 + 0.18 * jax.random.normal(seeds[7], (D,), jnp.float32), 0.099609375, 1.8984375).astype(jnp.bfloat16)
    ffn_gain = jnp.clip(1.0 + 0.18 * jax.random.normal(seeds[8], (D,), jnp.float32), 0.099609375, 1.8984375).astype(jnp.bfloat16)
    rel_bias = normal_values(seeds[9], (NBUCKET, HEADS), 0.5, 3.0, ((0, 4),))
    doc_lengths = draw_doc_lengths(jax.random.fold_in(seeds[12], 71), 0)
    cotangent = normal_values(seeds[11], (NDOCS, DOC_LEN, D), 1.0, 6.0, ((0, 8), (1, 4)))
    return dict(inputs=inputs, w_query=w_query, w_key=w_key, w_value=w_value, w_out=w_out, w_ffn_in=w_ffn_in, w_ffn_out=w_ffn_out, attn_gain=attn_gain, ffn_gain=ffn_gain, rel_bias=rel_bias, doc_lengths=doc_lengths, cotangent=cotangent)


EPS = 1e-06
THRESHOLDS = (12, 16, 23, 32, 46, 64, 91)

@jax.custom_vjp
def low(v):
    return lax.optimization_barrier(v.astype(jnp.bfloat16)).astype(jnp.float32)

@jax.custom_vjp
def low_back(v):
    return v

def low_keep(v):
    return (low(v), None)

def low_pass(kept, grad):
    return (grad,)

def back_keep(v):
    return (v, None)

def back_low(kept, grad):
    return (low(grad),)
low.defvjp(low_keep, low_pass)
low_back.defvjp(back_keep, back_low)

def bucket_ids(query_pos, key_pos):
    offset = key_pos[None, :] - query_pos[:, None]
    distance = jnp.abs(offset)
    upper = jnp.where(offset > 0, 16, 0).astype(jnp.int32)
    beyond = jnp.full(distance.shape, 8, jnp.int32)
    for threshold in THRESHOLDS:
        beyond = beyond + (distance >= threshold).astype(jnp.int32)
    return upper + jnp.where(distance < 8, distance, beyond).astype(jnp.int32)

def project(left, weight):
    return jnp.einsum('gld,de->gle', left, weight, precision=lax.Precision.HIGHEST)

def rms_norm(source, gain):
    return source * lax.rsqrt(lax.optimization_barrier(jnp.mean(source * source, -1, keepdims=True)) + EPS) * gain

def group_forward(source, lengths, weights, buckets):
    w_query, w_key, w_value, w_out, w_ffn_in, w_ffn_out, attn_gain, ffn_gain, rel_bias = weights
    groups = source.shape[0]
    normed_one = low(rms_norm(source, attn_gain))
    queries = low_back(low(project(normed_one, w_query))).reshape(groups, DOC_LEN, HEADS, HEAD_DIM)
    keys = low_back(low(project(normed_one, w_key))).reshape(groups, DOC_LEN, HEADS, HEAD_DIM)
    values = low_back(low(project(normed_one, w_value))).reshape(groups, DOC_LEN, HEADS, HEAD_DIM)
    scores = jnp.einsum('gqhe,gkhe->ghqk', queries, keys, precision=lax.Precision.HIGHEST)
    bias = jnp.transpose(rel_bias[buckets], (2, 0, 1))
    positions = jnp.arange(DOC_LEN, dtype=jnp.int32)
    key_valid = positions[None, :] < lengths[:, None]
    logits = low_back(jnp.where(key_valid[:, None, None, :], scores + bias[None], -1000000000.0))
    probs = low(jax.nn.softmax(logits, axis=-1))
    mixed = jnp.einsum('ghqk,gkhe->gqhe', probs, values, precision=lax.Precision.HIGHEST)
    mixed = low_back(low(mixed.reshape(groups, DOC_LEN, D)))
    hidden = source + low_back(project(mixed, w_out))
    normed_two = low(rms_norm(hidden, ffn_gain))
    pre_act = low_back(project(normed_two, w_ffn_in))
    active = low(jax.nn.gelu(pre_act, approximate=True))
    return hidden + low_back(project(active, w_ffn_out))

def reference(inputs, w_query, w_key, w_value, w_out, w_ffn_in, w_ffn_out, attn_gain, ffn_gain, rel_bias, doc_lengths, cotangent):
    params = (w_query.astype(jnp.float32), w_key.astype(jnp.float32), w_value.astype(jnp.float32), w_out.astype(jnp.float32), w_ffn_in.astype(jnp.float32), w_ffn_out.astype(jnp.float32), attn_gain.astype(jnp.float32), ffn_gain.astype(jnp.float32), rel_bias.astype(jnp.float32))
    positions = jnp.arange(DOC_LEN, dtype=jnp.int32)
    buckets = bucket_ids(positions, positions)
    group = math.gcd(NDOCS, max(1, 4096 // DOC_LEN))
    rounds = NDOCS // group
    block = jax.checkpoint(group_forward)

    def forward(source, weights):
        stacked = source.reshape(rounds, group, DOC_LEN, D)
        lengths = doc_lengths.reshape(rounds, group)
        result = lax.map(lambda pair: block(pair[0], pair[1], weights, buckets), (stacked, lengths))
        return result.reshape(NDOCS, DOC_LEN, D)
    outputs, pull = jax.vjp(forward, inputs.astype(jnp.float32), params)
    valid = (positions[None, :] < doc_lengths[:, None]).astype(jnp.float32)
    pooled = lax.optimization_barrier(jnp.sum(outputs * valid[:, :, None], 1)) / doc_lengths[:, None].astype(jnp.float32)
    grad_input, grads = pull(cotangent.astype(jnp.float32) * valid[:, :, None])
    return (pooled, grad_input, grads[0], grads[1], grads[2], grads[3], grads[4], grads[5], grads[6], grads[7], grads[8])
```

```python
import math

import jax
import jax.numpy as jnp
from jax import lax
from jax.experimental import pallas as pl
from jax.experimental.pallas import tpu as pltpu
from jax.sharding import PartitionSpec as P

EPS = 1e-06
THRESHOLDS = (12, 16, 23, 32, 46, 64, 91)
NEGATIVE = -1000000000.0
GELU_C = math.sqrt(2.0 / math.pi)
GELU_K = 0.044715


def bucket_ids(query_pos, key_pos):
    offset = key_pos[None, :] - query_pos[:, None]
    distance = jnp.abs(offset)
    upper = jnp.where(offset > 0, 16, 0).astype(jnp.int32)
    beyond = jnp.full(distance.shape, 8, jnp.int32)
    for threshold in THRESHOLDS:
        beyond = beyond + (distance >= threshold).astype(jnp.int32)
    return upper + jnp.where(distance < 8, distance, beyond)


def gelu_slope(value):
    inner = GELU_C * (value + GELU_K * value * value * value)
    tangent = jnp.tanh(inner)
    return 0.5 * (1.0 + tangent) + 0.5 * value * (1.0 - tangent * tangent) * GELU_C * (
        1.0 + 3.0 * GELU_K * value * value
    )


def outer_sum(left, right):
    return lax.dot_general(
        left, right, (((0,), (0,)), ((), ())), preferred_element_type=jnp.float32
    )


def back_project(grad, weight):
    return lax.dot_general(
        grad, weight, (((1,), (1,)), ((), ())), preferred_element_type=jnp.float32
    )


def norm_backward(source, scale, gain, grad_normed):
    grad_gain = jnp.sum(grad_normed * source * scale, 0)
    grad_scaled = grad_normed * gain
    grad_source = scale * grad_scaled - source * scale * scale * scale * jnp.mean(
        grad_scaled * source, -1, keepdims=True
    )
    return (grad_gain, grad_source)


SEQ, CORES, DEPTH = 4, 2, 4
BLK = 128
MESH = pl.DeviceIdType.MESH
F32 = jnp.float32
BF16 = jnp.bfloat16


VMEM_LIMIT = 60 << 20


def contract(left, right, left_dim, right_dim):
    return lax.dot_general(
        left, right, (((left_dim,), (right_dim,)), ((), ())), preferred_element_type=F32
    )


def await_copy(ref, sem):
    pltpu.make_async_copy(ref, ref, sem).wait()


def tile(index, size):
    return pl.ds(pl.multiple_of(index * size, size), size)


def bucket_of(offset):
    distance = jnp.abs(offset)
    beyond = jnp.full(distance.shape, 8, jnp.int32)
    for threshold in THRESHOLDS:
        beyond = beyond + (distance >= threshold).astype(jnp.int32)
    return jnp.where(offset > 0, 16, 0) + jnp.where(distance < 8, distance, beyond)


def full_sum(value):
    return jnp.sum(jnp.sum(value, 0, keepdims=True), 1, keepdims=True)


def fused_kernel(
    inputs,
    cotangent,
    w_query,
    w_key,
    w_value,
    w_out,
    w_in,
    w_down,
    small,
    pooled_o,
    gx_o,
    gq_o,
    gk_o,
    gv_o,
    go_o,
    gi_o,
    gd_o,
    gs_o,
    xown,
    grads,
    nrm1,
    wqkv,
    qkv,
    mixed,
    wo,
    psend,
    precv,
    hid,
    nrm2,
    wi,
    wd,
    act,
    gpre,
    gn,
    strip,
    vecs,
    maskc,
    lse,
    flip,
    dqkv,
    gmix,
    dk_acc,
    dv_acc,
    ds_buf,
    near,
    far,
    gqkv,
    rs_d,
    rs_i,
    rs_o,
    rs_q,
    za_d,
    za_i,
    za_o,
    za_q,
    zb_d,
    zb_i,
    zb_o,
    zb_q,
    zc_d,
    zc_i,
    zc_o,
    zc_q,
    gx_send,
    gx_recv,
    small_all,
    gains,
    asum,
    pp,
    pool_recv,
    sg,
    sg_plane,
    sg_depth,
    small_ss,
    small_rs,
    x_ss,
    x_rs,
    c_ss,
    c_rs,
    wqkv_ss,
    wqkv_rs,
    wo_ss,
    wo_rs,
    wi_ss,
    wi_rs,
    wd_ss,
    wd_rs,
    n1_ss,
    n1_rs,
    g_ss,
    g_rs,
    part_ss,
    part_rs,
    n2_ss,
    n2_rs,
    gn2_ss,
    gn2_rs,
    gat_ss,
    gat_rs,
    gn1_ss,
    gn1_rs,
    gx_ss,
    gx_rs,
    rsd_ss,
    rsd_rs,
    rsi_ss,
    rsi_rs,
    rso_ss,
    rso_rs,
    rsq_ss,
    rsq_rs,
    z_ss,
    z_rs,
    pool_ss,
    pool_rs,
    sgp_ss,
    sgp_rs,
    sgz_ss,
    sgz_rs,
    out_ss,
):
    dp = lax.axis_index("dp")
    chip = lax.axis_index("seq")
    depth, core = lax.div(dp, 2), lax.rem(dp, 2)
    row, col = lax.div(chip, 2), lax.rem(chip, 2)
    other = (depth * 2 + 1 - core, chip)
    tokens, width = nrm1.shape
    half = width // 2
    rows_w = w_query.shape[0]
    ff_part = act.shape[1]

    def remote(src, dst, send, recv, device):
        return pltpu.make_async_remote_copy(
            src_ref=src,
            dst_ref=dst,
            send_sem=send,
            recv_sem=recv,
            device_id=device,
            device_id_type=MESH,
        )

    def ahead(step):
        return lax.rem(chip + step, SEQ)

    pending = []

    barrier = pltpu.get_barrier_semaphore()
    for step in range(SEQ):
        if step:
            pl.semaphore_signal(barrier, inc=1, device_id=(dp, ahead(step)), device_id_type=MESH)
        pl.semaphore_signal(
            barrier, inc=1, device_id=(other[0], ahead(step)), device_id_type=MESH
        )
    for step in range(1, DEPTH):
        pl.semaphore_signal(
            barrier,
            inc=1,
            device_id=(lax.rem(depth + step, DEPTH) * 2 + core, chip),
            device_id_type=MESH,
        )
    pl.semaphore_wait(barrier, 2 * SEQ - 1 + DEPTH - 1)

    local = pltpu.make_async_copy(small, small_all.at[0], small_rs.at[0])
    local.start()
    for step in range(1, SEQ):
        copy = remote(
            small, small_all.at[step], small_ss.at[step], small_rs.at[step], (dp, ahead(step))
        )
        copy.start()
        pending.append(copy)
    copy = remote(small, small_all.at[SEQ], small_ss.at[SEQ], small_rs.at[SEQ], other)
    copy.start()
    pending.append(copy)

    def spread(source, dest_of, send, recv):
        for doc in range(2):
            for to in range(2):
                block = source.at[doc, pl.ds(to * BLK, BLK)]
                target = core * 2 + doc
                own = (target == chip) & (core == to)

                @pl.when(own)
                def _():
                    pltpu.make_async_copy(block, dest_of(), recv.at[chip]).start()

                @pl.when(jnp.logical_not(own))
                def _():
                    remote(
                        block,
                        dest_of(),
                        send.at[doc * 2 + to],
                        recv.at[chip],
                        (depth * 2 + to, target),
                    ).start()

    def spread_done(source, dest_of, send, recv):
        for doc in range(2):
            for to in range(2):
                block = source.at[doc, pl.ds(to * BLK, BLK)]
                target = core * 2 + doc

                @pl.when(jnp.logical_not((target == chip) & (core == to)))
                def _():
                    remote(
                        block,
                        dest_of(),
                        send.at[doc * 2 + to],
                        recv.at[chip],
                        (depth * 2 + to, target),
                    ).wait_send()

    x_slot = lambda: xown.at[chip]
    spread(inputs, x_slot, x_ss, x_rs)

    def gather(src, dst, send, recv):
        pltpu.make_async_copy(src, dst, recv.at[0]).start()
        for step in range(1, SEQ):
            copy = remote(src, dst, send.at[step], recv.at[step], (dp, ahead(step)))
            copy.start()
            pending.append(copy)

    own_rows = tile(chip, rows_w)
    core_cols = tile(core, half)
    for i, w in enumerate((w_query, w_key, w_value)):
        gather(
            w.at[:, core_cols],
            wqkv.at[own_rows, pl.ds(i * half, half)],
            wqkv_ss.at[i],
            wqkv_rs.at[i],
        )

    wo_part = rows_w // 2
    wo_src = w_out.at[tile(core, wo_part)]
    wo_dst = wo.at[tile(col * 2 + core, wo_part)]

    def wo_each(action):
        for to in range(SEQ):
            own = (chip == to) & (core == row)
            copy = remote(
                wo_src, wo_dst, wo_ss.at[to], wo_rs.at[col * 2 + core], (depth * 2 + row, to)
            )
            if action == "start":

                @pl.when(own)
                def _():
                    pltpu.make_async_copy(wo_src, wo_dst, wo_rs.at[col * 2 + core]).start()

            @pl.when(jnp.logical_not(own))
            def _():
                if action == "start":
                    copy.start()
                else:
                    copy.wait_send()

    wo_each("start")
    for f in range(SEQ):
        gather(
            w_in.at[:, tile(f * 2 + core, ff_part)],
            wi.at[own_rows, pl.ds(f * ff_part, ff_part)],
            wi_ss.at[f],
            wi_rs.at[f],
        )
    c_slot = lambda: grads.at[chip * 2 + core]
    for doc in range(2):
        for to in range(2):
            block = cotangent.at[doc, pl.ds(to * BLK, BLK)]
            target = core * 2 + doc
            own = (target == chip) & (core == to)

            @pl.when(own)
            def _():
                pltpu.make_async_copy(block, grads.at[chip * 2 + to], c_rs.at[chip]).start()

            @pl.when(jnp.logical_not(own))
            def _():
                remote(
                    block,
                    grads.at[chip * 2 + to],
                    c_ss.at[doc * 2 + to],
                    c_rs.at[chip],
                    (depth * 2 + to, target),
                ).start()

    gather(w_down.at[tile(core, ff_part)], wd.at[tile(chip, ff_part)], wd_ss, wd_rs)

    for step in range(SEQ + 1):
        await_copy(small_all.at[step], small_rs.at[step])
    summed = small_all[0] + small_all[1] + small_all[2] + small_all[3]
    for which in range(2):
        gains[which : which + 1, :] = jnp.concatenate(
            [summed[8 * which + i : 8 * which + i + 1, :] for i in range(width // BLK)], axis=1
        )
    length_row = jnp.where(row == core, small_all[0, 6:7, :], small_all[SEQ, 6:7, :])
    length = jnp.where(col == 0, length_row[:, 0:1], length_row[:, 1:2])
    own_lengths = small_all[0, 6:7, 0:2]
    table = summed[16:48, :].astype(BF16)
    lane = lax.broadcasted_iota(jnp.int32, (1, 2 * BLK), 1)
    minus = jnp.where(lane < BLK, lane, lane - 2 * BLK)
    for off in (-1, 0, 1):
        ids = bucket_of(off * BLK - minus)
        onehot = (lax.broadcasted_iota(jnp.int32, (32, 2 * BLK), 0) == ids).astype(BF16)
        vecs[off + 1] = contract(table, onehot, 0, 0)[0:16, :]

    @pl.loop(0, 6)
    def _(h):
        values = [vecs[i, pl.ds(core * 6 + h, 1), :] for i in range(3)]
        left = jnp.broadcast_to(values[0][:, BLK - 1 : BLK], (BLK, BLK))
        right = jnp.broadcast_to(values[2][:, BLK + 1 : BLK + 2], (BLK, BLK))
        for i in range(6):
            strip[h, i * BLK : (i + 1) * BLK, :] = left
            strip[h, (i + 9) * BLK : (i + 10) * BLK, :] = right
        for i in range(3):
            skewed = pltpu.roll(
                jnp.broadcast_to(values[i], (BLK, 2 * BLK)), 0, 1, stride=1, stride_axis=0
            )
            strip[h, (i + 6) * BLK : (i + 7) * BLK, :] = skewed[:, :BLK]

    maskc[...] = jnp.where(
        lax.broadcasted_iota(jnp.int32, maskc.shape, 0).astype(F32) < length, 0.0, NEGATIVE
    )

    def block_valid(b):
        pos = lax.broadcasted_iota(jnp.int32, (BLK, 1), 0) + b * BLK
        return (pos.astype(F32) < length).astype(F32)

    def n1_copy(i):
        block = nrm1.at[tile(2 * i + core, BLK)]
        return remote(block, block, n1_ss.at[i], n1_rs.at[i], other)

    @pl.loop(0, SEQ)
    def _(i):
        await_copy(xown.at[i], x_rs.at[i])
        source = xown[i].astype(F32)
        scale = lax.rsqrt(jnp.mean(source * source, -1, keepdims=True) + EPS)
        nrm1[tile(2 * i + core, BLK), :] = (source * scale * gains[0:1, :]).astype(BF16)
        n1_copy(i).start()

    for i in range(3):
        for step in range(SEQ):
            await_copy(wqkv.at[pl.ds(0, rows_w), pl.ds(0, half)], wqkv_rs.at[i, step])
    for i in range(SEQ):
        n1_copy(i).wait_recv()

    quarter = tokens // 4

    @pl.loop(0, 4)
    def _(i):
        rows = tile(i, quarter)
        qkv[rows, :] = contract(nrm1[rows, :], wqkv[...], 1, 0).astype(BF16)

    lane_pair = lax.broadcasted_iota(jnp.int32, (1, BLK), 1)
    flip[BLK : BLK + 16, :] = jnp.ones((16, tokens), BF16)

    def scores(pair, qb, h):
        keys = qkv[:, tile(3 + pair, BLK)]
        queries = qkv[tile(qb, quarter), tile(pair, BLK)]
        queries = jnp.where((lane_pair < 64) == (h == 0), queries, jnp.zeros_like(queries))
        raw = contract(keys, queries, 1, 1)
        head = pair * 2 + h
        biases = [
            strip[head, pl.ds(pl.multiple_of((7 - 2 * qb - i) * BLK, BLK), tokens), :]
            + maskc[...]
            for i in range(2)
        ]
        return raw + jnp.concatenate(biases, axis=1), queries

    @pl.loop(0, 3)
    def _(pair):
        flip[0:BLK, :] = jnp.transpose(qkv[:, tile(6 + pair, BLK)])

        @pl.loop(0, 4)
        def _(qb):
            parts = []
            for h in range(2):
                logits, _ = scores(pair, qb, h)
                highest = jnp.max(logits, 0, keepdims=True)
                raised = jnp.exp(logits - highest).astype(BF16)
                result = contract(flip[...], raised, 1, 0)
                total = result[BLK : BLK + 1, :]
                lse[pl.ds(pair * 2 + h, 1), tile(qb, quarter)] = highest + jnp.log(total)
                parts.append(result[64 * h : 64 * h + 64, :] / total)
            mixed[tile(qb, quarter), tile(pair, BLK)] = jnp.transpose(
                jnp.concatenate(parts, axis=0)
            ).astype(BF16)

    def swap_copy(i, send, recv):
        return remote(psend.at[i], precv.at[i], send.at[i], recv.at[i], other)

    for k in range(4):
        await_copy(wo.at[pl.ds(k * wo_part, wo_part)], wo_rs.at[k])

    @pl.loop(0, SEQ)
    def _(i):
        psend[i] = contract(mixed[tile(2 * i + 1 - core, BLK), :], wo[...], 1, 0)
        swap_copy(i, part_ss, part_rs).start()

    def n2_copy(i, send, recv):
        block = nrm2.at[tile(2 * i + core, BLK)]
        return remote(block, block, send.at[i], recv.at[i], other)

    pp[...] = jnp.zeros_like(pp)

    @pl.loop(0, SEQ)
    def _(i):
        hidden = xown[i].astype(F32) + contract(
            mixed[tile(2 * i + core, BLK), :], wo[...], 1, 0
        )
        swap_copy(i, part_ss, part_rs).wait_recv()
        hidden = hidden + precv[i]
        hid[i] = hidden
        scale = lax.rsqrt(jnp.mean(hidden * hidden, -1, keepdims=True) + EPS)
        nrm2[tile(2 * i + core, BLK), :] = (hidden * scale * gains[1:2, :]).astype(BF16)
        n2_copy(i, n2_ss, n2_rs).start()
        pp[0:1, :] += jnp.sum(hidden * block_valid(2 * i + core), 0, keepdims=True)

    def g_copy(i):
        block = grads.at[2 * i + core]
        return remote(block, block, g_ss.at[i], g_rs.at[i], other)

    for f in range(SEQ):
        for step in range(SEQ):
            await_copy(wi.at[pl.ds(0, rows_w), pl.ds(0, ff_part)], wi_rs.at[f, step])

    @pl.loop(0, SEQ)
    def _(i):
        b = 2 * i + core
        await_copy(grads.at[b], c_rs.at[i])
        grads[b] = (grads[b].astype(F32) * block_valid(b)).astype(BF16)
        g_copy(i).start()

    for step in range(SEQ):
        await_copy(wd.at[pl.ds(0, ff_part)], wd_rs.at[step])
    for i in range(SEQ):
        n2_copy(i, n2_ss, n2_rs).wait_recv()
        g_copy(i).wait_recv()

    def rsd_copy(step):
        return remote(
            wd.at[tile(ahead(step), ff_part)],
            rs_d.at[step - 1],
            rsd_ss.at[step - 1],
            rsd_rs.at[step - 1],
            (dp, ahead(step)),
        )

    def rsi_copy(part, step):
        return remote(
            wi.at[tile(ahead(step), rows_w), tile(part, ff_part)],
            rs_i.at[step - 1, :, tile(part, ff_part)],
            rsi_ss.at[part, step - 1],
            rsi_rs.at[part, step - 1],
            (dp, ahead(step)),
        )

    @pl.loop(0, SEQ)
    def _(turn):
        f = lax.rem(chip + turn, SEQ)
        f_cols = tile(f, ff_part)
        asum[...] = jnp.zeros_like(asum)

        @pl.loop(0, 4)
        def _(i):
            rows = tile(i, quarter)
            value = contract(nrm2[rows, :], wi[:, f_cols], 1, 0)
            square = value * value
            tangent = jnp.tanh(GELU_C * (value + GELU_K * value * square))
            half_up = 0.5 * (1.0 + tangent)
            active = (value * half_up).astype(BF16)
            slope = half_up + 0.5 * value * (1.0 - tangent * tangent) * GELU_C * (
                1.0 + 3.0 * GELU_K * square
            )
            upstream = grads[pl.ds(2 * i, 2)].reshape(quarter, width)
            grad = (contract(upstream, wd[f_cols, :], 1, 1) * slope).astype(BF16)
            act[rows, :] = active
            gpre[rows, :] = grad
            pos = lax.broadcasted_iota(jnp.int32, (8, quarter), 1) + i * quarter
            valid = (pos.astype(F32) < length).astype(BF16)
            asum[...] += contract(valid, active, 1, 0)
            back = contract(grad, wi[:, f_cols], 1, 1)

            @pl.when(turn == 0)
            def _():
                gn[rows, :] = back

            @pl.when(turn > 0)
            def _():
                gn[rows, :] += back

        total = asum[0:1, :]
        high = total.astype(BF16)
        rest = total - high.astype(F32)
        middle = rest.astype(BF16)
        low = (rest - middle.astype(F32)).astype(BF16)
        for piece in (high, middle, low):
            pp[0:1, :] += contract(
                jnp.broadcast_to(piece, (16, ff_part)), wd[f_cols, :], 1, 0
            )[0:1, :]

        @pl.loop(0, ff_part // BLK)
        def _(i):
            down = contract(act[:, tile(i, BLK)], grads[...].reshape(tokens, width), 0, 0)
            wd[pl.ds(pl.multiple_of(f * ff_part + i * BLK, BLK), BLK), :] = down.astype(BF16)

        for step in range(1, SEQ):

            @pl.when(turn == step)
            def _():
                rsd_copy(step).start()

        @pl.loop(0, width // BLK)
        def _(i):
            wi[tile(i, BLK), f_cols] = contract(nrm2[:, tile(i, BLK)], gpre[...], 0, 0).astype(
                BF16
            )

        for step in range(1, SEQ):
            rsi_copy(f, step).start()

    def pool_each(action):
        for to in range(SEQ):
            own = (chip == to) & (core == row)
            dst = pool_recv.at[col * 2 + core]
            copy = remote(pp, dst, pool_ss.at[to], pool_rs.at[col * 2 + core], (depth * 2 + row, to))
            if action == "start":

                @pl.when(own)
                def _():
                    pltpu.make_async_copy(pp, dst, pool_rs.at[col * 2 + core]).start()

            @pl.when(jnp.logical_not(own))
            def _():
                if action == "start":
                    copy.start()
                else:
                    copy.wait_send()

    pool_each("start")

    for i in range(SEQ):
        swap_copy(i, part_ss, part_rs).wait_send()
        n2_copy(i, n2_ss, n2_rs).wait_send()

    @pl.loop(0, SEQ)
    def _(i):
        psend[i] = gn[tile(2 * i + 1 - core, BLK), :]
        swap_copy(i, gn2_ss, gn2_rs).start()

    sg[...] = jnp.zeros_like(sg)

    def add_gain(first, value):
        for i in range(width // BLK):
            sg[first + i : first + i + 1, :] += value[:, i * BLK : (i + 1) * BLK]

    @pl.loop(0, SEQ)
    def _(i):
        b = 2 * i + core
        swap_copy(i, gn2_ss, gn2_rs).wait_recv()
        normed = gn[tile(b, BLK), :] + precv[i]
        hidden = hid[i]
        scale = lax.rsqrt(jnp.mean(hidden * hidden, -1, keepdims=True) + EPS)
        add_gain(8, jnp.sum(normed * hidden * scale, 0, keepdims=True))
        scaled = normed * gains[1:2, :]
        inner = jnp.mean(scaled * hidden, -1, keepdims=True)
        result = grads[b].astype(F32) + scale * scaled - hidden * (scale * scale * scale) * inner
        hid[i] = result
        nrm2[tile(b, BLK), :] = result.astype(BF16)
        n2_copy(i, gat_ss, gat_rs).start()

    for i in range(SEQ):
        n2_copy(i, gat_ss, gat_rs).wait_recv()

    @pl.loop(0, 4)
    def _(i):
        rows = tile(i, quarter)
        gmix[rows, :] = contract(nrm2[rows, :], wo[...], 1, 1).astype(BF16)

    wo_each("wait")

    @pl.loop(0, half // BLK)
    def _(i):
        wo[tile(i, BLK), :] = contract(mixed[:, tile(i, BLK)], nrm2[...], 0, 0).astype(BF16)

    def rso_each(action):
        for k in range(2):
            for to in range(2):
                target = core * 2 + k
                own = (chip == target) & (core == to)
                src = wo.at[pl.ds((2 * k + to) * wo_part, wo_part)]
                dst = rs_o.at[chip]
                copy = remote(
                    src, dst, rso_ss.at[2 * k + to], rso_rs.at[chip], (depth * 2 + to, target)
                )
                if action == "start":

                    @pl.when(own)
                    def _():
                        pltpu.make_async_copy(src, dst, rso_rs.at[chip]).start()

                @pl.when(jnp.logical_not(own))
                def _():
                    if action == "start":
                        copy.start()
                    else:
                        copy.wait_send()

    rso_each("start")

    sub = lax.broadcasted_iota(jnp.int32, (16, tokens), 0)
    key_block = lax.div(lax.broadcasted_iota(jnp.int32, (16, tokens), 1), BLK)
    flip[BLK : BLK + 16, :] = (sub == key_block).astype(BF16)
    near[...] = jnp.zeros_like(near)
    far[...] = jnp.zeros_like(far)
    ds_buf[0:BLK, :] = jnp.zeros((BLK, quarter), BF16)
    ds_buf[tokens + BLK :, :] = jnp.zeros((BLK, quarter), BF16)

    def rsq_copy(pair, step):
        return remote(
            gqkv.at[pair, tile(ahead(step), rows_w)],
            rs_q.at[pair, step - 1],
            rsq_ss.at[pair, step - 1],
            rsq_rs.at[pair, step - 1],
            (dp, ahead(step)),
        )

    @pl.loop(0, 3)
    def _(pair):
        flip[0:BLK, :] = jnp.transpose(qkv[:, tile(3 + pair, BLK)])
        dk_acc[...] = jnp.zeros_like(dk_acc)
        dv_acc[...] = jnp.zeros_like(dv_acc)

        @pl.loop(0, 4)
        def _(qb):
            rows = tile(qb, quarter)
            cols = tile(pair, BLK)
            upstream = gmix[rows, cols]
            product = jnp.transpose(upstream.astype(F32) * mixed[rows, cols].astype(F32))
            parts = []
            for h in range(2):
                head = pair * 2 + h
                logits, queries = scores(pair, qb, h)
                probs = jnp.exp(logits - lse[pl.ds(head, 1), rows])
                masked = jnp.where((lane_pair < 64) == (h == 0), upstream, jnp.zeros_like(upstream))
                grad_probs = contract(qkv[:, tile(6 + pair, BLK)], masked, 1, 1)
                inner = jnp.sum(product[64 * h : 64 * h + 64, :], 0, keepdims=True)
                grad_logits = (probs * (grad_probs - inner)).astype(BF16)
                dv_acc[...] += contract(probs.astype(BF16), masked, 1, 0)
                dk_acc[...] += contract(grad_logits, queries, 1, 0)
                ds_buf[BLK : tokens + BLK, :] = grad_logits
                result = contract(flip[...], grad_logits, 1, 0)
                parts.append(result[64 * h : 64 * h + 64, :])
                sums = result[BLK : BLK + 8, :]
                block_row = lax.broadcasted_iota(jnp.int32, sums.shape, 0)
                query_block = 2 * qb + lax.div(
                    lax.broadcasted_iota(jnp.int32, sums.shape, 1), BLK
                )
                gap = block_row - query_block
                far[head, 0:8, :] += jnp.where(gap <= -2, sums, 0.0)
                far[head, 8:16, :] += jnp.where(gap >= 2, sums, 0.0)
                for i in range(2):
                    for off in range(3):
                        start = pl.multiple_of((2 * qb + i + off) * BLK, BLK)
                        near[head * 3 + off] += ds_buf[
                            pl.ds(start, BLK), i * BLK : (i + 1) * BLK
                        ].astype(F32)
            dqkv[rows, cols] = jnp.transpose(jnp.concatenate(parts, axis=0)).astype(BF16)

        dqkv[:, tile(3 + pair, BLK)] = dk_acc[...].astype(BF16)
        dqkv[:, tile(6 + pair, BLK)] = dv_acc[...].astype(BF16)

        @pl.loop(0, width // BLK)
        def _(i):
            source = nrm1[:, tile(i, BLK)]
            for j in range(3):
                gqkv[pair, tile(i, BLK), j * BLK : (j + 1) * BLK] = contract(
                    source, dqkv[:, tile(3 * j + pair, BLK)], 0, 0
                ).astype(BF16)

        for step in range(1, SEQ):
            rsq_copy(pair, step).start()

    for i in range(SEQ):
        swap_copy(i, gn2_ss, gn2_rs).wait_send()

    @pl.loop(0, SEQ)
    def _(i):
        psend[i] = contract(dqkv[tile(2 * i + 1 - core, BLK), :], wqkv[...], 1, 1)
        swap_copy(i, gn1_ss, gn1_rs).start()

    def gx_each(i, action):
        own = (chip == i) & (core == row)
        dst = gx_recv.at[col * 2 + core]
        copy = remote(
            gx_send.at[i], dst, gx_ss.at[i], gx_rs.at[col * 2 + core], (depth * 2 + row, i)
        )
        if action == "start":

            @pl.when(own)
            def _():
                pltpu.make_async_copy(gx_send.at[i], dst, gx_rs.at[col * 2 + core]).start()

        @pl.when(jnp.logical_not(own))
        def _():
            if action == "start":
                copy.start()
            else:
                copy.wait_send()

    @pl.loop(0, SEQ)
    def _(i):
        own = contract(dqkv[tile(2 * i + core, BLK), :], wqkv[...], 1, 1)
        swap_copy(i, gn1_ss, gn1_rs).wait_recv()
        normed = own + precv[i]
        source = xown[i].astype(F32)
        scale = lax.rsqrt(jnp.mean(source * source, -1, keepdims=True) + EPS)
        add_gain(0, jnp.sum(normed * source * scale, 0, keepdims=True))
        scaled = normed * gains[0:1, :]
        inner = jnp.mean(scaled * source, -1, keepdims=True)
        result = hid[i] + scale * scaled - source * (scale * scale * scale) * inner
        gx_send[i] = result.astype(BF16)
        gx_each(i, "start")

    diag_row = lax.broadcasted_iota(jnp.int32, (BLK, BLK), 0)
    diag_col = lax.broadcasted_iota(jnp.int32, (BLK, BLK), 1)
    upper = diag_col >= diag_row
    mirror = (diag_row + diag_col == BLK - 1).astype(F32)
    shift = lax.broadcasted_iota(jnp.int32, (1, BLK), 1) + 1
    shift = jnp.where(shift == BLK, 0, shift)
    ids = bucket_of(jnp.concatenate([-shift, BLK - shift], axis=1))
    onehot = (lax.broadcasted_iota(jnp.int32, (BLK, 2 * BLK), 0) == ids).astype(F32)
    bucket_lane = lax.broadcasted_iota(jnp.int32, (1, BLK), 1)

    @pl.loop(0, 6)
    def _(h):
        def skew(x):
            mirrored = lax.dot_general(
                mirror,
                x,
                (((1,), (0,)), ((), ())),
                preferred_element_type=F32,
                precision=lax.Precision.HIGHEST,
            )
            return pltpu.roll(mirrored, 0, 1, stride=1, stride_axis=0)

        tiles = [near[h * 3 + i] for i in range(3)]
        at = [
            jnp.sum(
                skew(jnp.where(upper, tiles[i + 1], 0.0) + jnp.where(upper, 0.0, tiles[i])),
                0,
                keepdims=True,
            )
            for i in range(2)
        ]
        below = full_sum(jnp.where(upper, tiles[0], 0.0)) + full_sum(far[h, 0:8, :])
        above = full_sum(jnp.where(upper, 0.0, tiles[2])) + full_sum(far[h, 8:16, :])
        sums = lax.dot_general(
            jnp.broadcast_to(jnp.concatenate(at, axis=1), (8, 2 * BLK)),
            onehot,
            (((1,), (1,)), ((), ())),
            preferred_element_type=F32,
            precision=lax.Precision.HIGHEST,
        )[0:1, :]
        sums = sums + jnp.where(bucket_lane == 15, below, 0.0)
        sums = sums + jnp.where(bucket_lane == 31, above, 0.0)
        sg[pl.ds(16 + core * 8 + h, 1), :] = sums

    place = core * SEQ + chip

    def sgp_each(action):
        for step in range(SEQ):
            for cross in range(2):
                if step == 0 and cross == 0:
                    continue
                to = ahead(step)
                to_core = lax.rem(core + cross, 2)
                copy = remote(
                    sg,
                    sg_plane.at[place],
                    sgp_ss.at[step * 2 + cross],
                    sgp_rs.at[place],
                    (depth * 2 + to_core, to),
                )
                if action == "start":
                    copy.start()
                else:
                    copy.wait_send()

    sgp_each("start")
    pltpu.make_async_copy(sg, sg_plane.at[place], sgp_rs.at[place]).start()

    inner_z = (depth == 1) | (depth == 2)
    end_z = jnp.logical_not(inner_z)
    toward = jnp.where(depth == 0, 1, 2)
    outward = jnp.where(depth == 1, 0, 3)
    across = jnp.where(depth == 1, 2, 1)

    def z_dev(z):
        return (z * 2 + core, chip)

    items = []

    def item(reduced, za, zb, final, zc):
        index = len(items)
        sem = lambda i: (z_ss.at[index, i], z_rs.at[index, i])
        items.append(
            dict(
                reduced=reduced,
                za=za,
                zb=zb,
                final=final,
                zc=zc,
                to_inner=remote(reduced, za, *sem(0), z_dev(toward)),
                swap=remote(reduced, zb, *sem(1), z_dev(across)),
                to_end=remote(final, final, *sem(2), z_dev(outward)),
                to_core=remote(final, zc, *sem(3), other),
            )
        )

    def stage_first(it):
        @pl.when(end_z)
        def _():
            it["to_inner"].start()

    def stage_second(it):
        @pl.when(inner_z)
        def _():
            it["to_inner"].wait_recv()
            it["reduced"][...] = (
                it["reduced"][...].astype(F32) + it["za"][...].astype(F32)
            ).astype(BF16)
            it["swap"].start()

    def stage_third(it):
        @pl.when(inner_z)
        def _():
            it["swap"].wait_recv()
            it["final"][...] = (
                it["reduced"][...].astype(F32) + it["zb"][...].astype(F32)
            ).astype(BF16)
            it["to_end"].start()

    def stage_fourth(it):
        @pl.when(end_z)
        def _():
            it["to_end"].wait_recv()

        it["to_core"].start()

    def add_up(dest, sources):
        total = sources[0][...].astype(F32)
        for more in sources[1:]:
            total = total + more[...].astype(F32)
        dest[...] = total.astype(BF16)

    for step in range(1, SEQ):
        rsd_copy(step).wait_recv()
    own_down = wd.at[tile(chip, ff_part)]
    add_up(rs_d.at[0], [own_down, rs_d.at[0], rs_d.at[1], rs_d.at[2]])
    item(rs_d.at[0], za_d, zb_d, rs_d.at[1], zc_d)
    stage_first(items[0])
    for part in range(SEQ):
        for step in range(1, SEQ):
            rsi_copy(part, step).wait_recv()
    add_up(rs_i.at[0], [wi.at[tile(chip, rows_w)], rs_i.at[0], rs_i.at[1], rs_i.at[2]])
    item(rs_i.at[0], za_i, zb_i, rs_i.at[1], zc_i)
    stage_first(items[1])
    stage_second(items[0])
    for i in range(SEQ):
        await_copy(rs_o.at[i], rso_rs.at[i])
    add_up(rs_o.at[0], [rs_o.at[0], rs_o.at[1], rs_o.at[2], rs_o.at[3]])
    item(rs_o.at[0], za_o, zb_o, rs_o.at[1], zc_o)
    stage_first(items[2])
    stage_second(items[1])
    stage_third(items[0])
    for pair in range(3):
        for step in range(1, SEQ):
            rsq_copy(pair, step).wait_recv()
        q = rs_q.at[pair]
        add_up(q.at[0], [gqkv.at[pair, tile(chip, rows_w)], q.at[0], q.at[1], q.at[2]])
        item(q.at[0], za_q.at[pair], zb_q.at[pair], q.at[1], zc_q.at[pair])
        stage_first(items[3 + pair])
        stage_second(items[2 + pair])
        stage_third(items[1 + pair])
        stage_fourth(items[pair])
    for i in range(8):
        await_copy(sg_plane.at[i], sgp_rs.at[i])
    total = sg_plane[0]
    for i in range(1, 8):
        total = total + sg_plane[i]
    sg_depth[depth] = total

    def sgz_copy(step):
        return remote(
            sg_depth.at[depth],
            sg_depth.at[depth],
            sgz_ss.at[step],
            sgz_rs.at[depth],
            z_dev(lax.rem(depth + step, DEPTH)),
        )

    for step in range(1, DEPTH):
        sgz_copy(step).start()
    stage_second(items[5])
    stage_third(items[4])
    stage_fourth(items[3])
    stage_third(items[5])
    stage_fourth(items[4])
    stage_fourth(items[5])

    for i in range(4):
        await_copy(gx_recv.at[i], gx_rs.at[i])
    for i in range(4):
        hid[i] = gx_recv[i].astype(F32)
    out_copies = []
    for i in range(4):
        copy = pltpu.make_async_copy(
            hid.at[i], gx_o.at[i // 2, pl.ds((i % 2) * BLK, BLK)], out_ss.at[i]
        )
        copy.start()
        out_copies.append(copy)
    for i in range(4):
        await_copy(pool_recv.at[i], pool_rs.at[i])
    for doc in range(2):
        pooled_o[doc : doc + 1, :] = (
            pool_recv[2 * doc, 0:1, :] + pool_recv[2 * doc + 1, 0:1, :]
        ) / own_lengths[:, doc : doc + 1]

    for it in items:
        it["to_core"].wait_recv()
    other_core = 1 - core
    for k, (src, c) in enumerate(((rs_d.at[1], core), (zc_d, other_core))):
        for i in range(ff_part // BLK):
            rows = pl.ds(pl.multiple_of(c * ff_part + i * BLK, BLK), BLK)
            gn[rows, :] = src[i * BLK : (i + 1) * BLK, :].astype(F32)
    copy = pltpu.make_async_copy(gn.at[pl.ds(0, 2 * ff_part)], gd_o, out_ss.at[4])
    copy.start()
    out_copies.append(copy)
    for src, c in ((rs_i.at[1], core), (zc_i, other_core)):
        for f in range(SEQ):
            gi_o[:, tile(2 * f + c, ff_part)] = src[:, f * ff_part : (f + 1) * ff_part].astype(F32)
    for src, c in ((rs_o.at[1], core), (zc_o, other_core)):
        go_o[tile(c, wo_part), :] = src[...].astype(F32)
    for pair in range(3):
        for src, c in ((rs_q.at[pair, 1], core), (zc_q.at[pair], other_core)):
            for j, out in enumerate((gq_o, gk_o, gv_o)):
                out[:, tile(c * 3 + pair, BLK)] = src[:, j * BLK : (j + 1) * BLK].astype(F32)
    for step in range(1, DEPTH):
        z = lax.rem(depth + DEPTH - step, DEPTH)
        await_copy(sg_depth.at[z], sgz_rs.at[z])
    gs_o[...] = sg_depth[0] + sg_depth[1] + sg_depth[2] + sg_depth[3]

    for copy in out_copies:
        copy.wait()
    for copy in pending:
        copy.wait_send()
    spread_done(inputs, x_slot, x_ss, x_rs)
    spread_done(cotangent, c_slot, c_ss, c_rs)
    pool_each("wait")
    rso_each("wait")
    sgp_each("wait")
    for i in range(SEQ):
        n1_copy(i).wait_send()
        g_copy(i).wait_send()
        n2_copy(i, gat_ss, gat_rs).wait_send()
        swap_copy(i, gn1_ss, gn1_rs).wait_send()
        gx_each(i, "wait")
    for step in range(1, SEQ):
        rsd_copy(step).wait_send()
        sgz_copy(step).wait_send()
        for part in range(SEQ):
            rsi_copy(part, step).wait_send()
        for pair in range(3):
            rsq_copy(pair, step).wait_send()
    for it in items:

        @pl.when(end_z)
        def _():
            it["to_inner"].wait_send()

        @pl.when(inner_z)
        def _():
            it["swap"].wait_send()
            it["to_end"].wait_send()

        it["to_core"].wait_send()


def on_device(
    inputs,
    w_query,
    w_key,
    w_value,
    w_out,
    w_ffn_in,
    w_ffn_out,
    attn_gain,
    ffn_gain,
    rel_bias,
    doc_lengths,
    cotangent,
):
    blocks, shard_len, width = inputs.shape
    heads = rel_bias.shape[1]
    head_dim = width // heads
    full_len = shard_len * lax.axis_size("seq")
    total_rows = blocks * shard_len
    gathered = (
        lax.all_gather(w_query, "seq", axis=0, tiled=True),
        lax.all_gather(w_key, "seq", axis=0, tiled=True),
        lax.all_gather(w_value, "seq", axis=0, tiled=True),
        lax.all_gather(w_out, "seq", axis=0, tiled=True),
        lax.all_gather(w_ffn_in, "seq", axis=0, tiled=True),
        lax.all_gather(w_ffn_out, "seq", axis=0, tiled=True),
        lax.all_gather(attn_gain, "seq", axis=0, tiled=True),
        lax.all_gather(ffn_gain, "seq", axis=0, tiled=True),
        lax.all_gather(rel_bias, "seq", axis=0, tiled=True),
    )
    (
        full_query,
        full_key,
        full_value,
        full_out,
        full_in,
        full_down,
        gain_one,
        gain_two,
        bias_table,
    ) = gathered
    gain_one = gain_one.astype(jnp.float32)
    gain_two = gain_two.astype(jnp.float32)
    bucket_range = jnp.arange(bias_table.shape[0], dtype=jnp.int32)
    query_pos = lax.axis_index("seq") * shard_len + jnp.arange(shard_len, dtype=jnp.int32)
    key_pos = jnp.arange(full_len, dtype=jnp.int32)
    onehot = (bucket_ids(query_pos, key_pos)[:, :, None] == bucket_range).astype(jnp.bfloat16)
    bias_heads = jnp.einsum("qkn,nh->hqk", onehot, bias_table, preferred_element_type=jnp.float32)
    key_valid = key_pos[None, :] < doc_lengths[:, None]
    query_valid = (query_pos[None, :] < doc_lengths[:, None]).astype(jnp.float32)
    flat = inputs.astype(jnp.float32).reshape(total_rows, width)
    scale_one = lax.rsqrt(jnp.mean(flat * flat, -1, keepdims=True) + EPS)
    normed_one = (flat * scale_one * gain_one).astype(jnp.bfloat16)
    queries = jnp.dot(normed_one, full_query, preferred_element_type=jnp.float32).astype(
        jnp.bfloat16
    )
    keys_local = jnp.dot(normed_one, full_key, preferred_element_type=jnp.float32).astype(
        jnp.bfloat16
    )
    values_local = jnp.dot(normed_one, full_value, preferred_element_type=jnp.float32).astype(
        jnp.bfloat16
    )
    queries_heads = queries.reshape(blocks, shard_len, heads, head_dim)
    keys_all, values_all = (
        lax.all_gather(keys_local.reshape(blocks, shard_len, width), "seq", axis=1, tiled=True),
        lax.all_gather(values_local.reshape(blocks, shard_len, width), "seq", axis=1, tiled=True),
    )
    scores = jnp.einsum(
        "bqhe,bkhe->bhqk",
        queries_heads,
        keys_all.reshape(blocks, full_len, heads, head_dim),
        preferred_element_type=jnp.float32,
    )
    logits = jnp.where(key_valid[:, None, None, :], scores + bias_heads[None], NEGATIVE)
    highest = jnp.max(logits, -1, keepdims=True)
    log_total = highest + jnp.log(jnp.sum(jnp.exp(logits - highest), -1, keepdims=True))
    probs_low = jnp.exp(logits - log_total).astype(jnp.bfloat16)
    mixed = jnp.einsum(
        "bhqk,bkhe->bqhe",
        probs_low,
        values_all.reshape(blocks, full_len, heads, head_dim),
        preferred_element_type=jnp.float32,
    )
    mixed = mixed.astype(jnp.bfloat16).reshape(total_rows, width)
    hidden = flat + jnp.dot(mixed, full_out, preferred_element_type=jnp.float32)
    scale_two = lax.rsqrt(jnp.mean(hidden * hidden, -1, keepdims=True) + EPS)
    normed_two = (hidden * scale_two * gain_two).astype(jnp.bfloat16)
    pre_act = jnp.dot(normed_two, full_in, preferred_element_type=jnp.float32)
    active = jax.nn.gelu(pre_act, approximate=True).astype(jnp.bfloat16)
    outputs = hidden + jnp.dot(active, full_down, preferred_element_type=jnp.float32)
    partial_pool = jnp.sum(outputs.reshape(blocks, shard_len, width) * query_valid[:, :, None], 1)
    pooled = lax.psum(partial_pool, "seq") / doc_lengths[:, None].astype(jnp.float32)
    regathered = (
        lax.all_gather(w_query, "seq", axis=0, tiled=True),
        lax.all_gather(w_key, "seq", axis=0, tiled=True),
        lax.all_gather(w_value, "seq", axis=0, tiled=True),
        lax.all_gather(w_out, "seq", axis=0, tiled=True),
        lax.all_gather(w_ffn_in, "seq", axis=0, tiled=True),
        lax.all_gather(w_ffn_out, "seq", axis=0, tiled=True),
        lax.all_gather(attn_gain, "seq", axis=0, tiled=True),
        lax.all_gather(ffn_gain, "seq", axis=0, tiled=True),
    )
    full_query, full_key, full_value, full_out, full_in, full_down, gain_back_one, gain_back_two = (
        regathered
    )
    gain_one = gain_back_one.astype(jnp.float32)
    gain_two = gain_back_two.astype(jnp.float32)
    grad_out = (cotangent.astype(jnp.float32) * query_valid[:, :, None]).reshape(total_rows, width)
    grad_branch = grad_out.astype(jnp.bfloat16)
    grad_down = outer_sum(active, grad_branch)
    grad_pre = (back_project(grad_branch, full_down) * gelu_slope(pre_act)).astype(jnp.bfloat16)
    grad_in = outer_sum(normed_two, grad_pre)
    grad_normed_two = back_project(grad_pre, full_in)
    grad_gain_two, grad_hidden_norm = norm_backward(hidden, scale_two, gain_two, grad_normed_two)
    grad_hidden = grad_out + grad_hidden_norm
    grad_attended = grad_hidden.astype(jnp.bfloat16)
    grad_out_proj = outer_sum(mixed, grad_attended)
    grad_mixed = (
        back_project(grad_attended, full_out)
        .astype(jnp.bfloat16)
        .reshape(blocks, shard_len, heads, head_dim)
    )
    keys_back, values_back = (keys_all, values_all)
    probs = jnp.exp(logits - log_total)
    grad_probs = jnp.einsum(
        "bqhe,bkhe->bhqk",
        grad_mixed,
        values_back.reshape(blocks, full_len, heads, head_dim),
        preferred_element_type=jnp.float32,
    )
    inner_term = jnp.sum(probs * grad_probs, -1, keepdims=True)
    grad_logits = (probs * (grad_probs - inner_term)).astype(jnp.bfloat16)
    grad_queries = jnp.einsum(
        "bhqk,bkhe->bqhe",
        grad_logits,
        keys_back.reshape(blocks, full_len, heads, head_dim),
        preferred_element_type=jnp.float32,
    )
    grad_queries = grad_queries.astype(jnp.bfloat16).reshape(total_rows, width)
    grad_table = jnp.einsum("bhqk,qkn->nh", grad_logits, onehot, preferred_element_type=jnp.float32)
    key_terms = jnp.einsum(
        "bhqk,bqhe->bkhe", grad_logits, queries_heads, preferred_element_type=jnp.float32
    ).reshape(blocks, full_len, width)
    value_terms = jnp.einsum(
        "bhqk,bqhe->bkhe", probs_low, grad_mixed, preferred_element_type=jnp.float32
    ).reshape(blocks, full_len, width)
    grad_keys, grad_values = (
        lax.psum_scatter(
            key_terms.astype(jnp.bfloat16), "seq", scatter_dimension=1, tiled=True
        ).astype(jnp.float32),
        lax.psum_scatter(
            value_terms.astype(jnp.bfloat16), "seq", scatter_dimension=1, tiled=True
        ).astype(jnp.float32),
    )
    grad_keys = grad_keys.astype(jnp.bfloat16).reshape(total_rows, width)
    grad_values = grad_values.astype(jnp.bfloat16).reshape(total_rows, width)
    grad_query_w = outer_sum(normed_one, grad_queries)
    grad_key_w = outer_sum(normed_one, grad_keys)
    grad_value_w = outer_sum(normed_one, grad_values)
    grad_normed_one = (
        back_project(grad_queries, full_query)
        + back_project(grad_keys, full_key)
        + back_project(grad_values, full_value)
    )
    grad_gain_one, grad_input_norm = norm_backward(flat, scale_one, gain_one, grad_normed_one)
    grad_input = (grad_hidden + grad_input_norm).reshape(blocks, shard_len, width)
    shards = (
        lax.psum_scatter(
            grad_query_w.astype(jnp.bfloat16), "seq", scatter_dimension=0, tiled=True
        ).astype(jnp.float32),
        lax.psum_scatter(
            grad_key_w.astype(jnp.bfloat16), "seq", scatter_dimension=0, tiled=True
        ).astype(jnp.float32),
        lax.psum_scatter(
            grad_value_w.astype(jnp.bfloat16), "seq", scatter_dimension=0, tiled=True
        ).astype(jnp.float32),
        lax.psum_scatter(
            grad_out_proj.astype(jnp.bfloat16), "seq", scatter_dimension=0, tiled=True
        ).astype(jnp.float32),
        lax.psum_scatter(
            grad_in.astype(jnp.bfloat16), "seq", scatter_dimension=0, tiled=True
        ).astype(jnp.float32),
        lax.psum_scatter(
            grad_down.astype(jnp.bfloat16), "seq", scatter_dimension=0, tiled=True
        ).astype(jnp.float32),
        lax.psum_scatter(
            grad_gain_one.astype(jnp.bfloat16), "seq", scatter_dimension=0, tiled=True
        ).astype(jnp.float32),
        lax.psum_scatter(
            grad_gain_two.astype(jnp.bfloat16), "seq", scatter_dimension=0, tiled=True
        ).astype(jnp.float32),
        lax.psum_scatter(
            grad_table.astype(jnp.bfloat16), "seq", scatter_dimension=0, tiled=True
        ).astype(jnp.float32),
    )
    totals = (
        lax.psum(shards[0].astype(jnp.bfloat16), "dp").astype(jnp.float32),
        lax.psum(shards[1].astype(jnp.bfloat16), "dp").astype(jnp.float32),
        lax.psum(shards[2].astype(jnp.bfloat16), "dp").astype(jnp.float32),
        lax.psum(shards[3].astype(jnp.bfloat16), "dp").astype(jnp.float32),
        lax.psum(shards[4].astype(jnp.bfloat16), "dp").astype(jnp.float32),
        lax.psum(shards[5].astype(jnp.bfloat16), "dp").astype(jnp.float32),
        lax.psum(shards[6].astype(jnp.bfloat16), "dp").astype(jnp.float32),
        lax.psum(shards[7].astype(jnp.bfloat16), "dp").astype(jnp.float32),
        lax.psum(shards[8].astype(jnp.bfloat16), "dp").astype(jnp.float32),
    )
    return (
        pooled,
        grad_input,
        totals[0],
        totals[1],
        totals[2],
        totals[3],
        totals[4],
        totals[5],
        totals[6],
        totals[7],
        totals[8],
    )


def fused_on_device(
    inputs,
    w_query,
    w_key,
    w_value,
    w_out,
    w_ffn_in,
    w_ffn_out,
    attn_gain,
    ffn_gain,
    rel_bias,
    doc_lengths,
    cotangent,
):
    docs, shard_len, width = inputs.shape
    rows_w, hidden_units = w_ffn_in.shape
    tokens = shard_len * SEQ
    half = width // 2
    part = hidden_units // (2 * SEQ)
    blocks = tokens // BLK
    pairs = half // BLK
    buckets, heads = rel_bias.shape[0] * SEQ, rel_bias.shape[1]
    chip = lax.axis_index("seq")
    here = (jnp.arange(SEQ, dtype=jnp.int32) == chip).astype(F32)

    def placed(value):
        value = value.astype(F32)
        return (here.reshape((SEQ,) + (1,) * value.ndim) * value).reshape(
            (-1,) + value.shape[1:]
        )

    lengths = jnp.pad(doc_lengths.astype(F32).reshape(1, docs), ((0, 1), (0, BLK - docs)))
    small = jnp.concatenate(
        [
            placed(attn_gain).reshape(width // BLK, BLK),
            lengths,
            placed(ffn_gain).reshape(width // BLK, BLK),
            jnp.zeros((2, BLK), F32),
            jnp.pad(placed(rel_bias), ((0, 0), (0, BLK - heads))),
        ],
        axis=0,
    )
    anywhere = pl.BlockSpec(memory_space=pl.ANY)
    vmem = pl.BlockSpec(memory_space=pltpu.VMEM)
    shape = jax.ShapeDtypeStruct
    out_shape = (
        shape((docs, width), F32),
        shape((docs, shard_len, width), F32),
        shape((rows_w, width), F32),
        shape((rows_w, width), F32),
        shape((rows_w, width), F32),
        shape((rows_w, width), F32),
        shape((rows_w, hidden_units), F32),
        shape((2 * part, width), F32),
        shape((32, BLK), F32),
    )
    out_specs = (vmem, anywhere, vmem, vmem, vmem, vmem, vmem, anywhere, vmem)
    quarter = tokens // 4
    out_part = rows_w // 2
    scratch = [
        ((SEQ, BLK, width), BF16),
        ((blocks, BLK, width), BF16),
        ((tokens, width), BF16),
        ((width, 3 * half), BF16),
        ((tokens, 3 * half), BF16),
        ((tokens, half), BF16),
        ((half, width), BF16),
        ((SEQ, BLK, width), F32),
        ((SEQ, BLK, width), F32),
        ((SEQ, BLK, width), F32),
        ((tokens, width), BF16),
        ((width, SEQ * part), BF16),
        ((SEQ * part, width), BF16),
        ((tokens, part), BF16),
        ((tokens, part), BF16),
        ((tokens, width), F32),
        ((2 * pairs, 2 * tokens - BLK, BLK), F32),
        ((3, 16, 2 * BLK), F32),
        ((tokens, BLK), F32),
        ((8, tokens), F32),
        ((BLK + 16, tokens), BF16),
        ((tokens, 3 * half), BF16),
        ((tokens, half), BF16),
        ((tokens, BLK), F32),
        ((tokens, BLK), F32),
        ((tokens + 2 * BLK, quarter), BF16),
        ((6 * pairs, BLK, BLK), F32),
        ((2 * pairs, 16, quarter), F32),
        ((pairs, width, 3 * BLK), BF16),
        ((3, part, width), BF16),
        ((3, rows_w, SEQ * part), BF16),
        ((SEQ, out_part, width), BF16),
        ((pairs, 3, rows_w, 3 * BLK), BF16),
    ]
    for _ in range(3):
        scratch += [
            ((part, width), BF16),
            ((rows_w, SEQ * part), BF16),
            ((out_part, width), BF16),
            ((pairs, rows_w, 3 * BLK), BF16),
        ]
    scratch += [
        ((SEQ, BLK, width), BF16),
        ((SEQ, BLK, width), BF16),
        ((SEQ + 1, 48, BLK), F32),
        ((8, width), F32),
        ((8, part), F32),
        ((8, width), F32),
        ((4, 8, width), F32),
        ((32, BLK), F32),
        ((8, 32, BLK), F32),
        ((4, 32, BLK), F32),
    ]
    scratch = [pltpu.VMEM(*s) for s in scratch]
    pair_of = lambda *dims: [pltpu.SemaphoreType.DMA(dims)] * 2
    semaphores = (
        pair_of(5)
        + pair_of(4)
        + pair_of(4)
        + pair_of(3, 4)
        + pair_of(4)
        + pair_of(4, 4)
        + pair_of(4)
        + pair_of(4) * 8
        + pair_of(3)
        + pair_of(4, 3)
        + pair_of(4)
        + pair_of(3, 3)
        + pair_of(6, 4)
        + pair_of(4)
        + pair_of(8)
        + pair_of(4)
        + [pltpu.SemaphoreType.DMA((5,))]
    )
    pooled, gx, gq, gk, gv, go, gi, gd, gs = pl.pallas_call(
        fused_kernel,
        out_shape=out_shape,
        in_specs=[anywhere] * 9,
        out_specs=out_specs,
        scratch_shapes=scratch + semaphores,
        compiler_params=pltpu.CompilerParams(
            collective_id=0, has_side_effects=True, vmem_limit_bytes=VMEM_LIMIT
        ),
        name="block",
    )(inputs, cotangent, w_query, w_key, w_value, w_out, w_ffn_in, w_ffn_out, small)

    def own_part(value, axis, size):
        return lax.dynamic_slice_in_dim(value, chip * size, size, axis)

    gain_one = own_part(gs[0 : width // BLK].reshape(width), 0, rows_w)
    gain_two = own_part(gs[8 : 8 + width // BLK].reshape(width), 0, rows_w)
    per_core = jnp.concatenate([gs[16 : 16 + 2 * pairs], gs[24 : 24 + 2 * pairs]], axis=0)
    table = own_part(per_core[:, :buckets].T, 0, buckets // SEQ)
    return (pooled, gx, gq, gk, gv, go, gi, gd, gain_one, gain_two, table)


def fits(mesh):
    return mesh.shape["dp"] == CORES * DEPTH and mesh.shape["seq"] == SEQ


def solution(mesh):
    in_specs = (
        P("dp", "seq", None),
        P("seq", None),
        P("seq", None),
        P("seq", None),
        P("seq", None),
        P("seq", None),
        P("seq", None),
        P("seq"),
        P("seq"),
        P("seq", None),
        P("dp"),
        P("dp", "seq", None),
    )
    out_specs = (
        P("dp", None),
        P("dp", "seq", None),
        P("seq", None),
        P("seq", None),
        P("seq", None),
        P("seq", None),
        P("seq", None),
        P("seq", None),
        P("seq"),
        P("seq"),
        P("seq", None),
    )
    return jax.shard_map(
        fused_on_device if fits(mesh) else on_device, mesh=mesh, in_specs=in_specs, out_specs=out_specs, check_vma=False
    )
```

```python
import math

import jax
import jax.numpy as jnp
from jax import lax
from jax.experimental import pallas as pl
from jax.experimental.pallas import tpu as pltpu
from jax.sharding import PartitionSpec as P

EPS = 1e-06
THRESHOLDS = (12, 16, 23, 32, 46, 64, 91)
NEGATIVE = -1000000000.0
GELU_C = math.sqrt(2.0 / math.pi)
GELU_K = 0.044715


def bucket_ids(query_pos, key_pos):
    offset = key_pos[None, :] - query_pos[:, None]
    distance = jnp.abs(offset)
    upper = jnp.where(offset > 0, 16, 0).astype(jnp.int32)
    beyond = jnp.full(distance.shape, 8, jnp.int32)
    for threshold in THRESHOLDS:
        beyond = beyond + (distance >= threshold).astype(jnp.int32)
    return upper + jnp.where(distance < 8, distance, beyond)


def gelu_slope(value):
    inner = GELU_C * (value + GELU_K * value * value * value)
    tangent = jnp.tanh(inner)
    return 0.5 * (1.0 + tangent) + 0.5 * value * (1.0 - tangent * tangent) * GELU_C * (
        1.0 + 3.0 * GELU_K * value * value
    )


def outer_sum(left, right):
    return lax.dot_general(
        left, right, (((0,), (0,)), ((), ())), preferred_element_type=jnp.float32
    )


def back_project(grad, weight):
    return lax.dot_general(
        grad, weight, (((1,), (1,)), ((), ())), preferred_element_type=jnp.float32
    )


def norm_backward(source, scale, gain, grad_normed):
    grad_gain = jnp.sum(grad_normed * source * scale, 0)
    grad_scaled = grad_normed * gain
    grad_source = scale * grad_scaled - source * scale * scale * scale * jnp.mean(
        grad_scaled * source, -1, keepdims=True
    )
    return (grad_gain, grad_source)


SEQ, CORES, DEPTH = 4, 2, 4
BLK = 128
MESH = pl.DeviceIdType.MESH
F32 = jnp.float32
BF16 = jnp.bfloat16
VMEM_LIMIT = 60 << 20


def contract(left, right, left_dim, right_dim):
    return lax.dot_general(
        left, right, (((left_dim,), (right_dim,)), ((), ())), preferred_element_type=F32
    )


def exact(left, right, left_dim, right_dim):
    return lax.dot_general(
        left,
        right,
        (((left_dim,), (right_dim,)), ((), ())),
        preferred_element_type=F32,
        precision=lax.Precision.HIGHEST,
    )


def await_copy(ref, sem):
    pltpu.make_async_copy(ref, ref, sem).wait()


def tile(index, size):
    return pl.ds(pl.multiple_of(index * size, size), size)


def bucket_of(offset):
    distance = jnp.abs(offset)
    beyond = jnp.full(distance.shape, 8, jnp.int32)
    for threshold in THRESHOLDS:
        beyond = beyond + (distance >= threshold).astype(jnp.int32)
    return jnp.where(offset > 0, 16, 0) + jnp.where(distance < 8, distance, beyond)


def full_sum(value):
    return jnp.sum(jnp.sum(value, 0, keepdims=True), 1, keepdims=True)


def fused_kernel(
    inputs,
    cotangent,
    w_query,
    w_key,
    w_value,
    w_out,
    w_in,
    w_down,
    gains_in,
    bias_in,
    lengths_in,
    pooled_o,
    small_o,
    table_o,
    gx_o,
    gq_o,
    gk_o,
    gv_o,
    go_o,
    gi_o,
    gd_o,
    xown,
    grads,
    nrm1,
    wqkv,
    qkv,
    mixed,
    wo,
    psend,
    precv,
    hid,
    nrm2,
    wi,
    wd,
    act,
    slope,
    gpre,
    gn,
    strip,
    vecs,
    maskc,
    kaug,
    lse,
    flip,
    dqkv,
    dpair,
    gmix,
    dk_acc,
    dv_acc,
    ds_buf,
    near,
    far,
    gqkv,
    gdn,
    d_dx,
    d_dy,
    d_rx,
    d_ry,
    d_za,
    d_zb,
    i_dx,
    i_dy,
    i_rx,
    i_ry,
    i_za,
    i_zb,
    q_dx,
    q_dy,
    q_rx,
    q_ry,
    q_za,
    q_zb,
    rs_o,
    o_za,
    o_zb,
    gx_send,
    small_all,
    wide,
    gains,
    asum,
    pp,
    pool_recv,
    sg,
    sg_plane,
    sg_depth,
    turned,
    small_ss,
    small_rs,
    x_ss,
    x_rs,
    c_ss,
    c_rs,
    wg_ss,
    wg_rs,
    wo_ss,
    wo_rs,
    n1_ss,
    n1_rs,
    g_ss,
    g_rs,
    part_ss,
    part_rs,
    n2_ss,
    n2_rs,
    gn2_ss,
    gn2_rs,
    gat_ss,
    gat_rs,
    gn1_ss,
    gn1_rs,
    gx_ss,
    gx_rs,
    rs_ss,
    rs_rs,
    rso_ss,
    rso_rs,
    z_ss,
    z_rs,
    pool_ss,
    pool_rs,
    sgp_ss,
    sgp_rs,
    sgz_ss,
    sgz_rs,
    out_s,
):
    dp = lax.axis_index("dp")
    chip = lax.axis_index("seq")
    depth, core = lax.div(dp, 2), lax.rem(dp, 2)
    row, col = lax.div(chip, 2), lax.rem(chip, 2)
    other = (depth * 2 + 1 - core, chip)
    xn = row * 2 + 1 - col
    yn = (1 - row) * 2 + col
    dn = (1 - row) * 2 + 1 - col
    tokens, width = nrm1.shape
    half = width // 2
    rows_w = w_query.shape[0]
    ff_part = gpre.shape[1]
    quarter = tokens // 4

    def remote(src, dst, send, recv, device):
        return pltpu.make_async_remote_copy(
            src_ref=src,
            dst_ref=dst,
            send_sem=send,
            recv_sem=recv,
            device_id=device,
            device_id_type=MESH,
        )

    def ahead(step):
        return lax.rem(chip + step, SEQ)

    pending = []

    def send_now(*args):
        copy = remote(*args)
        copy.start()
        pending.append(copy)

    lane = lax.broadcasted_iota(jnp.int32, (1, BLK), 1)
    wide[...] = jnp.zeros_like(wide)
    wide[0:2, 0:rows_w] = gains_in[...]
    turned_gains = pltpu.roll(wide[...], chip * rows_w, 1)
    small_all[0] = jnp.zeros_like(small_all[0])
    for which in range(2):
        for i in range(width // BLK):
            small_all[0, 8 * which + i : 8 * which + i + 1, :] = turned_gains[
                which : which + 1, i * BLK : (i + 1) * BLK
            ]
    small_all[0, 6:7, :] = jnp.where(
        lane == 0, lengths_in[0].astype(F32), lengths_in[1].astype(F32)
    )
    small_all[0, tile(2 + chip, 8), 0 : bias_in.shape[1]] = bias_in[...].astype(F32)

    barrier = pltpu.get_barrier_semaphore()
    for step in range(SEQ):
        if step:
            pl.semaphore_signal(barrier, inc=1, device_id=(dp, ahead(step)), device_id_type=MESH)
        pl.semaphore_signal(
            barrier, inc=1, device_id=(other[0], ahead(step)), device_id_type=MESH
        )
    for step in range(1, DEPTH):
        pl.semaphore_signal(
            barrier,
            inc=1,
            device_id=(lax.rem(depth + step, DEPTH) * 2 + core, chip),
            device_id_type=MESH,
        )
    pl.semaphore_wait(barrier, 2 * SEQ - 1 + DEPTH - 1)

    mine = small_all.at[0]
    for step in range(1, SEQ):
        send_now(
            mine, small_all.at[step], small_ss.at[step], small_rs.at[step], (dp, ahead(step))
        )
    send_now(mine, small_all.at[SEQ], small_ss.at[SEQ], small_rs.at[SEQ], other)

    def spread(source, dest_of, send, recv, action):
        for doc in range(2):
            for to in range(2):
                block = source.at[doc, pl.ds(to * BLK, BLK)]
                target = core * 2 + doc
                own = (target == chip) & (core == to)
                copy = remote(
                    block,
                    dest_of(to),
                    send.at[doc * 2 + to],
                    recv.at[chip],
                    (depth * 2 + to, target),
                )
                if action == "start":

                    @pl.when(own)
                    def _():
                        pltpu.make_async_copy(block, dest_of(to), recv.at[chip]).start()

                @pl.when(jnp.logical_not(own))
                def _():
                    if action == "start":
                        copy.start()
                    else:
                        copy.wait_send()

    x_slot = lambda to: xown.at[chip]
    c_slot = lambda to: grads.at[chip * 2 + to]
    spread(inputs, x_slot, x_ss, x_rs, "start")

    class Gather:
        def __init__(self, index, pieces, place):
            self.index, self.pieces, self.place = index, pieces, place
            self.bind()

        def half_of(self, owner, which):
            ref = self.place(owner)
            size = ref.shape[0] // 2
            return ref.at[pl.ds(which * size, size)]

        def bind(self):
            k = self.index
            self.local, self.one, self.two = [], [], []
            for src, cut in self.pieces:
                dst = cut(self.place(chip))
                self.local.append(pltpu.make_async_copy(src, dst, wg_rs.at[k, 0]))
                self.one.append(remote(src, dst, wg_ss.at[k, 0], wg_rs.at[k, 1], (dp, xn)))
                self.one.append(remote(src, dst, wg_ss.at[k, 1], wg_rs.at[k, 2], (dp, yn)))
            via_x, via_y = self.half_of(xn, 1), self.half_of(yn, 0)
            self.two = [
                remote(via_x, via_x, wg_ss.at[k, 2], wg_rs.at[k, 3], (dp, yn)),
                remote(via_y, via_y, wg_ss.at[k, 3], wg_rs.at[k, 4], (dp, xn)),
            ]
            self.from_x, self.from_y = self.place(xn), self.place(yn)
            self.last = [self.half_of(dn, 1), self.half_of(dn, 0)]
            self.own = self.place(chip)

        def first(self):
            for copy in self.local + self.one:
                copy.start()

        def second(self):
            k = self.index
            await_copy(self.from_x, wg_rs.at[k, 1])
            self.two[0].start()
            await_copy(self.from_y, wg_rs.at[k, 2])
            self.two[1].start()

        def done(self):
            k = self.index
            await_copy(self.own, wg_rs.at[k, 0])
            await_copy(self.last[0], wg_rs.at[k, 3])
            await_copy(self.last[1], wg_rs.at[k, 4])

        def sent(self):
            k = self.index
            for copy in self.two:
                copy.wait_send()
            await_copy(self.own, wg_ss.at[k, 0])
            await_copy(self.own, wg_ss.at[k, 1])

    core_cols = tile(core, half)
    whole = lambda ref: ref
    row_half = rows_w // 2

    def qkv_item(index, part):
        return Gather(
            index,
            [
                (
                    w.at[pl.ds(part * row_half, row_half), core_cols],
                    lambda ref, i=i: ref.at[:, pl.ds(i * half, half)],
                )
                for i, w in enumerate((w_query, w_key, w_value))
            ],
            lambda owner: wqkv.at[
                pl.ds(pl.multiple_of(owner * rows_w + part * row_half, row_half), row_half)
            ],
        )

    def in_item(index, part):
        return Gather(
            index,
            [
                (
                    w_in.at[:, tile((2 * part + f) * 2 + core, ff_part)],
                    lambda ref, f=f: ref.at[:, pl.ds(f * ff_part, ff_part)],
                )
                for f in range(2)
            ],
            lambda owner: wi.at[tile(owner, rows_w), pl.ds(part * 2 * ff_part, 2 * ff_part)],
        )

    def down_item(index, part):
        size = ff_part // 2
        return Gather(
            index,
            [(w_down.at[pl.ds(pl.multiple_of(core * ff_part + part * size, size), size)], whole)],
            lambda owner: wd.at[
                pl.ds(pl.multiple_of(owner * ff_part + part * size, size), size)
            ],
        )

    qkv_items = [qkv_item(0, 0), qkv_item(1, 1)]
    in_items = [in_item(2, 0), in_item(3, 1)]
    down_items = [down_item(4, 0), down_item(5, 1)]
    for it in qkv_items:
        it.first()

    wo_part = rows_w // 2
    wo_src = w_out.at[tile(core, wo_part)]
    wo_dst = wo.at[tile(col * 2 + core, wo_part)]

    def wo_each(action):
        for to in range(SEQ):
            own = (chip == to) & (core == row)
            copy = remote(
                wo_src, wo_dst, wo_ss.at[to], wo_rs.at[col * 2 + core], (depth * 2 + row, to)
            )
            if action == "start":

                @pl.when(own)
                def _():
                    pltpu.make_async_copy(wo_src, wo_dst, wo_rs.at[col * 2 + core]).start()

            @pl.when(jnp.logical_not(own))
            def _():
                if action == "start":
                    copy.start()
                else:
                    copy.wait_send()

    for step in range(1, SEQ + 1):
        await_copy(small_all.at[step], small_rs.at[step])
    summed = small_all[0] + small_all[1] + small_all[2] + small_all[3]
    for which in range(2):
        gains[which : which + 1, :] = jnp.concatenate(
            [summed[8 * which + i : 8 * which + i + 1, :] for i in range(width // BLK)], axis=1
        )
    length_row = jnp.where(row == core, small_all[0, 6:7, :], small_all[SEQ, 6:7, :])
    length = jnp.where(col == 0, length_row[:, 0:1], length_row[:, 1:2])
    own_lengths = small_all[0, 6:7, 0:2]
    table = summed[16:48, :].astype(BF16)
    lane_two = lax.broadcasted_iota(jnp.int32, (1, 2 * BLK), 1)
    minus = jnp.where(lane_two < BLK, lane_two, lane_two - 2 * BLK)
    for off in (-1, 0, 1):
        ids = bucket_of(off * BLK - minus)
        onehot = (lax.broadcasted_iota(jnp.int32, (32, 2 * BLK), 0) == ids).astype(BF16)
        vecs[off + 1] = contract(table, onehot, 0, 0)[0:16, :]

    @pl.loop(0, 6)
    def _(h):
        values = [vecs[i, pl.ds(core * 6 + h, 1), :] for i in range(3)]
        left = jnp.broadcast_to(values[0][:, BLK - 1 : BLK], (BLK, BLK))
        right = jnp.broadcast_to(values[2][:, BLK + 1 : BLK + 2], (BLK, BLK))
        for i in range(6):
            strip[h, i * BLK : (i + 1) * BLK, :] = left
            strip[h, (i + 9) * BLK : (i + 10) * BLK, :] = right
        for i in range(3):
            skewed = pltpu.roll(
                jnp.broadcast_to(values[i], (BLK, 2 * BLK)), 0, 1, stride=1, stride_axis=0
            )
            strip[h, (i + 6) * BLK : (i + 7) * BLK, :] = skewed[:, :BLK]

    maskc[...] = jnp.where(
        lax.broadcasted_iota(jnp.int32, maskc.shape, 0).astype(F32) < length, 0.0, NEGATIVE
    ).astype(BF16)

    def block_valid(b):
        pos = lax.broadcasted_iota(jnp.int32, (BLK, 1), 0) + b * BLK
        return (pos.astype(F32) < length).astype(F32)

    def n1_copy(i):
        block = nrm1.at[tile(2 * i + core, BLK)]
        return remote(block, block, n1_ss.at[i], n1_rs.at[i], other)

    @pl.loop(0, SEQ)
    def _(i):
        await_copy(xown.at[i], x_rs.at[i])
        source = xown[i].astype(F32)
        scale = lax.rsqrt(jnp.mean(source * source, -1, keepdims=True) + EPS)
        nrm1[tile(2 * i + core, BLK), :] = (source * scale * gains[0:1, :]).astype(BF16)
        n1_copy(i).start()

    for it in qkv_items:
        it.second()
    wo_each("start")
    for it in in_items:
        it.first()
    for it in qkv_items:
        it.done()
    for i in range(SEQ):
        n1_copy(i).wait_recv()

    @pl.loop(0, 4)
    def _(i):
        rows = tile(i, quarter)
        qkv[rows, :] = contract(nrm1[rows, :], wqkv[...], 1, 0).astype(BF16)

    flip[BLK : BLK + 16, :] = jnp.ones((16, tokens), BF16)
    mine_lanes = [lane < 64, lane >= 64]
    spare = [lane == 64, lane == 0]

    def prepare_keys(pair):
        keys = qkv[:, tile(3 + pair, BLK)]
        for h in range(2):
            kaug[h] = jnp.where(mine_lanes[h], keys, jnp.where(spare[h], maskc[...], 0))

    def scores(pair, qb, h):
        queries = qkv[tile(qb, quarter), tile(pair, BLK)]
        plain = jnp.where(mine_lanes[h], queries, jnp.zeros_like(queries))
        raised = jnp.where(spare[h], jnp.ones_like(queries), plain)
        raw = contract(kaug[h], raised, 1, 1)
        head = pair * 2 + h
        biases = [
            strip[head, pl.ds(pl.multiple_of((7 - 2 * qb - i) * BLK, BLK), tokens), :]
            for i in range(2)
        ]
        return raw + jnp.concatenate(biases, axis=1), plain

    def serve(now, table):
        for when, actions in table.items():

            @pl.when(now == when)
            def _():
                for action in actions:
                    action()

    def forward_in_tail():
        in_items[1].second()
        spread(cotangent, c_slot, c_ss, c_rs, "start")
        for it in down_items:
            it.first()

    @pl.loop(0, 12)
    def _(now):
        pair, qb = lax.div(now, 4), lax.rem(now, 4)

        @pl.when(qb == 0)
        def _():
            flip[0:BLK, :] = jnp.transpose(qkv[:, tile(6 + pair, BLK)])
            prepare_keys(pair)

        parts = []
        for h in range(2):
            logits, _ = scores(pair, qb, h)
            highest = jnp.max(logits, 0, keepdims=True)
            raised = jnp.exp(logits - highest).astype(BF16)
            result = contract(flip[...], raised, 1, 0)
            total = result[BLK : BLK + 1, :]
            lse[pl.ds(pair * 2 + h, 1), tile(qb, quarter)] = highest + jnp.log(total)
            parts.append(result[64 * h : 64 * h + 64, :] / total)
        mixed[tile(qb, quarter), tile(pair, BLK)] = jnp.transpose(
            jnp.concatenate(parts, axis=0)
        ).astype(BF16)
        serve(now, {5: [in_items[0].second], 9: [forward_in_tail]})

    def swap_copy(i, send, recv):
        return remote(psend.at[i], precv.at[i], send.at[i], recv.at[i], other)

    for k in range(4):
        await_copy(wo.at[pl.ds(k * wo_part, wo_part)], wo_rs.at[k])

    def blocks_of(ref, i, parity):
        return jnp.concatenate(
            [ref[tile(2 * (2 * i + j) + parity, BLK), :] for j in range(2)], axis=0
        )

    @pl.loop(0, 2)
    def _(i):
        result = contract(blocks_of(mixed, i, 1 - core), wo[...], 1, 0)
        for j in range(2):
            psend[2 * i + j] = result[j * BLK : (j + 1) * BLK, :]
            swap_copy(2 * i + j, part_ss, part_rs).start()

    def n2_copy(i, send, recv):
        block = nrm2.at[tile(2 * i + core, BLK)]
        return remote(block, block, send.at[i], recv.at[i], other)

    pp[...] = jnp.zeros_like(pp)

    @pl.loop(0, 2)
    def _(k):
        result = contract(blocks_of(mixed, k, core), wo[...], 1, 0)
        for j in range(2):
            i = 2 * k + j
            hidden = xown[i].astype(F32) + result[j * BLK : (j + 1) * BLK, :]
            swap_copy(i, part_ss, part_rs).wait_recv()
            hidden = hidden + precv[i]
            hid[i] = hidden
            scale = lax.rsqrt(jnp.mean(hidden * hidden, -1, keepdims=True) + EPS)
            nrm2[tile(2 * i + core, BLK), :] = (hidden * scale * gains[1:2, :]).astype(BF16)
            n2_copy(i, n2_ss, n2_rs).start()
            pp[0:1, :] += jnp.sum(hidden * block_valid(2 * i + core), 0, keepdims=True)

    for it in in_items:
        it.done()
    for i in range(SEQ):
        n2_copy(i, n2_ss, n2_rs).wait_recv()

    def g_copy(i):
        block = grads.at[2 * i + core]
        return remote(block, block, g_ss.at[i], g_rs.at[i], other)

    def take_cotangent():
        @pl.loop(0, SEQ)
        def _(i):
            b = 2 * i + core
            await_copy(grads.at[b], c_rs.at[i])
            grads[b] = (grads[b].astype(F32) * block_valid(b)).astype(BF16)
            g_copy(i).start()

    asum[...] = jnp.zeros_like(asum)

    @pl.loop(0, 16)
    def _(now):
        f, i = lax.div(now, 4), lax.rem(now, 4)
        rows, f_cols = tile(i, quarter), tile(f, ff_part)
        value = contract(nrm2[rows, :], wi[:, f_cols], 1, 0)
        square = value * value
        tangent = jnp.tanh(GELU_C * (value + GELU_K * value * square))
        half_up = 0.5 * (1.0 + tangent)
        active = (value * half_up).astype(BF16)
        act[rows, f_cols] = active
        slope[rows, f_cols] = (
            half_up
            + 0.5
            * value
            * (1.0 - tangent * tangent)
            * GELU_C
            * (1.0 + 3.0 * GELU_K * square)
        ).astype(BF16)
        pos = lax.broadcasted_iota(jnp.int32, (8, quarter), 1) + i * quarter
        valid = (pos.astype(F32) < length).astype(BF16)
        asum[:, f_cols] += contract(valid, active, 1, 0)
        serve(now, {11: [take_cotangent], 15: [down_items[0].second]})

    for i in range(SEQ):
        g_copy(i).wait_recv()
    g_all = lambda: grads[...].reshape(tokens, width)

    class Chunk:
        made = 0

        def __init__(self, src, dx, dy, rx, ry, za, zb, outs):
            self.index = Chunk.made
            Chunk.made += 1
            self.src, self.dx, self.dy, self.rx, self.ry = src, dx, dy, rx, ry
            self.za, self.zb, self.outs = za, zb, outs
            self.bind()

        def bind(self):
            k = self.index
            size = self.dx.shape[0]
            cut = lambda ref, which: ref.at[pl.ds(which * size, size)]
            ss, rs = (lambda i: rs_ss.at[k, i]), (lambda i: rs_rs.at[k, i])
            to_x, to_y = (dp, xn), (dp, yn)
            self.one = [
                remote(cut(self.src(dn), 1), self.dx, ss(0), rs(0), to_x),
                remote(cut(self.src(dn), 0), self.dy, ss(1), rs(1), to_y),
                remote(cut(self.src(xn), 1), cut(self.rx, 1), ss(2), rs(2), to_x),
                remote(cut(self.src(yn), 0), cut(self.ry, 0), ss(3), rs(3), to_y),
            ]
            self.sum_y, self.sum_x = cut(self.src(yn), 1), cut(self.src(xn), 0)
            self.two = [
                remote(self.sum_y, cut(self.ry, 1), ss(4), rs(4), to_y),
                remote(self.sum_x, cut(self.rx, 0), ss(5), rs(5), to_x),
            ]
            self.bind_z(self.rx, self.ry)

        def bind_z(self, reduced, final):
            k = self.index
            self.reduced, self.final = reduced, final
            sem = lambda i: (z_ss.at[k, i], z_rs.at[k, i])
            self.to_inner = remote(reduced, self.za, *sem(0), z_dev(toward))
            self.swap = remote(reduced, self.zb, *sem(1), z_dev(across))
            self.to_end = remote(final, final, *sem(2), z_dev(outward))

        def start(self):
            for copy in self.one:
                copy.start()

        def middle(self):
            for at, sent, sums, copy in (
                (0, self.dx, self.sum_y, self.two[0]),
                (1, self.dy, self.sum_x, self.two[1]),
            ):
                self.one[at].wait_recv()
                sums[...] = (sums[...].astype(F32) + sent[...].astype(F32)).astype(BF16)
                copy.start()

        def total(self):
            for copy in (self.one[2], self.one[3], *self.two):
                copy.wait_recv()
            self.rx[...] = (
                self.src(chip)[...].astype(F32)
                + self.rx[...].astype(F32)
                + self.ry[...].astype(F32)
            ).astype(BF16)

        def z_one(self):
            self.total()

            @pl.when(end_z)
            def _():
                self.to_inner.start()

        def z_two(self):
            @pl.when(inner_z)
            def _():
                self.to_inner.wait_recv()
                self.reduced[...] = (
                    self.reduced[...].astype(F32) + self.za[...].astype(F32)
                ).astype(BF16)
                self.swap.start()

        def z_three(self):
            @pl.when(inner_z)
            def _():
                self.swap.wait_recv()
                self.final[...] = (
                    self.reduced[...].astype(F32) + self.zb[...].astype(F32)
                ).astype(BF16)
                self.to_end.start()

        def each_out(self, act_on):
            k = self.index
            for n, (cols, place) in enumerate(self.outs):
                src = self.final if cols is None else self.final.at[:, cols]
                act_on(
                    remote(src, place(core), z_ss.at[k, 3 + n], z_rs.at[k, 3 + n], other),
                    pltpu.make_async_copy(src, place(core), out_s.at[k, n]),
                )

        def z_four(self):
            @pl.when(end_z)
            def _():
                self.to_end.wait_recv()

            self.each_out(lambda there, here: (there.start(), here.start()))

        def finish(self):
            self.each_out(
                lambda there, here: (there.wait_recv(), there.wait_send(), here.wait())
            )

            @pl.when(end_z)
            def _():
                self.to_inner.wait_send()

            @pl.when(inner_z)
            def _():
                self.swap.wait_send()
                self.to_end.wait_send()

            for copy in self.plane_sends():
                copy.wait_send()

        def plane_sends(self):
            return self.one + self.two

    inner_z = (depth == 1) | (depth == 2)
    end_z = jnp.logical_not(inner_z)
    toward = jnp.where(depth == 0, 1, 2)
    outward = jnp.where(depth == 1, 0, 3)
    across = jnp.where(depth == 1, 2, 1)

    def z_dev(z):
        return (z * 2 + core, chip)

    d_chunks = [
        Chunk(
            lambda owner, i=i: gdn.at[i, owner],
            d_dx.at[i],
            d_dy.at[i],
            d_rx.at[i],
            d_ry.at[i],
            d_za.at[i],
            d_zb.at[i],
            [
                (
                    None,
                    lambda c, i=i: gd_o.at[
                        pl.ds(pl.multiple_of(c * ff_part + i * BLK, BLK), BLK)
                    ],
                )
            ],
        )
        for i in range(ff_part // BLK)
    ]

    for i in range(ff_part // BLK):
        columns = jnp.concatenate(
            [act[:, f * ff_part + i * BLK : f * ff_part + (i + 1) * BLK] for f in range(SEQ)],
            axis=1,
        )
        gdn[i] = contract(columns, g_all(), 0, 0).astype(BF16).reshape(SEQ, BLK, width)
        if i == 1:
            down_items[1].second()
            d_chunks[0].start()
            d_chunks[1].start()
    d_chunks[2].start()
    for it in down_items:
        it.done()
    for it in in_items:
        it.sent()

    def pooled_part(f):
        cols = slice(f * ff_part, (f + 1) * ff_part)
        total = asum[0:1, cols]
        high = total.astype(BF16)
        rest = total - high.astype(F32)
        middle = rest.astype(BF16)
        low = (rest - middle.astype(F32)).astype(BF16)
        for piece in (high, middle, low):
            pp[0:1, :] += contract(jnp.broadcast_to(piece, (16, ff_part)), wd[cols, :], 1, 0)[
                0:1, :
            ]

    i_chunks = [
        Chunk(
            lambda owner, f=f: wi.at[tile(owner, rows_w), pl.ds(f * ff_part, ff_part)],
            i_dx.at[f],
            i_dy.at[f],
            i_rx.at[f],
            i_ry.at[f],
            i_za.at[f],
            i_zb.at[f],
            [(None, lambda c, f=f: gi_o.at[:, tile(2 * f + c, ff_part)])],
        )
        for f in range(SEQ)
    ]
    for f in range(SEQ):
        f_cols = slice(f * ff_part, (f + 1) * ff_part)

        @pl.loop(0, 4)
        def _(i):
            rows = tile(i, quarter)
            upstream = grads[pl.ds(2 * i, 2)].reshape(quarter, width)
            grad = contract(upstream, wd[f_cols, :], 1, 1) * slope[rows, f_cols].astype(F32)
            grad = grad.astype(BF16)
            gpre[rows, :] = grad
            back = contract(grad, wi[:, f_cols], 1, 1)
            if f == 0:
                gn[rows, :] = back
            else:
                gn[rows, :] += back

        pooled_part(f)

        @pl.loop(0, width // (2 * BLK))
        def _(i):
            wi[tile(i, 2 * BLK), f_cols] = contract(
                nrm2[:, tile(i, 2 * BLK)], gpre[...], 0, 0
            ).astype(BF16)

        if f < 3:
            d_chunks[f].middle()
        if f:
            i_chunks[f - 1].middle()
        i_chunks[f].start()

    def pool_each(action):
        for to in range(SEQ):
            own = (chip == to) & (core == row)
            dst = pool_recv.at[col * 2 + core]
            copy = remote(pp, dst, pool_ss.at[to], pool_rs.at[col * 2 + core], (depth * 2 + row, to))
            if action == "start":

                @pl.when(own)
                def _():
                    pltpu.make_async_copy(pp, dst, pool_rs.at[col * 2 + core]).start()

            @pl.when(jnp.logical_not(own))
            def _():
                if action == "start":
                    copy.start()
                else:
                    copy.wait_send()

    for i in range(SEQ):
        swap_copy(i, part_ss, part_rs).wait_send()
        n2_copy(i, n2_ss, n2_rs).wait_send()

    @pl.loop(0, SEQ)
    def _(i):
        psend[i] = gn[tile(2 * i + 1 - core, BLK), :]
        swap_copy(i, gn2_ss, gn2_rs).start()

    sg[...] = jnp.zeros_like(sg)

    def add_gain(first, value):
        for i in range(width // BLK):
            sg[first + i : first + i + 1, :] += value[:, i * BLK : (i + 1) * BLK]

    @pl.loop(0, SEQ)
    def _(i):
        b = 2 * i + core
        swap_copy(i, gn2_ss, gn2_rs).wait_recv()
        normed = gn[tile(b, BLK), :] + precv[i]
        hidden = hid[i]
        scale = lax.rsqrt(jnp.mean(hidden * hidden, -1, keepdims=True) + EPS)
        add_gain(8, jnp.sum(normed * hidden * scale, 0, keepdims=True))
        scaled = normed * gains[1:2, :]
        inner = jnp.mean(scaled * hidden, -1, keepdims=True)
        result = grads[b].astype(F32) + scale * scaled - hidden * (scale * scale * scale) * inner
        hid[i] = result
        nrm2[tile(b, BLK), :] = result.astype(BF16)
        n2_copy(i, gat_ss, gat_rs).start()

    pool_each("start")
    for i in range(SEQ):
        n2_copy(i, gat_ss, gat_rs).wait_recv()

    @pl.loop(0, 4)
    def _(i):
        rows = tile(i, quarter)
        gmix[rows, :] = contract(nrm2[rows, :], wo[...], 1, 1).astype(BF16)

    wo[...] = contract(mixed[...], nrm2[...], 0, 0).astype(BF16)

    def rso_each(action):
        for k in range(2):
            for to in range(2):
                target = core * 2 + k
                own = (chip == target) & (core == to)
                src = wo.at[pl.ds((2 * k + to) * wo_part, wo_part)]
                dst = rs_o.at[chip]
                copy = remote(
                    src, dst, rso_ss.at[2 * k + to], rso_rs.at[chip], (depth * 2 + to, target)
                )
                if action == "start":

                    @pl.when(own)
                    def _():
                        pltpu.make_async_copy(src, dst, rso_rs.at[chip]).start()

                @pl.when(jnp.logical_not(own))
                def _():
                    if action == "start":
                        copy.start()
                    else:
                        copy.wait_send()

    class OutChunk(Chunk):
        def bind(self):
            self.bind_z(self.src.at[0], self.src.at[1])

        def total(self):
            for i in range(SEQ):
                await_copy(self.src.at[i], rso_rs.at[i])
            value = self.src[0].astype(F32)
            for i in range(1, SEQ):
                value = value + self.src[i].astype(F32)
            self.reduced[...] = value.astype(BF16)

        def plane_sends(self):
            return []

    o_chunk = OutChunk(
        rs_o, None, None, None, None, o_za, o_zb, [(None, lambda c: go_o.at[tile(c, wo_part)])]
    )
    rso_each("start")

    sub = lax.broadcasted_iota(jnp.int32, (16, tokens), 0)
    key_block = lax.div(lax.broadcasted_iota(jnp.int32, (16, tokens), 1), BLK)
    flip[BLK : BLK + 16, :] = (sub == key_block).astype(BF16)
    near[...] = jnp.zeros_like(near)
    far[...] = jnp.zeros_like(far)
    ds_buf[0:BLK, :] = jnp.zeros((BLK, quarter), BF16)
    ds_buf[tokens + BLK :, :] = jnp.zeros((BLK, quarter), BF16)

    q_chunks = [
        Chunk(
            lambda owner, p=p: gqkv.at[p, tile(owner, rows_w)],
            q_dx.at[p],
            q_dy.at[p],
            q_rx.at[p],
            q_ry.at[p],
            q_za.at[p],
            q_zb.at[p],
            [
                (
                    pl.ds(j * BLK, BLK),
                    lambda c, p=p, o=o: o.at[:, tile(c * 3 + p, BLK)],
                )
                for j, o in enumerate((gq_o, gk_o, gv_o))
            ],
        )
        for p in range(3)
    ]
    backward_table = {
        0: [i_chunks[3].middle],
        1: [d_chunks[0].z_one],
        2: [d_chunks[1].z_one],
        3: [d_chunks[2].z_one, d_chunks[0].z_two],
        4: [d_chunks[1].z_two],
        5: [q_chunks[0].middle, i_chunks[0].z_one, d_chunks[2].z_two, d_chunks[0].z_three],
        6: [i_chunks[1].z_one, d_chunks[1].z_three],
        7: [i_chunks[0].z_two, d_chunks[2].z_three, d_chunks[0].z_four],
        8: [i_chunks[2].z_one, i_chunks[1].z_two, d_chunks[1].z_four],
        9: [q_chunks[1].middle, i_chunks[3].z_one, i_chunks[0].z_three, d_chunks[2].z_four],
        10: [i_chunks[2].z_two, i_chunks[1].z_three, o_chunk.z_one],
        11: [i_chunks[3].z_two, i_chunks[2].z_three, i_chunks[0].z_four],
    }

    @pl.loop(0, 12)
    def _(now):
        pair, qb = lax.div(now, 4), lax.rem(now, 4)

        @pl.when(qb == 0)
        def _():
            flip[0:BLK, :] = jnp.transpose(qkv[:, tile(3 + pair, BLK)])
            prepare_keys(pair)
            dk_acc[...] = jnp.zeros_like(dk_acc)
            dv_acc[...] = jnp.zeros_like(dv_acc)

        rows = tile(qb, quarter)
        cols = tile(pair, BLK)
        upstream = gmix[rows, cols]
        product = jnp.transpose(upstream.astype(F32) * mixed[rows, cols].astype(F32))
        parts = []
        for h in range(2):
            head = pair * 2 + h
            logits, queries = scores(pair, qb, h)
            probs = jnp.exp(logits - lse[pl.ds(head, 1), rows])
            masked = jnp.where(mine_lanes[h], upstream, jnp.zeros_like(upstream))
            grad_probs = contract(qkv[:, tile(6 + pair, BLK)], masked, 1, 1)
            inner = jnp.sum(product[64 * h : 64 * h + 64, :], 0, keepdims=True)
            grad_logits = (probs * (grad_probs - inner)).astype(BF16)
            dv_acc[...] += contract(probs.astype(BF16), masked, 1, 0)
            dk_acc[...] += contract(grad_logits, queries, 1, 0)
            ds_buf[BLK : tokens + BLK, :] = grad_logits
            result = contract(flip[...], grad_logits, 1, 0)
            parts.append(result[64 * h : 64 * h + 64, :])
            sums = result[BLK : BLK + 8, :]
            block_row = lax.broadcasted_iota(jnp.int32, sums.shape, 0)
            query_block = 2 * qb + lax.div(lax.broadcasted_iota(jnp.int32, sums.shape, 1), BLK)
            gap = block_row - query_block
            far[head, 0:8, :] += jnp.where(gap <= -2, sums, 0.0)
            far[head, 8:16, :] += jnp.where(gap >= 2, sums, 0.0)
            for i in range(2):
                for off in range(3):
                    start = pl.multiple_of((2 * qb + i + off) * BLK, BLK)
                    near[head * 3 + off] += ds_buf[
                        pl.ds(start, BLK), i * BLK : (i + 1) * BLK
                    ].astype(F32)
        dq = jnp.transpose(jnp.concatenate(parts, axis=0)).astype(BF16)
        dqkv[rows, cols] = dq
        dpair[rows, 0:BLK] = dq

        @pl.when(qb == 3)
        def _():
            for j, acc in ((1, dk_acc), (2, dv_acc)):
                value = acc[...].astype(BF16)
                dqkv[:, tile(3 * j + pair, BLK)] = value
                dpair[:, j * BLK : (j + 1) * BLK] = value

            @pl.loop(0, width // (2 * BLK))
            def _(i):
                gqkv[pair, tile(i, 2 * BLK), :] = contract(
                    nrm1[:, tile(i, 2 * BLK)], dpair[...], 0, 0
                ).astype(BF16)

            for p in range(3):

                @pl.when(pair == p)
                def _():
                    q_chunks[p].start()

        serve(now, backward_table)

    for i in range(SEQ):
        swap_copy(i, gn2_ss, gn2_rs).wait_send()

    @pl.loop(0, 2)
    def _(i):
        result = contract(blocks_of(dqkv, i, 1 - core), wqkv[...], 1, 1)
        for j in range(2):
            psend[2 * i + j] = result[j * BLK : (j + 1) * BLK, :]
            swap_copy(2 * i + j, gn1_ss, gn1_rs).start()

    q_chunks[2].middle()
    i_chunks[3].z_three()
    i_chunks[1].z_four()
    o_chunk.z_two()
    q_chunks[0].z_one()

    def gx_each(i, action):
        own = (chip == i) & (core == row)
        dst = gx_o.at[col, tile(core, BLK)]
        copy = remote(
            gx_send.at[i], dst, gx_ss.at[i], gx_rs.at[col * 2 + core], (depth * 2 + row, i)
        )
        if action == "start":

            @pl.when(own)
            def _():
                pltpu.make_async_copy(gx_send.at[i], dst, gx_rs.at[col * 2 + core]).start()

        @pl.when(jnp.logical_not(own))
        def _():
            if action == "start":
                copy.start()
            else:
                copy.wait_send()

    @pl.loop(0, 2)
    def _(k):
        both = contract(blocks_of(dqkv, k, core), wqkv[...], 1, 1)
        for j in range(2):
            i = 2 * k + j
            swap_copy(i, gn1_ss, gn1_rs).wait_recv()
            normed = both[j * BLK : (j + 1) * BLK, :] + precv[i]
            source = xown[i].astype(F32)
            scale = lax.rsqrt(jnp.mean(source * source, -1, keepdims=True) + EPS)
            add_gain(0, jnp.sum(normed * source * scale, 0, keepdims=True))
            scaled = normed * gains[0:1, :]
            inner = jnp.mean(scaled * source, -1, keepdims=True)
            result = hid[i] + scale * scaled - source * (scale * scale * scale) * inner
            gx_send[i] = result.astype(BF16)
            gx_each(i, "start")

    i_chunks[2].z_four()
    o_chunk.z_three()
    q_chunks[0].z_two()
    q_chunks[1].z_one()

    diag_row = lax.broadcasted_iota(jnp.int32, (BLK, BLK), 0)
    diag_col = lax.broadcasted_iota(jnp.int32, (BLK, BLK), 1)
    upper = diag_col >= diag_row
    mirror = (diag_row + diag_col == BLK - 1).astype(F32)
    shift = lax.broadcasted_iota(jnp.int32, (1, BLK), 1) + 1
    shift = jnp.where(shift == BLK, 0, shift)
    ids = bucket_of(jnp.concatenate([-shift, BLK - shift], axis=1))
    onehot = (lax.broadcasted_iota(jnp.int32, (BLK, 2 * BLK), 0) == ids).astype(F32)

    @pl.loop(0, 6)
    def _(h):
        def skew(x):
            return pltpu.roll(exact(mirror, x, 1, 0), 0, 1, stride=1, stride_axis=0)

        tiles = [near[h * 3 + i] for i in range(3)]
        at = [
            jnp.sum(
                skew(jnp.where(upper, tiles[i + 1], 0.0) + jnp.where(upper, 0.0, tiles[i])),
                0,
                keepdims=True,
            )
            for i in range(2)
        ]
        below = full_sum(jnp.where(upper, tiles[0], 0.0)) + full_sum(far[h, 0:8, :])
        above = full_sum(jnp.where(upper, 0.0, tiles[2])) + full_sum(far[h, 8:16, :])
        sums = exact(jnp.broadcast_to(jnp.concatenate(at, axis=1), (8, 2 * BLK)), onehot, 1, 1)
        sums = sums[0:1, :] + jnp.where(lane == 15, below, 0.0) + jnp.where(lane == 31, above, 0.0)
        sg[pl.ds(16 + core * 6 + h, 1), :] = sums

    place = core * SEQ + chip

    def sgp_each(action):
        for step in range(SEQ):
            for cross in range(2):
                if step == 0 and cross == 0:
                    continue
                to_core = lax.rem(core + cross, 2)
                copy = remote(
                    sg,
                    sg_plane.at[place],
                    sgp_ss.at[step * 2 + cross],
                    sgp_rs.at[place],
                    (depth * 2 + to_core, ahead(step)),
                )
                if action == "start":
                    copy.start()
                else:
                    copy.wait_send()

    sgp_each("start")
    pltpu.make_async_copy(sg, sg_plane.at[place], sgp_rs.at[place]).start()
    q_chunks[2].z_one()
    q_chunks[1].z_two()
    q_chunks[0].z_three()
    i_chunks[3].z_four()
    o_chunk.z_four()
    for i in range(8):
        await_copy(sg_plane.at[i], sgp_rs.at[i])
    total = sg_plane[0]
    for i in range(1, 8):
        total = total + sg_plane[i]
    sg_depth[depth] = total

    def sgz_copy(step):
        return remote(
            sg_depth.at[depth],
            sg_depth.at[depth],
            sgz_ss.at[step],
            sgz_rs.at[depth],
            z_dev(lax.rem(depth + step, DEPTH)),
        )

    for step in range(1, DEPTH):
        sgz_copy(step).start()
    q_chunks[2].z_two()
    q_chunks[1].z_three()
    q_chunks[0].z_four()
    q_chunks[2].z_three()
    q_chunks[1].z_four()
    q_chunks[2].z_four()

    for i in range(4):
        await_copy(pool_recv.at[i], pool_rs.at[i])
    for doc in range(2):
        pooled_o[doc : doc + 1, :] = (
            pool_recv[2 * doc, 0:1, :] + pool_recv[2 * doc + 1, 0:1, :]
        ) / own_lengths[:, doc : doc + 1]
    for step in range(1, DEPTH):
        z = lax.rem(depth + DEPTH - step, DEPTH)
        await_copy(sg_depth.at[z], sgz_rs.at[z])
    total = sg_depth[0] + sg_depth[1] + sg_depth[2] + sg_depth[3]
    for which in range(2):
        wide[which : which + 1, :] = jnp.concatenate(
            [total[8 * which + i : 8 * which + i + 1, :] for i in range(width // BLK)], axis=1
        )
    small_o[...] = pltpu.roll(wide[...], lax.rem(width - chip * rows_w, width), 1)[:, : small_o.shape[1]]
    turned[:, 0:16] = jnp.transpose(total[16:32, :])
    table_o[...] = turned[tile(chip, 8), :]

    for i in range(4):
        await_copy(gx_o.at[i // 2, pl.ds((i % 2) * BLK, BLK)], gx_rs.at[i])
    for copy in pending:
        copy.wait_send()
    spread(inputs, x_slot, x_ss, x_rs, "wait")
    spread(cotangent, c_slot, c_ss, c_rs, "wait")
    for it in qkv_items + down_items:
        it.sent()
    wo_each("wait")
    pool_each("wait")
    rso_each("wait")
    sgp_each("wait")
    for i in range(SEQ):
        n1_copy(i).wait_send()
        g_copy(i).wait_send()
        n2_copy(i, gat_ss, gat_rs).wait_send()
        swap_copy(i, gn1_ss, gn1_rs).wait_send()
        gx_each(i, "wait")
    for step in range(1, DEPTH):
        sgz_copy(step).wait_send()
    for chunk in (*d_chunks, *i_chunks, o_chunk, *q_chunks):
        chunk.finish()


def widen_kernel(pooled, small, table, gx, gq, gk, gv, go, gi, gd, *outs):
    pooled_out, one_out, two_out, table_out, *outs = outs
    pooled_out[...] = pooled[...]
    one_out[...] = small[0:1, : one_out.shape[1]]
    two_out[...] = small[1:2, : two_out.shape[1]]
    table_out[...] = table[:, : table_out.shape[1]]
    for value, out in zip((gx, gq, gk, gv, go, gi, gd), outs):
        out[...] = value[...].astype(F32)


def on_device(
    inputs,
    w_query,
    w_key,
    w_value,
    w_out,
    w_ffn_in,
    w_ffn_out,
    attn_gain,
    ffn_gain,
    rel_bias,
    doc_lengths,
    cotangent,
):
    blocks, shard_len, width = inputs.shape
    heads = rel_bias.shape[1]
    head_dim = width // heads
    full_len = shard_len * lax.axis_size("seq")
    total_rows = blocks * shard_len
    gathered = (
        lax.all_gather(w_query, "seq", axis=0, tiled=True),
        lax.all_gather(w_key, "seq", axis=0, tiled=True),
        lax.all_gather(w_value, "seq", axis=0, tiled=True),
        lax.all_gather(w_out, "seq", axis=0, tiled=True),
        lax.all_gather(w_ffn_in, "seq", axis=0, tiled=True),
        lax.all_gather(w_ffn_out, "seq", axis=0, tiled=True),
        lax.all_gather(attn_gain, "seq", axis=0, tiled=True),
        lax.all_gather(ffn_gain, "seq", axis=0, tiled=True),
        lax.all_gather(rel_bias, "seq", axis=0, tiled=True),
    )
    (
        full_query,
        full_key,
        full_value,
        full_out,
        full_in,
        full_down,
        gain_one,
        gain_two,
        bias_table,
    ) = gathered
    gain_one = gain_one.astype(jnp.float32)
    gain_two = gain_two.astype(jnp.float32)
    bucket_range = jnp.arange(bias_table.shape[0], dtype=jnp.int32)
    query_pos = lax.axis_index("seq") * shard_len + jnp.arange(shard_len, dtype=jnp.int32)
    key_pos = jnp.arange(full_len, dtype=jnp.int32)
    onehot = (bucket_ids(query_pos, key_pos)[:, :, None] == bucket_range).astype(jnp.bfloat16)
    bias_heads = jnp.einsum("qkn,nh->hqk", onehot, bias_table, preferred_element_type=jnp.float32)
    key_valid = key_pos[None, :] < doc_lengths[:, None]
    query_valid = (query_pos[None, :] < doc_lengths[:, None]).astype(jnp.float32)
    flat = inputs.astype(jnp.float32).reshape(total_rows, width)
    scale_one = lax.rsqrt(jnp.mean(flat * flat, -1, keepdims=True) + EPS)
    normed_one = (flat * scale_one * gain_one).astype(jnp.bfloat16)
    queries = jnp.dot(normed_one, full_query, preferred_element_type=jnp.float32).astype(
        jnp.bfloat16
    )
    keys_local = jnp.dot(normed_one, full_key, preferred_element_type=jnp.float32).astype(
        jnp.bfloat16
    )
    values_local = jnp.dot(normed_one, full_value, preferred_element_type=jnp.float32).astype(
        jnp.bfloat16
    )
    queries_heads = queries.reshape(blocks, shard_len, heads, head_dim)
    keys_all, values_all = (
        lax.all_gather(keys_local.reshape(blocks, shard_len, width), "seq", axis=1, tiled=True),
        lax.all_gather(values_local.reshape(blocks, shard_len, width), "seq", axis=1, tiled=True),
    )
    scores = jnp.einsum(
        "bqhe,bkhe->bhqk",
        queries_heads,
        keys_all.reshape(blocks, full_len, heads, head_dim),
        preferred_element_type=jnp.float32,
    )
    logits = jnp.where(key_valid[:, None, None, :], scores + bias_heads[None], NEGATIVE)
    highest = jnp.max(logits, -1, keepdims=True)
    log_total = highest + jnp.log(jnp.sum(jnp.exp(logits - highest), -1, keepdims=True))
    probs_low = jnp.exp(logits - log_total).astype(jnp.bfloat16)
    mixed = jnp.einsum(
        "bhqk,bkhe->bqhe",
        probs_low,
        values_all.reshape(blocks, full_len, heads, head_dim),
        preferred_element_type=jnp.float32,
    )
    mixed = mixed.astype(jnp.bfloat16).reshape(total_rows, width)
    hidden = flat + jnp.dot(mixed, full_out, preferred_element_type=jnp.float32)
    scale_two = lax.rsqrt(jnp.mean(hidden * hidden, -1, keepdims=True) + EPS)
    normed_two = (hidden * scale_two * gain_two).astype(jnp.bfloat16)
    pre_act = jnp.dot(normed_two, full_in, preferred_element_type=jnp.float32)
    active = jax.nn.gelu(pre_act, approximate=True).astype(jnp.bfloat16)
    outputs = hidden + jnp.dot(active, full_down, preferred_element_type=jnp.float32)
    partial_pool = jnp.sum(outputs.reshape(blocks, shard_len, width) * query_valid[:, :, None], 1)
    pooled = lax.psum(partial_pool, "seq") / doc_lengths[:, None].astype(jnp.float32)
    regathered = (
        lax.all_gather(w_query, "seq", axis=0, tiled=True),
        lax.all_gather(w_key, "seq", axis=0, tiled=True),
        lax.all_gather(w_value, "seq", axis=0, tiled=True),
        lax.all_gather(w_out, "seq", axis=0, tiled=True),
        lax.all_gather(w_ffn_in, "seq", axis=0, tiled=True),
        lax.all_gather(w_ffn_out, "seq", axis=0, tiled=True),
        lax.all_gather(attn_gain, "seq", axis=0, tiled=True),
        lax.all_gather(ffn_gain, "seq", axis=0, tiled=True),
    )
    full_query, full_key, full_value, full_out, full_in, full_down, gain_back_one, gain_back_two = (
        regathered
    )
    gain_one = gain_back_one.astype(jnp.float32)
    gain_two = gain_back_two.astype(jnp.float32)
    grad_out = (cotangent.astype(jnp.float32) * query_valid[:, :, None]).reshape(total_rows, width)
    grad_branch = grad_out.astype(jnp.bfloat16)
    grad_down = outer_sum(active, grad_branch)
    grad_pre = (back_project(grad_branch, full_down) * gelu_slope(pre_act)).astype(jnp.bfloat16)
    grad_in = outer_sum(normed_two, grad_pre)
    grad_normed_two = back_project(grad_pre, full_in)
    grad_gain_two, grad_hidden_norm = norm_backward(hidden, scale_two, gain_two, grad_normed_two)
    grad_hidden = grad_out + grad_hidden_norm
    grad_attended = grad_hidden.astype(jnp.bfloat16)
    grad_out_proj = outer_sum(mixed, grad_attended)
    grad_mixed = (
        back_project(grad_attended, full_out)
        .astype(jnp.bfloat16)
        .reshape(blocks, shard_len, heads, head_dim)
    )
    keys_back, values_back = (keys_all, values_all)
    probs = jnp.exp(logits - log_total)
    grad_probs = jnp.einsum(
        "bqhe,bkhe->bhqk",
        grad_mixed,
        values_back.reshape(blocks, full_len, heads, head_dim),
        preferred_element_type=jnp.float32,
    )
    inner_term = jnp.sum(probs * grad_probs, -1, keepdims=True)
    grad_logits = (probs * (grad_probs - inner_term)).astype(jnp.bfloat16)
    grad_queries = jnp.einsum(
        "bhqk,bkhe->bqhe",
        grad_logits,
        keys_back.reshape(blocks, full_len, heads, head_dim),
        preferred_element_type=jnp.float32,
    )
    grad_queries = grad_queries.astype(jnp.bfloat16).reshape(total_rows, width)
    grad_table = jnp.einsum("bhqk,qkn->nh", grad_logits, onehot, preferred_element_type=jnp.float32)
    key_terms = jnp.einsum(
        "bhqk,bqhe->bkhe", grad_logits, queries_heads, preferred_element_type=jnp.float32
    ).reshape(blocks, full_len, width)
    value_terms = jnp.einsum(
        "bhqk,bqhe->bkhe", probs_low, grad_mixed, preferred_element_type=jnp.float32
    ).reshape(blocks, full_len, width)
    grad_keys, grad_values = (
        lax.psum_scatter(
            key_terms.astype(jnp.bfloat16), "seq", scatter_dimension=1, tiled=True
        ).astype(jnp.float32),
        lax.psum_scatter(
            value_terms.astype(jnp.bfloat16), "seq", scatter_dimension=1, tiled=True
        ).astype(jnp.float32),
    )
    grad_keys = grad_keys.astype(jnp.bfloat16).reshape(total_rows, width)
    grad_values = grad_values.astype(jnp.bfloat16).reshape(total_rows, width)
    grad_query_w = outer_sum(normed_one, grad_queries)
    grad_key_w = outer_sum(normed_one, grad_keys)
    grad_value_w = outer_sum(normed_one, grad_values)
    grad_normed_one = (
        back_project(grad_queries, full_query)
        + back_project(grad_keys, full_key)
        + back_project(grad_values, full_value)
    )
    grad_gain_one, grad_input_norm = norm_backward(flat, scale_one, gain_one, grad_normed_one)
    grad_input = (grad_hidden + grad_input_norm).reshape(blocks, shard_len, width)
    shards = (
        lax.psum_scatter(
            grad_query_w.astype(jnp.bfloat16), "seq", scatter_dimension=0, tiled=True
        ).astype(jnp.float32),
        lax.psum_scatter(
            grad_key_w.astype(jnp.bfloat16), "seq", scatter_dimension=0, tiled=True
        ).astype(jnp.float32),
        lax.psum_scatter(
            grad_value_w.astype(jnp.bfloat16), "seq", scatter_dimension=0, tiled=True
        ).astype(jnp.float32),
        lax.psum_scatter(
            grad_out_proj.astype(jnp.bfloat16), "seq", scatter_dimension=0, tiled=True
        ).astype(jnp.float32),
        lax.psum_scatter(
            grad_in.astype(jnp.bfloat16), "seq", scatter_dimension=0, tiled=True
        ).astype(jnp.float32),
        lax.psum_scatter(
            grad_down.astype(jnp.bfloat16), "seq", scatter_dimension=0, tiled=True
        ).astype(jnp.float32),
        lax.psum_scatter(
            grad_gain_one.astype(jnp.bfloat16), "seq", scatter_dimension=0, tiled=True
        ).astype(jnp.float32),
        lax.psum_scatter(
            grad_gain_two.astype(jnp.bfloat16), "seq", scatter_dimension=0, tiled=True
        ).astype(jnp.float32),
        lax.psum_scatter(
            grad_table.astype(jnp.bfloat16), "seq", scatter_dimension=0, tiled=True
        ).astype(jnp.float32),
    )
    totals = (
        lax.psum(shards[0].astype(jnp.bfloat16), "dp").astype(jnp.float32),
        lax.psum(shards[1].astype(jnp.bfloat16), "dp").astype(jnp.float32),
        lax.psum(shards[2].astype(jnp.bfloat16), "dp").astype(jnp.float32),
        lax.psum(shards[3].astype(jnp.bfloat16), "dp").astype(jnp.float32),
        lax.psum(shards[4].astype(jnp.bfloat16), "dp").astype(jnp.float32),
        lax.psum(shards[5].astype(jnp.bfloat16), "dp").astype(jnp.float32),
        lax.psum(shards[6].astype(jnp.bfloat16), "dp").astype(jnp.float32),
        lax.psum(shards[7].astype(jnp.bfloat16), "dp").astype(jnp.float32),
        lax.psum(shards[8].astype(jnp.bfloat16), "dp").astype(jnp.float32),
    )
    return (
        pooled,
        grad_input,
        totals[0],
        totals[1],
        totals[2],
        totals[3],
        totals[4],
        totals[5],
        totals[6],
        totals[7],
        totals[8],
    )


def fused_on_device(
    inputs,
    w_query,
    w_key,
    w_value,
    w_out,
    w_ffn_in,
    w_ffn_out,
    attn_gain,
    ffn_gain,
    rel_bias,
    doc_lengths,
    cotangent,
):
    docs, shard_len, width = inputs.shape
    rows_w, hidden_units = w_ffn_in.shape
    tokens = shard_len * SEQ
    half = width // 2
    part = hidden_units // (2 * SEQ)
    blocks = tokens // BLK
    pairs = half // BLK
    parts = part // BLK
    heads = rel_bias.shape[1]
    gains = jnp.stack([attn_gain, ffn_gain]).astype(F32)
    anywhere = pl.BlockSpec(memory_space=pl.ANY)
    vmem = pl.BlockSpec(memory_space=pltpu.VMEM)
    smem = pl.BlockSpec(memory_space=pltpu.SMEM)
    shape = jax.ShapeDtypeStruct
    narrow = [
        (docs, shard_len, width),
        (rows_w, width),
        (rows_w, width),
        (rows_w, width),
        (rows_w, width),
        (rows_w, hidden_units),
        (2 * part, width),
    ]
    out_shape = (
        shape((docs, width), F32),
        shape((8, 2 * BLK), F32),
        shape((8, BLK), F32),
        *(shape(s, BF16) for s in narrow),
    )
    quarter = tokens // 4
    out_part = rows_w // 2

    def sums(count, size, columns):
        return [((count, size // 2, columns), BF16)] * 2 + [((count, size, columns), BF16)] * 4

    scratch = [
        ((SEQ, BLK, width), BF16),
        ((blocks, BLK, width), BF16),
        ((tokens, width), BF16),
        ((width, 3 * half), BF16),
        ((tokens, 3 * half), BF16),
        ((tokens, half), BF16),
        ((half, width), BF16),
        ((SEQ, BLK, width), F32),
        ((SEQ, BLK, width), F32),
        ((SEQ, BLK, width), F32),
        ((tokens, width), BF16),
        ((width, SEQ * part), BF16),
        ((SEQ * part, width), BF16),
        ((tokens, SEQ * part), BF16),
        ((tokens, SEQ * part), BF16),
        ((tokens, part), BF16),
        ((tokens, width), F32),
        ((2 * pairs, 2 * tokens - BLK, BLK), F32),
        ((3, 16, 2 * BLK), F32),
        ((tokens, BLK), BF16),
        ((2, tokens, BLK), BF16),
        ((8, tokens), F32),
        ((BLK + 16, tokens), BF16),
        ((tokens, 3 * half), BF16),
        ((tokens, 3 * BLK), BF16),
        ((tokens, half), BF16),
        ((tokens, BLK), F32),
        ((tokens, BLK), F32),
        ((tokens + 2 * BLK, quarter), BF16),
        ((6 * pairs, BLK, BLK), F32),
        ((2 * pairs, 16, quarter), F32),
        ((pairs, width, 3 * BLK), BF16),
        ((parts, SEQ, BLK, width), BF16),
        *sums(parts, BLK, width),
        *sums(SEQ, rows_w, part),
        *sums(pairs, rows_w, 3 * BLK),
        ((SEQ, out_part, width), BF16),
        ((out_part, width), BF16),
        ((out_part, width), BF16),
        ((SEQ, BLK, width), BF16),
        ((SEQ + 1, 48, BLK), F32),
        ((8, width), F32),
        ((8, width), F32),
        ((8, SEQ * part), F32),
        ((8, width), F32),
        ((4, 8, width), F32),
        ((32, BLK), F32),
        ((8, 32, BLK), F32),
        ((4, 32, BLK), F32),
        ((BLK, BLK), F32),
    ]
    chunks = parts + SEQ + pairs + 1
    pair_of = lambda *dims: [pltpu.SemaphoreType.DMA(dims)] * 2
    semaphores = (
        pair_of(5)
        + pair_of(4)
        + pair_of(4)
        + pair_of(6, 5)
        + pair_of(4)
        + pair_of(4) * 8
        + pair_of(chunks, 6)
        + pair_of(4)
        + pair_of(chunks, 6)
        + pair_of(4)
        + pair_of(8)
        + pair_of(4)
        + [pltpu.SemaphoreType.DMA((chunks, 3))]
    )
    results = pl.pallas_call(
        fused_kernel,
        out_shape=out_shape,
        in_specs=[anywhere] * 8 + [vmem, vmem, smem],
        out_specs=(vmem, vmem, vmem) + (anywhere,) * 7,
        scratch_shapes=[pltpu.VMEM(*s) for s in scratch] + semaphores,
        compiler_params=pltpu.CompilerParams(
            collective_id=0, has_side_effects=True, vmem_limit_bytes=VMEM_LIMIT
        ),
        name="block",
    )(
        inputs,
        cotangent,
        w_query,
        w_key,
        w_value,
        w_out,
        w_ffn_in,
        w_ffn_out,
        gains,
        rel_bias,
        doc_lengths,
    )

    steps = 4

    def rows_spec(s):
        if len(s) == 3:
            return pl.BlockSpec(
                (1, s[1] * s[0] // steps, s[2]),
                lambda i: (i // (steps // s[0]), i % (steps // s[0]), 0),
            )
        return pl.BlockSpec((s[0] // steps, s[1]), lambda i: (i, 0))

    def whole_spec(s):
        return pl.BlockSpec(s, lambda i: (0,) * len(s))

    tiny = [(docs, width), (1, rows_w), (1, rows_w), (8, heads)]
    pooled, one, two, table, gx, gq, gk, gv, go, gi, gd = pl.pallas_call(
        widen_kernel,
        out_shape=[shape(s, F32) for s in tiny + narrow],
        grid=(steps,),
        in_specs=[whole_spec(r.shape) for r in results[:3]] + [rows_spec(s) for s in narrow],
        out_specs=[whole_spec(s) for s in tiny] + [rows_spec(s) for s in narrow],
        compiler_params=pltpu.CompilerParams(vmem_limit_bytes=VMEM_LIMIT),
        name="widen",
    )(*results)
    return (pooled, gx, gq, gk, gv, go, gi, gd, one[0], two[0], table)


def fits(mesh):
    return mesh.shape["dp"] == CORES * DEPTH and mesh.shape["seq"] == SEQ


def solution(mesh):
    in_specs = (
        P("dp", "seq", None),
        P("seq", None),
        P("seq", None),
        P("seq", None),
        P("seq", None),
        P("seq", None),
        P("seq", None),
        P("seq"),
        P("seq"),
        P("seq", None),
        P("dp"),
        P("dp", "seq", None),
    )
    out_specs = (
        P("dp", None),
        P("dp", "seq", None),
        P("seq", None),
        P("seq", None),
        P("seq", None),
        P("seq", None),
        P("seq", None),
        P("seq", None),
        P("seq"),
        P("seq"),
        P("seq", None),
    )
    return jax.shard_map(
        fused_on_device if fits(mesh) else on_device, mesh=mesh, in_specs=in_specs, out_specs=out_specs, check_vma=False
    )
```

```python
import math

import jax
import jax.numpy as jnp
from jax import lax
from jax.experimental import pallas as pl
from jax.experimental.pallas import tpu as pltpu
from jax.sharding import PartitionSpec as P

EPS = 1e-06
THRESHOLDS = (12, 16, 23, 32, 46, 64, 91)
NEGATIVE = -1000000000.0
GELU_C = math.sqrt(2.0 / math.pi)
GELU_K = 0.044715


def bucket_ids(query_pos, key_pos):
    offset = key_pos[None, :] - query_pos[:, None]
    distance = jnp.abs(offset)
    upper = jnp.where(offset > 0, 16, 0).astype(jnp.int32)
    beyond = jnp.full(distance.shape, 8, jnp.int32)
    for threshold in THRESHOLDS:
        beyond = beyond + (distance >= threshold).astype(jnp.int32)
    return upper + jnp.where(distance < 8, distance, beyond)


def gelu_slope(value):
    inner = GELU_C * (value + GELU_K * value * value * value)
    tangent = jnp.tanh(inner)
    return 0.5 * (1.0 + tangent) + 0.5 * value * (1.0 - tangent * tangent) * GELU_C * (
        1.0 + 3.0 * GELU_K * value * value
    )


def outer_sum(left, right):
    return lax.dot_general(
        left, right, (((0,), (0,)), ((), ())), preferred_element_type=jnp.float32
    )


def back_project(grad, weight):
    return lax.dot_general(
        grad, weight, (((1,), (1,)), ((), ())), preferred_element_type=jnp.float32
    )


def norm_backward(source, scale, gain, grad_normed):
    grad_gain = jnp.sum(grad_normed * source * scale, 0)
    grad_scaled = grad_normed * gain
    grad_source = scale * grad_scaled - source * scale * scale * scale * jnp.mean(
        grad_scaled * source, -1, keepdims=True
    )
    return (grad_gain, grad_source)


SEQ, CORES, DEPTH = 4, 2, 4
BLK = 128
MESH = pl.DeviceIdType.MESH
F32 = jnp.float32
BF16 = jnp.bfloat16
VMEM_LIMIT = 60 << 20


def contract(left, right, left_dim, right_dim):
    return lax.dot_general(
        left, right, (((left_dim,), (right_dim,)), ((), ())), preferred_element_type=F32
    )


def exact(left, right, left_dim, right_dim):
    return lax.dot_general(
        left,
        right,
        (((left_dim,), (right_dim,)), ((), ())),
        preferred_element_type=F32,
        precision=lax.Precision.HIGHEST,
    )


def await_copy(ref, sem):
    pltpu.make_async_copy(ref, ref, sem).wait()


def tile(index, size):
    return pl.ds(pl.multiple_of(index * size, size), size)


def bucket_of(offset):
    distance = jnp.abs(offset)
    beyond = jnp.full(distance.shape, 8, jnp.int32)
    for threshold in THRESHOLDS:
        beyond = beyond + (distance >= threshold).astype(jnp.int32)
    return jnp.where(offset > 0, 16, 0) + jnp.where(distance < 8, distance, beyond)


def full_sum(value):
    return jnp.sum(jnp.sum(value, 0, keepdims=True), 1, keepdims=True)


def fused_kernel(
    inputs,
    cotangent,
    w_query,
    w_key,
    w_value,
    w_out,
    w_in,
    w_down,
    gains_in,
    bias_in,
    lengths_in,
    pooled_o,
    small_o,
    table_o,
    gx_o,
    gq_o,
    gk_o,
    gv_o,
    go_o,
    gi_o,
    gd_o,
    raised_o,
    xown,
    grads,
    nrm1,
    wqkv,
    qkv,
    mixed,
    wo,
    psend,
    precv,
    hid,
    nrm2,
    wi,
    wd,
    act,
    slope,
    gn,
    strip,
    vecs,
    maskc,
    gscale,
    flip,
    dqkv,
    gmix,
    dk_acc,
    dv_acc,
    near,
    far,
    gqkv,
    gdn,
    d_dx,
    d_dy,
    d_rx,
    d_ry,
    d_za,
    d_zb,
    i_dx,
    i_dy,
    i_rx,
    i_ry,
    i_za,
    i_zb,
    q_dx,
    q_dy,
    q_rx,
    q_ry,
    q_za,
    q_zb,
    rs_o,
    o_za,
    o_zb,
    small_all,
    wide,
    gains,
    asum,
    pp,
    pool_recv,
    sg,
    sg_plane,
    sg_depth,
    turned,
    small_ss,
    small_rs,
    x_ss,
    x_rs,
    c_ss,
    c_rs,
    wg_ss,
    wg_rs,
    wo_ss,
    wo_rs,
    n1_ss,
    n1_rs,
    g_ss,
    g_rs,
    part_ss,
    part_rs,
    n2_ss,
    n2_rs,
    gn2_ss,
    gn2_rs,
    gat_ss,
    gat_rs,
    gn1_ss,
    gn1_rs,
    gx_ss,
    gx_rs,
    rs_ss,
    rs_rs,
    rso_ss,
    rso_rs,
    z_ss,
    z_rs,
    pool_ss,
    pool_rs,
    sgp_ss,
    sgp_rs,
    sgz_ss,
    sgz_rs,
    out_s,
    raised_s,
):
    dp = lax.axis_index("dp")
    chip = lax.axis_index("seq")
    depth, core = lax.div(dp, 2), lax.rem(dp, 2)
    row, col = lax.div(chip, 2), lax.rem(chip, 2)
    other = (depth * 2 + 1 - core, chip)
    xn = row * 2 + 1 - col
    yn = (1 - row) * 2 + col
    dn = (1 - row) * 2 + 1 - col
    tokens, width = nrm1.shape
    half = width // 2
    rows_w = w_query.shape[0]
    ff_part = gdn.shape[0] * BLK
    quarter, middle_q = tokens // 4, tokens // 2
    middle_w = width // 2

    def remote(src, dst, send, recv, device):
        return pltpu.make_async_remote_copy(
            src_ref=src,
            dst_ref=dst,
            send_sem=send,
            recv_sem=recv,
            device_id=device,
            device_id_type=MESH,
        )

    def ahead(step):
        return lax.rem(chip + step, SEQ)

    pending = []

    def send_now(*args):
        copy = remote(*args)
        copy.start()
        pending.append(copy)

    lane = lax.broadcasted_iota(jnp.int32, (1, BLK), 1)
    wide[...] = jnp.zeros_like(wide)
    wide[0:2, 0:rows_w] = gains_in[...]
    turned_gains = pltpu.roll(wide[...], chip * rows_w, 1)
    small_all[0] = jnp.zeros_like(small_all[0])
    for which in range(2):
        for i in range(width // BLK):
            small_all[0, 8 * which + i : 8 * which + i + 1, :] = turned_gains[
                which : which + 1, i * BLK : (i + 1) * BLK
            ]
    small_all[0, 6:7, :] = jnp.where(
        lane == 0, lengths_in[0].astype(F32), lengths_in[1].astype(F32)
    )
    small_all[0, tile(2 + chip, 8), 0 : bias_in.shape[1]] = bias_in[...].astype(F32)

    barrier = pltpu.get_barrier_semaphore()
    for step in range(SEQ):
        if step:
            pl.semaphore_signal(barrier, inc=1, device_id=(dp, ahead(step)), device_id_type=MESH)
        pl.semaphore_signal(
            barrier, inc=1, device_id=(other[0], ahead(step)), device_id_type=MESH
        )
    for step in range(1, DEPTH):
        pl.semaphore_signal(
            barrier,
            inc=1,
            device_id=(lax.rem(depth + step, DEPTH) * 2 + core, chip),
            device_id_type=MESH,
        )
    pl.semaphore_wait(barrier, 2 * SEQ - 1 + DEPTH - 1)

    mine = small_all.at[0]
    for step in range(1, SEQ):
        send_now(
            mine, small_all.at[step], small_ss.at[step], small_rs.at[step], (dp, ahead(step))
        )
    send_now(mine, small_all.at[SEQ], small_ss.at[SEQ], small_rs.at[SEQ], other)

    def spread(source, dest_of, send, recv, action):
        for doc in range(2):
            for to in range(2):
                block = source.at[doc, pl.ds(to * BLK, BLK)]
                target = core * 2 + doc
                own = (target == chip) & (core == to)
                copy = remote(
                    block,
                    dest_of(to),
                    send.at[doc * 2 + to],
                    recv.at[chip],
                    (depth * 2 + to, target),
                )
                if action == "start":

                    @pl.when(own)
                    def _():
                        pltpu.make_async_copy(block, dest_of(to), recv.at[chip]).start()

                @pl.when(jnp.logical_not(own))
                def _():
                    if action == "start":
                        copy.start()
                    else:
                        copy.wait_send()

    x_slot = lambda to: xown.at[chip]
    c_slot = lambda to: grads.at[chip * 2 + to]
    spread(inputs, x_slot, x_ss, x_rs, "start")

    class Gather:
        def __init__(self, index, pieces, place):
            self.index, self.pieces, self.place = index, pieces, place
            self.bind()

        def half_of(self, owner, which):
            ref = self.place(owner)
            size = ref.shape[0] // 2
            return ref.at[pl.ds(which * size, size)]

        def bind(self):
            k = self.index
            self.local, self.one, self.two = [], [], []
            for src, cut in self.pieces:
                dst = cut(self.place(chip))
                self.local.append(pltpu.make_async_copy(src, dst, wg_rs.at[k, 0]))
                self.one.append(remote(src, dst, wg_ss.at[k, 0], wg_rs.at[k, 1], (dp, xn)))
                self.one.append(remote(src, dst, wg_ss.at[k, 1], wg_rs.at[k, 2], (dp, yn)))
            via_x, via_y = self.half_of(xn, 1), self.half_of(yn, 0)
            self.two = [
                remote(via_x, via_x, wg_ss.at[k, 2], wg_rs.at[k, 3], (dp, yn)),
                remote(via_y, via_y, wg_ss.at[k, 3], wg_rs.at[k, 4], (dp, xn)),
            ]
            self.from_x, self.from_y = self.place(xn), self.place(yn)
            self.last = [self.half_of(dn, 1), self.half_of(dn, 0)]
            self.own = self.place(chip)

        def first(self):
            for copy in self.local + self.one:
                copy.start()

        def second(self):
            k = self.index
            await_copy(self.from_x, wg_rs.at[k, 1])
            self.two[0].start()
            await_copy(self.from_y, wg_rs.at[k, 2])
            self.two[1].start()

        def done(self):
            k = self.index
            await_copy(self.own, wg_rs.at[k, 0])
            await_copy(self.last[0], wg_rs.at[k, 3])
            await_copy(self.last[1], wg_rs.at[k, 4])

        def sent(self):
            k = self.index
            for copy in self.two:
                copy.wait_send()
            await_copy(self.own, wg_ss.at[k, 0])
            await_copy(self.own, wg_ss.at[k, 1])

    class SharedGather(Gather):
        def part(self, owner, which):
            ref = self.place(owner)
            size = ref.shape[0] // 2
            return ref.at[tile(which, size)]

        def bind(self):
            k = self.index
            mine, theirs = lax.rem(depth, 2), 1 - lax.rem(depth, 2)
            beside = ((depth + theirs - mine) * 2 + core, chip)
            self.local, self.one = [], []
            for src, cut in self.pieces:
                size = src.shape[0] // 2
                self.local.append(
                    pltpu.make_async_copy(src, cut(self.place(chip)), wg_rs.at[k, 0])
                )
                dst = cut(self.part(chip, mine))
                src = src.at[tile(mine, size)]
                self.one.append(remote(src, dst, wg_ss.at[k, 0], wg_rs.at[k, 1], (dp, xn)))
                self.one.append(remote(src, dst, wg_ss.at[k, 1], wg_rs.at[k, 2], (dp, yn)))
            self.from_x, self.from_y = self.part(xn, mine), self.part(yn, mine)
            far = self.part(dn, mine)
            size = far.shape[0] // 2
            cut = lambda ref, which: ref.at[pl.ds(which * size, size)]
            via_x, via_y = cut(self.from_x, 1), cut(self.from_y, 0)
            self.last = [cut(far, 1), cut(far, 0)]
            self.two = [
                remote(via_x, via_x, wg_ss.at[k, 2], wg_rs.at[k, 3], (dp, yn)),
                remote(via_y, via_y, wg_ss.at[k, 3], wg_rs.at[k, 4], (dp, xn)),
            ]
            self.beside = [
                remote(ref, ref, wg_ss.at[k, 4 + n], wg_rs.at[k, 5 + n], beside)
                for n, ref in enumerate((self.from_x, self.from_y, far))
            ]
            self.own = self.place(chip)
            self.half = self.part(chip, mine)

        def second(self):
            super().second()
            for copy in self.beside[:2]:
                copy.start()

        def third(self):
            k = self.index
            await_copy(self.last[0], wg_rs.at[k, 3])
            await_copy(self.last[1], wg_rs.at[k, 4])
            self.beside[2].start()

        def done(self):
            await_copy(self.own, wg_rs.at[self.index, 0])
            for copy in self.beside:
                copy.wait_recv()

        def sent(self):
            k = self.index
            for copy in self.two + self.beside:
                copy.wait_send()
            await_copy(self.half, wg_ss.at[k, 0])
            await_copy(self.half, wg_ss.at[k, 1])

    core_cols = tile(core, half)
    whole = lambda ref: ref
    row_half = rows_w // 2

    def qkv_item(index, part):
        return Gather(
            index,
            [
                (
                    w.at[pl.ds(part * row_half, row_half), core_cols],
                    lambda ref, i=i: ref.at[:, pl.ds(i * half, half)],
                )
                for i, w in enumerate((w_query, w_key, w_value))
            ],
            lambda owner: wqkv.at[
                pl.ds(pl.multiple_of(owner * rows_w + part * row_half, row_half), row_half)
            ],
        )

    def in_item(index, part):
        return SharedGather(
            index,
            [
                (
                    w_in.at[:, tile((2 * part + f) * 2 + core, ff_part)],
                    lambda ref, f=f: ref.at[:, pl.ds(f * ff_part, ff_part)],
                )
                for f in range(2)
            ],
            lambda owner: wi.at[tile(owner, rows_w), pl.ds(part * 2 * ff_part, 2 * ff_part)],
        )

    def down_item(index, part):
        size = ff_part // 2
        return (SharedGather if part == 0 else Gather)(
            index,
            [(w_down.at[pl.ds(pl.multiple_of(core * ff_part + part * size, size), size)], whole)],
            lambda owner: wd.at[
                pl.ds(pl.multiple_of(owner * ff_part + part * size, size), size)
            ],
        )

    qkv_items = [qkv_item(0, 0), qkv_item(1, 1)]
    in_items = [in_item(2, 0), in_item(3, 1)]
    down_items = [down_item(4, 0), down_item(5, 1)]
    for it in qkv_items:
        it.first()

    wo_part = rows_w // 2
    wo_src = w_out.at[tile(core, wo_part)]
    wo_dst = wo.at[tile(col * 2 + core, wo_part)]

    def wo_each(action):
        for to in range(SEQ):
            own = (chip == to) & (core == row)
            copy = remote(
                wo_src, wo_dst, wo_ss.at[to], wo_rs.at[col * 2 + core], (depth * 2 + row, to)
            )
            if action == "start":

                @pl.when(own)
                def _():
                    pltpu.make_async_copy(wo_src, wo_dst, wo_rs.at[col * 2 + core]).start()

            @pl.when(jnp.logical_not(own))
            def _():
                if action == "start":
                    copy.start()
                else:
                    copy.wait_send()

    for step in range(1, SEQ + 1):
        await_copy(small_all.at[step], small_rs.at[step])
    summed = small_all[0] + small_all[1] + small_all[2] + small_all[3]
    for which in range(2):
        gains[which : which + 1, :] = jnp.concatenate(
            [summed[8 * which + i : 8 * which + i + 1, :] for i in range(width // BLK)], axis=1
        )
    length_row = jnp.where(row == core, small_all[0, 6:7, :], small_all[SEQ, 6:7, :])
    length = jnp.where(col == 0, length_row[:, 0:1], length_row[:, 1:2])
    own_lengths = small_all[0, 6:7, 0:2]
    table = summed[16:48, :].astype(BF16)
    lane_two = lax.broadcasted_iota(jnp.int32, (1, 2 * BLK), 1)
    minus = jnp.where(lane_two < BLK, lane_two, lane_two - 2 * BLK)
    for off in (-1, 0, 1):
        ids = bucket_of(off * BLK - minus)
        onehot = (lax.broadcasted_iota(jnp.int32, (32, 2 * BLK), 0) == ids).astype(BF16)
        vecs[off + 1] = contract(table, onehot, 0, 0)[0:16, :]

    @pl.loop(0, 6)
    def _(h):
        values = [vecs[i, pl.ds(core * 6 + h, 1), :] for i in range(3)]
        left = jnp.broadcast_to(values[0][:, BLK - 1 : BLK], (BLK, BLK))
        right = jnp.broadcast_to(values[2][:, BLK + 1 : BLK + 2], (BLK, BLK))
        strip[h, 0:BLK, :] = left
        strip[h, 4 * BLK :, :] = right
        for i in range(3):
            skewed = pltpu.roll(
                jnp.broadcast_to(values[i], (BLK, 2 * BLK)), 0, 1, stride=1, stride_axis=0
            )
            strip[h, (i + 1) * BLK : (i + 2) * BLK, :] = skewed[:, :BLK]

    key_pos = lax.broadcasted_iota(jnp.int32, maskc.shape, 0).astype(F32)
    maskc[...] = jnp.where((key_pos < length) | (lane > 0), 0.0, NEGATIVE).astype(BF16)

    def block_valid(b):
        pos = lax.broadcasted_iota(jnp.int32, (BLK, 1), 0) + b * BLK
        return (pos.astype(F32) < length).astype(F32)

    def n1_copy(i):
        block = nrm1.at[tile(2 * i + core, BLK)]
        return remote(block, block, n1_ss.at[i], n1_rs.at[i], other)

    @pl.loop(0, SEQ)
    def _(i):
        await_copy(xown.at[i], x_rs.at[i])
        source = xown[i].astype(F32)
        scale = lax.rsqrt(jnp.mean(source * source, -1, keepdims=True) + EPS)
        nrm1[tile(2 * i + core, BLK), :] = (source * scale * gains[0:1, :]).astype(BF16)
        n1_copy(i).start()

    qkv_items[0].second()
    qkv_items[1].second()
    wo_each("start")
    for it in in_items:
        it.first()
    for it in qkv_items:
        it.done()
    for i in range(SEQ):
        n1_copy(i).wait_recv()

    @pl.loop(0, 4)
    def _(i):
        rows = tile(i, quarter)
        qkv[rows, :] = contract(nrm1[rows, :], wqkv[...], 1, 0).astype(BF16)

    flip[BLK : BLK + 16, :] = jnp.ones((16, tokens), BF16)
    mine_lanes = [lane < 64, lane >= 64]
    slots = [ref.at[:, pl.ds(0, tokens)] for ref in (act, slope)]

    def by_head(value):
        return jnp.concatenate(
            [jnp.where(lanes, value, jnp.zeros_like(value)) for lanes in mine_lanes], axis=0
        )

    def serve(now, table):
        for when, actions in table.items():

            @pl.when(now == when)
            def _():
                for action in actions:
                    action()

    def keep(pair, qb):
        return pltpu.make_async_copy(slots[qb], raised_o.at[2 * pair + qb], raised_s.at[qb])

    def fetch(pair, qb):
        return pltpu.make_async_copy(raised_o.at[2 * pair + qb], slots[qb], raised_s.at[qb])

    def later_inputs():
        spread(cotangent, c_slot, c_ss, c_rs, "start")
        for it in down_items:
            it.first()

    forward_table = {
        2: [in_items[0].second],
        3: [in_items[1].second, later_inputs],
        4: [in_items[0].third],
    }

    @pl.loop(0, 3)
    def _(pair):
        cols = tile(pair, BLK)
        flip[0:BLK, :] = jnp.transpose(qkv[:, tile(6 + pair, BLK)])
        keys = jnp.concatenate([qkv[:, tile(3 + pair, BLK)], maskc[...]], axis=1)
        for qb in range(2):
            rows = pl.ds(qb * middle_q, middle_q)
            queries = by_head(qkv[rows, cols])
            flag = jnp.broadcast_to(jnp.where(lane == 0, 1.0, 0.0).astype(BF16), queries.shape)
            biases = [
                jnp.concatenate(
                    [
                        strip[
                            pair * 2 + h, pl.ds((min(max(kb - q, -2), 2) + 2) * BLK, BLK), :
                        ]
                        for kb in range(tokens // BLK)
                    ],
                    axis=0,
                )
                for h in range(2)
                for q in range(qb * middle_q // BLK, (qb + 1) * middle_q // BLK)
            ]
            logits = contract(keys, jnp.concatenate([queries, flag], axis=1), 1, 1)
            logits = logits + jnp.concatenate(biases, axis=1)
            highest = jnp.max(logits, 0, keepdims=True)
            raised = jnp.exp(logits - highest).astype(BF16)

            @pl.when(pair > 0)
            def _():
                keep(pair - 1, qb).wait()

            slots[qb][...] = raised
            keep(pair, qb).start()
            result = contract(flip[...], raised, 1, 0)
            inverse = 1.0 / result[BLK : BLK + 1, :]
            scaled = result[0:BLK, :] * inverse
            mixed[rows, cols] = jnp.transpose(
                jnp.concatenate([scaled[0:64, 0:middle_q], scaled[64:BLK, middle_q:]], axis=0)
            ).astype(BF16)
            for h in range(2):
                gscale[pl.ds(2 * pair + h, 1), rows] = inverse[:, h * middle_q : (h + 1) * middle_q]
            serve(2 * pair + qb, forward_table)

    def swap_copy(i, send, recv):
        return remote(psend.at[i], precv.at[i], send.at[i], recv.at[i], other)

    in_items[1].third()
    for k in range(4):
        await_copy(wo.at[pl.ds(k * wo_part, wo_part)], wo_rs.at[k])

    def blocks_of(ref, parity):
        return jnp.concatenate(
            [ref[tile(2 * i + parity, BLK), :] for i in range(SEQ)], axis=0
        )

    def swap_out(result, send, recv):
        for i in range(SEQ):
            psend[i] = result[i * BLK : (i + 1) * BLK, :]
            swap_copy(i, send, recv).start()

    swap_out(contract(blocks_of(mixed, 1 - core), wo[...], 1, 0), part_ss, part_rs)

    def n2_copy(i, send, recv):
        block = nrm2.at[tile(2 * i + core, BLK)]
        return remote(block, block, send.at[i], recv.at[i], other)

    pp[...] = jnp.zeros_like(pp)
    result = contract(blocks_of(mixed, core), wo[...], 1, 0)
    for i in range(SEQ):
        hidden = xown[i].astype(F32) + result[i * BLK : (i + 1) * BLK, :]
        swap_copy(i, part_ss, part_rs).wait_recv()
        hidden = hidden + precv[i]
        hid[i] = hidden
        scale = lax.rsqrt(jnp.mean(hidden * hidden, -1, keepdims=True) + EPS)
        nrm2[tile(2 * i + core, BLK), :] = (hidden * scale * gains[1:2, :]).astype(BF16)
        n2_copy(i, n2_ss, n2_rs).start()
        pp[0:1, :] += jnp.sum(hidden * block_valid(2 * i + core), 0, keepdims=True)
    for i in range(SEQ):
        n2_copy(i, n2_ss, n2_rs).wait_recv()
    for qb in range(2):
        keep(2, qb).wait()

    def g_copy(i):
        block = grads.at[2 * i + core]
        return remote(block, block, g_ss.at[i], g_rs.at[i], other)

    def take_cotangent():
        @pl.loop(0, SEQ)
        def _(i):
            b = 2 * i + core
            await_copy(grads.at[b], c_rs.at[i])
            grads[b] = (grads[b].astype(F32) * block_valid(b)).astype(BF16)
            g_copy(i).start()

    asum[...] = jnp.zeros_like(asum)
    wide_part = 2 * ff_part
    for part in range(2):
        part_cols = slice(part * wide_part, (part + 1) * wide_part)
        if part == 1:
            down_items[0].second()
            take_cotangent()
        in_items[part].done()

        @pl.loop(0, 2)
        def _(i):
            rows = tile(i, middle_q)
            value = contract(nrm2[rows, :], wi[:, part_cols], 1, 0)
            square = value * value
            tangent = jnp.tanh(value * (GELU_C + GELU_C * GELU_K * square))
            half_up = 0.5 + 0.5 * tangent
            active = (value * half_up).astype(BF16)
            act[rows, part_cols] = active
            slope[rows, part_cols] = (
                half_up
                + value
                * (1.0 - tangent * tangent)
                * (0.5 * GELU_C + 1.5 * GELU_C * GELU_K * square)
            ).astype(BF16)
            pos = lax.broadcasted_iota(jnp.int32, (8, middle_q), 1) + i * middle_q
            valid = (pos.astype(F32) < length).astype(BF16)
            asum[:, part_cols] += contract(valid, active, 1, 0)


    for i in range(SEQ):
        g_copy(i).wait_recv()
    g_all = lambda: grads[...].reshape(tokens, width)

    class Chunk:
        made = 0

        def __init__(self, src, dx, dy, rx, ry, za, zb, outs):
            self.index = Chunk.made
            Chunk.made += 1
            self.src, self.dx, self.dy, self.rx, self.ry = src, dx, dy, rx, ry
            self.za, self.zb, self.outs = za, zb, outs
            self.bind()

        def bind(self):
            k = self.index
            size = self.dx.shape[0]
            cut = lambda ref, which: ref.at[pl.ds(which * size, size)]
            ss, rs = (lambda i: rs_ss.at[k, i]), (lambda i: rs_rs.at[k, i])
            to_x, to_y = (dp, xn), (dp, yn)
            self.one = [
                remote(cut(self.src(dn), 1), self.dx, ss(0), rs(0), to_x),
                remote(cut(self.src(dn), 0), self.dy, ss(1), rs(1), to_y),
                remote(cut(self.src(xn), 1), cut(self.rx, 1), ss(2), rs(2), to_x),
                remote(cut(self.src(yn), 0), cut(self.ry, 0), ss(3), rs(3), to_y),
            ]
            self.sum_y, self.sum_x = cut(self.src(yn), 1), cut(self.src(xn), 0)
            self.two = [
                remote(self.sum_y, cut(self.ry, 1), ss(4), rs(4), to_y),
                remote(self.sum_x, cut(self.rx, 0), ss(5), rs(5), to_x),
            ]
            self.bind_z(self.rx, self.ry)

        def bind_z(self, reduced, final):
            k = self.index
            self.reduced, self.final = reduced, final
            sem = lambda i: (z_ss.at[k, i], z_rs.at[k, i])
            self.to_inner = remote(reduced, self.za, *sem(0), z_dev(toward))
            self.swap = remote(reduced, self.zb, *sem(1), z_dev(across))
            self.to_end = remote(final, final, *sem(2), z_dev(outward))

        def start(self):
            for copy in self.one:
                copy.start()

        def middle(self):
            for at, sent, sums, copy in (
                (0, self.dx, self.sum_y, self.two[0]),
                (1, self.dy, self.sum_x, self.two[1]),
            ):
                self.one[at].wait_recv()
                sums[...] = (sums[...].astype(F32) + sent[...].astype(F32)).astype(BF16)
                copy.start()

        def total(self):
            for copy in (self.one[2], self.one[3], *self.two):
                copy.wait_recv()
            self.rx[...] = (
                self.src(chip)[...].astype(F32)
                + self.rx[...].astype(F32)
                + self.ry[...].astype(F32)
            ).astype(BF16)

        def z_one(self):
            self.total()

            @pl.when(end_z)
            def _():
                self.to_inner.start()

        def z_two(self):
            @pl.when(inner_z)
            def _():
                self.to_inner.wait_recv()
                self.reduced[...] = (
                    self.reduced[...].astype(F32) + self.za[...].astype(F32)
                ).astype(BF16)
                self.swap.start()

        def z_three(self):
            @pl.when(inner_z)
            def _():
                self.swap.wait_recv()
                self.final[...] = (
                    self.reduced[...].astype(F32) + self.zb[...].astype(F32)
                ).astype(BF16)
                self.to_end.start()

        def each_out(self, act_on):
            k = self.index
            for n, (cols, place) in enumerate(self.outs):
                src = self.final if cols is None else self.final.at[:, cols]
                act_on(
                    remote(src, place(core), z_ss.at[k, 3 + n], z_rs.at[k, 3 + n], other),
                    pltpu.make_async_copy(src, place(core), out_s.at[k, n]),
                )

        def z_four(self):
            @pl.when(end_z)
            def _():
                self.to_end.wait_recv()

            self.each_out(lambda there, here: (there.start(), here.start()))

        def finish(self):
            self.each_out(
                lambda there, here: (there.wait_recv(), there.wait_send(), here.wait())
            )

            @pl.when(end_z)
            def _():
                self.to_inner.wait_send()

            @pl.when(inner_z)
            def _():
                self.swap.wait_send()
                self.to_end.wait_send()

            for copy in self.plane_sends():
                copy.wait_send()

        def plane_sends(self):
            return self.one + self.two

    inner_z = (depth == 1) | (depth == 2)
    end_z = jnp.logical_not(inner_z)
    toward = jnp.where(depth == 0, 1, 2)
    outward = jnp.where(depth == 1, 0, 3)
    across = jnp.where(depth == 1, 2, 1)

    def z_dev(z):
        return (z * 2 + core, chip)

    d_chunks = [
        Chunk(
            lambda owner, i=i: gdn.at[i, owner],
            d_dx.at[i],
            d_dy.at[i],
            d_rx.at[i],
            d_ry.at[i],
            d_za.at[i],
            d_zb.at[i],
            [
                (
                    None,
                    lambda c, i=i: gd_o.at[
                        pl.ds(pl.multiple_of(c * ff_part + i * BLK, BLK), BLK)
                    ],
                )
            ],
        )
        for i in range(ff_part // BLK)
    ]

    for i in range(ff_part // BLK):
        columns = jnp.concatenate(
            [act[:, f * ff_part + i * BLK : f * ff_part + (i + 1) * BLK] for f in range(SEQ)],
            axis=1,
        )
        gdn[i] = contract(columns, g_all(), 0, 0).astype(BF16).reshape(SEQ, BLK, width)
        if i == 0:
            down_items[1].second()
    down_items[0].third()
    for chunk in d_chunks:
        chunk.start()
    for it in down_items:
        it.done()
    for it in in_items:
        it.sent()

    def pooled_part(cols):
        total = asum[0:1, cols]
        high = total.astype(BF16)
        rest = total - high.astype(F32)
        middle = rest.astype(BF16)
        low = (rest - middle.astype(F32)).astype(BF16)
        pieces = jnp.concatenate(
            [jnp.broadcast_to(piece, (16, piece.shape[1])) for piece in (high, middle, low)], axis=0
        )
        result = contract(pieces, wd[cols, :], 1, 0)
        pp[0:1, :] += result[0:1, :] + result[16:17, :] + result[32:33, :]

    i_chunks = [
        Chunk(
            lambda owner, f=f: wi.at[tile(owner, rows_w), pl.ds(f * ff_part, ff_part)],
            i_dx.at[f],
            i_dy.at[f],
            i_rx.at[f],
            i_ry.at[f],
            i_za.at[f],
            i_zb.at[f],
            [(None, lambda c, f=f: gi_o.at[:, tile(2 * f + c, ff_part)])],
        )
        for f in range(SEQ)
    ]
    for part in range(2):
        part_cols = slice(part * wide_part, (part + 1) * wide_part)

        @pl.loop(0, 2)
        def _(i):
            rows = tile(i, middle_q)
            upstream = grads[pl.ds(4 * i, 4)].reshape(middle_q, width)
            grad = contract(upstream, wd[part_cols, :], 1, 1) * slope[rows, part_cols].astype(F32)
            slope[rows, part_cols] = grad.astype(BF16)

        pooled_part(part_cols)

    d_chunks[0].middle()

    for i in range(SEQ):
        swap_copy(i, part_ss, part_rs).wait_send()
    swap_out(contract(blocks_of(slope, 1 - core), wi[...], 1, 1), gn2_ss, gn2_rs)
    gn[...] = contract(blocks_of(slope, core), wi[...], 1, 1).reshape(SEQ, BLK, width)
    d_chunks[1].middle()
    for part in range(2):
        part_cols = slice(part * wide_part, (part + 1) * wide_part)

        @pl.loop(0, width // (2 * BLK))
        def _(i):
            wi[tile(i, 2 * BLK), part_cols] = contract(
                nrm2[:, tile(i, 2 * BLK)], slope[:, part_cols], 0, 0
            ).astype(BF16)

        if part == 1:
            d_chunks[2].middle()
        i_chunks[2 * part].start()
        i_chunks[2 * part + 1].start()
    def pool_each(action):
        for to in range(SEQ):
            own = (chip == to) & (core == row)
            dst = pool_recv.at[col * 2 + core]
            copy = remote(pp, dst, pool_ss.at[to], pool_rs.at[col * 2 + core], (depth * 2 + row, to))
            if action == "start":

                @pl.when(own)
                def _():
                    pltpu.make_async_copy(pp, dst, pool_rs.at[col * 2 + core]).start()

            @pl.when(jnp.logical_not(own))
            def _():
                if action == "start":
                    copy.start()
                else:
                    copy.wait_send()

    def gat_copy(i):
        block = act.at[tile(2 * i + core, BLK), pl.ds(0, width)]
        return remote(block, block, gat_ss.at[i], gat_rs.at[i], other)

    for i in range(SEQ):
        n2_copy(i, n2_ss, n2_rs).wait_send()
    sg[...] = jnp.zeros_like(sg)

    def add_gain(first, value):
        for i in range(width // BLK):
            sg[first + i : first + i + 1, :] += value[:, i * BLK : (i + 1) * BLK]

    @pl.loop(0, SEQ)
    def _(i):
        b = 2 * i + core
        swap_copy(i, gn2_ss, gn2_rs).wait_recv()
        normed = gn[i] + precv[i]
        hidden = hid[i]
        scale = lax.rsqrt(jnp.mean(hidden * hidden, -1, keepdims=True) + EPS)
        add_gain(8, jnp.sum(normed * hidden * scale, 0, keepdims=True))
        scaled = normed * gains[1:2, :]
        inner = jnp.mean(scaled * hidden, -1, keepdims=True)
        result = grads[b].astype(F32) + scale * scaled - hidden * (scale * scale * scale) * inner
        hid[i] = result
        act[tile(b, BLK), 0:width] = result.astype(BF16)
        gat_copy(i).start()

    pool_each("start")
    d_chunks[0].z_one()
    for i in range(SEQ):
        gat_copy(i).wait_recv()

    @pl.loop(0, 2)
    def _(i):
        rows = tile(i, middle_q)
        inverse = jnp.concatenate(
            [
                jnp.transpose(
                    jnp.concatenate(
                        [
                            jnp.broadcast_to(gscale[2 * p + h : 2 * p + h + 1, rows], (64, middle_q))
                            for h in range(2)
                        ],
                        axis=0,
                    )
                )
                for p in range(3)
            ],
            axis=1,
        )
        gmix[rows, :] = (contract(act[rows, 0:width], wo[...], 1, 1) * inverse).astype(BF16)

    wo[...] = contract(mixed[...], act[:, 0:width], 0, 0).astype(BF16)
    for i in range(SEQ):
        gat_copy(i).wait_send()
    for qb in range(2):
        fetch(0, qb).start()
    d_chunks[1].z_one()

    def rso_each(action):
        for k in range(2):
            for to in range(2):
                target = core * 2 + k
                own = (chip == target) & (core == to)
                src = wo.at[pl.ds((2 * k + to) * wo_part, wo_part)]
                dst = rs_o.at[chip]
                copy = remote(
                    src, dst, rso_ss.at[2 * k + to], rso_rs.at[chip], (depth * 2 + to, target)
                )
                if action == "start":

                    @pl.when(own)
                    def _():
                        pltpu.make_async_copy(src, dst, rso_rs.at[chip]).start()

                @pl.when(jnp.logical_not(own))
                def _():
                    if action == "start":
                        copy.start()
                    else:
                        copy.wait_send()

    class OutChunk(Chunk):
        def bind(self):
            self.bind_z(self.src.at[0], self.src.at[1])

        def total(self):
            for i in range(SEQ):
                await_copy(self.src.at[i], rso_rs.at[i])
            value = self.src[0].astype(F32)
            for i in range(1, SEQ):
                value = value + self.src[i].astype(F32)
            self.reduced[...] = value.astype(BF16)

        def plane_sends(self):
            return []

    o_chunk = OutChunk(
        rs_o, None, None, None, None, o_za, o_zb, [(None, lambda c: go_o.at[tile(c, wo_part)])]
    )

    sub = lax.broadcasted_iota(jnp.int32, (16, tokens), 0)
    key_block = lax.div(lax.broadcasted_iota(jnp.int32, (16, tokens), 1), BLK)
    flip[BLK : BLK + 16, :] = (sub == key_block).astype(BF16)
    near[...] = jnp.zeros_like(near)
    far[...] = jnp.zeros_like(far)

    q_chunks = [
        Chunk(
            lambda owner, p=p: gqkv.at[p, tile(owner, rows_w)],
            q_dx.at[p],
            q_dy.at[p],
            q_rx.at[p],
            q_ry.at[p],
            q_za.at[p],
            q_zb.at[p],
            [
                (
                    pl.ds(j * BLK, BLK),
                    lambda c, p=p, o=o: o.at[:, tile(c * 3 + p, BLK)],
                )
                for j, o in enumerate((gq_o, gk_o, gv_o))
            ],
        )
        for p in range(3)
    ]
    backward_table = {
        0: [i_chunks[0].middle, d_chunks[2].z_one, d_chunks[0].z_two],
        1: [i_chunks[1].middle, i_chunks[2].middle, d_chunks[1].z_two],
        2: [
            lambda: rso_each("start"),
            i_chunks[3].middle,
            d_chunks[0].z_three,
            d_chunks[2].z_two,
            i_chunks[0].z_one,
        ],
        3: [d_chunks[1].z_three, i_chunks[1].z_one, i_chunks[0].z_two],
        4: [
            q_chunks[0].middle,
            d_chunks[2].z_three,
            d_chunks[0].z_four,
            i_chunks[2].z_one,
            i_chunks[1].z_two,
        ],
        5: [i_chunks[3].z_one, i_chunks[0].z_three, d_chunks[1].z_four, i_chunks[2].z_two],
    }

    @pl.loop(0, 3)
    def _(pair):
        cols = tile(pair, BLK)
        flip[0:BLK, :] = jnp.transpose(qkv[:, tile(3 + pair, BLK)])
        for qb in range(2):
            rows = pl.ds(qb * middle_q, middle_q)
            upstream = gmix[rows, cols]
            masked = by_head(upstream)
            queries = by_head(qkv[rows, cols])
            product = jnp.transpose(upstream.astype(F32) * mixed[rows, cols].astype(F32))
            inner = jnp.concatenate(
                [jnp.sum(product[64 * h : 64 * h + 64, :], 0, keepdims=True) for h in range(2)],
                axis=1,
            )
            fetch(pair, qb).wait()
            raised = slots[qb][...]
            grad_probs = contract(qkv[:, tile(6 + pair, BLK)], masked, 1, 1)
            grad_logits = (raised.astype(F32) * (grad_probs - inner)).astype(BF16)
            grad_values = contract(raised, masked, 1, 0)
            grad_keys = contract(grad_logits, queries, 1, 0)
            if qb == 0:
                dv_acc[...] = grad_values
                dk_acc[...] = grad_keys
            else:
                dv_acc[...] += grad_values
                dk_acc[...] += grad_keys
            result = contract(flip[...], grad_logits, 1, 0)
            dqkv[rows, cols] = jnp.transpose(
                jnp.concatenate([result[0:64, 0:middle_q], result[64:BLK, middle_q:]], axis=0)
            ).astype(BF16)
            sums = result[BLK : BLK + 8, :]
            block_row = lax.broadcasted_iota(jnp.int32, sums.shape, 0)
            block_col = lax.rem(
                lax.div(lax.broadcasted_iota(jnp.int32, sums.shape, 1), BLK), middle_q // BLK
            )
            gap = block_row - block_col - qb * (middle_q // BLK)
            far[pair, 0] += jnp.where(gap <= -2, sums, 0.0)
            far[pair, 1] += jnp.where(gap >= 2, sums, 0.0)
            for h in range(2):
                for off in range(3):
                    total = near[(pair * 2 + h) * 3 + off]
                    for i in range(middle_q // BLK):
                        kb = qb * (middle_q // BLK) + i + off - 1
                        if 0 <= kb < tokens // BLK:
                            first = h * middle_q + i * BLK
                            total = total + grad_logits[
                                kb * BLK : (kb + 1) * BLK, first : first + BLK
                            ].astype(F32)
                    near[(pair * 2 + h) * 3 + off] = total

            @pl.when(pair < 2)
            def _():
                fetch(pair + 1, qb).start()

            if qb == 1:
                dqkv[:, tile(3 + pair, BLK)] = dk_acc[...].astype(BF16)
                dqkv[:, tile(6 + pair, BLK)] = dv_acc[...].astype(BF16)
                right = jnp.concatenate(
                    [dqkv[:, tile(3 * j + pair, BLK)] for j in range(3)], axis=1
                )

                @pl.loop(0, width // middle_w)
                def _(i):
                    gqkv[pair, tile(i, middle_w), :] = contract(
                        nrm1[:, tile(i, middle_w)], right, 0, 0
                    ).astype(BF16)

                for p in range(3):

                    @pl.when(pair == p)
                    def _():
                        q_chunks[p].start()

            serve(2 * pair + qb, backward_table)

    for i in range(SEQ):
        swap_copy(i, gn2_ss, gn2_rs).wait_send()

    swap_out(contract(blocks_of(dqkv, 1 - core), wqkv[...], 1, 1), gn1_ss, gn1_rs)
    i_chunks[1].z_three()
    d_chunks[2].z_four()
    i_chunks[3].z_two()

    def gx_each(i, action):
        own = (chip == i) & (core == row)
        dst = gx_o.at[col, tile(core, BLK)]
        copy = remote(
            nrm2.at[pl.ds(i * BLK, BLK)], dst, gx_ss.at[i], gx_rs.at[col * 2 + core], (depth * 2 + row, i)
        )
        if action == "start":

            @pl.when(own)
            def _():
                pltpu.make_async_copy(nrm2.at[pl.ds(i * BLK, BLK)], dst, gx_rs.at[col * 2 + core]).start()

        @pl.when(jnp.logical_not(own))
        def _():
            if action == "start":
                copy.start()
            else:
                copy.wait_send()

    both = contract(blocks_of(dqkv, core), wqkv[...], 1, 1)
    for i in range(SEQ):
        swap_copy(i, gn1_ss, gn1_rs).wait_recv()
        normed = both[i * BLK : (i + 1) * BLK, :] + precv[i]
        source = xown[i].astype(F32)
        scale = lax.rsqrt(jnp.mean(source * source, -1, keepdims=True) + EPS)
        add_gain(0, jnp.sum(normed * source * scale, 0, keepdims=True))
        scaled = normed * gains[0:1, :]
        inner = jnp.mean(scaled * source, -1, keepdims=True)
        result = hid[i] + scale * scaled - source * (scale * scale * scale) * inner
        nrm2[i * BLK : (i + 1) * BLK, :] = result.astype(BF16)

    q_chunks[1].middle()
    o_chunk.z_one()
    q_chunks[0].z_one()
    i_chunks[2].z_three()
    i_chunks[0].z_four()

    diag_row = lax.broadcasted_iota(jnp.int32, (BLK, BLK), 0)
    diag_col = lax.broadcasted_iota(jnp.int32, (BLK, BLK), 1)
    upper = diag_col >= diag_row
    mirror = (diag_row + diag_col == BLK - 1).astype(F32)
    shift = lax.broadcasted_iota(jnp.int32, (1, BLK), 1) + 1
    shift = jnp.where(shift == BLK, 0, shift)
    ids = bucket_of(jnp.concatenate([-shift, BLK - shift], axis=1))
    onehot = (lax.broadcasted_iota(jnp.int32, (BLK, 2 * BLK), 0) == ids).astype(F32)

    @pl.loop(0, 6)
    def _(h):
        def skew(x):
            return pltpu.roll(exact(mirror, x, 1, 0), 0, 1, stride=1, stride_axis=0)

        def far_of(h, side):
            both = far[lax.div(h, 2), side]
            return jnp.where(lax.rem(h, 2) == 0, both[:, 0:middle_q], both[:, middle_q:])

        tiles = [near[h * 3 + i] for i in range(3)]
        at = [
            jnp.sum(
                skew(jnp.where(upper, tiles[i + 1], 0.0) + jnp.where(upper, 0.0, tiles[i])),
                0,
                keepdims=True,
            )
            for i in range(2)
        ]
        below = full_sum(jnp.where(upper, tiles[0], 0.0)) + full_sum(far_of(h, 0))
        above = full_sum(jnp.where(upper, 0.0, tiles[2])) + full_sum(far_of(h, 1))
        sums = exact(jnp.broadcast_to(jnp.concatenate(at, axis=1), (8, 2 * BLK)), onehot, 1, 1)
        sums = sums[0:1, :] + jnp.where(lane == 15, below, 0.0) + jnp.where(lane == 31, above, 0.0)
        sg[pl.ds(16 + core * 6 + h, 1), :] = sums

    place = core * SEQ + chip

    def sgp_each(action):
        for step in range(SEQ):
            for cross in range(2):
                if step == 0 and cross == 0:
                    continue
                to_core = lax.rem(core + cross, 2)
                copy = remote(
                    sg,
                    sg_plane.at[place],
                    sgp_ss.at[step * 2 + cross],
                    sgp_rs.at[place],
                    (depth * 2 + to_core, ahead(step)),
                )
                if action == "start":
                    copy.start()
                else:
                    copy.wait_send()

    sgp_each("start")
    pltpu.make_async_copy(sg, sg_plane.at[place], sgp_rs.at[place]).start()
    q_chunks[2].middle()
    for i in range(SEQ):
        gx_each(i, "start")
    i_chunks[1].z_four()
    i_chunks[3].z_three()
    o_chunk.z_two()
    q_chunks[0].z_two()
    q_chunks[1].z_one()
    for i in range(8):
        await_copy(sg_plane.at[i], sgp_rs.at[i])
    total = sg_plane[0]
    for i in range(1, 8):
        total = total + sg_plane[i]
    sg_depth[depth] = total

    def sgz_copy(step):
        return remote(
            sg_depth.at[depth],
            sg_depth.at[depth],
            sgz_ss.at[step],
            sgz_rs.at[depth],
            z_dev(lax.rem(depth + step, DEPTH)),
        )

    for step in range(1, DEPTH):
        sgz_copy(step).start()
    i_chunks[2].z_four()
    o_chunk.z_three()
    q_chunks[2].z_one()
    q_chunks[1].z_two()
    q_chunks[0].z_three()
    i_chunks[3].z_four()
    o_chunk.z_four()
    q_chunks[2].z_two()
    q_chunks[1].z_three()
    q_chunks[0].z_four()
    q_chunks[2].z_three()
    q_chunks[1].z_four()
    q_chunks[2].z_four()

    for i in range(4):
        await_copy(pool_recv.at[i], pool_rs.at[i])
    for doc in range(2):
        pooled_o[doc : doc + 1, :] = (
            pool_recv[2 * doc, 0:1, :] + pool_recv[2 * doc + 1, 0:1, :]
        ) / own_lengths[:, doc : doc + 1]
    for step in range(1, DEPTH):
        z = lax.rem(depth + DEPTH - step, DEPTH)
        await_copy(sg_depth.at[z], sgz_rs.at[z])
    total = sg_depth[0] + sg_depth[1] + sg_depth[2] + sg_depth[3]
    for which in range(2):
        wide[which : which + 1, :] = jnp.concatenate(
            [total[8 * which + i : 8 * which + i + 1, :] for i in range(width // BLK)], axis=1
        )
    small_o[...] = pltpu.roll(wide[...], lax.rem(width - chip * rows_w, width), 1)[:, : small_o.shape[1]]
    turned[:, 0:16] = jnp.transpose(total[16:32, :])
    table_o[...] = turned[tile(chip, 8), :]

    for i in range(4):
        await_copy(gx_o.at[i // 2, pl.ds((i % 2) * BLK, BLK)], gx_rs.at[i])
    for copy in pending:
        copy.wait_send()
    spread(inputs, x_slot, x_ss, x_rs, "wait")
    spread(cotangent, c_slot, c_ss, c_rs, "wait")
    for it in qkv_items + down_items:
        it.sent()
    wo_each("wait")
    pool_each("wait")
    rso_each("wait")
    sgp_each("wait")
    for i in range(SEQ):
        n1_copy(i).wait_send()
        g_copy(i).wait_send()
        swap_copy(i, gn1_ss, gn1_rs).wait_send()
        gx_each(i, "wait")
    for step in range(1, DEPTH):
        sgz_copy(step).wait_send()
    for chunk in (*d_chunks, *i_chunks, o_chunk, *q_chunks):
        chunk.finish()


def widen_kernel(pooled, small, table, gx, gq, gk, gv, go, gi, gd, *outs):
    pooled_out, one_out, two_out, table_out, *outs = outs
    pooled_out[...] = pooled[...]
    one_out[...] = small[0:1, : one_out.shape[1]]
    two_out[...] = small[1:2, : two_out.shape[1]]
    table_out[...] = table[:, : table_out.shape[1]]
    for value, out in zip((gx, gq, gk, gv, go, gi, gd), outs):
        out[...] = value[...].astype(F32)


def on_device(
    inputs,
    w_query,
    w_key,
    w_value,
    w_out,
    w_ffn_in,
    w_ffn_out,
    attn_gain,
    ffn_gain,
    rel_bias,
    doc_lengths,
    cotangent,
):
    blocks, shard_len, width = inputs.shape
    heads = rel_bias.shape[1]
    head_dim = width // heads
    full_len = shard_len * lax.axis_size("seq")
    total_rows = blocks * shard_len
    gathered = (
        lax.all_gather(w_query, "seq", axis=0, tiled=True),
        lax.all_gather(w_key, "seq", axis=0, tiled=True),
        lax.all_gather(w_value, "seq", axis=0, tiled=True),
        lax.all_gather(w_out, "seq", axis=0, tiled=True),
        lax.all_gather(w_ffn_in, "seq", axis=0, tiled=True),
        lax.all_gather(w_ffn_out, "seq", axis=0, tiled=True),
        lax.all_gather(attn_gain, "seq", axis=0, tiled=True),
        lax.all_gather(ffn_gain, "seq", axis=0, tiled=True),
        lax.all_gather(rel_bias, "seq", axis=0, tiled=True),
    )
    (
        full_query,
        full_key,
        full_value,
        full_out,
        full_in,
        full_down,
        gain_one,
        gain_two,
        bias_table,
    ) = gathered
    gain_one = gain_one.astype(jnp.float32)
    gain_two = gain_two.astype(jnp.float32)
    bucket_range = jnp.arange(bias_table.shape[0], dtype=jnp.int32)
    query_pos = lax.axis_index("seq") * shard_len + jnp.arange(shard_len, dtype=jnp.int32)
    key_pos = jnp.arange(full_len, dtype=jnp.int32)
    onehot = (bucket_ids(query_pos, key_pos)[:, :, None] == bucket_range).astype(jnp.bfloat16)
    bias_heads = jnp.einsum("qkn,nh->hqk", onehot, bias_table, preferred_element_type=jnp.float32)
    key_valid = key_pos[None, :] < doc_lengths[:, None]
    query_valid = (query_pos[None, :] < doc_lengths[:, None]).astype(jnp.float32)
    flat = inputs.astype(jnp.float32).reshape(total_rows, width)
    scale_one = lax.rsqrt(jnp.mean(flat * flat, -1, keepdims=True) + EPS)
    normed_one = (flat * scale_one * gain_one).astype(jnp.bfloat16)
    queries = jnp.dot(normed_one, full_query, preferred_element_type=jnp.float32).astype(
        jnp.bfloat16
    )
    keys_local = jnp.dot(normed_one, full_key, preferred_element_type=jnp.float32).astype(
        jnp.bfloat16
    )
    values_local = jnp.dot(normed_one, full_value, preferred_element_type=jnp.float32).astype(
        jnp.bfloat16
    )
    queries_heads = queries.reshape(blocks, shard_len, heads, head_dim)
    keys_all, values_all = (
        lax.all_gather(keys_local.reshape(blocks, shard_len, width), "seq", axis=1, tiled=True),
        lax.all_gather(values_local.reshape(blocks, shard_len, width), "seq", axis=1, tiled=True),
    )
    scores = jnp.einsum(
        "bqhe,bkhe->bhqk",
        queries_heads,
        keys_all.reshape(blocks, full_len, heads, head_dim),
        preferred_element_type=jnp.float32,
    )
    logits = jnp.where(key_valid[:, None, None, :], scores + bias_heads[None], NEGATIVE)
    highest = jnp.max(logits, -1, keepdims=True)
    log_total = highest + jnp.log(jnp.sum(jnp.exp(logits - highest), -1, keepdims=True))
    probs_low = jnp.exp(logits - log_total).astype(jnp.bfloat16)
    mixed = jnp.einsum(
        "bhqk,bkhe->bqhe",
        probs_low,
        values_all.reshape(blocks, full_len, heads, head_dim),
        preferred_element_type=jnp.float32,
    )
    mixed = mixed.astype(jnp.bfloat16).reshape(total_rows, width)
    hidden = flat + jnp.dot(mixed, full_out, preferred_element_type=jnp.float32)
    scale_two = lax.rsqrt(jnp.mean(hidden * hidden, -1, keepdims=True) + EPS)
    normed_two = (hidden * scale_two * gain_two).astype(jnp.bfloat16)
    pre_act = jnp.dot(normed_two, full_in, preferred_element_type=jnp.float32)
    active = jax.nn.gelu(pre_act, approximate=True).astype(jnp.bfloat16)
    outputs = hidden + jnp.dot(active, full_down, preferred_element_type=jnp.float32)
    partial_pool = jnp.sum(outputs.reshape(blocks, shard_len, width) * query_valid[:, :, None], 1)
    pooled = lax.psum(partial_pool, "seq") / doc_lengths[:, None].astype(jnp.float32)
    regathered = (
        lax.all_gather(w_query, "seq", axis=0, tiled=True),
        lax.all_gather(w_key, "seq", axis=0, tiled=True),
        lax.all_gather(w_value, "seq", axis=0, tiled=True),
        lax.all_gather(w_out, "seq", axis=0, tiled=True),
        lax.all_gather(w_ffn_in, "seq", axis=0, tiled=True),
        lax.all_gather(w_ffn_out, "seq", axis=0, tiled=True),
        lax.all_gather(attn_gain, "seq", axis=0, tiled=True),
        lax.all_gather(ffn_gain, "seq", axis=0, tiled=True),
    )
    full_query, full_key, full_value, full_out, full_in, full_down, gain_back_one, gain_back_two = (
        regathered
    )
    gain_one = gain_back_one.astype(jnp.float32)
    gain_two = gain_back_two.astype(jnp.float32)
    grad_out = (cotangent.astype(jnp.float32) * query_valid[:, :, None]).reshape(total_rows, width)
    grad_branch = grad_out.astype(jnp.bfloat16)
    grad_down = outer_sum(active, grad_branch)
    grad_pre = (back_project(grad_branch, full_down) * gelu_slope(pre_act)).astype(jnp.bfloat16)
    grad_in = outer_sum(normed_two, grad_pre)
    grad_normed_two = back_project(grad_pre, full_in)
    grad_gain_two, grad_hidden_norm = norm_backward(hidden, scale_two, gain_two, grad_normed_two)
    grad_hidden = grad_out + grad_hidden_norm
    grad_attended = grad_hidden.astype(jnp.bfloat16)
    grad_out_proj = outer_sum(mixed, grad_attended)
    grad_mixed = (
        back_project(grad_attended, full_out)
        .astype(jnp.bfloat16)
        .reshape(blocks, shard_len, heads, head_dim)
    )
    keys_back, values_back = (keys_all, values_all)
    probs = jnp.exp(logits - log_total)
    grad_probs = jnp.einsum(
        "bqhe,bkhe->bhqk",
        grad_mixed,
        values_back.reshape(blocks, full_len, heads, head_dim),
        preferred_element_type=jnp.float32,
    )
    inner_term = jnp.sum(probs * grad_probs, -1, keepdims=True)
    grad_logits = (probs * (grad_probs - inner_term)).astype(jnp.bfloat16)
    grad_queries = jnp.einsum(
        "bhqk,bkhe->bqhe",
        grad_logits,
        keys_back.reshape(blocks, full_len, heads, head_dim),
        preferred_element_type=jnp.float32,
    )
    grad_queries = grad_queries.astype(jnp.bfloat16).reshape(total_rows, width)
    grad_table = jnp.einsum("bhqk,qkn->nh", grad_logits, onehot, preferred_element_type=jnp.float32)
    key_terms = jnp.einsum(
        "bhqk,bqhe->bkhe", grad_logits, queries_heads, preferred_element_type=jnp.float32
    ).reshape(blocks, full_len, width)
    value_terms = jnp.einsum(
        "bhqk,bqhe->bkhe", probs_low, grad_mixed, preferred_element_type=jnp.float32
    ).reshape(blocks, full_len, width)
    grad_keys, grad_values = (
        lax.psum_scatter(
            key_terms.astype(jnp.bfloat16), "seq", scatter_dimension=1, tiled=True
        ).astype(jnp.float32),
        lax.psum_scatter(
            value_terms.astype(jnp.bfloat16), "seq", scatter_dimension=1, tiled=True
        ).astype(jnp.float32),
    )
    grad_keys = grad_keys.astype(jnp.bfloat16).reshape(total_rows, width)
    grad_values = grad_values.astype(jnp.bfloat16).reshape(total_rows, width)
    grad_query_w = outer_sum(normed_one, grad_queries)
    grad_key_w = outer_sum(normed_one, grad_keys)
    grad_value_w = outer_sum(normed_one, grad_values)
    grad_normed_one = (
        back_project(grad_queries, full_query)
        + back_project(grad_keys, full_key)
        + back_project(grad_values, full_value)
    )
    grad_gain_one, grad_input_norm = norm_backward(flat, scale_one, gain_one, grad_normed_one)
    grad_input = (grad_hidden + grad_input_norm).reshape(blocks, shard_len, width)
    shards = (
        lax.psum_scatter(
            grad_query_w.astype(jnp.bfloat16), "seq", scatter_dimension=0, tiled=True
        ).astype(jnp.float32),
        lax.psum_scatter(
            grad_key_w.astype(jnp.bfloat16), "seq", scatter_dimension=0, tiled=True
        ).astype(jnp.float32),
        lax.psum_scatter(
            grad_value_w.astype(jnp.bfloat16), "seq", scatter_dimension=0, tiled=True
        ).astype(jnp.float32),
        lax.psum_scatter(
            grad_out_proj.astype(jnp.bfloat16), "seq", scatter_dimension=0, tiled=True
        ).astype(jnp.float32),
        lax.psum_scatter(
            grad_in.astype(jnp.bfloat16), "seq", scatter_dimension=0, tiled=True
        ).astype(jnp.float32),
        lax.psum_scatter(
            grad_down.astype(jnp.bfloat16), "seq", scatter_dimension=0, tiled=True
        ).astype(jnp.float32),
        lax.psum_scatter(
            grad_gain_one.astype(jnp.bfloat16), "seq", scatter_dimension=0, tiled=True
        ).astype(jnp.float32),
        lax.psum_scatter(
            grad_gain_two.astype(jnp.bfloat16), "seq", scatter_dimension=0, tiled=True
        ).astype(jnp.float32),
        lax.psum_scatter(
            grad_table.astype(jnp.bfloat16), "seq", scatter_dimension=0, tiled=True
        ).astype(jnp.float32),
    )
    totals = (
        lax.psum(shards[0].astype(jnp.bfloat16), "dp").astype(jnp.float32),
        lax.psum(shards[1].astype(jnp.bfloat16), "dp").astype(jnp.float32),
        lax.psum(shards[2].astype(jnp.bfloat16), "dp").astype(jnp.float32),
        lax.psum(shards[3].astype(jnp.bfloat16), "dp").astype(jnp.float32),
        lax.psum(shards[4].astype(jnp.bfloat16), "dp").astype(jnp.float32),
        lax.psum(shards[5].astype(jnp.bfloat16), "dp").astype(jnp.float32),
        lax.psum(shards[6].astype(jnp.bfloat16), "dp").astype(jnp.float32),
        lax.psum(shards[7].astype(jnp.bfloat16), "dp").astype(jnp.float32),
        lax.psum(shards[8].astype(jnp.bfloat16), "dp").astype(jnp.float32),
    )
    return (
        pooled,
        grad_input,
        totals[0],
        totals[1],
        totals[2],
        totals[3],
        totals[4],
        totals[5],
        totals[6],
        totals[7],
        totals[8],
    )


def fused_on_device(
    inputs,
    w_query,
    w_key,
    w_value,
    w_out,
    w_ffn_in,
    w_ffn_out,
    attn_gain,
    ffn_gain,
    rel_bias,
    doc_lengths,
    cotangent,
):
    docs, shard_len, width = inputs.shape
    rows_w, hidden_units = w_ffn_in.shape
    tokens = shard_len * SEQ
    half = width // 2
    part = hidden_units // (2 * SEQ)
    blocks = tokens // BLK
    pairs = half // BLK
    parts = part // BLK
    heads = rel_bias.shape[1]
    gains = jnp.stack([attn_gain, ffn_gain]).astype(F32)
    anywhere = pl.BlockSpec(memory_space=pl.ANY)
    vmem = pl.BlockSpec(memory_space=pltpu.VMEM)
    smem = pl.BlockSpec(memory_space=pltpu.SMEM)
    shape = jax.ShapeDtypeStruct
    narrow = [
        (docs, shard_len, width),
        (rows_w, width),
        (rows_w, width),
        (rows_w, width),
        (rows_w, width),
        (rows_w, hidden_units),
        (2 * part, width),
    ]
    out_shape = (
        shape((docs, width), F32),
        shape((8, 2 * BLK), F32),
        shape((8, BLK), F32),
        *(shape(s, BF16) for s in narrow),
        shape((2 * pairs, tokens, tokens), BF16),
    )
    out_part = rows_w // 2

    def sums(count, size, columns):
        return [((count, size // 2, columns), BF16)] * 2 + [((count, size, columns), BF16)] * 4

    scratch = [
        ((SEQ, BLK, width), BF16),
        ((blocks, BLK, width), BF16),
        ((tokens, width), BF16),
        ((width, 3 * half), BF16),
        ((tokens, 3 * half), BF16),
        ((tokens, half), BF16),
        ((half, width), BF16),
        ((SEQ, BLK, width), F32),
        ((SEQ, BLK, width), F32),
        ((SEQ, BLK, width), F32),
        ((tokens, width), BF16),
        ((width, SEQ * part), BF16),
        ((SEQ * part, width), BF16),
        ((tokens, SEQ * part), BF16),
        ((tokens, SEQ * part), BF16),
        ((SEQ, BLK, width), F32),
        ((2 * pairs, 5 * BLK, BLK), F32),
        ((3, 16, 2 * BLK), F32),
        ((tokens, BLK), BF16),
        ((8, tokens), F32),
        ((BLK + 16, tokens), BF16),
        ((tokens, 3 * half), BF16),
        ((tokens, half), BF16),
        ((tokens, BLK), F32),
        ((tokens, BLK), F32),
        ((6 * pairs, BLK, BLK), F32),
        ((pairs, 2, 8, tokens), F32),
        ((pairs, width, 3 * BLK), BF16),
        ((parts, SEQ, BLK, width), BF16),
        *sums(parts, BLK, width),
        *sums(SEQ, rows_w, part),
        *sums(pairs, rows_w, 3 * BLK),
        ((SEQ, out_part, width), BF16),
        ((out_part, width), BF16),
        ((out_part, width), BF16),
        ((SEQ + 1, 48, BLK), F32),
        ((8, width), F32),
        ((8, width), F32),
        ((8, SEQ * part), F32),
        ((8, width), F32),
        ((4, 8, width), F32),
        ((32, BLK), F32),
        ((8, 32, BLK), F32),
        ((4, 32, BLK), F32),
        ((BLK, BLK), F32),
    ]
    chunks = parts + SEQ + pairs + 1
    pair_of = lambda *dims: [pltpu.SemaphoreType.DMA(dims)] * 2
    semaphores = (
        pair_of(5)
        + pair_of(4)
        + pair_of(4)
        + pair_of(6, 8)
        + pair_of(4)
        + pair_of(4) * 8
        + pair_of(chunks, 6)
        + pair_of(4)
        + pair_of(chunks, 6)
        + pair_of(4)
        + pair_of(8)
        + pair_of(4)
        + [pltpu.SemaphoreType.DMA((chunks, 3))]
        + [pltpu.SemaphoreType.DMA((2,))]
    )
    results = pl.pallas_call(
        fused_kernel,
        out_shape=out_shape,
        in_specs=[anywhere] * 8 + [vmem, vmem, smem],
        out_specs=(vmem, vmem, vmem) + (anywhere,) * 8,
        scratch_shapes=[pltpu.VMEM(*s) for s in scratch] + semaphores,
        compiler_params=pltpu.CompilerParams(
            collective_id=0, has_side_effects=True, vmem_limit_bytes=VMEM_LIMIT
        ),
        name="block",
    )(
        inputs,
        cotangent,
        w_query,
        w_key,
        w_value,
        w_out,
        w_ffn_in,
        w_ffn_out,
        gains,
        rel_bias,
        doc_lengths,
    )

    steps = 4

    def rows_spec(s):
        if len(s) == 3:
            return pl.BlockSpec(
                (1, s[1] * s[0] // steps, s[2]),
                lambda i: (i // (steps // s[0]), i % (steps // s[0]), 0),
            )
        return pl.BlockSpec((s[0] // steps, s[1]), lambda i: (i, 0))

    def whole_spec(s):
        return pl.BlockSpec(s, lambda i: (0,) * len(s))

    tiny = [(docs, width), (1, rows_w), (1, rows_w), (8, heads)]
    pooled, one, two, table, gx, gq, gk, gv, go, gi, gd = pl.pallas_call(
        widen_kernel,
        out_shape=[shape(s, F32) for s in tiny + narrow],
        grid=(steps,),
        in_specs=[whole_spec(r.shape) for r in results[:3]] + [rows_spec(s) for s in narrow],
        out_specs=[whole_spec(s) for s in tiny] + [rows_spec(s) for s in narrow],
        compiler_params=pltpu.CompilerParams(vmem_limit_bytes=VMEM_LIMIT),
        name="widen",
    )(*results[:-1])
    return (pooled, gx, gq, gk, gv, go, gi, gd, one[0], two[0], table)


def fits(mesh):
    return mesh.shape["dp"] == CORES * DEPTH and mesh.shape["seq"] == SEQ


def solution(mesh):
    in_specs = (
        P("dp", "seq", None),
        P("seq", None),
        P("seq", None),
        P("seq", None),
        P("seq", None),
        P("seq", None),
        P("seq", None),
        P("seq"),
        P("seq"),
        P("seq", None),
        P("dp"),
        P("dp", "seq", None),
    )
    out_specs = (
        P("dp", None),
        P("dp", "seq", None),
        P("seq", None),
        P("seq", None),
        P("seq", None),
        P("seq", None),
        P("seq", None),
        P("seq", None),
        P("seq"),
        P("seq"),
        P("seq", None),
    )
    return jax.shard_map(
        fused_on_device if fits(mesh) else on_device, mesh=mesh, in_specs=in_specs, out_specs=out_specs, check_vma=False
    )
```

```python
import math

import jax
import jax.numpy as jnp
from jax import lax
from jax.experimental import pallas as pl
from jax.experimental.pallas import tpu as pltpu
from jax.sharding import PartitionSpec as P

EPS = 1e-06
THRESHOLDS = (12, 16, 23, 32, 46, 64, 91)
NEGATIVE = -1000000000.0
GELU_C = math.sqrt(2.0 / math.pi)
GELU_K = 0.044715


def bucket_ids(query_pos, key_pos):
    offset = key_pos[None, :] - query_pos[:, None]
    distance = jnp.abs(offset)
    upper = jnp.where(offset > 0, 16, 0).astype(jnp.int32)
    beyond = jnp.full(distance.shape, 8, jnp.int32)
    for threshold in THRESHOLDS:
        beyond = beyond + (distance >= threshold).astype(jnp.int32)
    return upper + jnp.where(distance < 8, distance, beyond)


def gelu_slope(value):
    inner = GELU_C * (value + GELU_K * value * value * value)
    tangent = jnp.tanh(inner)
    return 0.5 * (1.0 + tangent) + 0.5 * value * (1.0 - tangent * tangent) * GELU_C * (
        1.0 + 3.0 * GELU_K * value * value
    )


def outer_sum(left, right):
    return lax.dot_general(
        left, right, (((0,), (0,)), ((), ())), preferred_element_type=jnp.float32
    )


def back_project(grad, weight):
    return lax.dot_general(
        grad, weight, (((1,), (1,)), ((), ())), preferred_element_type=jnp.float32
    )


def norm_backward(source, scale, gain, grad_normed):
    grad_gain = jnp.sum(grad_normed * source * scale, 0)
    grad_scaled = grad_normed * gain
    grad_source = scale * grad_scaled - source * scale * scale * scale * jnp.mean(
        grad_scaled * source, -1, keepdims=True
    )
    return (grad_gain, grad_source)


SEQ, CORES, DEPTH = 4, 2, 4
BLK = 128
MESH = pl.DeviceIdType.MESH
F32 = jnp.float32
BF16 = jnp.bfloat16
VMEM_LIMIT = 60 << 20


def contract(left, right, left_dim, right_dim):
    return lax.dot_general(
        left, right, (((left_dim,), (right_dim,)), ((), ())), preferred_element_type=F32
    )


def exact(left, right, left_dim, right_dim):
    return lax.dot_general(
        left,
        right,
        (((left_dim,), (right_dim,)), ((), ())),
        preferred_element_type=F32,
        precision=lax.Precision.HIGHEST,
    )


def await_copy(ref, sem):
    pltpu.make_async_copy(ref, ref, sem).wait()


def tile(index, size):
    return pl.ds(pl.multiple_of(index * size, size), size)


def bucket_of(offset):
    distance = jnp.abs(offset)
    beyond = jnp.full(distance.shape, 8, jnp.int32)
    for threshold in THRESHOLDS:
        beyond = beyond + (distance >= threshold).astype(jnp.int32)
    return jnp.where(offset > 0, 16, 0) + jnp.where(distance < 8, distance, beyond)


STEPS = dict(s="start", m="middle", z1="z_one", z2="z_two", z3="z_three", z4="z_four")
SCHEDULE = {
    "gdn0": [],
    "gdn1": [("d1", "s"), ("d0", "s")],
    "gdn2": [],
    "wd": [],
    "gact": [("d2", "s")],
    "gn": [],
    "gin0": [("d1", "m")],
    "gin1": [("d2", "m"), ("i2", "s")],
    "n2": [("d1", "z1"), ("i0", "s"), ("d0", "m")],
    "op": [("d2", "z1"), ("i3", "s")],
    "u0": [("i2", "m")],
    "u1": [("d0", "z1"), ("i0", "m"), ("d2", "z2"), ("i1", "s"), ("d1", "z2")],
    "u2": [],
    "u3": [("i3", "m"), ("d0", "z2"), ("d2", "z3"), ("q1", "s"), ("i2", "z1")],
    "u4": [("d1", "z3"), ("i1", "m"), ("q0", "s"), ("i0", "z1")],
    "u5": [("i2", "z2"), ("i3", "z1"), ("d0", "z3")],
    "sw": [("q1", "m")],
    "b0": [("i0", "z2"), ("q2", "s")],
    "b1": [("i2", "z3"), ("q0", "m"), ("i3", "z2"), ("q1", "z1")],
    "g1": [("i0", "z3"), ("q2", "m"), ("i1", "z1"), ("q1", "z2"), ("o", "s"), ("i3", "z3"), ("q0", "z1"), ("i1", "z2"), ("q2", "z1"), ("i2", "z4"), ("q1", "z3"), ("q0", "z2"), ("d2", "z4"), ("sm", "s"), ("i3", "z4"), ("i1", "z3"), ("q2", "z2"), ("d1", "z4"), ("o", "z1"), ("q1", "z4"), ("q0", "z3"), ("gx", "s"), ("o", "z2"), ("q0", "z4"), ("q2", "z3"), ("q2", "z4"), ("o", "z3"), ("i1", "z4"), ("d0", "z4"), ("i0", "z4"), ("o", "z4")],
    "end": [],
}


def full_sum(value):
    return jnp.sum(jnp.sum(value, 0, keepdims=True), 1, keepdims=True)


def fused_kernel(
    inputs,
    cotangent,
    w_query,
    w_key,
    w_value,
    w_out,
    w_in,
    w_down,
    gains_in,
    bias_in,
    lengths_in,
    pooled_o,
    small_o,
    table_o,
    gx_o,
    gq_o,
    gk_o,
    gv_o,
    go_o,
    gi_o,
    gd_o,
    raised_o,
    xown,
    grads,
    nrm1,
    wqkv,
    qkv,
    mixed,
    wo,
    psend,
    precv,
    hid,
    nrm2,
    wi,
    wd,
    act,
    slope,
    gn,
    strip,
    vecs,
    maskc,
    gscale,
    flip,
    dqkv,
    gmix,
    dk_acc,
    dv_acc,
    near,
    far,
    gqkv,
    gdn,
    d_dx,
    d_dy,
    d_rx,
    d_ry,
    d_za,
    d_zb,
    i_dx,
    i_dy,
    i_rx,
    i_ry,
    i_za,
    i_zb,
    q_dx,
    q_dy,
    q_rx,
    q_ry,
    q_za,
    q_zb,
    rs_o,
    o_za,
    o_zb,
    small_all,
    wide,
    gains,
    asum,
    pp,
    pool_recv,
    sg,
    sg_plane,
    sg_depth,
    turned,
    small_ss,
    small_rs,
    x_ss,
    x_rs,
    c_ss,
    c_rs,
    wg_ss,
    wg_rs,
    wo_ss,
    wo_rs,
    n1_ss,
    n1_rs,
    g_ss,
    g_rs,
    part_ss,
    part_rs,
    n2_ss,
    n2_rs,
    gn2_ss,
    gn2_rs,
    gat_ss,
    gat_rs,
    gn1_ss,
    gn1_rs,
    gx_ss,
    gx_rs,
    rs_ss,
    rs_rs,
    rso_ss,
    rso_rs,
    z_ss,
    z_rs,
    pool_ss,
    pool_rs,
    sgp_ss,
    sgp_rs,
    sgz_ss,
    sgz_rs,
    out_s,
    raised_s,
):
    dp = lax.axis_index("dp")
    chip = lax.axis_index("seq")
    depth, core = lax.div(dp, 2), lax.rem(dp, 2)
    row, col = lax.div(chip, 2), lax.rem(chip, 2)
    other = (depth * 2 + 1 - core, chip)
    xn = row * 2 + 1 - col
    yn = (1 - row) * 2 + col
    dn = (1 - row) * 2 + 1 - col
    tokens, width = nrm1.shape
    half = width // 2
    rows_w = w_query.shape[0]
    ff_part = gdn.shape[0] * BLK
    quarter, middle_q = tokens // 4, tokens // 2
    middle_w = width // 2

    def remote(src, dst, send, recv, device):
        return pltpu.make_async_remote_copy(
            src_ref=src,
            dst_ref=dst,
            send_sem=send,
            recv_sem=recv,
            device_id=device,
            device_id_type=MESH,
        )

    def ahead(step):
        return lax.rem(chip + step, SEQ)

    pending = []

    def send_now(*args):
        copy = remote(*args)
        copy.start()
        pending.append(copy)

    lane = lax.broadcasted_iota(jnp.int32, (1, BLK), 1)
    wide[...] = jnp.zeros_like(wide)
    wide[0:2, 0:rows_w] = gains_in[...]
    turned_gains = pltpu.roll(wide[...], chip * rows_w, 1)
    small_all[0] = jnp.zeros_like(small_all[0])
    for which in range(2):
        for i in range(width // BLK):
            small_all[0, 8 * which + i : 8 * which + i + 1, :] = turned_gains[
                which : which + 1, i * BLK : (i + 1) * BLK
            ]
    small_all[0, 6:7, :] = jnp.where(
        lane == 0, lengths_in[0].astype(F32), lengths_in[1].astype(F32)
    )
    small_all[0, tile(2 + chip, 8), 0 : bias_in.shape[1]] = bias_in[...].astype(F32)

    barrier = pltpu.get_barrier_semaphore()
    for step in range(SEQ):
        if step:
            pl.semaphore_signal(barrier, inc=1, device_id=(dp, ahead(step)), device_id_type=MESH)
        pl.semaphore_signal(
            barrier, inc=1, device_id=(other[0], ahead(step)), device_id_type=MESH
        )
    for step in range(1, DEPTH):
        pl.semaphore_signal(
            barrier,
            inc=1,
            device_id=(lax.rem(depth + step, DEPTH) * 2 + core, chip),
            device_id_type=MESH,
        )
    pl.semaphore_wait(barrier, 2 * SEQ - 1 + DEPTH - 1)

    mine = small_all.at[0]
    for step in range(1, SEQ):
        send_now(
            mine, small_all.at[step], small_ss.at[step], small_rs.at[step], (dp, ahead(step))
        )
    send_now(mine, small_all.at[SEQ], small_ss.at[SEQ], small_rs.at[SEQ], other)

    def spread(source, dest_of, send, recv, action):
        for doc in range(2):
            for to in range(2):
                block = source.at[doc, pl.ds(to * BLK, BLK)]
                target = core * 2 + doc
                own = (target == chip) & (core == to)
                copy = remote(
                    block,
                    dest_of(to),
                    send.at[doc * 2 + to],
                    recv.at[chip],
                    (depth * 2 + to, target),
                )
                if action == "start":

                    @pl.when(own)
                    def _():
                        pltpu.make_async_copy(block, dest_of(to), recv.at[chip]).start()

                @pl.when(jnp.logical_not(own))
                def _():
                    if action == "start":
                        copy.start()
                    else:
                        copy.wait_send()

    x_slot = lambda to: xown.at[chip]
    c_slot = lambda to: grads.at[chip * 2 + to]
    spread(inputs, x_slot, x_ss, x_rs, "start")

    class Gather:
        def __init__(self, index, pieces, place):
            self.index, self.pieces, self.place = index, pieces, place
            self.bind()

        def half_of(self, owner, which):
            ref = self.place(owner)
            size = ref.shape[0] // 2
            return ref.at[pl.ds(which * size, size)]

        def bind(self):
            k = self.index
            self.local, self.one, self.two = [], [], []
            for src, cut in self.pieces:
                dst = cut(self.place(chip))
                self.local.append(pltpu.make_async_copy(src, dst, wg_rs.at[k, 0]))
                self.one.append(remote(src, dst, wg_ss.at[k, 0], wg_rs.at[k, 1], (dp, xn)))
                self.one.append(remote(src, dst, wg_ss.at[k, 1], wg_rs.at[k, 2], (dp, yn)))
            via_x, via_y = self.half_of(xn, 1), self.half_of(yn, 0)
            self.two = [
                remote(via_x, via_x, wg_ss.at[k, 2], wg_rs.at[k, 3], (dp, yn)),
                remote(via_y, via_y, wg_ss.at[k, 3], wg_rs.at[k, 4], (dp, xn)),
            ]
            self.from_x, self.from_y = self.place(xn), self.place(yn)
            self.last = [self.half_of(dn, 1), self.half_of(dn, 0)]
            self.own = self.place(chip)

        def first(self):
            for copy in self.local + self.one:
                copy.start()

        def second(self):
            k = self.index
            await_copy(self.from_x, wg_rs.at[k, 1])
            self.two[0].start()
            await_copy(self.from_y, wg_rs.at[k, 2])
            self.two[1].start()

        def done(self):
            k = self.index
            await_copy(self.own, wg_rs.at[k, 0])
            await_copy(self.last[0], wg_rs.at[k, 3])
            await_copy(self.last[1], wg_rs.at[k, 4])

        def sent(self):
            k = self.index
            for copy in self.two:
                copy.wait_send()
            await_copy(self.own, wg_ss.at[k, 0])
            await_copy(self.own, wg_ss.at[k, 1])

    class SharedGather(Gather):
        def part(self, owner, which):
            ref = self.place(owner)
            size = ref.shape[0] // 2
            return ref.at[tile(which, size)]

        def bind(self):
            k = self.index
            mine, theirs = lax.rem(depth, 2), 1 - lax.rem(depth, 2)
            beside = ((depth + theirs - mine) * 2 + core, chip)
            self.local, self.one = [], []
            for src, cut in self.pieces:
                size = src.shape[0] // 2
                self.local.append(
                    pltpu.make_async_copy(src, cut(self.place(chip)), wg_rs.at[k, 0])
                )
                dst = cut(self.part(chip, mine))
                src = src.at[tile(mine, size)]
                self.one.append(remote(src, dst, wg_ss.at[k, 0], wg_rs.at[k, 1], (dp, xn)))
                self.one.append(remote(src, dst, wg_ss.at[k, 1], wg_rs.at[k, 2], (dp, yn)))
            self.from_x, self.from_y = self.part(xn, mine), self.part(yn, mine)
            far = self.part(dn, mine)
            size = far.shape[0] // 2
            cut = lambda ref, which: ref.at[pl.ds(which * size, size)]
            via_x, via_y = cut(self.from_x, 1), cut(self.from_y, 0)
            self.last = [cut(far, 1), cut(far, 0)]
            self.two = [
                remote(via_x, via_x, wg_ss.at[k, 2], wg_rs.at[k, 3], (dp, yn)),
                remote(via_y, via_y, wg_ss.at[k, 3], wg_rs.at[k, 4], (dp, xn)),
            ]
            self.beside = [
                remote(ref, ref, wg_ss.at[k, 4 + n], wg_rs.at[k, 5 + n], beside)
                for n, ref in enumerate((self.from_x, self.from_y, far))
            ]
            self.own = self.place(chip)
            self.half = self.part(chip, mine)

        def second(self):
            super().second()
            self.show()

        def forward(self):
            super().second()

        def show(self):
            for copy in self.beside[:2]:
                copy.start()

        def third(self):
            k = self.index
            await_copy(self.last[0], wg_rs.at[k, 3])
            await_copy(self.last[1], wg_rs.at[k, 4])
            self.beside[2].start()

        def done(self):
            await_copy(self.own, wg_rs.at[self.index, 0])
            for copy in self.beside:
                copy.wait_recv()

        def sent(self):
            k = self.index
            for copy in self.two + self.beside:
                copy.wait_send()
            await_copy(self.half, wg_ss.at[k, 0])
            await_copy(self.half, wg_ss.at[k, 1])

    core_cols = tile(core, half)
    whole = lambda ref: ref
    pair_w = 3 * BLK

    def qkv_item(index, pair):
        return SharedGather(
            index,
            [
                (
                    w.at[:, tile(core * 3 + pair, BLK)],
                    lambda ref, i=i: ref.at[:, pl.ds(i * BLK, BLK)],
                )
                for i, w in enumerate((w_query, w_key, w_value))
            ],
            lambda owner: wqkv.at[tile(owner, rows_w), pl.ds(pair * pair_w, pair_w)],
        )

    def in_item(index, part):
        return SharedGather(
            index,
            [
                (
                    w_in.at[:, tile((2 * part + f) * 2 + core, ff_part)],
                    lambda ref, f=f: ref.at[:, pl.ds(f * ff_part, ff_part)],
                )
                for f in range(2)
            ],
            lambda owner: wi.at[tile(owner, rows_w), pl.ds(part * 2 * ff_part, 2 * ff_part)],
        )

    def down_item(index, part):
        size = ff_part // 2
        return (SharedGather if part == 0 else Gather)(
            index,
            [(w_down.at[pl.ds(pl.multiple_of(core * ff_part + part * size, size), size)], whole)],
            lambda owner: wd.at[
                pl.ds(pl.multiple_of(owner * ff_part + part * size, size), size)
            ],
        )

    qkv_items = [qkv_item(i, i) for i in range(3)]
    in_items = [in_item(3, 0), in_item(4, 1)]
    down_items = [down_item(5, 0), down_item(6, 1)]
    for it in qkv_items:
        it.first()

    wo_part = rows_w // 2
    wo_src = w_out.at[tile(core, wo_part)]
    wo_dst = wo.at[tile(col * 2 + core, wo_part)]

    def wo_each(action):
        for to in range(SEQ):
            own = (chip == to) & (core == row)
            copy = remote(
                wo_src, wo_dst, wo_ss.at[to], wo_rs.at[col * 2 + core], (depth * 2 + row, to)
            )
            if action == "start":

                @pl.when(own)
                def _():
                    pltpu.make_async_copy(wo_src, wo_dst, wo_rs.at[col * 2 + core]).start()

            @pl.when(jnp.logical_not(own))
            def _():
                if action == "start":
                    copy.start()
                else:
                    copy.wait_send()

    for step in range(1, SEQ + 1):
        await_copy(small_all.at[step], small_rs.at[step])
    summed = small_all[0] + small_all[1] + small_all[2] + small_all[3]
    for which in range(2):
        gains[which : which + 1, :] = jnp.concatenate(
            [summed[8 * which + i : 8 * which + i + 1, :] for i in range(width // BLK)], axis=1
        )
    length_row = jnp.where(row == core, small_all[0, 6:7, :], small_all[SEQ, 6:7, :])
    length = jnp.where(col == 0, length_row[:, 0:1], length_row[:, 1:2])
    own_lengths = small_all[0, 6:7, 0:2]
    table = summed[16:48, :].astype(BF16)
    lane_two = lax.broadcasted_iota(jnp.int32, (1, 2 * BLK), 1)
    minus = jnp.where(lane_two < BLK, lane_two, lane_two - 2 * BLK)
    for off in (-1, 0, 1):
        ids = bucket_of(off * BLK - minus)
        onehot = (lax.broadcasted_iota(jnp.int32, (32, 2 * BLK), 0) == ids).astype(BF16)
        vecs[off + 1] = contract(table, onehot, 0, 0)[0:16, :]

    @pl.loop(0, 6)
    def _(h):
        values = [vecs[i, pl.ds(core * 6 + h, 1), :] for i in range(3)]
        left = jnp.broadcast_to(values[0][:, BLK - 1 : BLK], (BLK, BLK))
        right = jnp.broadcast_to(values[2][:, BLK + 1 : BLK + 2], (BLK, BLK))
        strip[h, 0:BLK, :] = left
        strip[h, 4 * BLK :, :] = right
        for i in range(3):
            skewed = pltpu.roll(
                jnp.broadcast_to(values[i], (BLK, 2 * BLK)), 0, 1, stride=1, stride_axis=0
            )
            strip[h, (i + 1) * BLK : (i + 2) * BLK, :] = skewed[:, :BLK]

    key_pos = lax.broadcasted_iota(jnp.int32, maskc.shape, 0).astype(F32)
    maskc[...] = jnp.where((key_pos < length) | (lane > 0), 0.0, NEGATIVE).astype(BF16)

    def block_valid(b):
        pos = lax.broadcasted_iota(jnp.int32, (BLK, 1), 0) + b * BLK
        return (pos.astype(F32) < length).astype(F32)

    def n1_copy(i):
        block = nrm1.at[tile(2 * i + core, BLK)]
        return remote(block, block, n1_ss.at[i], n1_rs.at[i], other)

    @pl.loop(0, SEQ)
    def _(i):
        await_copy(xown.at[i], x_rs.at[i])
        source = xown[i].astype(F32)
        scale = lax.rsqrt(jnp.mean(source * source, -1, keepdims=True) + EPS)
        nrm1[tile(2 * i + core, BLK), :] = (source * scale * gains[0:1, :]).astype(BF16)
        n1_copy(i).start()

    qkv_items[0].second()
    for it in qkv_items[1:]:
        it.forward()
    wo_each("start")
    for it in in_items:
        it.first()
    qkv_items[0].third()
    for it in qkv_items[1:]:
        it.show()
        it.third()
    for i in range(SEQ):
        n1_copy(i).wait_recv()

    flip[BLK : BLK + 16, :] = jnp.ones((16, tokens), BF16)
    mine_lanes = [lane < 64, lane >= 64]
    slots = [ref.at[:, pl.ds(0, tokens)] for ref in (act, slope)]

    def by_head(value):
        return jnp.concatenate(
            [jnp.where(lanes, value, jnp.zeros_like(value)) for lanes in mine_lanes], axis=0
        )

    def serve(now, table):
        for when, actions in table.items():

            @pl.when(now == when)
            def _():
                for action in actions:
                    action()

    def keep(pair, qb):
        return pltpu.make_async_copy(slots[qb], raised_o.at[2 * pair + qb], raised_s.at[qb])

    def fetch(pair, qb):
        return pltpu.make_async_copy(raised_o.at[2 * pair + qb], slots[qb], raised_s.at[qb])

    def later_inputs():
        spread(cotangent, c_slot, c_ss, c_rs, "start")
        for it in down_items:
            it.first()

    forward_table = {
        2: [in_items[0].second],
        3: [in_items[1].forward, later_inputs, in_items[0].third, in_items[1].show],
        5: [in_items[1].third],
    }

    @pl.loop(0, 3)
    def _(pair):
        cols = tile(pair, BLK)
        for p in range(3):

            @pl.when(pair == p)
            def _():
                qkv_items[p].done()

        qkv[:, tile(pair, pair_w)] = contract(
            nrm1[...], wqkv[:, tile(pair, pair_w)], 1, 0
        ).astype(BF16)
        flip[0:BLK, :] = jnp.transpose(qkv[:, tile(3 * pair + 2, BLK)])
        keys = jnp.concatenate([qkv[:, tile(3 * pair + 1, BLK)], maskc[...]], axis=1)
        for qb in range(2):
            rows = pl.ds(qb * middle_q, middle_q)
            queries = by_head(qkv[rows, tile(3 * pair, BLK)])
            flag = jnp.broadcast_to(jnp.where(lane == 0, 1.0, 0.0).astype(BF16), queries.shape)
            biases = [
                jnp.concatenate(
                    [
                        strip[
                            pair * 2 + h, pl.ds((min(max(kb - q, -2), 2) + 2) * BLK, BLK), :
                        ]
                        for kb in range(tokens // BLK)
                    ],
                    axis=0,
                )
                for h in range(2)
                for q in range(qb * middle_q // BLK, (qb + 1) * middle_q // BLK)
            ]
            logits = contract(keys, jnp.concatenate([queries, flag], axis=1), 1, 1)
            logits = logits + jnp.concatenate(biases, axis=1)
            highest = jnp.max(logits, 0, keepdims=True)
            raised = jnp.exp(logits - highest).astype(BF16)

            @pl.when(pair > 0)
            def _():
                keep(pair - 1, qb).wait()

            slots[qb][...] = raised
            keep(pair, qb).start()
            result = contract(flip[...], raised, 1, 0)
            inverse = 1.0 / result[BLK : BLK + 1, :]
            scaled = result[0:BLK, :] * inverse
            mixed[rows, cols] = jnp.transpose(
                jnp.concatenate([scaled[0:64, 0:middle_q], scaled[64:BLK, middle_q:]], axis=0)
            ).astype(BF16)
            for h in range(2):
                gscale[pl.ds(2 * pair + h, 1), rows] = inverse[:, h * middle_q : (h + 1) * middle_q]
            serve(2 * pair + qb, forward_table)

    def swap_copy(i, send, recv):
        return remote(psend.at[i], precv.at[i], send.at[i], recv.at[i], other)

    for k in range(4):
        await_copy(wo.at[pl.ds(k * wo_part, wo_part)], wo_rs.at[k])

    def blocks_of(ref, parity):
        return jnp.concatenate(
            [ref[tile(2 * i + parity, BLK), :] for i in range(SEQ)], axis=0
        )

    def swap_out(result, send, recv):
        for i in range(SEQ):
            psend[i] = result[i * BLK : (i + 1) * BLK, :].astype(BF16)
            swap_copy(i, send, recv).start()

    swap_out(contract(blocks_of(mixed, 1 - core), wo[...], 1, 0), part_ss, part_rs)

    def n2_copy(i, send, recv):
        block = nrm2.at[tile(2 * i + core, BLK)]
        return remote(block, block, send.at[i], recv.at[i], other)

    pp[...] = jnp.zeros_like(pp)
    result = contract(blocks_of(mixed, core), wo[...], 1, 0)
    for i in range(SEQ):
        hidden = xown[i].astype(F32) + result[i * BLK : (i + 1) * BLK, :]
        swap_copy(i, part_ss, part_rs).wait_recv()
        hidden = hidden + precv[i].astype(F32)
        hid[i] = hidden
        scale = lax.rsqrt(jnp.mean(hidden * hidden, -1, keepdims=True) + EPS)
        nrm2[tile(2 * i + core, BLK), :] = (hidden * scale * gains[1:2, :]).astype(BF16)
        n2_copy(i, n2_ss, n2_rs).start()
        pp[0:1, :] += jnp.sum(hidden * block_valid(2 * i + core), 0, keepdims=True)
    for i in range(SEQ):
        n2_copy(i, n2_ss, n2_rs).wait_recv()
    for qb in range(2):
        keep(2, qb).wait()

    def g_copy(i):
        block = grads.at[2 * i + core]
        return remote(block, block, g_ss.at[i], g_rs.at[i], other)

    def take_cotangent():
        @pl.loop(0, SEQ)
        def _(i):
            b = 2 * i + core
            await_copy(grads.at[b], c_rs.at[i])
            grads[b] = (grads[b].astype(F32) * block_valid(b)).astype(BF16)
            g_copy(i).start()

    asum[...] = jnp.zeros_like(asum)
    wide_part = 2 * ff_part
    for part in range(2):
        part_cols = slice(part * wide_part, (part + 1) * wide_part)
        if part == 1:
            down_items[0].second()
            take_cotangent()
        in_items[part].done()

        @pl.loop(0, 2)
        def _(i):
            rows = tile(i, middle_q)
            value = contract(nrm2[rows, :], wi[:, part_cols], 1, 0)
            square = value * value
            tangent = jnp.tanh(value * (GELU_C + GELU_C * GELU_K * square))
            half_up = 0.5 + 0.5 * tangent
            active = (value * half_up).astype(BF16)
            act[rows, part_cols] = active
            slope[rows, part_cols] = (
                half_up
                + value
                * (1.0 - tangent * tangent)
                * (0.5 * GELU_C + 1.5 * GELU_C * GELU_K * square)
            ).astype(BF16)
            pos = lax.broadcasted_iota(jnp.int32, (8, middle_q), 1) + i * middle_q
            valid = (pos.astype(F32) < length).astype(BF16)
            asum[:, part_cols] += contract(valid, active, 1, 0)


    for i in range(SEQ):
        g_copy(i).wait_recv()
    g_all = lambda: grads[...].reshape(tokens, width)

    class Chunk:
        made = 0

        def __init__(self, src, dx, dy, rx, ry, za, zb, outs):
            self.index = Chunk.made
            Chunk.made += 1
            self.src, self.dx, self.dy, self.rx, self.ry = src, dx, dy, rx, ry
            self.za, self.zb, self.outs = za, zb, outs
            self.bind()

        def bind(self):
            k = self.index
            size = self.dx.shape[0]
            cut = lambda ref, which: ref.at[pl.ds(which * size, size)]
            ss, rs = (lambda i: rs_ss.at[k, i]), (lambda i: rs_rs.at[k, i])
            to_x, to_y = (dp, xn), (dp, yn)
            self.one = [
                remote(cut(self.src(dn), 1), self.dx, ss(0), rs(0), to_x),
                remote(cut(self.src(dn), 0), self.dy, ss(1), rs(1), to_y),
                remote(cut(self.src(xn), 1), cut(self.rx, 1), ss(2), rs(2), to_x),
                remote(cut(self.src(yn), 0), cut(self.ry, 0), ss(3), rs(3), to_y),
            ]
            self.sum_y, self.sum_x = cut(self.src(yn), 1), cut(self.src(xn), 0)
            self.two = [
                remote(self.sum_y, cut(self.ry, 1), ss(4), rs(4), to_y),
                remote(self.sum_x, cut(self.rx, 0), ss(5), rs(5), to_x),
            ]
            self.bind_z(self.rx, self.ry)

        def bind_z(self, reduced, final):
            k = self.index
            self.reduced, self.final = reduced, final
            sem = lambda i: (z_ss.at[k, i], z_rs.at[k, i])
            self.to_inner = remote(reduced, self.za, *sem(0), z_dev(toward))
            self.swap = remote(reduced, self.zb, *sem(1), z_dev(across))
            self.to_end = remote(final, final, *sem(2), z_dev(outward))

        def start(self):
            for copy in self.one:
                copy.start()

        def middle(self):
            for at, sent, sums, copy in (
                (0, self.dx, self.sum_y, self.two[0]),
                (1, self.dy, self.sum_x, self.two[1]),
            ):
                self.one[at].wait_recv()
                sums[...] = (sums[...].astype(F32) + sent[...].astype(F32)).astype(BF16)
                copy.start()

        def total(self):
            for copy in (self.one[2], self.one[3], *self.two):
                copy.wait_recv()
            self.rx[...] = (
                self.src(chip)[...].astype(F32)
                + self.rx[...].astype(F32)
                + self.ry[...].astype(F32)
            ).astype(BF16)

        def z_one(self):
            self.total()

            @pl.when(end_z)
            def _():
                self.to_inner.start()

        def z_two(self):
            @pl.when(inner_z)
            def _():
                self.to_inner.wait_recv()
                self.reduced[...] = (
                    self.reduced[...].astype(F32) + self.za[...].astype(F32)
                ).astype(BF16)
                self.swap.start()

        def z_three(self):
            @pl.when(inner_z)
            def _():
                self.swap.wait_recv()
                self.final[...] = (
                    self.reduced[...].astype(F32) + self.zb[...].astype(F32)
                ).astype(BF16)
                self.to_end.start()

        def each_out(self, act_on):
            k = self.index
            for n, (cols, place) in enumerate(self.outs):
                src = self.final if cols is None else self.final.at[:, cols]
                act_on(
                    remote(src, place(core), z_ss.at[k, 3 + n], z_rs.at[k, 3 + n], other),
                    pltpu.make_async_copy(src, place(core), out_s.at[k, n]),
                )

        def z_four(self):
            @pl.when(end_z)
            def _():
                self.to_end.wait_recv()

            self.each_out(lambda there, here: (there.start(), here.start()))

        def finish(self):
            self.each_out(
                lambda there, here: (there.wait_recv(), there.wait_send(), here.wait())
            )

            @pl.when(end_z)
            def _():
                self.to_inner.wait_send()

            @pl.when(inner_z)
            def _():
                self.swap.wait_send()
                self.to_end.wait_send()

            for copy in self.plane_sends():
                copy.wait_send()

        def plane_sends(self):
            return self.one + self.two

    inner_z = (depth == 1) | (depth == 2)
    end_z = jnp.logical_not(inner_z)
    toward = jnp.where(depth == 0, 1, 2)
    outward = jnp.where(depth == 1, 0, 3)
    across = jnp.where(depth == 1, 2, 1)

    def z_dev(z):
        return (z * 2 + core, chip)

    d_chunks = [
        Chunk(
            lambda owner, i=i: gdn.at[i, owner],
            d_dx.at[i],
            d_dy.at[i],
            d_rx.at[i],
            d_ry.at[i],
            d_za.at[i],
            d_zb.at[i],
            [
                (
                    None,
                    lambda c, i=i: gd_o.at[
                        pl.ds(pl.multiple_of(c * ff_part + i * BLK, BLK), BLK)
                    ],
                )
            ],
        )
        for i in range(ff_part // BLK)
    ]

    i_chunks = [
        Chunk(
            lambda owner, f=f: wi.at[tile(owner, rows_w), pl.ds(f * ff_part, ff_part)],
            i_dx.at[f],
            i_dy.at[f],
            i_rx.at[f],
            i_ry.at[f],
            i_za.at[f],
            i_zb.at[f],
            [(None, lambda c, f=f: gi_o.at[:, tile(2 * f + c, ff_part)])],
        )
        for f in range(SEQ)
    ]
    q_chunks = [
        Chunk(
            lambda owner, p=p: gqkv.at[p, tile(owner, rows_w)],
            q_dx.at[p],
            q_dy.at[p],
            q_rx.at[p],
            q_ry.at[p],
            q_za.at[p],
            q_zb.at[p],
            [
                (
                    pl.ds(j * BLK, BLK),
                    lambda c, p=p, o=o: o.at[:, tile(c * 3 + p, BLK)],
                )
                for j, o in enumerate((gq_o, gk_o, gv_o))
            ],
        )
        for p in range(3)
    ]
    def rso_each(action):
        for k in range(2):
            for to in range(2):
                target = core * 2 + k
                own = (chip == target) & (core == to)
                src = wo.at[pl.ds((2 * k + to) * wo_part, wo_part)]
                dst = rs_o.at[chip]
                copy = remote(
                    src, dst, rso_ss.at[2 * k + to], rso_rs.at[chip], (depth * 2 + to, target)
                )
                if action == "start":

                    @pl.when(own)
                    def _():
                        pltpu.make_async_copy(src, dst, rso_rs.at[chip]).start()

                @pl.when(jnp.logical_not(own))
                def _():
                    if action == "start":
                        copy.start()
                    else:
                        copy.wait_send()

    class OutChunk(Chunk):
        def bind(self):
            self.bind_z(self.src.at[0], self.src.at[1])

        def total(self):
            for i in range(SEQ):
                await_copy(self.src.at[i], rso_rs.at[i])
            value = self.src[0].astype(F32)
            for i in range(1, SEQ):
                value = value + self.src[i].astype(F32)
            self.reduced[...] = value.astype(BF16)

        def plane_sends(self):
            return []

    o_chunk = OutChunk(
        rs_o, None, None, None, None, o_za, o_zb, [(None, lambda c: go_o.at[tile(c, wo_part)])]
    )
    def gx_each(i, action):
        own = (chip == i) & (core == row)
        dst = gx_o.at[col, tile(core, BLK)]
        copy = remote(
            nrm2.at[pl.ds(i * BLK, BLK)], dst, gx_ss.at[i], gx_rs.at[col * 2 + core], (depth * 2 + row, i)
        )
        if action == "start":

            @pl.when(own)
            def _():
                pltpu.make_async_copy(nrm2.at[pl.ds(i * BLK, BLK)], dst, gx_rs.at[col * 2 + core]).start()

        @pl.when(jnp.logical_not(own))
        def _():
            if action == "start":
                copy.start()
            else:
                copy.wait_send()

    def sgz_copy(step):
        return remote(
            sg_depth.at[depth],
            sg_depth.at[depth],
            sgz_ss.at[step],
            sgz_rs.at[depth],
            z_dev(lax.rem(depth + step, DEPTH)),
        )

    def small_along_z():
        for i in range(8):
            await_copy(sg_plane.at[i], sgp_rs.at[i])
        total = sg_plane[0]
        for i in range(1, 8):
            total = total + sg_plane[i]
        sg_depth[depth] = total
        for step in range(1, DEPTH):
            sgz_copy(step).start()

    by_name = dict(
        [(f"d{i}", c) for i, c in enumerate(d_chunks)]
        + [(f"i{i}", c) for i, c in enumerate(i_chunks)]
        + [(f"q{i}", c) for i, c in enumerate(q_chunks)]
        + [("o", o_chunk)]
    )

    def after(block):
        for name, step in SCHEDULE[block]:
            if name == "gx":
                for i in range(SEQ):
                    gx_each(i, "start")
            elif name == "sm":
                small_along_z()
            elif name == "o" and step == "s":
                rso_each("start")
            else:
                getattr(by_name[name], STEPS[step])()

    down_items[1].second()
    down_items[0].third()
    for i in range(ff_part // BLK):
        columns = jnp.concatenate(
            [act[:, f * ff_part + i * BLK : f * ff_part + (i + 1) * BLK] for f in range(SEQ)],
            axis=1,
        )
        gdn[i] = contract(columns, g_all(), 0, 0).astype(BF16).reshape(SEQ, BLK, width)
        after(f"gdn{i}")
    for it in down_items:
        it.done()
    for it in in_items:
        it.sent()
    after("wd")

    def pooled_part(cols):
        total = asum[0:1, cols]
        high = total.astype(BF16)
        rest = total - high.astype(F32)
        middle = rest.astype(BF16)
        low = (rest - middle.astype(F32)).astype(BF16)
        pieces = jnp.concatenate(
            [jnp.broadcast_to(piece, (16, piece.shape[1])) for piece in (high, middle, low)], axis=0
        )
        result = contract(pieces, wd[cols, :], 1, 0)
        pp[0:1, :] += result[0:1, :] + result[16:17, :] + result[32:33, :]

    for part in range(2):
        part_cols = slice(part * wide_part, (part + 1) * wide_part)

        @pl.loop(0, 2)
        def _(i):
            rows = tile(i, middle_q)
            upstream = grads[pl.ds(4 * i, 4)].reshape(middle_q, width)
            grad = contract(upstream, wd[part_cols, :], 1, 1) * slope[rows, part_cols].astype(F32)
            slope[rows, part_cols] = grad.astype(BF16)

        pooled_part(part_cols)

    after("gact")

    for i in range(SEQ):
        swap_copy(i, part_ss, part_rs).wait_send()
    swap_out(contract(blocks_of(slope, 1 - core), wi[...], 1, 1), gn2_ss, gn2_rs)
    gn[...] = contract(blocks_of(slope, core), wi[...], 1, 1).reshape(SEQ, BLK, width)
    after("gn")
    for part in range(2):
        part_cols = slice(part * wide_part, (part + 1) * wide_part)

        @pl.loop(0, width // (2 * BLK))
        def _(i):
            wi[tile(i, 2 * BLK), part_cols] = contract(
                nrm2[:, tile(i, 2 * BLK)], slope[:, part_cols], 0, 0
            ).astype(BF16)

        after(f"gin{part}")
    def pool_each(action):
        for to in range(SEQ):
            own = (chip == to) & (core == row)
            dst = pool_recv.at[col * 2 + core]
            copy = remote(pp, dst, pool_ss.at[to], pool_rs.at[col * 2 + core], (depth * 2 + row, to))
            if action == "start":

                @pl.when(own)
                def _():
                    pltpu.make_async_copy(pp, dst, pool_rs.at[col * 2 + core]).start()

            @pl.when(jnp.logical_not(own))
            def _():
                if action == "start":
                    copy.start()
                else:
                    copy.wait_send()

    def gat_copy(i):
        block = act.at[tile(2 * i + core, BLK), pl.ds(0, width)]
        return remote(block, block, gat_ss.at[i], gat_rs.at[i], other)

    for i in range(SEQ):
        n2_copy(i, n2_ss, n2_rs).wait_send()
    sg[...] = jnp.zeros_like(sg)

    def add_gain(first, value):
        for i in range(width // BLK):
            sg[first + i : first + i + 1, :] += value[:, i * BLK : (i + 1) * BLK]

    @pl.loop(0, SEQ)
    def _(i):
        b = 2 * i + core
        swap_copy(i, gn2_ss, gn2_rs).wait_recv()
        normed = gn[i] + precv[i].astype(F32)
        hidden = hid[i]
        scale = lax.rsqrt(jnp.mean(hidden * hidden, -1, keepdims=True) + EPS)
        add_gain(8, jnp.sum(normed * hidden * scale, 0, keepdims=True))
        scaled = normed * gains[1:2, :]
        inner = jnp.mean(scaled * hidden, -1, keepdims=True)
        result = grads[b].astype(F32) + scale * scaled - hidden * (scale * scale * scale) * inner
        hid[i] = result
        act[tile(b, BLK), 0:width] = result.astype(BF16)
        gat_copy(i).start()

    pool_each("start")
    after("n2")
    for i in range(SEQ):
        gat_copy(i).wait_recv()

    @pl.loop(0, 2)
    def _(i):
        rows = tile(i, middle_q)
        inverse = jnp.concatenate(
            [
                jnp.transpose(
                    jnp.concatenate(
                        [
                            jnp.broadcast_to(gscale[2 * p + h : 2 * p + h + 1, rows], (64, middle_q))
                            for h in range(2)
                        ],
                        axis=0,
                    )
                )
                for p in range(3)
            ],
            axis=1,
        )
        gmix[rows, :] = (contract(act[rows, 0:width], wo[...], 1, 1) * inverse).astype(BF16)

    wo[...] = contract(mixed[...], act[:, 0:width], 0, 0).astype(BF16)
    for i in range(SEQ):
        gat_copy(i).wait_send()
    for qb in range(2):
        fetch(0, qb).start()
    after("op")


    sub = lax.broadcasted_iota(jnp.int32, (16, tokens), 0)
    key_block = lax.div(lax.broadcasted_iota(jnp.int32, (16, tokens), 1), BLK)
    flip[BLK : BLK + 16, :] = (sub == key_block).astype(BF16)
    near[...] = jnp.zeros_like(near)
    far[...] = jnp.zeros_like(far)

    backward_table = {i: [lambda i=i: after(f"u{i}")] for i in range(6)}

    @pl.loop(0, 3)
    def _(pair):
        cols = tile(pair, BLK)
        flip[0:BLK, :] = jnp.transpose(qkv[:, tile(3 * pair + 1, BLK)])
        for qb in range(2):
            rows = pl.ds(qb * middle_q, middle_q)
            upstream = gmix[rows, cols]
            masked = by_head(upstream)
            queries = by_head(qkv[rows, tile(3 * pair, BLK)])
            product = jnp.transpose(upstream.astype(F32) * mixed[rows, cols].astype(F32))
            inner = jnp.concatenate(
                [jnp.sum(product[64 * h : 64 * h + 64, :], 0, keepdims=True) for h in range(2)],
                axis=1,
            )
            fetch(pair, qb).wait()
            raised = slots[qb][...]
            grad_probs = contract(qkv[:, tile(3 * pair + 2, BLK)], masked, 1, 1)
            grad_logits = (raised.astype(F32) * (grad_probs - inner)).astype(BF16)
            grad_values = contract(raised, masked, 1, 0)
            grad_keys = contract(grad_logits, queries, 1, 0)
            if qb == 0:
                dv_acc[...] = grad_values
                dk_acc[...] = grad_keys
            else:
                dv_acc[...] += grad_values
                dk_acc[...] += grad_keys
            result = contract(flip[...], grad_logits, 1, 0)
            dqkv[rows, tile(3 * pair, BLK)] = jnp.transpose(
                jnp.concatenate([result[0:64, 0:middle_q], result[64:BLK, middle_q:]], axis=0)
            ).astype(BF16)
            sums = result[BLK : BLK + 8, :]
            block_row = lax.broadcasted_iota(jnp.int32, sums.shape, 0)
            block_col = lax.rem(
                lax.div(lax.broadcasted_iota(jnp.int32, sums.shape, 1), BLK), middle_q // BLK
            )
            gap = block_row - block_col - qb * (middle_q // BLK)
            far[pair, 0] += jnp.where(gap <= -2, sums, 0.0)
            far[pair, 1] += jnp.where(gap >= 2, sums, 0.0)
            for h in range(2):
                for off in range(3):
                    total = near[(pair * 2 + h) * 3 + off]
                    for i in range(middle_q // BLK):
                        kb = qb * (middle_q // BLK) + i + off - 1
                        if 0 <= kb < tokens // BLK:
                            first = h * middle_q + i * BLK
                            total = total + grad_logits[
                                kb * BLK : (kb + 1) * BLK, first : first + BLK
                            ].astype(F32)
                    near[(pair * 2 + h) * 3 + off] = total

            @pl.when(pair < 2)
            def _():
                fetch(pair + 1, qb).start()

            if qb == 1:
                dqkv[:, tile(3 * pair + 1, BLK)] = dk_acc[...].astype(BF16)
                dqkv[:, tile(3 * pair + 2, BLK)] = dv_acc[...].astype(BF16)
                right = dqkv[:, tile(pair, pair_w)]

                @pl.loop(0, width // middle_w)
                def _(i):
                    gqkv[pair, tile(i, middle_w), :] = contract(
                        nrm1[:, tile(i, middle_w)], right, 0, 0
                    ).astype(BF16)

            serve(2 * pair + qb, backward_table)

    for i in range(SEQ):
        swap_copy(i, gn2_ss, gn2_rs).wait_send()

    swap_out(contract(blocks_of(dqkv, 1 - core), wqkv[...], 1, 1), gn1_ss, gn1_rs)
    diag_row = lax.broadcasted_iota(jnp.int32, (BLK, BLK), 0)
    diag_col = lax.broadcasted_iota(jnp.int32, (BLK, BLK), 1)
    upper = diag_col >= diag_row
    mirror = (diag_row + diag_col == BLK - 1).astype(F32)
    shift = lax.broadcasted_iota(jnp.int32, (1, BLK), 1) + 1
    shift = jnp.where(shift == BLK, 0, shift)
    ids = bucket_of(jnp.concatenate([-shift, BLK - shift], axis=1))
    onehot = (lax.broadcasted_iota(jnp.int32, (BLK, 2 * BLK), 0) == ids).astype(F32)

    def bias_head(h):
        def skew(x):
            return pltpu.roll(exact(mirror, x, 1, 0), 0, 1, stride=1, stride_axis=0)

        def far_of(h, side):
            both = far[lax.div(h, 2), side]
            return jnp.where(lax.rem(h, 2) == 0, both[:, 0:middle_q], both[:, middle_q:])

        tiles = [near[h * 3 + i] for i in range(3)]
        at = [
            jnp.sum(
                skew(jnp.where(upper, tiles[i + 1], 0.0) + jnp.where(upper, 0.0, tiles[i])),
                0,
                keepdims=True,
            )
            for i in range(2)
        ]
        below = full_sum(jnp.where(upper, tiles[0], 0.0)) + full_sum(far_of(h, 0))
        above = full_sum(jnp.where(upper, 0.0, tiles[2])) + full_sum(far_of(h, 1))
        sums = exact(jnp.broadcast_to(jnp.concatenate(at, axis=1), (8, 2 * BLK)), onehot, 1, 1)
        sums = sums[0:1, :] + jnp.where(lane == 15, below, 0.0) + jnp.where(lane == 31, above, 0.0)
        sg[pl.ds(16 + core * 6 + h, 1), :] = sums

    after("sw")

    @pl.loop(0, 3)
    def _(h):
        bias_head(h)

    after("b0")

    @pl.loop(3, 6)
    def _(h):
        bias_head(h)

    after("b1")
    both = contract(blocks_of(dqkv, core), wqkv[...], 1, 1)
    for i in range(SEQ):
        swap_copy(i, gn1_ss, gn1_rs).wait_recv()
        normed = both[i * BLK : (i + 1) * BLK, :] + precv[i].astype(F32)
        source = xown[i].astype(F32)
        scale = lax.rsqrt(jnp.mean(source * source, -1, keepdims=True) + EPS)
        add_gain(0, jnp.sum(normed * source * scale, 0, keepdims=True))
        scaled = normed * gains[0:1, :]
        inner = jnp.mean(scaled * source, -1, keepdims=True)
        result = hid[i] + scale * scaled - source * (scale * scale * scale) * inner
        nrm2[i * BLK : (i + 1) * BLK, :] = result.astype(BF16)

    place = core * SEQ + chip

    def sgp_each(action):
        for step in range(SEQ):
            for cross in range(2):
                if step == 0 and cross == 0:
                    continue
                to_core = lax.rem(core + cross, 2)
                copy = remote(
                    sg,
                    sg_plane.at[place],
                    sgp_ss.at[step * 2 + cross],
                    sgp_rs.at[place],
                    (depth * 2 + to_core, ahead(step)),
                )
                if action == "start":
                    copy.start()
                else:
                    copy.wait_send()

    sgp_each("start")
    pltpu.make_async_copy(sg, sg_plane.at[place], sgp_rs.at[place]).start()
    after("g1")
    after("end")
    for i in range(4):
        await_copy(pool_recv.at[i], pool_rs.at[i])
    for doc in range(2):
        pooled_o[doc : doc + 1, :] = (
            pool_recv[2 * doc, 0:1, :] + pool_recv[2 * doc + 1, 0:1, :]
        ) / own_lengths[:, doc : doc + 1]
    for step in range(1, DEPTH):
        z = lax.rem(depth + DEPTH - step, DEPTH)
        await_copy(sg_depth.at[z], sgz_rs.at[z])
    total = sg_depth[0] + sg_depth[1] + sg_depth[2] + sg_depth[3]
    for which in range(2):
        wide[which : which + 1, :] = jnp.concatenate(
            [total[8 * which + i : 8 * which + i + 1, :] for i in range(width // BLK)], axis=1
        )
    small_o[...] = pltpu.roll(wide[...], lax.rem(width - chip * rows_w, width), 1)[:, : small_o.shape[1]]
    turned[:, 0:16] = jnp.transpose(total[16:32, :])
    table_o[...] = turned[tile(chip, 8), :]

    for i in range(4):
        await_copy(gx_o.at[i // 2, pl.ds((i % 2) * BLK, BLK)], gx_rs.at[i])
    for copy in pending:
        copy.wait_send()
    spread(inputs, x_slot, x_ss, x_rs, "wait")
    spread(cotangent, c_slot, c_ss, c_rs, "wait")
    for it in qkv_items + down_items:
        it.sent()
    wo_each("wait")
    pool_each("wait")
    rso_each("wait")
    sgp_each("wait")
    for i in range(SEQ):
        n1_copy(i).wait_send()
        g_copy(i).wait_send()
        swap_copy(i, gn1_ss, gn1_rs).wait_send()
        gx_each(i, "wait")
    for step in range(1, DEPTH):
        sgz_copy(step).wait_send()
    for chunk in (*d_chunks, *i_chunks, o_chunk, *q_chunks):
        chunk.finish()


def widen_kernel(pooled, small, table, gx, gq, gk, gv, go, gi, gd, *outs):
    pooled_out, one_out, two_out, table_out, *outs = outs
    pooled_out[...] = pooled[...]
    one_out[...] = small[0:1, : one_out.shape[1]]
    two_out[...] = small[1:2, : two_out.shape[1]]
    table_out[...] = table[:, : table_out.shape[1]]
    for value, out in zip((gx, gq, gk, gv, go, gi, gd), outs):
        out[...] = value[...].astype(F32)


def on_device(
    inputs,
    w_query,
    w_key,
    w_value,
    w_out,
    w_ffn_in,
    w_ffn_out,
    attn_gain,
    ffn_gain,
    rel_bias,
    doc_lengths,
    cotangent,
):
    blocks, shard_len, width = inputs.shape
    heads = rel_bias.shape[1]
    head_dim = width // heads
    full_len = shard_len * lax.axis_size("seq")
    total_rows = blocks * shard_len
    gathered = (
        lax.all_gather(w_query, "seq", axis=0, tiled=True),
        lax.all_gather(w_key, "seq", axis=0, tiled=True),
        lax.all_gather(w_value, "seq", axis=0, tiled=True),
        lax.all_gather(w_out, "seq", axis=0, tiled=True),
        lax.all_gather(w_ffn_in, "seq", axis=0, tiled=True),
        lax.all_gather(w_ffn_out, "seq", axis=0, tiled=True),
        lax.all_gather(attn_gain, "seq", axis=0, tiled=True),
        lax.all_gather(ffn_gain, "seq", axis=0, tiled=True),
        lax.all_gather(rel_bias, "seq", axis=0, tiled=True),
    )
    (
        full_query,
        full_key,
        full_value,
        full_out,
        full_in,
        full_down,
        gain_one,
        gain_two,
        bias_table,
    ) = gathered
    gain_one = gain_one.astype(jnp.float32)
    gain_two = gain_two.astype(jnp.float32)
    bucket_range = jnp.arange(bias_table.shape[0], dtype=jnp.int32)
    query_pos = lax.axis_index("seq") * shard_len + jnp.arange(shard_len, dtype=jnp.int32)
    key_pos = jnp.arange(full_len, dtype=jnp.int32)
    onehot = (bucket_ids(query_pos, key_pos)[:, :, None] == bucket_range).astype(jnp.bfloat16)
    bias_heads = jnp.einsum("qkn,nh->hqk", onehot, bias_table, preferred_element_type=jnp.float32)
    key_valid = key_pos[None, :] < doc_lengths[:, None]
    query_valid = (query_pos[None, :] < doc_lengths[:, None]).astype(jnp.float32)
    flat = inputs.astype(jnp.float32).reshape(total_rows, width)
    scale_one = lax.rsqrt(jnp.mean(flat * flat, -1, keepdims=True) + EPS)
    normed_one = (flat * scale_one * gain_one).astype(jnp.bfloat16)
    queries = jnp.dot(normed_one, full_query, preferred_element_type=jnp.float32).astype(
        jnp.bfloat16
    )
    keys_local = jnp.dot(normed_one, full_key, preferred_element_type=jnp.float32).astype(
        jnp.bfloat16
    )
    values_local = jnp.dot(normed_one, full_value, preferred_element_type=jnp.float32).astype(
        jnp.bfloat16
    )
    queries_heads = queries.reshape(blocks, shard_len, heads, head_dim)
    keys_all, values_all = (
        lax.all_gather(keys_local.reshape(blocks, shard_len, width), "seq", axis=1, tiled=True),
        lax.all_gather(values_local.reshape(blocks, shard_len, width), "seq", axis=1, tiled=True),
    )
    scores = jnp.einsum(
        "bqhe,bkhe->bhqk",
        queries_heads,
        keys_all.reshape(blocks, full_len, heads, head_dim),
        preferred_element_type=jnp.float32,
    )
    logits = jnp.where(key_valid[:, None, None, :], scores + bias_heads[None], NEGATIVE)
    highest = jnp.max(logits, -1, keepdims=True)
    log_total = highest + jnp.log(jnp.sum(jnp.exp(logits - highest), -1, keepdims=True))
    probs_low = jnp.exp(logits - log_total).astype(jnp.bfloat16)
    mixed = jnp.einsum(
        "bhqk,bkhe->bqhe",
        probs_low,
        values_all.reshape(blocks, full_len, heads, head_dim),
        preferred_element_type=jnp.float32,
    )
    mixed = mixed.astype(jnp.bfloat16).reshape(total_rows, width)
    hidden = flat + jnp.dot(mixed, full_out, preferred_element_type=jnp.float32)
    scale_two = lax.rsqrt(jnp.mean(hidden * hidden, -1, keepdims=True) + EPS)
    normed_two = (hidden * scale_two * gain_two).astype(jnp.bfloat16)
    pre_act = jnp.dot(normed_two, full_in, preferred_element_type=jnp.float32)
    active = jax.nn.gelu(pre_act, approximate=True).astype(jnp.bfloat16)
    outputs = hidden + jnp.dot(active, full_down, preferred_element_type=jnp.float32)
    partial_pool = jnp.sum(outputs.reshape(blocks, shard_len, width) * query_valid[:, :, None], 1)
    pooled = lax.psum(partial_pool, "seq") / doc_lengths[:, None].astype(jnp.float32)
    regathered = (
        lax.all_gather(w_query, "seq", axis=0, tiled=True),
        lax.all_gather(w_key, "seq", axis=0, tiled=True),
        lax.all_gather(w_value, "seq", axis=0, tiled=True),
        lax.all_gather(w_out, "seq", axis=0, tiled=True),
        lax.all_gather(w_ffn_in, "seq", axis=0, tiled=True),
        lax.all_gather(w_ffn_out, "seq", axis=0, tiled=True),
        lax.all_gather(attn_gain, "seq", axis=0, tiled=True),
        lax.all_gather(ffn_gain, "seq", axis=0, tiled=True),
    )
    full_query, full_key, full_value, full_out, full_in, full_down, gain_back_one, gain_back_two = (
        regathered
    )
    gain_one = gain_back_one.astype(jnp.float32)
    gain_two = gain_back_two.astype(jnp.float32)
    grad_out = (cotangent.astype(jnp.float32) * query_valid[:, :, None]).reshape(total_rows, width)
    grad_branch = grad_out.astype(jnp.bfloat16)
    grad_down = outer_sum(active, grad_branch)
    grad_pre = (back_project(grad_branch, full_down) * gelu_slope(pre_act)).astype(jnp.bfloat16)
    grad_in = outer_sum(normed_two, grad_pre)
    grad_normed_two = back_project(grad_pre, full_in)
    grad_gain_two, grad_hidden_norm = norm_backward(hidden, scale_two, gain_two, grad_normed_two)
    grad_hidden = grad_out + grad_hidden_norm
    grad_attended = grad_hidden.astype(jnp.bfloat16)
    grad_out_proj = outer_sum(mixed, grad_attended)
    grad_mixed = (
        back_project(grad_attended, full_out)
        .astype(jnp.bfloat16)
        .reshape(blocks, shard_len, heads, head_dim)
    )
    keys_back, values_back = (keys_all, values_all)
    probs = jnp.exp(logits - log_total)
    grad_probs = jnp.einsum(
        "bqhe,bkhe->bhqk",
        grad_mixed,
        values_back.reshape(blocks, full_len, heads, head_dim),
        preferred_element_type=jnp.float32,
    )
    inner_term = jnp.sum(probs * grad_probs, -1, keepdims=True)
    grad_logits = (probs * (grad_probs - inner_term)).astype(jnp.bfloat16)
    grad_queries = jnp.einsum(
        "bhqk,bkhe->bqhe",
        grad_logits,
        keys_back.reshape(blocks, full_len, heads, head_dim),
        preferred_element_type=jnp.float32,
    )
    grad_queries = grad_queries.astype(jnp.bfloat16).reshape(total_rows, width)
    grad_table = jnp.einsum("bhqk,qkn->nh", grad_logits, onehot, preferred_element_type=jnp.float32)
    key_terms = jnp.einsum(
        "bhqk,bqhe->bkhe", grad_logits, queries_heads, preferred_element_type=jnp.float32
    ).reshape(blocks, full_len, width)
    value_terms = jnp.einsum(
        "bhqk,bqhe->bkhe", probs_low, grad_mixed, preferred_element_type=jnp.float32
    ).reshape(blocks, full_len, width)
    grad_keys, grad_values = (
        lax.psum_scatter(
            key_terms.astype(jnp.bfloat16), "seq", scatter_dimension=1, tiled=True
        ).astype(jnp.float32),
        lax.psum_scatter(
            value_terms.astype(jnp.bfloat16), "seq", scatter_dimension=1, tiled=True
        ).astype(jnp.float32),
    )
    grad_keys = grad_keys.astype(jnp.bfloat16).reshape(total_rows, width)
    grad_values = grad_values.astype(jnp.bfloat16).reshape(total_rows, width)
    grad_query_w = outer_sum(normed_one, grad_queries)
    grad_key_w = outer_sum(normed_one, grad_keys)
    grad_value_w = outer_sum(normed_one, grad_values)
    grad_normed_one = (
        back_project(grad_queries, full_query)
        + back_project(grad_keys, full_key)
        + back_project(grad_values, full_value)
    )
    grad_gain_one, grad_input_norm = norm_backward(flat, scale_one, gain_one, grad_normed_one)
    grad_input = (grad_hidden + grad_input_norm).reshape(blocks, shard_len, width)
    shards = (
        lax.psum_scatter(
            grad_query_w.astype(jnp.bfloat16), "seq", scatter_dimension=0, tiled=True
        ).astype(jnp.float32),
        lax.psum_scatter(
            grad_key_w.astype(jnp.bfloat16), "seq", scatter_dimension=0, tiled=True
        ).astype(jnp.float32),
        lax.psum_scatter(
            grad_value_w.astype(jnp.bfloat16), "seq", scatter_dimension=0, tiled=True
        ).astype(jnp.float32),
        lax.psum_scatter(
            grad_out_proj.astype(jnp.bfloat16), "seq", scatter_dimension=0, tiled=True
        ).astype(jnp.float32),
        lax.psum_scatter(
            grad_in.astype(jnp.bfloat16), "seq", scatter_dimension=0, tiled=True
        ).astype(jnp.float32),
        lax.psum_scatter(
            grad_down.astype(jnp.bfloat16), "seq", scatter_dimension=0, tiled=True
        ).astype(jnp.float32),
        lax.psum_scatter(
            grad_gain_one.astype(jnp.bfloat16), "seq", scatter_dimension=0, tiled=True
        ).astype(jnp.float32),
        lax.psum_scatter(
            grad_gain_two.astype(jnp.bfloat16), "seq", scatter_dimension=0, tiled=True
        ).astype(jnp.float32),
        lax.psum_scatter(
            grad_table.astype(jnp.bfloat16), "seq", scatter_dimension=0, tiled=True
        ).astype(jnp.float32),
    )
    totals = (
        lax.psum(shards[0].astype(jnp.bfloat16), "dp").astype(jnp.float32),
        lax.psum(shards[1].astype(jnp.bfloat16), "dp").astype(jnp.float32),
        lax.psum(shards[2].astype(jnp.bfloat16), "dp").astype(jnp.float32),
        lax.psum(shards[3].astype(jnp.bfloat16), "dp").astype(jnp.float32),
        lax.psum(shards[4].astype(jnp.bfloat16), "dp").astype(jnp.float32),
        lax.psum(shards[5].astype(jnp.bfloat16), "dp").astype(jnp.float32),
        lax.psum(shards[6].astype(jnp.bfloat16), "dp").astype(jnp.float32),
        lax.psum(shards[7].astype(jnp.bfloat16), "dp").astype(jnp.float32),
        lax.psum(shards[8].astype(jnp.bfloat16), "dp").astype(jnp.float32),
    )
    return (
        pooled,
        grad_input,
        totals[0],
        totals[1],
        totals[2],
        totals[3],
        totals[4],
        totals[5],
        totals[6],
        totals[7],
        totals[8],
    )


def fused_on_device(
    inputs,
    w_query,
    w_key,
    w_value,
    w_out,
    w_ffn_in,
    w_ffn_out,
    attn_gain,
    ffn_gain,
    rel_bias,
    doc_lengths,
    cotangent,
):
    docs, shard_len, width = inputs.shape
    rows_w, hidden_units = w_ffn_in.shape
    tokens = shard_len * SEQ
    half = width // 2
    part = hidden_units // (2 * SEQ)
    blocks = tokens // BLK
    pairs = half // BLK
    parts = part // BLK
    heads = rel_bias.shape[1]
    gains = jnp.stack([attn_gain, ffn_gain]).astype(F32)
    anywhere = pl.BlockSpec(memory_space=pl.ANY)
    vmem = pl.BlockSpec(memory_space=pltpu.VMEM)
    smem = pl.BlockSpec(memory_space=pltpu.SMEM)
    shape = jax.ShapeDtypeStruct
    narrow = [
        (docs, shard_len, width),
        (rows_w, width),
        (rows_w, width),
        (rows_w, width),
        (rows_w, width),
        (rows_w, hidden_units),
        (2 * part, width),
    ]
    out_shape = (
        shape((docs, width), F32),
        shape((8, 2 * BLK), F32),
        shape((8, BLK), F32),
        *(shape(s, BF16) for s in narrow),
        shape((2 * pairs, tokens, tokens), BF16),
    )
    out_part = rows_w // 2

    def sums(count, size, columns):
        return [((count, size // 2, columns), BF16)] * 2 + [((count, size, columns), BF16)] * 4

    scratch = [
        ((SEQ, BLK, width), BF16),
        ((blocks, BLK, width), BF16),
        ((tokens, width), BF16),
        ((width, 3 * half), BF16),
        ((tokens, 3 * half), BF16),
        ((tokens, half), BF16),
        ((half, width), BF16),
        ((SEQ, BLK, width), BF16),
        ((SEQ, BLK, width), BF16),
        ((SEQ, BLK, width), F32),
        ((tokens, width), BF16),
        ((width, SEQ * part), BF16),
        ((SEQ * part, width), BF16),
        ((tokens, SEQ * part), BF16),
        ((tokens, SEQ * part), BF16),
        ((SEQ, BLK, width), F32),
        ((2 * pairs, 5 * BLK, BLK), F32),
        ((3, 16, 2 * BLK), F32),
        ((tokens, BLK), BF16),
        ((8, tokens), F32),
        ((BLK + 16, tokens), BF16),
        ((tokens, 3 * half), BF16),
        ((tokens, half), BF16),
        ((tokens, BLK), F32),
        ((tokens, BLK), F32),
        ((6 * pairs, BLK, BLK), F32),
        ((pairs, 2, 8, tokens), F32),
        ((pairs, width, 3 * BLK), BF16),
        ((parts, SEQ, BLK, width), BF16),
        *sums(parts, BLK, width),
        *sums(SEQ, rows_w, part),
        *sums(pairs, rows_w, 3 * BLK),
        ((SEQ, out_part, width), BF16),
        ((out_part, width), BF16),
        ((out_part, width), BF16),
        ((SEQ + 1, 48, BLK), F32),
        ((8, width), F32),
        ((8, width), F32),
        ((8, SEQ * part), F32),
        ((8, width), F32),
        ((4, 8, width), F32),
        ((32, BLK), F32),
        ((8, 32, BLK), F32),
        ((4, 32, BLK), F32),
        ((BLK, BLK), F32),
    ]
    chunks = parts + SEQ + pairs + 1
    pair_of = lambda *dims: [pltpu.SemaphoreType.DMA(dims)] * 2
    semaphores = (
        pair_of(5)
        + pair_of(4)
        + pair_of(4)
        + pair_of(7, 8)
        + pair_of(4)
        + pair_of(4) * 8
        + pair_of(chunks, 6)
        + pair_of(4)
        + pair_of(chunks, 6)
        + pair_of(4)
        + pair_of(8)
        + pair_of(4)
        + [pltpu.SemaphoreType.DMA((chunks, 3))]
        + [pltpu.SemaphoreType.DMA((2,))]
    )
    results = pl.pallas_call(
        fused_kernel,
        out_shape=out_shape,
        in_specs=[anywhere] * 8 + [vmem, vmem, smem],
        out_specs=(vmem, vmem, vmem) + (anywhere,) * 8,
        scratch_shapes=[pltpu.VMEM(*s) for s in scratch] + semaphores,
        compiler_params=pltpu.CompilerParams(
            collective_id=0, has_side_effects=True, vmem_limit_bytes=VMEM_LIMIT
        ),
        name="block",
    )(
        inputs,
        cotangent,
        w_query,
        w_key,
        w_value,
        w_out,
        w_ffn_in,
        w_ffn_out,
        gains,
        rel_bias,
        doc_lengths,
    )

    steps = 4

    def rows_spec(s):
        if len(s) == 3:
            return pl.BlockSpec(
                (1, s[1] * s[0] // steps, s[2]),
                lambda i: (i // (steps // s[0]), i % (steps // s[0]), 0),
            )
        return pl.BlockSpec((s[0] // steps, s[1]), lambda i: (i, 0))

    def whole_spec(s):
        return pl.BlockSpec(s, lambda i: (0,) * len(s))

    tiny = [(docs, width), (1, rows_w), (1, rows_w), (8, heads)]
    pooled, one, two, table, gx, gq, gk, gv, go, gi, gd = pl.pallas_call(
        widen_kernel,
        out_shape=[shape(s, F32) for s in tiny + narrow],
        grid=(steps,),
        in_specs=[whole_spec(r.shape) for r in results[:3]] + [rows_spec(s) for s in narrow],
        out_specs=[whole_spec(s) for s in tiny] + [rows_spec(s) for s in narrow],
        compiler_params=pltpu.CompilerParams(vmem_limit_bytes=VMEM_LIMIT),
        name="widen",
    )(*results[:-1])
    return (pooled, gx, gq, gk, gv, go, gi, gd, one[0], two[0], table)


def fits(mesh):
    return mesh.shape["dp"] == CORES * DEPTH and mesh.shape["seq"] == SEQ


def solution(mesh):
    in_specs = (
        P("dp", "seq", None),
        P("seq", None),
        P("seq", None),
        P("seq", None),
        P("seq", None),
        P("seq", None),
        P("seq", None),
        P("seq"),
        P("seq"),
        P("seq", None),
        P("dp"),
        P("dp", "seq", None),
    )
    out_specs = (
        P("dp", None),
        P("dp", "seq", None),
        P("seq", None),
        P("seq", None),
        P("seq", None),
        P("seq", None),
        P("seq", None),
        P("seq", None),
        P("seq"),
        P("seq"),
        P("seq", None),
    )
    return jax.shard_map(
        fused_on_device if fits(mesh) else on_device, mesh=mesh, in_specs=in_specs, out_specs=out_specs, check_vma=False
    )
```

```python
import math

import jax
import jax.numpy as jnp
from jax import lax
from jax.experimental import pallas as pl
from jax.experimental.pallas import tpu as pltpu
from jax.sharding import PartitionSpec as P

EPS = 1e-06
THRESHOLDS = (12, 16, 23, 32, 46, 64, 91)
NEGATIVE = -1000000000.0
GELU_C = math.sqrt(2.0 / math.pi)
GELU_K = 0.044715


def bucket_ids(query_pos, key_pos):
    offset = key_pos[None, :] - query_pos[:, None]
    distance = jnp.abs(offset)
    upper = jnp.where(offset > 0, 16, 0).astype(jnp.int32)
    beyond = jnp.full(distance.shape, 8, jnp.int32)
    for threshold in THRESHOLDS:
        beyond = beyond + (distance >= threshold).astype(jnp.int32)
    return upper + jnp.where(distance < 8, distance, beyond)


def gelu_slope(value):
    inner = GELU_C * (value + GELU_K * value * value * value)
    tangent = jnp.tanh(inner)
    return 0.5 * (1.0 + tangent) + 0.5 * value * (1.0 - tangent * tangent) * GELU_C * (
        1.0 + 3.0 * GELU_K * value * value
    )


def outer_sum(left, right):
    return lax.dot_general(
        left, right, (((0,), (0,)), ((), ())), preferred_element_type=jnp.float32
    )


def back_project(grad, weight):
    return lax.dot_general(
        grad, weight, (((1,), (1,)), ((), ())), preferred_element_type=jnp.float32
    )


def norm_backward(source, scale, gain, grad_normed):
    grad_gain = jnp.sum(grad_normed * source * scale, 0)
    grad_scaled = grad_normed * gain
    grad_source = scale * grad_scaled - source * scale * scale * scale * jnp.mean(
        grad_scaled * source, -1, keepdims=True
    )
    return (grad_gain, grad_source)


SEQ, CORES, DEPTH = 4, 2, 4
BLK = 128
MESH = pl.DeviceIdType.MESH
F32 = jnp.float32
BF16 = jnp.bfloat16
VMEM_LIMIT = 60 << 20


def contract(left, right, left_dim, right_dim):
    return lax.dot_general(
        left, right, (((left_dim,), (right_dim,)), ((), ())), preferred_element_type=F32
    )


def exact(left, right, left_dim, right_dim):
    return lax.dot_general(
        left,
        right,
        (((left_dim,), (right_dim,)), ((), ())),
        preferred_element_type=F32,
        precision=lax.Precision.HIGHEST,
    )


def await_copy(ref, sem):
    pltpu.make_async_copy(ref, ref, sem).wait()


def tile(index, size):
    return pl.ds(pl.multiple_of(index * size, size), size)


def bucket_of(offset):
    distance = jnp.abs(offset)
    beyond = jnp.full(distance.shape, 8, jnp.int32)
    for threshold in THRESHOLDS:
        beyond = beyond + (distance >= threshold).astype(jnp.int32)
    return jnp.where(offset > 0, 16, 0) + jnp.where(distance < 8, distance, beyond)


STEPS = dict(s="start", m="middle", z1="z_one", z2="z_two", z3="z_three", z4="z_four")
SCHEDULE = {
    "gdn2": [("d2", "s"), ("d1", "s")],
    "wd": [],
    "gact": [("d2", "m")],
    "gn": [("d1", "m")],
    "gin0": [],
    "gin1": [("d0", "s")],
    "n2": [("i2", "s")],
    "op": [("d1", "z1"), ("d2", "z1"), ("d0", "m")],
    "u0": [("i3", "s")],
    "u1": [("d1", "z2"), ("i2", "m"), ("d2", "z2"), ("i3", "m"), ("d0", "z1"), ("i0", "s")],
    "u2": [("q0", "s"), ("d1", "z3"), ("d0", "z2"), ("i1", "s")],
    "u3": [("d2", "z3"), ("i3", "z1")],
    "u4": [("i0", "m"), ("d0", "z3"), ("q0", "m"), ("i3", "z2"), ("i2", "z1"), ("i1", "m")],
    "u5": [("i0", "z1"), ("i2", "z2"), ("q2", "s")],
    "sw": [],
    "b0": [("q0", "z1"), ("q1", "s"), ("i3", "z3"), ("i0", "z2"), ("i1", "z1"), ("q2", "m"), ("i2", "z3"), ("q0", "z2"), ("d0", "z4"), ("q1", "m"), ("o", "s")],
    "b1": [("d1", "z4"), ("i0", "z3"), ("i1", "z2"), ("q0", "z3"), ("q2", "z1")],
    "g1": [("i3", "z4"), ("q2", "z2"), ("i1", "z3"), ("q1", "z1"), ("i0", "z4"), ("o", "z1"), ("q0", "z4"), ("q1", "z2"), ("q2", "z3"), ("o", "z2"), ("i2", "z4"), ("q1", "z3"), ("gx", "s"), ("sm", "s"), ("q2", "z4"), ("d2", "z4"), ("q1", "z4"), ("i1", "z4"), ("o", "z3"), ("o", "z4")],
    "end": [],
}


def full_sum(value):
    return jnp.sum(jnp.sum(value, 0, keepdims=True), 1, keepdims=True)


def fused_kernel(
    inputs,
    cotangent,
    w_query,
    w_key,
    w_value,
    w_out,
    w_in,
    w_down,
    gain_one,
    gain_two,
    bias_in,
    lengths_in,
    pooled_o,
    small_o,
    table_o,
    gx_o,
    gq_o,
    gk_o,
    gv_o,
    go_o,
    gi_o,
    gd_o,
    raised_o,
    xown,
    grads,
    nrm1,
    wqkv,
    qkv,
    mixed,
    wo,
    psend,
    precv,
    hid,
    nrm2,
    wi,
    wd,
    act,
    slope,
    gn,
    strip,
    vecs,
    maskc,
    gscale,
    flip,
    dqkv,
    gmix,
    dk_acc,
    dv_acc,
    near,
    far,
    gqkv,
    gdn,
    d_dx,
    d_dy,
    d_rx,
    d_ry,
    d_za,
    d_zb,
    i_dx,
    i_dy,
    i_rx,
    i_ry,
    i_za,
    i_zb,
    q_dx,
    q_dy,
    q_rx,
    q_ry,
    q_za,
    q_zb,
    rs_o,
    o_za,
    o_zb,
    small_all,
    wide,
    gains,
    asum,
    pp,
    pool_recv,
    sg,
    sg_plane,
    sg_depth,
    turned,
    small_ss,
    small_rs,
    x_ss,
    x_rs,
    c_ss,
    c_rs,
    wg_ss,
    wg_rs,
    wo_ss,
    wo_rs,
    n1_ss,
    n1_rs,
    g_ss,
    g_rs,
    part_ss,
    part_rs,
    n2_ss,
    n2_rs,
    gn2_ss,
    gn2_rs,
    gat_ss,
    gat_rs,
    gn1_ss,
    gn1_rs,
    gx_ss,
    gx_rs,
    rs_ss,
    rs_rs,
    rso_ss,
    rso_rs,
    z_ss,
    z_rs,
    pool_ss,
    pool_rs,
    sgp_ss,
    sgp_rs,
    sgz_ss,
    sgz_rs,
    out_s,
    raised_s,
):
    dp = lax.axis_index("dp")
    chip = lax.axis_index("seq")
    depth, core = lax.div(dp, 2), lax.rem(dp, 2)
    row, col = lax.div(chip, 2), lax.rem(chip, 2)
    other = (depth * 2 + 1 - core, chip)
    xn = row * 2 + 1 - col
    yn = (1 - row) * 2 + col
    dn = (1 - row) * 2 + 1 - col
    tokens, width = nrm1.shape
    half = width // 2
    rows_w = w_query.shape[0]
    ff_part = gdn.shape[0] * BLK
    quarter, middle_q = tokens // 4, tokens // 2
    middle_w = width // 2

    def remote(src, dst, send, recv, device):
        return pltpu.make_async_remote_copy(
            src_ref=src,
            dst_ref=dst,
            send_sem=send,
            recv_sem=recv,
            device_id=device,
            device_id_type=MESH,
        )

    def ahead(step):
        return lax.rem(chip + step, SEQ)

    pending = []

    def send_now(*args):
        copy = remote(*args)
        copy.start()
        pending.append(copy)

    lane = lax.broadcasted_iota(jnp.int32, (1, BLK), 1)
    wide[...] = jnp.zeros_like(wide)
    wide[0:1, 0:rows_w] = gain_one[...].astype(F32).reshape(1, rows_w)
    wide[1:2, 0:rows_w] = gain_two[...].astype(F32).reshape(1, rows_w)
    turned_gains = pltpu.roll(wide[...], chip * rows_w, 1)
    small_all[0] = jnp.zeros_like(small_all[0])
    for which in range(2):
        for i in range(width // BLK):
            small_all[0, 8 * which + i : 8 * which + i + 1, :] = turned_gains[
                which : which + 1, i * BLK : (i + 1) * BLK
            ]
    small_all[0, 6:7, :] = jnp.where(
        lane == 0, lengths_in[0].astype(F32), lengths_in[1].astype(F32)
    )
    small_all[0, tile(2 + chip, 8), 0 : bias_in.shape[1]] = bias_in[...].astype(F32)

    barrier = pltpu.get_barrier_semaphore()
    for step in range(SEQ):
        if step:
            pl.semaphore_signal(barrier, inc=1, device_id=(dp, ahead(step)), device_id_type=MESH)
        pl.semaphore_signal(
            barrier, inc=1, device_id=(other[0], ahead(step)), device_id_type=MESH
        )
    for step in range(1, DEPTH):
        pl.semaphore_signal(
            barrier,
            inc=1,
            device_id=(lax.rem(depth + step, DEPTH) * 2 + core, chip),
            device_id_type=MESH,
        )
    pl.semaphore_wait(barrier, 2 * SEQ - 1 + DEPTH - 1)

    mine = small_all.at[0]
    for step in range(1, SEQ):
        send_now(
            mine, small_all.at[step], small_ss.at[step], small_rs.at[step], (dp, ahead(step))
        )
    send_now(mine, small_all.at[SEQ], small_ss.at[SEQ], small_rs.at[SEQ], other)

    def spread(source, dest_of, send, recv, action, halves=(0, 1)):
        for doc in (1 - col, col):
            for to in halves:
                block = source.at[doc, pl.ds(to * BLK, BLK)]
                target = core * 2 + doc
                own = (target == chip) & (core == to)
                copy = remote(
                    block,
                    dest_of(to),
                    send.at[doc * 2 + to],
                    recv.at[chip],
                    (depth * 2 + to, target),
                )
                if action == "start":

                    @pl.when(own)
                    def _():
                        pltpu.make_async_copy(block, dest_of(to), recv.at[chip]).start()

                @pl.when(jnp.logical_not(own))
                def _():
                    if action == "start":
                        copy.start()
                    else:
                        copy.wait_send()

    x_slot = lambda to: xown.at[chip]
    c_slot = lambda to: grads.at[chip * 2 + to]

    class Gather:
        def __init__(self, index, pieces, place):
            self.index, self.pieces, self.place = index, pieces, place
            self.bind()

        def half_of(self, owner, which):
            ref = self.place(owner)
            size = ref.shape[0] // 2
            return ref.at[pl.ds(which * size, size)]

        def bind(self):
            k = self.index
            self.local, self.one, self.two = [], [], []
            for src, cut in self.pieces:
                dst = cut(self.place(chip))
                self.local.append(pltpu.make_async_copy(src, dst, wg_rs.at[k, 0]))
                self.one.append(remote(src, dst, wg_ss.at[k, 0], wg_rs.at[k, 1], (dp, xn)))
                self.one.append(remote(src, dst, wg_ss.at[k, 1], wg_rs.at[k, 2], (dp, yn)))
            via_x, via_y = self.half_of(xn, 1), self.half_of(yn, 0)
            self.two = [
                remote(via_x, via_x, wg_ss.at[k, 2], wg_rs.at[k, 3], (dp, yn)),
                remote(via_y, via_y, wg_ss.at[k, 3], wg_rs.at[k, 4], (dp, xn)),
            ]
            self.from_x, self.from_y = self.place(xn), self.place(yn)
            self.last = [self.half_of(dn, 1), self.half_of(dn, 0)]
            self.own = self.place(chip)

        def first(self):
            for copy in self.local + self.one:
                copy.start()

        def second(self):
            k = self.index
            await_copy(self.from_x, wg_rs.at[k, 1])
            self.two[0].start()
            await_copy(self.from_y, wg_rs.at[k, 2])
            self.two[1].start()

        def done(self):
            k = self.index
            await_copy(self.own, wg_rs.at[k, 0])
            await_copy(self.last[0], wg_rs.at[k, 3])
            await_copy(self.last[1], wg_rs.at[k, 4])

        def sent(self):
            k = self.index
            for copy in self.two:
                copy.wait_send()
            await_copy(self.own, wg_ss.at[k, 0])
            await_copy(self.own, wg_ss.at[k, 1])

    class SharedGather(Gather):
        def part(self, owner, which):
            ref = self.place(owner)
            size = ref.shape[0] // 2
            return ref.at[tile(which, size)]

        def bind(self):
            k = self.index
            mine, theirs = lax.rem(depth, 2), 1 - lax.rem(depth, 2)
            beside = ((depth + theirs - mine) * 2 + core, chip)
            self.local, self.one = [], []
            for src, cut in self.pieces:
                size = src.shape[0] // 2
                self.local.append(
                    pltpu.make_async_copy(src, cut(self.place(chip)), wg_rs.at[k, 0])
                )
                dst = cut(self.part(chip, mine))
                src = src.at[tile(mine, size)]
                self.one.append(remote(src, dst, wg_ss.at[k, 0], wg_rs.at[k, 1], (dp, xn)))
                self.one.append(remote(src, dst, wg_ss.at[k, 1], wg_rs.at[k, 2], (dp, yn)))
            self.from_x, self.from_y = self.part(xn, mine), self.part(yn, mine)
            far = self.part(dn, mine)
            size = far.shape[0] // 2
            cut = lambda ref, which: ref.at[pl.ds(which * size, size)]
            via_x, via_y = cut(self.from_x, 1), cut(self.from_y, 0)
            self.last = [cut(far, 1), cut(far, 0)]
            self.two = [
                remote(via_x, via_x, wg_ss.at[k, 2], wg_rs.at[k, 3], (dp, yn)),
                remote(via_y, via_y, wg_ss.at[k, 3], wg_rs.at[k, 4], (dp, xn)),
            ]
            self.beside = [
                remote(ref, ref, wg_ss.at[k, 4 + n], wg_rs.at[k, 5 + n], beside)
                for n, ref in enumerate((self.from_x, self.from_y, far))
            ]
            self.own = self.place(chip)
            self.half = self.part(chip, mine)

        def second(self):
            super().second()
            self.show()

        def forward(self):
            super().second()

        def show(self):
            for copy in self.beside[:2]:
                copy.start()

        def third(self):
            k = self.index
            await_copy(self.last[0], wg_rs.at[k, 3])
            await_copy(self.last[1], wg_rs.at[k, 4])
            self.beside[2].start()

        def done(self):
            await_copy(self.own, wg_rs.at[self.index, 0])
            for copy in self.beside:
                copy.wait_recv()

        def sent(self):
            k = self.index
            for copy in self.two + self.beside:
                copy.wait_send()
            await_copy(self.half, wg_ss.at[k, 0])
            await_copy(self.half, wg_ss.at[k, 1])

    core_cols = tile(core, half)
    whole = lambda ref: ref
    pair_w = 3 * BLK

    def qkv_item(index, pair):
        return SharedGather(
            index,
            [
                (
                    w.at[:, tile(core * 3 + pair, BLK)],
                    lambda ref, i=i: ref.at[:, pl.ds(i * BLK, BLK)],
                )
                for i, w in enumerate((w_query, w_key, w_value))
            ],
            lambda owner: wqkv.at[tile(owner, rows_w), pl.ds(pair * pair_w, pair_w)],
        )

    def in_item(index, part):
        return SharedGather(
            index,
            [
                (
                    w_in.at[:, tile((2 * part + f) * 2 + core, ff_part)],
                    lambda ref, f=f: ref.at[:, pl.ds(f * ff_part, ff_part)],
                )
                for f in range(2)
            ],
            lambda owner: wi.at[tile(owner, rows_w), pl.ds(part * 2 * ff_part, 2 * ff_part)],
        )

    def down_item(kind, index, first, size):
        unit = ff_part // 4
        at = lambda base: pl.ds(pl.multiple_of(base + first * unit, unit), size * unit)
        return kind(
            index, [(w_down.at[at(core * ff_part)], whole)], lambda owner: wd.at[at(owner * ff_part)]
        )

    qkv_items = [qkv_item(i, i) for i in range(3)]
    in_items = [in_item(3, 0), in_item(4, 1)]
    down_items = [
        down_item(SharedGather, 5, 0, 2),
        down_item(Gather, 6, 2, 1),
        down_item(Gather, 7, 3, 1),
    ]
    for it in qkv_items:
        it.first()
    spread(inputs, x_slot, x_ss, x_rs, "start")

    wo_part = rows_w // 2
    wo_src = w_out.at[tile(core, wo_part)]
    wo_dst = wo.at[tile(col * 2 + core, wo_part)]

    def wo_each(action):
        for to in range(SEQ):
            own = (chip == to) & (core == row)
            copy = remote(
                wo_src, wo_dst, wo_ss.at[to], wo_rs.at[col * 2 + core], (depth * 2 + row, to)
            )
            if action == "start":

                @pl.when(own)
                def _():
                    pltpu.make_async_copy(wo_src, wo_dst, wo_rs.at[col * 2 + core]).start()

            @pl.when(jnp.logical_not(own))
            def _():
                if action == "start":
                    copy.start()
                else:
                    copy.wait_send()

    for step in range(1, SEQ + 1):
        await_copy(small_all.at[step], small_rs.at[step])
    summed = small_all[0] + small_all[1] + small_all[2] + small_all[3]
    for which in range(2):
        gains[which : which + 1, :] = jnp.concatenate(
            [summed[8 * which + i : 8 * which + i + 1, :] for i in range(width // BLK)], axis=1
        )
    length_row = jnp.where(row == core, small_all[0, 6:7, :], small_all[SEQ, 6:7, :])
    length = jnp.where(col == 0, length_row[:, 0:1], length_row[:, 1:2])
    own_lengths = small_all[0, 6:7, 0:2]
    table = summed[16:48, :].astype(BF16)
    lane_two = lax.broadcasted_iota(jnp.int32, (1, 2 * BLK), 1)
    minus = jnp.where(lane_two < BLK, lane_two, lane_two - 2 * BLK)
    for off in (-1, 0, 1):
        ids = bucket_of(off * BLK - minus)
        onehot = (lax.broadcasted_iota(jnp.int32, (32, 2 * BLK), 0) == ids).astype(BF16)
        vecs[off + 1] = contract(table, onehot, 0, 0)[0:16, :]

    @pl.loop(0, 6)
    def _(h):
        values = [vecs[i, pl.ds(core * 6 + h, 1), :] for i in range(3)]
        left = jnp.broadcast_to(values[0][:, BLK - 1 : BLK], (BLK, BLK))
        right = jnp.broadcast_to(values[2][:, BLK + 1 : BLK + 2], (BLK, BLK))
        strip[h, 0:BLK, :] = left
        strip[h, 4 * BLK :, :] = right
        for i in range(3):
            skewed = pltpu.roll(
                jnp.broadcast_to(values[i], (BLK, 2 * BLK)), 0, 1, stride=1, stride_axis=0
            )
            strip[h, (i + 1) * BLK : (i + 2) * BLK, :] = skewed[:, :BLK]

    key_pos = lax.broadcasted_iota(jnp.int32, maskc.shape, 0).astype(F32)
    maskc[...] = jnp.where((key_pos < length) | (lane > 0), 0.0, NEGATIVE).astype(BF16)

    def block_valid(b):
        pos = lax.broadcasted_iota(jnp.int32, (BLK, 1), 0) + b * BLK
        return (pos.astype(F32) < length).astype(F32)

    for it in qkv_items:
        it.second()

    def n1_copy(i):
        block = nrm1.at[tile(2 * i + core, BLK)]
        return remote(block, block, n1_ss.at[i], n1_rs.at[i], other)

    @pl.loop(0, SEQ)
    def _(i):
        await_copy(xown.at[i], x_rs.at[i])
        source = xown[i].astype(F32)
        scale = lax.rsqrt(jnp.mean(source * source, -1, keepdims=True) + EPS)
        nrm1[tile(2 * i + core, BLK), :] = (source * scale * gains[0:1, :]).astype(BF16)
        n1_copy(i).start()

    for it in in_items:
        it.first()
    for it in qkv_items:
        it.third()
    for i in range(SEQ):
        n1_copy(i).wait_recv()
    in_items[0].second()
    spread(cotangent, c_slot, c_ss, c_rs, "start", (0,))

    flip[BLK : BLK + 16, :] = jnp.ones((16, tokens), BF16)
    mine_lanes = [lane < 64, lane >= 64]
    slots = [ref.at[:, pl.ds(0, tokens)] for ref in (act, slope)]

    def by_head(value):
        return jnp.concatenate(
            [jnp.where(lanes, value, jnp.zeros_like(value)) for lanes in mine_lanes], axis=0
        )

    def serve(now, table):
        for when, actions in table.items():

            @pl.when(now == when)
            def _():
                for action in actions:
                    action()

    def keep(pair, qb):
        return pltpu.make_async_copy(slots[qb], raised_o.at[2 * pair + qb], raised_s.at[qb])

    def fetch(pair, qb):
        return pltpu.make_async_copy(raised_o.at[2 * pair + qb], slots[qb], raised_s.at[qb])

    def later_inputs():
        down_items[0].first()
        spread(cotangent, c_slot, c_ss, c_rs, "start", (1,))

    forward_table = {
        0: [in_items[1].second, lambda: wo_each("start")],
        1: [in_items[0].third, later_inputs],
        3: [in_items[1].third],
    }

    @pl.loop(0, 3)
    def _(pair):
        cols = tile(pair, BLK)
        for p in range(3):

            @pl.when(pair == p)
            def _():
                qkv_items[p].done()

        qkv[:, tile(pair, pair_w)] = contract(
            nrm1[...], wqkv[:, tile(pair, pair_w)], 1, 0
        ).astype(BF16)
        flip[0:BLK, :] = jnp.transpose(qkv[:, tile(3 * pair + 2, BLK)])
        keys = jnp.concatenate([qkv[:, tile(3 * pair + 1, BLK)], maskc[...]], axis=1)
        for qb in range(2):
            rows = pl.ds(qb * middle_q, middle_q)
            queries = by_head(qkv[rows, tile(3 * pair, BLK)])
            flag = jnp.broadcast_to(jnp.where(lane == 0, 1.0, 0.0).astype(BF16), queries.shape)
            biases = [
                jnp.concatenate(
                    [
                        strip[
                            pair * 2 + h, pl.ds((min(max(kb - q, -2), 2) + 2) * BLK, BLK), :
                        ]
                        for kb in range(tokens // BLK)
                    ],
                    axis=0,
                )
                for h in range(2)
                for q in range(qb * middle_q // BLK, (qb + 1) * middle_q // BLK)
            ]
            logits = contract(keys, jnp.concatenate([queries, flag], axis=1), 1, 1)
            logits = logits + jnp.concatenate(biases, axis=1)
            highest = jnp.max(logits, 0, keepdims=True)
            raised = jnp.exp(logits - highest).astype(BF16)

            @pl.when(pair > 0)
            def _():
                keep(pair - 1, qb).wait()

            slots[qb][...] = raised
            keep(pair, qb).start()
            result = contract(flip[...], raised, 1, 0)
            inverse = 1.0 / result[BLK : BLK + 1, :]
            scaled = result[0:BLK, :] * inverse
            mixed[rows, cols] = jnp.transpose(
                jnp.concatenate([scaled[0:64, 0:middle_q], scaled[64:BLK, middle_q:]], axis=0)
            ).astype(BF16)
            for h in range(2):
                gscale[pl.ds(2 * pair + h, 1), rows] = inverse[:, h * middle_q : (h + 1) * middle_q]
            serve(2 * pair + qb, forward_table)

    def swap_copy(i, send, recv):
        return remote(psend.at[i], precv.at[i], send.at[i], recv.at[i], other)

    for k in range(4):
        await_copy(wo.at[pl.ds(k * wo_part, wo_part)], wo_rs.at[k])

    def blocks_of(ref, parity):
        return jnp.concatenate(
            [ref[tile(2 * i + parity, BLK), :] for i in range(SEQ)], axis=0
        )

    def swap_out(result, send, recv):
        for i in range(SEQ):
            psend[i] = result[i * BLK : (i + 1) * BLK, :].astype(BF16)
            swap_copy(i, send, recv).start()

    swap_out(contract(blocks_of(mixed, 1 - core), wo[...], 1, 0), part_ss, part_rs)

    def n2_copy(i, send, recv):
        block = nrm2.at[tile(2 * i + core, BLK)]
        return remote(block, block, send.at[i], recv.at[i], other)

    pp[...] = jnp.zeros_like(pp)
    result = contract(blocks_of(mixed, core), wo[...], 1, 0)
    for i in range(SEQ):
        hidden = xown[i].astype(F32) + result[i * BLK : (i + 1) * BLK, :]
        swap_copy(i, part_ss, part_rs).wait_recv()
        hidden = hidden + precv[i].astype(F32)
        hid[i] = hidden
        scale = lax.rsqrt(jnp.mean(hidden * hidden, -1, keepdims=True) + EPS)
        nrm2[tile(2 * i + core, BLK), :] = (hidden * scale * gains[1:2, :]).astype(BF16)
        n2_copy(i, n2_ss, n2_rs).start()
        pp[0:1, :] += jnp.sum(hidden * block_valid(2 * i + core), 0, keepdims=True)
    down_items[0].second()
    for it in down_items[1:]:
        it.first()
    for i in range(SEQ):
        n2_copy(i, n2_ss, n2_rs).wait_recv()
    for qb in range(2):
        keep(2, qb).wait()

    def g_copy(i):
        block = grads.at[2 * i + core]
        return remote(block, block, g_ss.at[i], g_rs.at[i], other)

    def take_cotangent():
        @pl.loop(0, SEQ)
        def _(i):
            b = 2 * i + core
            await_copy(grads.at[b], c_rs.at[i])
            grads[b] = (grads[b].astype(F32) * block_valid(b)).astype(BF16)
            g_copy(i).start()

    asum[...] = jnp.zeros_like(asum)
    wide_part = 2 * ff_part
    for part in range(2):
        part_cols = slice(part * wide_part, (part + 1) * wide_part)
        if part == 1:
            take_cotangent()
            down_items[0].third()
        in_items[part].done()

        @pl.loop(0, 2)
        def _(i):
            rows = tile(i, middle_q)
            value = contract(nrm2[rows, :], wi[:, part_cols], 1, 0)
            square = value * value
            tangent = jnp.tanh(value * (GELU_C + GELU_C * GELU_K * square))
            half_up = 0.5 + 0.5 * tangent
            active = (value * half_up).astype(BF16)
            act[rows, part_cols] = active
            slope[rows, part_cols] = (
                half_up
                + value
                * (1.0 - tangent * tangent)
                * (0.5 * GELU_C + 1.5 * GELU_C * GELU_K * square)
            ).astype(BF16)
            pos = lax.broadcasted_iota(jnp.int32, (8, middle_q), 1) + i * middle_q
            valid = (pos.astype(F32) < length).astype(BF16)
            asum[:, part_cols] += contract(valid, active, 1, 0)


    for i in range(SEQ):
        g_copy(i).wait_recv()
    g_all = lambda: grads[...].reshape(tokens, width)

    class Chunk:
        made = 0

        def __init__(self, src, dx, dy, rx, ry, za, zb, outs):
            self.index = Chunk.made
            Chunk.made += 1
            self.src, self.dx, self.dy, self.rx, self.ry = src, dx, dy, rx, ry
            self.za, self.zb, self.outs = za, zb, outs
            self.bind()

        def bind(self):
            k = self.index
            size = self.dx.shape[0]
            cut = lambda ref, which: ref.at[pl.ds(which * size, size)]
            ss, rs = (lambda i: rs_ss.at[k, i]), (lambda i: rs_rs.at[k, i])
            to_x, to_y = (dp, xn), (dp, yn)
            self.one = [
                remote(cut(self.src(dn), 1), self.dx, ss(0), rs(0), to_x),
                remote(cut(self.src(dn), 0), self.dy, ss(1), rs(1), to_y),
                remote(cut(self.src(xn), 1), cut(self.rx, 1), ss(2), rs(2), to_x),
                remote(cut(self.src(yn), 0), cut(self.ry, 0), ss(3), rs(3), to_y),
            ]
            self.sum_y, self.sum_x = cut(self.src(yn), 1), cut(self.src(xn), 0)
            self.two = [
                remote(self.sum_y, cut(self.ry, 1), ss(4), rs(4), to_y),
                remote(self.sum_x, cut(self.rx, 0), ss(5), rs(5), to_x),
            ]
            self.bind_z(self.rx, self.ry)

        def bind_z(self, reduced, final):
            k = self.index
            self.reduced, self.final = reduced, final
            sem = lambda i: (z_ss.at[k, i], z_rs.at[k, i])
            self.to_inner = remote(reduced, self.za, *sem(0), z_dev(toward))
            self.swap = remote(reduced, self.zb, *sem(1), z_dev(across))
            self.to_end = remote(final, final, *sem(2), z_dev(outward))

        def start(self):
            for copy in self.one:
                copy.start()

        def middle(self):
            for at, sent, sums, copy in (
                (0, self.dx, self.sum_y, self.two[0]),
                (1, self.dy, self.sum_x, self.two[1]),
            ):
                self.one[at].wait_recv()
                sums[...] = (sums[...].astype(F32) + sent[...].astype(F32)).astype(BF16)
                copy.start()

        def total(self):
            for copy in (self.one[2], self.one[3], *self.two):
                copy.wait_recv()
            self.rx[...] = (
                self.src(chip)[...].astype(F32)
                + self.rx[...].astype(F32)
                + self.ry[...].astype(F32)
            ).astype(BF16)

        def z_one(self):
            self.total()

            @pl.when(end_z)
            def _():
                self.to_inner.start()

        def z_two(self):
            @pl.when(inner_z)
            def _():
                self.to_inner.wait_recv()
                self.reduced[...] = (
                    self.reduced[...].astype(F32) + self.za[...].astype(F32)
                ).astype(BF16)
                self.swap.start()

        def z_three(self):
            @pl.when(inner_z)
            def _():
                self.swap.wait_recv()
                self.final[...] = (
                    self.reduced[...].astype(F32) + self.zb[...].astype(F32)
                ).astype(BF16)
                self.to_end.start()

        def each_out(self, act_on):
            k = self.index
            for n, (cols, place) in enumerate(self.outs):
                src = self.final if cols is None else self.final.at[:, cols]
                act_on(
                    remote(src, place(core), z_ss.at[k, 3 + n], z_rs.at[k, 3 + n], other),
                    pltpu.make_async_copy(src, place(core), out_s.at[k, n]),
                )

        def z_four(self):
            @pl.when(end_z)
            def _():
                self.to_end.wait_recv()

            self.each_out(lambda there, here: (there.start(), here.start()))

        def finish(self):
            self.each_out(
                lambda there, here: (there.wait_recv(), there.wait_send(), here.wait())
            )

            @pl.when(end_z)
            def _():
                self.to_inner.wait_send()

            @pl.when(inner_z)
            def _():
                self.swap.wait_send()
                self.to_end.wait_send()

            for copy in self.plane_sends():
                copy.wait_send()

        def plane_sends(self):
            return self.one + self.two

    inner_z = (depth == 1) | (depth == 2)
    end_z = jnp.logical_not(inner_z)
    toward = jnp.where(depth == 0, 1, 2)
    outward = jnp.where(depth == 1, 0, 3)
    across = jnp.where(depth == 1, 2, 1)

    def z_dev(z):
        return (z * 2 + core, chip)

    d_chunks = [
        Chunk(
            lambda owner, i=i: gdn.at[i, owner],
            d_dx.at[i],
            d_dy.at[i],
            d_rx.at[i],
            d_ry.at[i],
            d_za.at[i],
            d_zb.at[i],
            [
                (
                    None,
                    lambda c, i=i: gd_o.at[
                        pl.ds(pl.multiple_of(c * ff_part + i * BLK, BLK), BLK)
                    ],
                )
            ],
        )
        for i in range(ff_part // BLK)
    ]

    i_chunks = [
        Chunk(
            lambda owner, f=f: wi.at[tile(owner, rows_w), pl.ds(f * ff_part, ff_part)],
            i_dx.at[f],
            i_dy.at[f],
            i_rx.at[f],
            i_ry.at[f],
            i_za.at[f],
            i_zb.at[f],
            [(None, lambda c, f=f: gi_o.at[:, tile(2 * f + c, ff_part)])],
        )
        for f in range(SEQ)
    ]
    q_chunks = [
        Chunk(
            lambda owner, p=p: gqkv.at[p, tile(owner, rows_w)],
            q_dx.at[p],
            q_dy.at[p],
            q_rx.at[p],
            q_ry.at[p],
            q_za.at[p],
            q_zb.at[p],
            [
                (
                    pl.ds(j * BLK, BLK),
                    lambda c, p=p, o=o: o.at[:, tile(c * 3 + p, BLK)],
                )
                for j, o in enumerate((gq_o, gk_o, gv_o))
            ],
        )
        for p in range(3)
    ]
    def rso_each(action):
        for k in range(2):
            for to in range(2):
                target = core * 2 + k
                own = (chip == target) & (core == to)
                src = wo.at[pl.ds((2 * k + to) * wo_part, wo_part)]
                dst = rs_o.at[chip]
                copy = remote(
                    src, dst, rso_ss.at[2 * k + to], rso_rs.at[chip], (depth * 2 + to, target)
                )
                if action == "start":

                    @pl.when(own)
                    def _():
                        pltpu.make_async_copy(src, dst, rso_rs.at[chip]).start()

                @pl.when(jnp.logical_not(own))
                def _():
                    if action == "start":
                        copy.start()
                    else:
                        copy.wait_send()

    class OutChunk(Chunk):
        def bind(self):
            self.bind_z(self.src.at[0], self.src.at[1])

        def total(self):
            for i in range(SEQ):
                await_copy(self.src.at[i], rso_rs.at[i])
            value = self.src[0].astype(F32)
            for i in range(1, SEQ):
                value = value + self.src[i].astype(F32)
            self.reduced[...] = value.astype(BF16)

        def plane_sends(self):
            return []

    o_chunk = OutChunk(
        rs_o, None, None, None, None, o_za, o_zb, [(None, lambda c: go_o.at[tile(c, wo_part)])]
    )
    def gx_each(i, action):
        own = (chip == i) & (core == row)
        dst = gx_o.at[col, tile(core, BLK)]
        copy = remote(
            nrm2.at[pl.ds(i * BLK, BLK)], dst, gx_ss.at[i], gx_rs.at[col * 2 + core], (depth * 2 + row, i)
        )
        if action == "start":

            @pl.when(own)
            def _():
                pltpu.make_async_copy(nrm2.at[pl.ds(i * BLK, BLK)], dst, gx_rs.at[col * 2 + core]).start()

        @pl.when(jnp.logical_not(own))
        def _():
            if action == "start":
                copy.start()
            else:
                copy.wait_send()

    def sgz_copy(step):
        return remote(
            sg_depth.at[depth],
            sg_depth.at[depth],
            sgz_ss.at[step],
            sgz_rs.at[depth],
            z_dev(lax.rem(depth + step, DEPTH)),
        )

    def small_along_z():
        for i in range(8):
            await_copy(sg_plane.at[i], sgp_rs.at[i])
        total = sg_plane[0]
        for i in range(1, 8):
            total = total + sg_plane[i]
        sg_depth[depth] = total
        for step in range(1, DEPTH):
            sgz_copy(step).start()

    by_name = dict(
        [(f"d{i}", c) for i, c in enumerate(d_chunks)]
        + [(f"i{i}", c) for i, c in enumerate(i_chunks)]
        + [(f"q{i}", c) for i, c in enumerate(q_chunks)]
        + [("o", o_chunk)]
    )

    def after(block):
        for name, step in SCHEDULE[block]:
            if name == "gx":
                for i in range(SEQ):
                    gx_each(i, "start")
            elif name == "sm":
                small_along_z()
            elif name == "o" and step == "s":
                rso_each("start")
            else:
                getattr(by_name[name], STEPS[step])()

    for it in down_items[1:]:
        it.second()
    for i in range(ff_part // BLK):
        columns = jnp.concatenate(
            [act[:, f * ff_part + i * BLK : f * ff_part + (i + 1) * BLK] for f in range(SEQ)],
            axis=1,
        )
        gdn[i] = contract(columns, g_all(), 0, 0).astype(BF16).reshape(SEQ, BLK, width)
    after("gdn2")
    for it in down_items:
        it.done()
    for it in in_items:
        it.sent()
    after("wd")

    def pooled_part(cols):
        total = asum[0:1, cols]
        high = total.astype(BF16)
        rest = total - high.astype(F32)
        middle = rest.astype(BF16)
        low = (rest - middle.astype(F32)).astype(BF16)
        pieces = jnp.concatenate(
            [jnp.broadcast_to(piece, (16, piece.shape[1])) for piece in (high, middle, low)], axis=0
        )
        result = contract(pieces, wd[cols, :], 1, 0)
        pp[0:1, :] += result[0:1, :] + result[16:17, :] + result[32:33, :]

    for part in range(2):
        part_cols = slice(part * wide_part, (part + 1) * wide_part)

        @pl.loop(0, 2)
        def _(i):
            rows = tile(i, middle_q)
            upstream = grads[pl.ds(4 * i, 4)].reshape(middle_q, width)
            grad = contract(upstream, wd[part_cols, :], 1, 1) * slope[rows, part_cols].astype(F32)
            slope[rows, part_cols] = grad.astype(BF16)

        pooled_part(part_cols)

    after("gact")

    for i in range(SEQ):
        swap_copy(i, part_ss, part_rs).wait_send()
    swap_out(contract(blocks_of(slope, 1 - core), wi[...], 1, 1), gn2_ss, gn2_rs)
    gn[...] = contract(blocks_of(slope, core), wi[...], 1, 1).reshape(SEQ, BLK, width)
    after("gn")
    for part in range(2):
        part_cols = slice(part * wide_part, (part + 1) * wide_part)

        @pl.loop(0, width // (2 * BLK))
        def _(i):
            wi[tile(i, 2 * BLK), part_cols] = contract(
                nrm2[:, tile(i, 2 * BLK)], slope[:, part_cols], 0, 0
            ).astype(BF16)

        after(f"gin{part}")
    def pool_each(action):
        for to in range(SEQ):
            own = (chip == to) & (core == row)
            dst = pool_recv.at[col * 2 + core]
            copy = remote(pp, dst, pool_ss.at[to], pool_rs.at[col * 2 + core], (depth * 2 + row, to))
            if action == "start":

                @pl.when(own)
                def _():
                    pltpu.make_async_copy(pp, dst, pool_rs.at[col * 2 + core]).start()

            @pl.when(jnp.logical_not(own))
            def _():
                if action == "start":
                    copy.start()
                else:
                    copy.wait_send()

    def gat_copy(i):
        block = act.at[tile(2 * i + core, BLK), pl.ds(0, width)]
        return remote(block, block, gat_ss.at[i], gat_rs.at[i], other)

    for i in range(SEQ):
        n2_copy(i, n2_ss, n2_rs).wait_send()
    sg[...] = jnp.zeros_like(sg)

    def add_gain(first, value):
        for i in range(width // BLK):
            sg[first + i : first + i + 1, :] += value[:, i * BLK : (i + 1) * BLK]

    @pl.loop(0, SEQ)
    def _(i):
        b = 2 * i + core
        swap_copy(i, gn2_ss, gn2_rs).wait_recv()
        normed = gn[i] + precv[i].astype(F32)
        hidden = hid[i]
        scale = lax.rsqrt(jnp.mean(hidden * hidden, -1, keepdims=True) + EPS)
        add_gain(8, jnp.sum(normed * hidden * scale, 0, keepdims=True))
        scaled = normed * gains[1:2, :]
        inner = jnp.mean(scaled * hidden, -1, keepdims=True)
        result = grads[b].astype(F32) + scale * scaled - hidden * (scale * scale * scale) * inner
        hid[i] = result
        act[tile(b, BLK), 0:width] = result.astype(BF16)
        gat_copy(i).start()

    pool_each("start")
    after("n2")
    for i in range(SEQ):
        gat_copy(i).wait_recv()

    @pl.loop(0, 2)
    def _(i):
        rows = tile(i, middle_q)
        inverse = jnp.concatenate(
            [
                jnp.transpose(
                    jnp.concatenate(
                        [
                            jnp.broadcast_to(gscale[2 * p + h : 2 * p + h + 1, rows], (64, middle_q))
                            for h in range(2)
                        ],
                        axis=0,
                    )
                )
                for p in range(3)
            ],
            axis=1,
        )
        gmix[rows, :] = (contract(act[rows, 0:width], wo[...], 1, 1) * inverse).astype(BF16)

    wo[...] = contract(mixed[...], act[:, 0:width], 0, 0).astype(BF16)
    for i in range(SEQ):
        gat_copy(i).wait_send()
    for qb in range(2):
        fetch(0, qb).start()
    after("op")


    sub = lax.broadcasted_iota(jnp.int32, (16, tokens), 0)
    key_block = lax.div(lax.broadcasted_iota(jnp.int32, (16, tokens), 1), BLK)
    flip[BLK : BLK + 16, :] = (sub == key_block).astype(BF16)
    near[...] = jnp.zeros_like(near)
    far[...] = jnp.zeros_like(far)

    backward_table = {i: [lambda i=i: after(f"u{i}")] for i in range(6)}

    @pl.loop(0, 3)
    def _(pair):
        cols = tile(pair, BLK)
        flip[0:BLK, :] = jnp.transpose(qkv[:, tile(3 * pair + 1, BLK)])
        for qb in range(2):
            rows = pl.ds(qb * middle_q, middle_q)
            upstream = gmix[rows, cols]
            masked = by_head(upstream)
            queries = by_head(qkv[rows, tile(3 * pair, BLK)])
            product = jnp.transpose(upstream.astype(F32) * mixed[rows, cols].astype(F32))
            inner = jnp.concatenate(
                [jnp.sum(product[64 * h : 64 * h + 64, :], 0, keepdims=True) for h in range(2)],
                axis=1,
            )
            fetch(pair, qb).wait()
            raised = slots[qb][...]
            grad_probs = contract(qkv[:, tile(3 * pair + 2, BLK)], masked, 1, 1)
            grad_logits = (raised.astype(F32) * (grad_probs - inner)).astype(BF16)
            grad_values = contract(raised, masked, 1, 0)
            grad_keys = contract(grad_logits, queries, 1, 0)
            if qb == 0:
                dv_acc[...] = grad_values
                dk_acc[...] = grad_keys
            else:
                dv_acc[...] += grad_values
                dk_acc[...] += grad_keys
            result = contract(flip[...], grad_logits, 1, 0)
            dqkv[rows, tile(3 * pair, BLK)] = jnp.transpose(
                jnp.concatenate([result[0:64, 0:middle_q], result[64:BLK, middle_q:]], axis=0)
            ).astype(BF16)
            sums = result[BLK : BLK + 8, :]
            block_row = lax.broadcasted_iota(jnp.int32, sums.shape, 0)
            block_col = lax.rem(
                lax.div(lax.broadcasted_iota(jnp.int32, sums.shape, 1), BLK), middle_q // BLK
            )
            gap = block_row - block_col - qb * (middle_q // BLK)
            far[pair, 0] += jnp.where(gap <= -2, sums, 0.0)
            far[pair, 1] += jnp.where(gap >= 2, sums, 0.0)
            for h in range(2):
                for off in range(3):
                    total = near[(pair * 2 + h) * 3 + off]
                    for i in range(middle_q // BLK):
                        kb = qb * (middle_q // BLK) + i + off - 1
                        if 0 <= kb < tokens // BLK:
                            first = h * middle_q + i * BLK
                            total = total + grad_logits[
                                kb * BLK : (kb + 1) * BLK, first : first + BLK
                            ].astype(F32)
                    near[(pair * 2 + h) * 3 + off] = total

            @pl.when(pair < 2)
            def _():
                fetch(pair + 1, qb).start()

            if qb == 1:
                dqkv[:, tile(3 * pair + 1, BLK)] = dk_acc[...].astype(BF16)
                dqkv[:, tile(3 * pair + 2, BLK)] = dv_acc[...].astype(BF16)
                right = dqkv[:, tile(pair, pair_w)]

                @pl.loop(0, width // middle_w)
                def _(i):
                    gqkv[pair, tile(i, middle_w), :] = contract(
                        nrm1[:, tile(i, middle_w)], right, 0, 0
                    ).astype(BF16)

            serve(2 * pair + qb, backward_table)

    for i in range(SEQ):
        swap_copy(i, gn2_ss, gn2_rs).wait_send()

    swap_out(contract(blocks_of(dqkv, 1 - core), wqkv[...], 1, 1), gn1_ss, gn1_rs)
    diag_row = lax.broadcasted_iota(jnp.int32, (BLK, BLK), 0)
    diag_col = lax.broadcasted_iota(jnp.int32, (BLK, BLK), 1)
    upper = diag_col >= diag_row
    mirror = (diag_row + diag_col == BLK - 1).astype(F32)
    shift = lax.broadcasted_iota(jnp.int32, (1, BLK), 1) + 1
    shift = jnp.where(shift == BLK, 0, shift)
    ids = bucket_of(jnp.concatenate([-shift, BLK - shift], axis=1))
    onehot = (lax.broadcasted_iota(jnp.int32, (BLK, 2 * BLK), 0) == ids).astype(F32)

    def bias_head(h):
        def skew(x):
            return pltpu.roll(exact(mirror, x, 1, 0), 0, 1, stride=1, stride_axis=0)

        def far_of(h, side):
            both = far[lax.div(h, 2), side]
            return jnp.where(lax.rem(h, 2) == 0, both[:, 0:middle_q], both[:, middle_q:])

        tiles = [near[h * 3 + i] for i in range(3)]
        at = [
            jnp.sum(
                skew(jnp.where(upper, tiles[i + 1], 0.0) + jnp.where(upper, 0.0, tiles[i])),
                0,
                keepdims=True,
            )
            for i in range(2)
        ]
        below = full_sum(jnp.where(upper, tiles[0], 0.0)) + full_sum(far_of(h, 0))
        above = full_sum(jnp.where(upper, 0.0, tiles[2])) + full_sum(far_of(h, 1))
        sums = exact(jnp.broadcast_to(jnp.concatenate(at, axis=1), (8, 2 * BLK)), onehot, 1, 1)
        sums = sums[0:1, :] + jnp.where(lane == 15, below, 0.0) + jnp.where(lane == 31, above, 0.0)
        sg[pl.ds(16 + core * 6 + h, 1), :] = sums

    after("sw")

    @pl.loop(0, 3)
    def _(h):
        bias_head(h)

    after("b0")

    @pl.loop(3, 6)
    def _(h):
        bias_head(h)

    after("b1")
    both = contract(blocks_of(dqkv, core), wqkv[...], 1, 1)
    for i in range(SEQ):
        swap_copy(i, gn1_ss, gn1_rs).wait_recv()
        normed = both[i * BLK : (i + 1) * BLK, :] + precv[i].astype(F32)
        source = xown[i].astype(F32)
        scale = lax.rsqrt(jnp.mean(source * source, -1, keepdims=True) + EPS)
        add_gain(0, jnp.sum(normed * source * scale, 0, keepdims=True))
        scaled = normed * gains[0:1, :]
        inner = jnp.mean(scaled * source, -1, keepdims=True)
        result = hid[i] + scale * scaled - source * (scale * scale * scale) * inner
        nrm2[i * BLK : (i + 1) * BLK, :] = result.astype(BF16)

    place = core * SEQ + chip

    def sgp_each(action):
        for step in range(SEQ):
            for cross in range(2):
                if step == 0 and cross == 0:
                    continue
                to_core = lax.rem(core + cross, 2)
                copy = remote(
                    sg,
                    sg_plane.at[place],
                    sgp_ss.at[step * 2 + cross],
                    sgp_rs.at[place],
                    (depth * 2 + to_core, ahead(step)),
                )
                if action == "start":
                    copy.start()
                else:
                    copy.wait_send()

    sgp_each("start")
    pltpu.make_async_copy(sg, sg_plane.at[place], sgp_rs.at[place]).start()
    after("g1")
    after("end")
    for i in range(4):
        await_copy(pool_recv.at[i], pool_rs.at[i])
    for doc in range(2):
        pooled_o[doc : doc + 1, :] = (
            pool_recv[2 * doc, 0:1, :] + pool_recv[2 * doc + 1, 0:1, :]
        ) / own_lengths[:, doc : doc + 1]
    for step in range(1, DEPTH):
        z = lax.rem(depth + DEPTH - step, DEPTH)
        await_copy(sg_depth.at[z], sgz_rs.at[z])
    total = sg_depth[0] + sg_depth[1] + sg_depth[2] + sg_depth[3]
    for which in range(2):
        wide[which : which + 1, :] = jnp.concatenate(
            [total[8 * which + i : 8 * which + i + 1, :] for i in range(width // BLK)], axis=1
        )
    small_o[...] = pltpu.roll(wide[...], lax.rem(width - chip * rows_w, width), 1)[:, : small_o.shape[1]]
    turned[:, 0:16] = jnp.transpose(total[16:32, :])
    table_o[...] = turned[tile(chip, 8), :]

    for i in range(4):
        await_copy(gx_o.at[i // 2, pl.ds((i % 2) * BLK, BLK)], gx_rs.at[i])
    for copy in pending:
        copy.wait_send()
    spread(inputs, x_slot, x_ss, x_rs, "wait")
    spread(cotangent, c_slot, c_ss, c_rs, "wait")
    for it in qkv_items + down_items:
        it.sent()
    wo_each("wait")
    pool_each("wait")
    rso_each("wait")
    sgp_each("wait")
    for i in range(SEQ):
        n1_copy(i).wait_send()
        g_copy(i).wait_send()
        swap_copy(i, gn1_ss, gn1_rs).wait_send()
        gx_each(i, "wait")
    for step in range(1, DEPTH):
        sgz_copy(step).wait_send()
    for chunk in (*d_chunks, *i_chunks, o_chunk, *q_chunks):
        chunk.finish()


def widen_kernel(pooled, small, table, gx, gq, gk, gv, go, gi, gd, *outs):
    pooled_out, one_out, two_out, table_out, *outs = outs
    pooled_out[...] = pooled[...]
    one_out[...] = small[0:1, : one_out.shape[1]]
    two_out[...] = small[1:2, : two_out.shape[1]]
    table_out[...] = table[:, : table_out.shape[1]]
    for value, out in zip((gx, gq, gk, gv, go, gi, gd), outs):
        out[...] = value[...].astype(F32)


def on_device(
    inputs,
    w_query,
    w_key,
    w_value,
    w_out,
    w_ffn_in,
    w_ffn_out,
    attn_gain,
    ffn_gain,
    rel_bias,
    doc_lengths,
    cotangent,
):
    blocks, shard_len, width = inputs.shape
    heads = rel_bias.shape[1]
    head_dim = width // heads
    full_len = shard_len * lax.axis_size("seq")
    total_rows = blocks * shard_len
    gathered = (
        lax.all_gather(w_query, "seq", axis=0, tiled=True),
        lax.all_gather(w_key, "seq", axis=0, tiled=True),
        lax.all_gather(w_value, "seq", axis=0, tiled=True),
        lax.all_gather(w_out, "seq", axis=0, tiled=True),
        lax.all_gather(w_ffn_in, "seq", axis=0, tiled=True),
        lax.all_gather(w_ffn_out, "seq", axis=0, tiled=True),
        lax.all_gather(attn_gain, "seq", axis=0, tiled=True),
        lax.all_gather(ffn_gain, "seq", axis=0, tiled=True),
        lax.all_gather(rel_bias, "seq", axis=0, tiled=True),
    )
    (
        full_query,
        full_key,
        full_value,
        full_out,
        full_in,
        full_down,
        gain_one,
        gain_two,
        bias_table,
    ) = gathered
    gain_one = gain_one.astype(jnp.float32)
    gain_two = gain_two.astype(jnp.float32)
    bucket_range = jnp.arange(bias_table.shape[0], dtype=jnp.int32)
    query_pos = lax.axis_index("seq") * shard_len + jnp.arange(shard_len, dtype=jnp.int32)
    key_pos = jnp.arange(full_len, dtype=jnp.int32)
    onehot = (bucket_ids(query_pos, key_pos)[:, :, None] == bucket_range).astype(jnp.bfloat16)
    bias_heads = jnp.einsum("qkn,nh->hqk", onehot, bias_table, preferred_element_type=jnp.float32)
    key_valid = key_pos[None, :] < doc_lengths[:, None]
    query_valid = (query_pos[None, :] < doc_lengths[:, None]).astype(jnp.float32)
    flat = inputs.astype(jnp.float32).reshape(total_rows, width)
    scale_one = lax.rsqrt(jnp.mean(flat * flat, -1, keepdims=True) + EPS)
    normed_one = (flat * scale_one * gain_one).astype(jnp.bfloat16)
    queries = jnp.dot(normed_one, full_query, preferred_element_type=jnp.float32).astype(
        jnp.bfloat16
    )
    keys_local = jnp.dot(normed_one, full_key, preferred_element_type=jnp.float32).astype(
        jnp.bfloat16
    )
    values_local = jnp.dot(normed_one, full_value, preferred_element_type=jnp.float32).astype(
        jnp.bfloat16
    )
    queries_heads = queries.reshape(blocks, shard_len, heads, head_dim)
    keys_all, values_all = (
        lax.all_gather(keys_local.reshape(blocks, shard_len, width), "seq", axis=1, tiled=True),
        lax.all_gather(values_local.reshape(blocks, shard_len, width), "seq", axis=1, tiled=True),
    )
    scores = jnp.einsum(
        "bqhe,bkhe->bhqk",
        queries_heads,
        keys_all.reshape(blocks, full_len, heads, head_dim),
        preferred_element_type=jnp.float32,
    )
    logits = jnp.where(key_valid[:, None, None, :], scores + bias_heads[None], NEGATIVE)
    highest = jnp.max(logits, -1, keepdims=True)
    log_total = highest + jnp.log(jnp.sum(jnp.exp(logits - highest), -1, keepdims=True))
    probs_low = jnp.exp(logits - log_total).astype(jnp.bfloat16)
    mixed = jnp.einsum(
        "bhqk,bkhe->bqhe",
        probs_low,
        values_all.reshape(blocks, full_len, heads, head_dim),
        preferred_element_type=jnp.float32,
    )
    mixed = mixed.astype(jnp.bfloat16).reshape(total_rows, width)
    hidden = flat + jnp.dot(mixed, full_out, preferred_element_type=jnp.float32)
    scale_two = lax.rsqrt(jnp.mean(hidden * hidden, -1, keepdims=True) + EPS)
    normed_two = (hidden * scale_two * gain_two).astype(jnp.bfloat16)
    pre_act = jnp.dot(normed_two, full_in, preferred_element_type=jnp.float32)
    active = jax.nn.gelu(pre_act, approximate=True).astype(jnp.bfloat16)
    outputs = hidden + jnp.dot(active, full_down, preferred_element_type=jnp.float32)
    partial_pool = jnp.sum(outputs.reshape(blocks, shard_len, width) * query_valid[:, :, None], 1)
    pooled = lax.psum(partial_pool, "seq") / doc_lengths[:, None].astype(jnp.float32)
    regathered = (
        lax.all_gather(w_query, "seq", axis=0, tiled=True),
        lax.all_gather(w_key, "seq", axis=0, tiled=True),
        lax.all_gather(w_value, "seq", axis=0, tiled=True),
        lax.all_gather(w_out, "seq", axis=0, tiled=True),
        lax.all_gather(w_ffn_in, "seq", axis=0, tiled=True),
        lax.all_gather(w_ffn_out, "seq", axis=0, tiled=True),
        lax.all_gather(attn_gain, "seq", axis=0, tiled=True),
        lax.all_gather(ffn_gain, "seq", axis=0, tiled=True),
    )
    full_query, full_key, full_value, full_out, full_in, full_down, gain_back_one, gain_back_two = (
        regathered
    )
    gain_one = gain_back_one.astype(jnp.float32)
    gain_two = gain_back_two.astype(jnp.float32)
    grad_out = (cotangent.astype(jnp.float32) * query_valid[:, :, None]).reshape(total_rows, width)
    grad_branch = grad_out.astype(jnp.bfloat16)
    grad_down = outer_sum(active, grad_branch)
    grad_pre = (back_project(grad_branch, full_down) * gelu_slope(pre_act)).astype(jnp.bfloat16)
    grad_in = outer_sum(normed_two, grad_pre)
    grad_normed_two = back_project(grad_pre, full_in)
    grad_gain_two, grad_hidden_norm = norm_backward(hidden, scale_two, gain_two, grad_normed_two)
    grad_hidden = grad_out + grad_hidden_norm
    grad_attended = grad_hidden.astype(jnp.bfloat16)
    grad_out_proj = outer_sum(mixed, grad_attended)
    grad_mixed = (
        back_project(grad_attended, full_out)
        .astype(jnp.bfloat16)
        .reshape(blocks, shard_len, heads, head_dim)
    )
    keys_back, values_back = (keys_all, values_all)
    probs = jnp.exp(logits - log_total)
    grad_probs = jnp.einsum(
        "bqhe,bkhe->bhqk",
        grad_mixed,
        values_back.reshape(blocks, full_len, heads, head_dim),
        preferred_element_type=jnp.float32,
    )
    inner_term = jnp.sum(probs * grad_probs, -1, keepdims=True)
    grad_logits = (probs * (grad_probs - inner_term)).astype(jnp.bfloat16)
    grad_queries = jnp.einsum(
        "bhqk,bkhe->bqhe",
        grad_logits,
        keys_back.reshape(blocks, full_len, heads, head_dim),
        preferred_element_type=jnp.float32,
    )
    grad_queries = grad_queries.astype(jnp.bfloat16).reshape(total_rows, width)
    grad_table = jnp.einsum("bhqk,qkn->nh", grad_logits, onehot, preferred_element_type=jnp.float32)
    key_terms = jnp.einsum(
        "bhqk,bqhe->bkhe", grad_logits, queries_heads, preferred_element_type=jnp.float32
    ).reshape(blocks, full_len, width)
    value_terms = jnp.einsum(
        "bhqk,bqhe->bkhe", probs_low, grad_mixed, preferred_element_type=jnp.float32
    ).reshape(blocks, full_len, width)
    grad_keys, grad_values = (
        lax.psum_scatter(
            key_terms.astype(jnp.bfloat16), "seq", scatter_dimension=1, tiled=True
        ).astype(jnp.float32),
        lax.psum_scatter(
            value_terms.astype(jnp.bfloat16), "seq", scatter_dimension=1, tiled=True
        ).astype(jnp.float32),
    )
    grad_keys = grad_keys.astype(jnp.bfloat16).reshape(total_rows, width)
    grad_values = grad_values.astype(jnp.bfloat16).reshape(total_rows, width)
    grad_query_w = outer_sum(normed_one, grad_queries)
    grad_key_w = outer_sum(normed_one, grad_keys)
    grad_value_w = outer_sum(normed_one, grad_values)
    grad_normed_one = (
        back_project(grad_queries, full_query)
        + back_project(grad_keys, full_key)
        + back_project(grad_values, full_value)
    )
    grad_gain_one, grad_input_norm = norm_backward(flat, scale_one, gain_one, grad_normed_one)
    grad_input = (grad_hidden + grad_input_norm).reshape(blocks, shard_len, width)
    shards = (
        lax.psum_scatter(
            grad_query_w.astype(jnp.bfloat16), "seq", scatter_dimension=0, tiled=True
        ).astype(jnp.float32),
        lax.psum_scatter(
            grad_key_w.astype(jnp.bfloat16), "seq", scatter_dimension=0, tiled=True
        ).astype(jnp.float32),
        lax.psum_scatter(
            grad_value_w.astype(jnp.bfloat16), "seq", scatter_dimension=0, tiled=True
        ).astype(jnp.float32),
        lax.psum_scatter(
            grad_out_proj.astype(jnp.bfloat16), "seq", scatter_dimension=0, tiled=True
        ).astype(jnp.float32),
        lax.psum_scatter(
            grad_in.astype(jnp.bfloat16), "seq", scatter_dimension=0, tiled=True
        ).astype(jnp.float32),
        lax.psum_scatter(
            grad_down.astype(jnp.bfloat16), "seq", scatter_dimension=0, tiled=True
        ).astype(jnp.float32),
        lax.psum_scatter(
            grad_gain_one.astype(jnp.bfloat16), "seq", scatter_dimension=0, tiled=True
        ).astype(jnp.float32),
        lax.psum_scatter(
            grad_gain_two.astype(jnp.bfloat16), "seq", scatter_dimension=0, tiled=True
        ).astype(jnp.float32),
        lax.psum_scatter(
            grad_table.astype(jnp.bfloat16), "seq", scatter_dimension=0, tiled=True
        ).astype(jnp.float32),
    )
    totals = (
        lax.psum(shards[0].astype(jnp.bfloat16), "dp").astype(jnp.float32),
        lax.psum(shards[1].astype(jnp.bfloat16), "dp").astype(jnp.float32),
        lax.psum(shards[2].astype(jnp.bfloat16), "dp").astype(jnp.float32),
        lax.psum(shards[3].astype(jnp.bfloat16), "dp").astype(jnp.float32),
        lax.psum(shards[4].astype(jnp.bfloat16), "dp").astype(jnp.float32),
        lax.psum(shards[5].astype(jnp.bfloat16), "dp").astype(jnp.float32),
        lax.psum(shards[6].astype(jnp.bfloat16), "dp").astype(jnp.float32),
        lax.psum(shards[7].astype(jnp.bfloat16), "dp").astype(jnp.float32),
        lax.psum(shards[8].astype(jnp.bfloat16), "dp").astype(jnp.float32),
    )
    return (
        pooled,
        grad_input,
        totals[0],
        totals[1],
        totals[2],
        totals[3],
        totals[4],
        totals[5],
        totals[6],
        totals[7],
        totals[8],
    )


def fused_on_device(
    inputs,
    w_query,
    w_key,
    w_value,
    w_out,
    w_ffn_in,
    w_ffn_out,
    attn_gain,
    ffn_gain,
    rel_bias,
    doc_lengths,
    cotangent,
):
    docs, shard_len, width = inputs.shape
    rows_w, hidden_units = w_ffn_in.shape
    tokens = shard_len * SEQ
    half = width // 2
    part = hidden_units // (2 * SEQ)
    blocks = tokens // BLK
    pairs = half // BLK
    parts = part // BLK
    heads = rel_bias.shape[1]
    anywhere = pl.BlockSpec(memory_space=pl.ANY)
    vmem = pl.BlockSpec(memory_space=pltpu.VMEM)
    smem = pl.BlockSpec(memory_space=pltpu.SMEM)
    shape = jax.ShapeDtypeStruct
    narrow = [
        (docs, shard_len, width),
        (rows_w, width),
        (rows_w, width),
        (rows_w, width),
        (rows_w, width),
        (rows_w, hidden_units),
        (2 * part, width),
    ]
    out_shape = (
        shape((docs, width), F32),
        shape((8, 2 * BLK), F32),
        shape((8, BLK), F32),
        *(shape(s, BF16) for s in narrow),
        shape((2 * pairs, tokens, tokens), BF16),
    )
    out_part = rows_w // 2

    def sums(count, size, columns):
        return [((count, size // 2, columns), BF16)] * 2 + [((count, size, columns), BF16)] * 4

    scratch = [
        ((SEQ, BLK, width), BF16),
        ((blocks, BLK, width), BF16),
        ((tokens, width), BF16),
        ((width, 3 * half), BF16),
        ((tokens, 3 * half), BF16),
        ((tokens, half), BF16),
        ((half, width), BF16),
        ((SEQ, BLK, width), BF16),
        ((SEQ, BLK, width), BF16),
        ((SEQ, BLK, width), F32),
        ((tokens, width), BF16),
        ((width, SEQ * part), BF16),
        ((SEQ * part, width), BF16),
        ((tokens, SEQ * part), BF16),
        ((tokens, SEQ * part), BF16),
        ((SEQ, BLK, width), F32),
        ((2 * pairs, 5 * BLK, BLK), F32),
        ((3, 16, 2 * BLK), F32),
        ((tokens, BLK), BF16),
        ((8, tokens), F32),
        ((BLK + 16, tokens), BF16),
        ((tokens, 3 * half), BF16),
        ((tokens, half), BF16),
        ((tokens, BLK), F32),
        ((tokens, BLK), F32),
        ((6 * pairs, BLK, BLK), F32),
        ((pairs, 2, 8, tokens), F32),
        ((pairs, width, 3 * BLK), BF16),
        ((parts, SEQ, BLK, width), BF16),
        *sums(parts, BLK, width),
        *sums(SEQ, rows_w, part),
        *sums(pairs, rows_w, 3 * BLK),
        ((SEQ, out_part, width), BF16),
        ((out_part, width), BF16),
        ((out_part, width), BF16),
        ((SEQ + 1, 48, BLK), F32),
        ((8, width), F32),
        ((8, width), F32),
        ((8, SEQ * part), F32),
        ((8, width), F32),
        ((4, 8, width), F32),
        ((32, BLK), F32),
        ((8, 32, BLK), F32),
        ((4, 32, BLK), F32),
        ((BLK, BLK), F32),
    ]
    chunks = parts + SEQ + pairs + 1
    pair_of = lambda *dims: [pltpu.SemaphoreType.DMA(dims)] * 2
    semaphores = (
        pair_of(5)
        + pair_of(4)
        + pair_of(4)
        + pair_of(8, 8)
        + pair_of(4)
        + pair_of(4) * 8
        + pair_of(chunks, 6)
        + pair_of(4)
        + pair_of(chunks, 6)
        + pair_of(4)
        + pair_of(8)
        + pair_of(4)
        + [pltpu.SemaphoreType.DMA((chunks, 3))]
        + [pltpu.SemaphoreType.DMA((2,))]
    )
    results = pl.pallas_call(
        fused_kernel,
        out_shape=out_shape,
        in_specs=[anywhere] * 8 + [vmem, vmem, vmem, smem],
        out_specs=(vmem, vmem, vmem) + (anywhere,) * 8,
        scratch_shapes=[pltpu.VMEM(*s) for s in scratch] + semaphores,
        compiler_params=pltpu.CompilerParams(
            collective_id=0, has_side_effects=True, vmem_limit_bytes=VMEM_LIMIT
        ),
        name="block",
    )(
        inputs,
        cotangent,
        w_query,
        w_key,
        w_value,
        w_out,
        w_ffn_in,
        w_ffn_out,
        attn_gain,
        ffn_gain,
        rel_bias,
        doc_lengths,
    )

    steps = 4

    def rows_spec(s):
        if len(s) == 3:
            return pl.BlockSpec(
                (1, s[1] * s[0] // steps, s[2]),
                lambda i: (i // (steps // s[0]), i % (steps // s[0]), 0),
            )
        return pl.BlockSpec((s[0] // steps, s[1]), lambda i: (i, 0))

    def whole_spec(s):
        return pl.BlockSpec(s, lambda i: (0,) * len(s))

    tiny = [(docs, width), (1, rows_w), (1, rows_w), (8, heads)]
    pooled, one, two, table, gx, gq, gk, gv, go, gi, gd = pl.pallas_call(
        widen_kernel,
        out_shape=[shape(s, F32) for s in tiny + narrow],
        grid=(steps,),
        in_specs=[whole_spec(r.shape) for r in results[:3]] + [rows_spec(s) for s in narrow],
        out_specs=[whole_spec(s) for s in tiny] + [rows_spec(s) for s in narrow],
        compiler_params=pltpu.CompilerParams(vmem_limit_bytes=VMEM_LIMIT),
        name="widen",
    )(*results[:-1])
    return (pooled, gx, gq, gk, gv, go, gi, gd, one[0], two[0], table)


def fits(mesh):
    return mesh.shape["dp"] == CORES * DEPTH and mesh.shape["seq"] == SEQ


def solution(mesh):
    in_specs = (
        P("dp", "seq", None),
        P("seq", None),
        P("seq", None),
        P("seq", None),
        P("seq", None),
        P("seq", None),
        P("seq", None),
        P("seq"),
        P("seq"),
        P("seq", None),
        P("dp"),
        P("dp", "seq", None),
    )
    out_specs = (
        P("dp", None),
        P("dp", "seq", None),
        P("seq", None),
        P("seq", None),
        P("seq", None),
        P("seq", None),
        P("seq", None),
        P("seq", None),
        P("seq"),
        P("seq"),
        P("seq", None),
    )
    return jax.shard_map(
        fused_on_device if fits(mesh) else on_device, mesh=mesh, in_specs=in_specs, out_specs=out_specs, check_vma=False
    )
```

```python
import math

import jax
import jax.numpy as jnp
from jax import lax
from jax.experimental import pallas as pl
from jax.experimental.pallas import tpu as pltpu
from jax.sharding import PartitionSpec as P

EPS = 1e-06
THRESHOLDS = (12, 16, 23, 32, 46, 64, 91)
NEGATIVE = -1000000000.0
GELU_C = math.sqrt(2.0 / math.pi)
GELU_K = 0.044715


def bucket_ids(query_pos, key_pos):
    offset = key_pos[None, :] - query_pos[:, None]
    distance = jnp.abs(offset)
    upper = jnp.where(offset > 0, 16, 0).astype(jnp.int32)
    beyond = jnp.full(distance.shape, 8, jnp.int32)
    for threshold in THRESHOLDS:
        beyond = beyond + (distance >= threshold).astype(jnp.int32)
    return upper + jnp.where(distance < 8, distance, beyond)


def gelu_slope(value):
    inner = GELU_C * (value + GELU_K * value * value * value)
    tangent = jnp.tanh(inner)
    return 0.5 * (1.0 + tangent) + 0.5 * value * (1.0 - tangent * tangent) * GELU_C * (
        1.0 + 3.0 * GELU_K * value * value
    )


def outer_sum(left, right):
    return lax.dot_general(
        left, right, (((0,), (0,)), ((), ())), preferred_element_type=jnp.float32
    )


def back_project(grad, weight):
    return lax.dot_general(
        grad, weight, (((1,), (1,)), ((), ())), preferred_element_type=jnp.float32
    )


def norm_backward(source, scale, gain, grad_normed):
    grad_gain = jnp.sum(grad_normed * source * scale, 0)
    grad_scaled = grad_normed * gain
    grad_source = scale * grad_scaled - source * scale * scale * scale * jnp.mean(
        grad_scaled * source, -1, keepdims=True
    )
    return (grad_gain, grad_source)


SEQ, CORES, DEPTH = 4, 2, 4
BLK = 128
MESH = pl.DeviceIdType.MESH
F32 = jnp.float32
BF16 = jnp.bfloat16
VMEM_LIMIT = 60 << 20


def contract(left, right, left_dim, right_dim):
    return lax.dot_general(
        left, right, (((left_dim,), (right_dim,)), ((), ())), preferred_element_type=F32
    )


def exact(left, right, left_dim, right_dim):
    return lax.dot_general(
        left,
        right,
        (((left_dim,), (right_dim,)), ((), ())),
        preferred_element_type=F32,
        precision=lax.Precision.HIGHEST,
    )


def await_copy(ref, sem):
    pltpu.make_async_copy(ref, ref, sem).wait()


def tile(index, size):
    return pl.ds(pl.multiple_of(index * size, size), size)


def bucket_of(offset):
    distance = jnp.abs(offset)
    beyond = jnp.full(distance.shape, 8, jnp.int32)
    for threshold in THRESHOLDS:
        beyond = beyond + (distance >= threshold).astype(jnp.int32)
    return jnp.where(offset > 0, 16, 0) + jnp.where(distance < 8, distance, beyond)


STEPS = dict(s="start", m="middle", z1="z_one", z2="z_two", z3="z_three", z4="z_four")
SCHEDULE = {
    "gdn2": [("d2", "s"), ("d1", "s")],
    "wd": [],
    "gact": [("d2", "m")],
    "gn": [("d1", "m")],
    "gin0": [],
    "gin1": [("d0", "s")],
    "n2": [("i2", "s")],
    "op": [("d1", "z1"), ("d2", "z1"), ("d0", "m")],
    "u0": [("i3", "s")],
    "u1": [("d1", "z2"), ("i2", "m"), ("d2", "z2"), ("i3", "m"), ("d0", "z1"), ("i0", "s")],
    "u2": [("q0", "s"), ("d1", "z3"), ("d0", "z2"), ("i1", "s")],
    "u3": [("d2", "z3"), ("i3", "z1")],
    "u4": [("i0", "m"), ("d0", "z3"), ("q0", "m"), ("i3", "z2"), ("i2", "z1"), ("i1", "m")],
    "u5": [("i0", "z1"), ("i2", "z2"), ("q2", "s")],
    "sw": [],
    "b0": [("q0", "z1"), ("q1", "s"), ("i3", "z3"), ("i0", "z2"), ("i1", "z1"), ("q2", "m"), ("i2", "z3"), ("q0", "z2"), ("d0", "z4"), ("q1", "m"), ("o", "s")],
    "b1": [("d1", "z4"), ("i0", "z3"), ("i1", "z2"), ("q0", "z3"), ("q2", "z1")],
    "g1": [("i3", "z4"), ("q2", "z2"), ("i1", "z3"), ("q1", "z1"), ("i0", "z4"), ("o", "z1"), ("q0", "z4"), ("q1", "z2"), ("q2", "z3"), ("o", "z2"), ("i2", "z4"), ("q1", "z3"), ("gx", "s"), ("sm", "s"), ("q2", "z4"), ("d2", "z4"), ("q1", "z4"), ("i1", "z4"), ("o", "z3"), ("o", "z4")],
    "end": [],
}


def full_sum(value):
    return jnp.sum(jnp.sum(value, 0, keepdims=True), 1, keepdims=True)


def fused_kernel(
    inputs,
    cotangent,
    w_query,
    w_key,
    w_value,
    w_out,
    w_in,
    w_down,
    gain_one,
    gain_two,
    bias_in,
    lengths_in,
    pooled_o,
    small_o,
    table_o,
    gx_o,
    gq_o,
    gk_o,
    gv_o,
    go_o,
    gi_o,
    gd_o,
    raised_o,
    xown,
    grads,
    nrm1,
    wqkv,
    qkv,
    mixed,
    wo,
    psend,
    precv,
    hid,
    nrm2,
    wi,
    wd,
    act,
    slope,
    gn,
    strip,
    vecs,
    maskc,
    gscale,
    flip,
    dqkv,
    gmix,
    dk_acc,
    dv_acc,
    near,
    far,
    gqkv,
    gdn,
    d_dx,
    d_dy,
    d_rx,
    d_ry,
    d_za,
    d_zb,
    i_dx,
    i_dy,
    i_rx,
    i_ry,
    i_za,
    i_zb,
    q_dx,
    q_dy,
    q_rx,
    q_ry,
    q_za,
    q_zb,
    rs_o,
    o_za,
    o_zb,
    small_all,
    wide,
    gains,
    asum,
    pp,
    pool_recv,
    sg,
    sg_plane,
    sg_depth,
    turned,
    small_ss,
    small_rs,
    x_ss,
    x_rs,
    c_ss,
    c_rs,
    wg_ss,
    wg_rs,
    wo_ss,
    wo_rs,
    n1_ss,
    n1_rs,
    g_ss,
    g_rs,
    part_ss,
    part_rs,
    n2_ss,
    n2_rs,
    gn2_ss,
    gn2_rs,
    gat_ss,
    gat_rs,
    gn1_ss,
    gn1_rs,
    gx_ss,
    gx_rs,
    rs_ss,
    rs_rs,
    rso_ss,
    rso_rs,
    z_ss,
    z_rs,
    pool_ss,
    pool_rs,
    sgp_ss,
    sgp_rs,
    sgz_ss,
    sgz_rs,
    out_s,
    raised_s,
):
    dp = lax.axis_index("dp")
    chip = lax.axis_index("seq")
    depth, core = lax.div(dp, 2), lax.rem(dp, 2)
    row, col = lax.div(chip, 2), lax.rem(chip, 2)
    other = (depth * 2 + 1 - core, chip)
    xn = row * 2 + 1 - col
    yn = (1 - row) * 2 + col
    dn = (1 - row) * 2 + 1 - col
    tokens, width = nrm1.shape
    half = width // 2
    rows_w = w_query.shape[0]
    ff_part = gdn.shape[0] * BLK
    quarter, middle_q = tokens // 4, tokens // 2
    middle_w = width // 2

    def remote(src, dst, send, recv, device):
        return pltpu.make_async_remote_copy(
            src_ref=src,
            dst_ref=dst,
            send_sem=send,
            recv_sem=recv,
            device_id=device,
            device_id_type=MESH,
        )

    def ahead(step):
        return lax.rem(chip + step, SEQ)

    pending = []

    def send_now(*args):
        copy = remote(*args)
        copy.start()
        pending.append(copy)

    lane = lax.broadcasted_iota(jnp.int32, (1, BLK), 1)
    wide[...] = jnp.zeros_like(wide)
    wide[0:1, 0:rows_w] = gain_one[...].astype(F32).reshape(1, rows_w)
    wide[1:2, 0:rows_w] = gain_two[...].astype(F32).reshape(1, rows_w)
    turned_gains = pltpu.roll(wide[...], chip * rows_w, 1)
    small_all[0] = jnp.zeros_like(small_all[0])
    for which in range(2):
        for i in range(width // BLK):
            small_all[0, 8 * which + i : 8 * which + i + 1, :] = turned_gains[
                which : which + 1, i * BLK : (i + 1) * BLK
            ]
    small_all[0, 6:7, :] = jnp.where(
        lane == 0, lengths_in[0].astype(F32), lengths_in[1].astype(F32)
    )
    small_all[0, tile(2 + chip, 8), 0 : bias_in.shape[1]] = bias_in[...].astype(F32)

    barrier = pltpu.get_barrier_semaphore()
    for step in range(SEQ):
        if step:
            pl.semaphore_signal(barrier, inc=1, device_id=(dp, ahead(step)), device_id_type=MESH)
        pl.semaphore_signal(
            barrier, inc=1, device_id=(other[0], ahead(step)), device_id_type=MESH
        )
    for step in range(1, DEPTH):
        pl.semaphore_signal(
            barrier,
            inc=1,
            device_id=(lax.rem(depth + step, DEPTH) * 2 + core, chip),
            device_id_type=MESH,
        )
    pl.semaphore_wait(barrier, 2 * SEQ - 1 + DEPTH - 1)

    mine = small_all.at[0]
    for step in range(1, SEQ):
        send_now(
            mine, small_all.at[step], small_ss.at[step], small_rs.at[step], (dp, ahead(step))
        )
    send_now(mine, small_all.at[SEQ], small_ss.at[SEQ], small_rs.at[SEQ], other)

    def spread(source, dest_of, send, recv, action, halves=(0, 1)):
        for doc in (1 - col, col):
            for to in halves:
                block = source.at[doc, pl.ds(to * BLK, BLK)]
                target = core * 2 + doc
                own = (target == chip) & (core == to)
                copy = remote(
                    block,
                    dest_of(to),
                    send.at[doc * 2 + to],
                    recv.at[chip],
                    (depth * 2 + to, target),
                )
                if action == "start":

                    @pl.when(own)
                    def _():
                        pltpu.make_async_copy(block, dest_of(to), recv.at[chip]).start()

                @pl.when(jnp.logical_not(own))
                def _():
                    if action == "start":
                        copy.start()
                    else:
                        copy.wait_send()

    x_slot = lambda to: xown.at[chip]
    c_slot = lambda to: grads.at[chip * 2 + to]

    class Gather:
        def __init__(self, index, pieces, place):
            self.index, self.pieces, self.place = index, pieces, place
            self.bind()

        def half_of(self, owner, which):
            ref = self.place(owner)
            size = ref.shape[0] // 2
            return ref.at[pl.ds(which * size, size)]

        def bind(self):
            k = self.index
            self.local, self.one, self.two = [], [], []
            for src, cut in self.pieces:
                dst = cut(self.place(chip))
                self.local.append(pltpu.make_async_copy(src, dst, wg_rs.at[k, 0]))
                self.one.append(remote(src, dst, wg_ss.at[k, 0], wg_rs.at[k, 1], (dp, xn)))
                self.one.append(remote(src, dst, wg_ss.at[k, 1], wg_rs.at[k, 2], (dp, yn)))
            via_x, via_y = self.half_of(xn, 1), self.half_of(yn, 0)
            self.two = [
                remote(via_x, via_x, wg_ss.at[k, 2], wg_rs.at[k, 3], (dp, yn)),
                remote(via_y, via_y, wg_ss.at[k, 3], wg_rs.at[k, 4], (dp, xn)),
            ]
            self.from_x, self.from_y = self.place(xn), self.place(yn)
            self.last = [self.half_of(dn, 1), self.half_of(dn, 0)]
            self.own = self.place(chip)

        def first(self):
            for copy in self.local + self.one:
                copy.start()

        def second(self):
            k = self.index
            await_copy(self.from_x, wg_rs.at[k, 1])
            self.two[0].start()
            await_copy(self.from_y, wg_rs.at[k, 2])
            self.two[1].start()

        def done(self):
            k = self.index
            await_copy(self.own, wg_rs.at[k, 0])
            await_copy(self.last[0], wg_rs.at[k, 3])
            await_copy(self.last[1], wg_rs.at[k, 4])

        def sent(self):
            k = self.index
            for copy in self.two:
                copy.wait_send()
            await_copy(self.own, wg_ss.at[k, 0])
            await_copy(self.own, wg_ss.at[k, 1])

    class SharedGather(Gather):
        def part(self, owner, which):
            ref = self.place(owner)
            size = ref.shape[0] // 2
            return ref.at[tile(which, size)]

        def bind(self):
            k = self.index
            mine, theirs = lax.rem(depth, 2), 1 - lax.rem(depth, 2)
            beside = ((depth + theirs - mine) * 2 + core, chip)
            self.local, self.one = [], []
            for src, cut in self.pieces:
                size = src.shape[0] // 2
                self.local.append(
                    pltpu.make_async_copy(src, cut(self.place(chip)), wg_rs.at[k, 0])
                )
                dst = cut(self.part(chip, mine))
                src = src.at[tile(mine, size)]
                self.one.append(remote(src, dst, wg_ss.at[k, 0], wg_rs.at[k, 1], (dp, xn)))
                self.one.append(remote(src, dst, wg_ss.at[k, 1], wg_rs.at[k, 2], (dp, yn)))
            self.from_x, self.from_y = self.part(xn, mine), self.part(yn, mine)
            far = self.part(dn, mine)
            size = far.shape[0] // 2
            cut = lambda ref, which: ref.at[pl.ds(which * size, size)]
            via_x, via_y = cut(self.from_x, 1), cut(self.from_y, 0)
            self.last = [cut(far, 1), cut(far, 0)]
            self.two = [
                remote(via_x, via_x, wg_ss.at[k, 2], wg_rs.at[k, 3], (dp, yn)),
                remote(via_y, via_y, wg_ss.at[k, 3], wg_rs.at[k, 4], (dp, xn)),
            ]
            self.beside = [
                remote(ref, ref, wg_ss.at[k, 4 + n], wg_rs.at[k, 5 + n], beside)
                for n, ref in enumerate((self.from_x, self.from_y, far))
            ]
            self.own = self.place(chip)
            self.half = self.part(chip, mine)

        def second(self):
            super().second()
            self.show()

        def forward(self):
            super().second()

        def show(self):
            for copy in self.beside[:2]:
                copy.start()

        def third(self):
            k = self.index
            await_copy(self.last[0], wg_rs.at[k, 3])
            await_copy(self.last[1], wg_rs.at[k, 4])
            self.beside[2].start()

        def done(self):
            await_copy(self.own, wg_rs.at[self.index, 0])
            for copy in self.beside:
                copy.wait_recv()

        def sent(self):
            k = self.index
            for copy in self.two + self.beside:
                copy.wait_send()
            await_copy(self.half, wg_ss.at[k, 0])
            await_copy(self.half, wg_ss.at[k, 1])

    core_cols = tile(core, half)
    whole = lambda ref: ref
    pair_w = 3 * BLK

    def qkv_item(index, pair):
        return SharedGather(
            index,
            [
                (
                    w.at[:, tile(core * 3 + pair, BLK)],
                    lambda ref, i=i: ref.at[:, pl.ds(i * BLK, BLK)],
                )
                for i, w in enumerate((w_query, w_key, w_value))
            ],
            lambda owner: wqkv.at[tile(owner, rows_w), pl.ds(pair * pair_w, pair_w)],
        )

    def in_item(index, part):
        return SharedGather(
            index,
            [
                (
                    w_in.at[:, tile((2 * part + f) * 2 + core, ff_part)],
                    lambda ref, f=f: ref.at[:, pl.ds(f * ff_part, ff_part)],
                )
                for f in range(2)
            ],
            lambda owner: wi.at[tile(owner, rows_w), pl.ds(part * 2 * ff_part, 2 * ff_part)],
        )

    def down_item(kind, index, first, size):
        unit = ff_part // 4
        at = lambda base: pl.ds(pl.multiple_of(base + first * unit, unit), size * unit)
        return kind(
            index, [(w_down.at[at(core * ff_part)], whole)], lambda owner: wd.at[at(owner * ff_part)]
        )

    qkv_items = [qkv_item(i, i) for i in range(3)]
    in_items = [in_item(3, 0), in_item(4, 1)]
    down_items = [
        down_item(SharedGather, 5, 0, 2),
        down_item(Gather, 6, 2, 1),
        down_item(Gather, 7, 3, 1),
    ]
    for it in qkv_items:
        it.first()
    spread(inputs, x_slot, x_ss, x_rs, "start")

    wo_part = rows_w // 2
    wo_src = w_out.at[tile(core, wo_part)]
    wo_dst = wo.at[tile(col * 2 + core, wo_part)]

    def wo_each(action):
        for to in range(SEQ):
            own = (chip == to) & (core == row)
            copy = remote(
                wo_src, wo_dst, wo_ss.at[to], wo_rs.at[col * 2 + core], (depth * 2 + row, to)
            )
            if action == "start":

                @pl.when(own)
                def _():
                    pltpu.make_async_copy(wo_src, wo_dst, wo_rs.at[col * 2 + core]).start()

            @pl.when(jnp.logical_not(own))
            def _():
                if action == "start":
                    copy.start()
                else:
                    copy.wait_send()

    for step in range(1, SEQ + 1):
        await_copy(small_all.at[step], small_rs.at[step])
    summed = small_all[0] + small_all[1] + small_all[2] + small_all[3]
    for which in range(2):
        gains[which : which + 1, :] = jnp.concatenate(
            [summed[8 * which + i : 8 * which + i + 1, :] for i in range(width // BLK)], axis=1
        )
    length_row = jnp.where(row == core, small_all[0, 6:7, :], small_all[SEQ, 6:7, :])
    length = jnp.where(col == 0, length_row[:, 0:1], length_row[:, 1:2])
    own_lengths = small_all[0, 6:7, 0:2]
    table = summed[16:48, :].astype(BF16)
    lane_two = lax.broadcasted_iota(jnp.int32, (1, 2 * BLK), 1)
    minus = jnp.where(lane_two < BLK, lane_two, lane_two - 2 * BLK)
    for off in (-1, 0, 1):
        ids = bucket_of(off * BLK - minus)
        onehot = (lax.broadcasted_iota(jnp.int32, (32, 2 * BLK), 0) == ids).astype(BF16)
        vecs[off + 1] = contract(table, onehot, 0, 0)[0:16, :]

    @pl.loop(0, 6)
    def _(h):
        values = [vecs[i, pl.ds(core * 6 + h, 1), :] for i in range(3)]
        left = jnp.broadcast_to(values[0][:, BLK - 1 : BLK], (BLK, BLK))
        right = jnp.broadcast_to(values[2][:, BLK + 1 : BLK + 2], (BLK, BLK))
        strip[h, 0:BLK, :] = left
        strip[h, 4 * BLK :, :] = right
        for i in range(3):
            skewed = pltpu.roll(
                jnp.broadcast_to(values[i], (BLK, 2 * BLK)), 0, 1, stride=1, stride_axis=0
            )
            strip[h, (i + 1) * BLK : (i + 2) * BLK, :] = skewed[:, :BLK]

    key_pos = lax.broadcasted_iota(jnp.int32, maskc.shape, 0).astype(F32)
    maskc[...] = jnp.where((key_pos < length) | (lane > 0), 0.0, NEGATIVE).astype(BF16)

    def block_valid(b):
        pos = lax.broadcasted_iota(jnp.int32, (BLK, 1), 0) + b * BLK
        return (pos.astype(F32) < length).astype(F32)

    for it in qkv_items:
        it.second()

    def n1_copy(i):
        block = nrm1.at[tile(2 * i + core, BLK)]
        return remote(block, block, n1_ss.at[i], n1_rs.at[i], other)

    @pl.loop(0, SEQ)
    def _(i):
        await_copy(xown.at[i], x_rs.at[i])
        source = xown[i].astype(F32)
        scale = lax.rsqrt(jnp.mean(source * source, -1, keepdims=True) + EPS)
        nrm1[tile(2 * i + core, BLK), :] = (source * scale * gains[0:1, :]).astype(BF16)
        n1_copy(i).start()

    for it in in_items:
        it.first()
    for it in qkv_items:
        it.third()
    for i in range(SEQ):
        n1_copy(i).wait_recv()
    in_items[0].second()
    spread(cotangent, c_slot, c_ss, c_rs, "start", (0,))

    flip[BLK : BLK + 16, :] = jnp.ones((16, tokens), BF16)
    mine_lanes = [lane < 64, lane >= 64]
    slots = [ref.at[:, pl.ds(0, tokens)] for ref in (act, slope)]

    def by_head(value):
        return jnp.concatenate(
            [jnp.where(lanes, value, jnp.zeros_like(value)) for lanes in mine_lanes], axis=0
        )

    def serve(now, table):
        for when, actions in table.items():

            @pl.when(now == when)
            def _():
                for action in actions:
                    action()

    def keep(pair, qb):
        return pltpu.make_async_copy(slots[qb], raised_o.at[2 * pair + qb], raised_s.at[qb])

    def fetch(pair, qb):
        return pltpu.make_async_copy(raised_o.at[2 * pair + qb], slots[qb], raised_s.at[qb])

    def later_inputs():
        down_items[0].first()
        spread(cotangent, c_slot, c_ss, c_rs, "start", (1,))

    forward_table = {
        0: [in_items[1].second, lambda: wo_each("start")],
        1: [in_items[0].third, later_inputs],
        3: [in_items[1].third],
    }

    @pl.loop(0, 3)
    def _(pair):
        cols = tile(pair, BLK)
        for p in range(3):

            @pl.when(pair == p)
            def _():
                qkv_items[p].done()

        qkv[:, tile(pair, pair_w)] = contract(
            nrm1[...], wqkv[:, tile(pair, pair_w)], 1, 0
        ).astype(BF16)
        flip[0:BLK, :] = jnp.transpose(qkv[:, tile(3 * pair + 2, BLK)])
        keys = jnp.concatenate([qkv[:, tile(3 * pair + 1, BLK)], maskc[...]], axis=1)
        for qb in range(2):
            rows = pl.ds(qb * middle_q, middle_q)
            queries = by_head(qkv[rows, tile(3 * pair, BLK)])
            flag = jnp.broadcast_to(jnp.where(lane == 0, 1.0, 0.0).astype(BF16), queries.shape)
            biases = [
                jnp.concatenate(
                    [
                        strip[
                            pair * 2 + h, pl.ds((min(max(kb - q, -2), 2) + 2) * BLK, BLK), :
                        ]
                        for kb in range(tokens // BLK)
                    ],
                    axis=0,
                )
                for h in range(2)
                for q in range(qb * middle_q // BLK, (qb + 1) * middle_q // BLK)
            ]
            logits = contract(keys, jnp.concatenate([queries, flag], axis=1), 1, 1)
            logits = logits + jnp.concatenate(biases, axis=1)
            highest = jnp.max(logits, 0, keepdims=True)
            raised = jnp.exp(logits - highest).astype(BF16)

            @pl.when(pair > 0)
            def _():
                keep(pair - 1, qb).wait()

            slots[qb][...] = raised
            keep(pair, qb).start()
            result = contract(flip[...], raised, 1, 0)
            inverse = 1.0 / result[BLK : BLK + 1, :]
            scaled = result[0:BLK, :] * inverse
            mixed[rows, cols] = jnp.transpose(
                jnp.concatenate([scaled[0:64, 0:middle_q], scaled[64:BLK, middle_q:]], axis=0)
            ).astype(BF16)
            for h in range(2):
                gscale[pl.ds(2 * pair + h, 1), rows] = inverse[:, h * middle_q : (h + 1) * middle_q]
            serve(2 * pair + qb, forward_table)

    def swap_copy(i, send, recv):
        return remote(psend.at[i], precv.at[i], send.at[i], recv.at[i], other)

    for k in range(4):
        await_copy(wo.at[pl.ds(k * wo_part, wo_part)], wo_rs.at[k])

    def blocks_of(ref, parity):
        return jnp.concatenate(
            [ref[tile(2 * i + parity, BLK), :] for i in range(SEQ)], axis=0
        )

    def swap_out(result, send, recv):
        for i in range(SEQ):
            psend[i] = result[i * BLK : (i + 1) * BLK, :].astype(BF16)
            swap_copy(i, send, recv).start()

    swap_out(contract(blocks_of(mixed, 1 - core), wo[...], 1, 0), part_ss, part_rs)

    def n2_copy(i, send, recv):
        block = nrm2.at[tile(2 * i + core, BLK)]
        return remote(block, block, send.at[i], recv.at[i], other)

    pp[...] = jnp.zeros_like(pp)
    result = contract(blocks_of(mixed, core), wo[...], 1, 0)
    for i in range(SEQ):
        hidden = xown[i].astype(F32) + result[i * BLK : (i + 1) * BLK, :]
        swap_copy(i, part_ss, part_rs).wait_recv()
        hidden = hidden + precv[i].astype(F32)
        hid[i] = hidden
        scale = lax.rsqrt(jnp.mean(hidden * hidden, -1, keepdims=True) + EPS)
        nrm2[tile(2 * i + core, BLK), :] = (hidden * scale * gains[1:2, :]).astype(BF16)
        n2_copy(i, n2_ss, n2_rs).start()
        pp[0:1, :] += jnp.sum(hidden * block_valid(2 * i + core), 0, keepdims=True)
    down_items[0].second()
    for it in down_items[1:]:
        it.first()
    for i in range(SEQ):
        n2_copy(i, n2_ss, n2_rs).wait_recv()
    for qb in range(2):
        keep(2, qb).wait()

    def g_copy(i):
        block = grads.at[2 * i + core]
        return remote(block, block, g_ss.at[i], g_rs.at[i], other)

    def take_cotangent():
        @pl.loop(0, SEQ)
        def _(i):
            b = 2 * i + core
            await_copy(grads.at[b], c_rs.at[i])
            grads[b] = (grads[b].astype(F32) * block_valid(b)).astype(BF16)
            g_copy(i).start()

    asum[...] = jnp.zeros_like(asum)
    wide_part = 2 * ff_part
    for part in range(2):
        part_cols = slice(part * wide_part, (part + 1) * wide_part)
        if part == 1:
            take_cotangent()
            down_items[0].third()
        in_items[part].done()

        @pl.loop(0, 2)
        def _(i):
            rows = tile(i, middle_q)
            value = contract(nrm2[rows, :], wi[:, part_cols], 1, 0)
            square = value * value
            tangent = jnp.tanh(value * (GELU_C + GELU_C * GELU_K * square))
            half_up = 0.5 + 0.5 * tangent
            active = (value * half_up).astype(BF16)
            act[rows, part_cols] = active
            slope[rows, part_cols] = (
                half_up
                + value
                * (1.0 - tangent * tangent)
                * (0.5 * GELU_C + 1.5 * GELU_C * GELU_K * square)
            ).astype(BF16)
            pos = lax.broadcasted_iota(jnp.int32, (8, middle_q), 1) + i * middle_q
            valid = (pos.astype(F32) < length).astype(BF16)
            asum[:, part_cols] += contract(valid, active, 1, 0)


    for i in range(SEQ):
        g_copy(i).wait_recv()
    g_all = lambda: grads[...].reshape(tokens, width)

    class Chunk:
        made = 0

        def __init__(self, src, dx, dy, rx, ry, za, zb, outs):
            self.index = Chunk.made
            Chunk.made += 1
            self.src, self.dx, self.dy, self.rx, self.ry = src, dx, dy, rx, ry
            self.za, self.zb, self.outs = za, zb, outs
            self.bind()

        def bind(self):
            k = self.index
            size = self.dx.shape[0]
            cut = lambda ref, which: ref.at[pl.ds(which * size, size)]
            ss, rs = (lambda i: rs_ss.at[k, i]), (lambda i: rs_rs.at[k, i])
            to_x, to_y = (dp, xn), (dp, yn)
            self.one = [
                remote(cut(self.src(dn), 1), self.dx, ss(0), rs(0), to_x),
                remote(cut(self.src(dn), 0), self.dy, ss(1), rs(1), to_y),
                remote(cut(self.src(xn), 1), cut(self.rx, 1), ss(2), rs(2), to_x),
                remote(cut(self.src(yn), 0), cut(self.ry, 0), ss(3), rs(3), to_y),
            ]
            self.sum_y, self.sum_x = cut(self.src(yn), 1), cut(self.src(xn), 0)
            self.two = [
                remote(self.sum_y, cut(self.ry, 1), ss(4), rs(4), to_y),
                remote(self.sum_x, cut(self.rx, 0), ss(5), rs(5), to_x),
            ]
            self.bind_z(self.rx, self.ry)

        def bind_z(self, reduced, final):
            k = self.index
            self.reduced, self.final = reduced, final
            sem = lambda i: (z_ss.at[k, i], z_rs.at[k, i])
            self.to_inner = remote(reduced, self.za, *sem(0), z_dev(toward))
            self.swap = remote(reduced, self.zb, *sem(1), z_dev(across))
            self.to_end = remote(final, final, *sem(2), z_dev(outward))

        def start(self):
            for copy in self.one:
                copy.start()

        def middle(self):
            for at, sent, sums, copy in (
                (0, self.dx, self.sum_y, self.two[0]),
                (1, self.dy, self.sum_x, self.two[1]),
            ):
                self.one[at].wait_recv()
                sums[...] = (sums[...].astype(F32) + sent[...].astype(F32)).astype(BF16)
                copy.start()

        def total(self):
            for copy in (self.one[2], self.one[3], *self.two):
                copy.wait_recv()
            self.rx[...] = (
                self.src(chip)[...].astype(F32)
                + self.rx[...].astype(F32)
                + self.ry[...].astype(F32)
            ).astype(BF16)

        def z_one(self):
            self.total()

            @pl.when(end_z)
            def _():
                self.to_inner.start()

        def z_two(self):
            @pl.when(inner_z)
            def _():
                self.to_inner.wait_recv()
                self.reduced[...] = (
                    self.reduced[...].astype(F32) + self.za[...].astype(F32)
                ).astype(BF16)
                self.swap.start()

        def z_three(self):
            @pl.when(inner_z)
            def _():
                self.swap.wait_recv()
                self.final[...] = (
                    self.reduced[...].astype(F32) + self.zb[...].astype(F32)
                ).astype(BF16)
                self.to_end.start()

        def each_out(self, act_on):
            k = self.index
            for n, (cols, place) in enumerate(self.outs):
                src = self.final if cols is None else self.final.at[:, cols]
                act_on(
                    remote(src, place(core), z_ss.at[k, 3 + n], z_rs.at[k, 3 + n], other),
                    pltpu.make_async_copy(src, place(core), out_s.at[k, n]),
                )

        def z_four(self):
            @pl.when(end_z)
            def _():
                self.to_end.wait_recv()

            self.each_out(lambda there, here: (there.start(), here.start()))

        def finish(self):
            self.each_out(
                lambda there, here: (there.wait_recv(), there.wait_send(), here.wait())
            )

            @pl.when(end_z)
            def _():
                self.to_inner.wait_send()

            @pl.when(inner_z)
            def _():
                self.swap.wait_send()
                self.to_end.wait_send()

            for copy in self.plane_sends():
                copy.wait_send()

        def plane_sends(self):
            return self.one + self.two

    inner_z = (depth == 1) | (depth == 2)
    end_z = jnp.logical_not(inner_z)
    toward = jnp.where(depth == 0, 1, 2)
    outward = jnp.where(depth == 1, 0, 3)
    across = jnp.where(depth == 1, 2, 1)

    def z_dev(z):
        return (z * 2 + core, chip)

    d_chunks = [
        Chunk(
            lambda owner, i=i: gdn.at[i, owner],
            d_dx.at[i],
            d_dy.at[i],
            d_rx.at[i],
            d_ry.at[i],
            d_za.at[i],
            d_zb.at[i],
            [
                (
                    None,
                    lambda c, i=i: gd_o.at[
                        pl.ds(pl.multiple_of(c * ff_part + i * BLK, BLK), BLK)
                    ],
                )
            ],
        )
        for i in range(ff_part // BLK)
    ]

    i_chunks = [
        Chunk(
            lambda owner, f=f: wi.at[tile(owner, rows_w), pl.ds(f * ff_part, ff_part)],
            i_dx.at[f],
            i_dy.at[f],
            i_rx.at[f],
            i_ry.at[f],
            i_za.at[f],
            i_zb.at[f],
            [(None, lambda c, f=f: gi_o.at[:, tile(2 * f + c, ff_part)])],
        )
        for f in range(SEQ)
    ]
    q_chunks = [
        Chunk(
            lambda owner, p=p: gqkv.at[p, tile(owner, rows_w)],
            q_dx.at[p],
            q_dy.at[p],
            q_rx.at[p],
            q_ry.at[p],
            q_za.at[p],
            q_zb.at[p],
            [
                (
                    pl.ds(j * BLK, BLK),
                    lambda c, p=p, o=o: o.at[:, tile(c * 3 + p, BLK)],
                )
                for j, o in enumerate((gq_o, gk_o, gv_o))
            ],
        )
        for p in range(3)
    ]
    def rso_each(action):
        for k in range(2):
            for to in range(2):
                target = core * 2 + k
                own = (chip == target) & (core == to)
                src = wo.at[pl.ds((2 * k + to) * wo_part, wo_part)]
                dst = rs_o.at[chip]
                copy = remote(
                    src, dst, rso_ss.at[2 * k + to], rso_rs.at[chip], (depth * 2 + to, target)
                )
                if action == "start":

                    @pl.when(own)
                    def _():
                        pltpu.make_async_copy(src, dst, rso_rs.at[chip]).start()

                @pl.when(jnp.logical_not(own))
                def _():
                    if action == "start":
                        copy.start()
                    else:
                        copy.wait_send()

    class OutChunk(Chunk):
        def bind(self):
            self.bind_z(self.src.at[0], self.src.at[1])

        def total(self):
            for i in range(SEQ):
                await_copy(self.src.at[i], rso_rs.at[i])
            value = self.src[0].astype(F32)
            for i in range(1, SEQ):
                value = value + self.src[i].astype(F32)
            self.reduced[...] = value.astype(BF16)

        def plane_sends(self):
            return []

    o_chunk = OutChunk(
        rs_o, None, None, None, None, o_za, o_zb, [(None, lambda c: go_o.at[tile(c, wo_part)])]
    )
    def gx_each(i, action):
        own = (chip == i) & (core == row)
        dst = gx_o.at[col, tile(core, BLK)]
        copy = remote(
            nrm2.at[pl.ds(i * BLK, BLK)], dst, gx_ss.at[i], gx_rs.at[col * 2 + core], (depth * 2 + row, i)
        )
        if action == "start":

            @pl.when(own)
            def _():
                pltpu.make_async_copy(nrm2.at[pl.ds(i * BLK, BLK)], dst, gx_rs.at[col * 2 + core]).start()

        @pl.when(jnp.logical_not(own))
        def _():
            if action == "start":
                copy.start()
            else:
                copy.wait_send()

    def sgz_copy(step):
        return remote(
            sg_depth.at[depth],
            sg_depth.at[depth],
            sgz_ss.at[step],
            sgz_rs.at[depth],
            z_dev(lax.rem(depth + step, DEPTH)),
        )

    def small_along_z():
        for i in range(8):
            await_copy(sg_plane.at[i], sgp_rs.at[i])
        total = sg_plane[0]
        for i in range(1, 8):
            total = total + sg_plane[i]
        sg_depth[depth] = total
        for step in range(1, DEPTH):
            sgz_copy(step).start()

    by_name = dict(
        [(f"d{i}", c) for i, c in enumerate(d_chunks)]
        + [(f"i{i}", c) for i, c in enumerate(i_chunks)]
        + [(f"q{i}", c) for i, c in enumerate(q_chunks)]
        + [("o", o_chunk)]
    )

    def after(block):
        for name, step in SCHEDULE[block]:
            if name == "gx":
                for i in range(SEQ):
                    gx_each(i, "start")
            elif name == "sm":
                small_along_z()
            elif name == "o" and step == "s":
                rso_each("start")
            else:
                getattr(by_name[name], STEPS[step])()

    for it in down_items[1:]:
        it.second()
    for i in range(ff_part // BLK):
        columns = jnp.concatenate(
            [act[:, f * ff_part + i * BLK : f * ff_part + (i + 1) * BLK] for f in range(SEQ)],
            axis=1,
        )
        gdn[i] = contract(columns, g_all(), 0, 0).astype(BF16).reshape(SEQ, BLK, width)
    after("gdn2")
    for it in down_items:
        it.done()
    for it in in_items:
        it.sent()
    after("wd")

    def pooled_part(cols):
        total = asum[0:1, cols]
        high = total.astype(BF16)
        rest = total - high.astype(F32)
        middle = rest.astype(BF16)
        low = (rest - middle.astype(F32)).astype(BF16)
        pieces = jnp.concatenate(
            [jnp.broadcast_to(piece, (16, piece.shape[1])) for piece in (high, middle, low)], axis=0
        )
        result = contract(pieces, wd[cols, :], 1, 0)
        pp[0:1, :] += result[0:1, :] + result[16:17, :] + result[32:33, :]

    for part in range(2):
        part_cols = slice(part * wide_part, (part + 1) * wide_part)

        @pl.loop(0, 2)
        def _(i):
            rows = tile(i, middle_q)
            upstream = grads[pl.ds(4 * i, 4)].reshape(middle_q, width)
            grad = contract(upstream, wd[part_cols, :], 1, 1) * slope[rows, part_cols].astype(F32)
            slope[rows, part_cols] = grad.astype(BF16)

        pooled_part(part_cols)

    after("gact")

    for i in range(SEQ):
        swap_copy(i, part_ss, part_rs).wait_send()
    swap_out(contract(blocks_of(slope, 1 - core), wi[...], 1, 1), gn2_ss, gn2_rs)
    gn[...] = contract(blocks_of(slope, core), wi[...], 1, 1).reshape(SEQ, BLK, width)
    after("gn")
    for part in range(2):
        part_cols = slice(part * wide_part, (part + 1) * wide_part)

        @pl.loop(0, width // (2 * BLK))
        def _(i):
            wi[tile(i, 2 * BLK), part_cols] = contract(
                nrm2[:, tile(i, 2 * BLK)], slope[:, part_cols], 0, 0
            ).astype(BF16)

        after(f"gin{part}")
    def pool_each(action):
        for to in range(SEQ):
            own = (chip == to) & (core == row)
            dst = pool_recv.at[col * 2 + core]
            copy = remote(pp, dst, pool_ss.at[to], pool_rs.at[col * 2 + core], (depth * 2 + row, to))
            if action == "start":

                @pl.when(own)
                def _():
                    pltpu.make_async_copy(pp, dst, pool_rs.at[col * 2 + core]).start()

            @pl.when(jnp.logical_not(own))
            def _():
                if action == "start":
                    copy.start()
                else:
                    copy.wait_send()

    def gat_copy(i):
        block = act.at[tile(2 * i + core, BLK), pl.ds(0, width)]
        return remote(block, block, gat_ss.at[i], gat_rs.at[i], other)

    for i in range(SEQ):
        n2_copy(i, n2_ss, n2_rs).wait_send()
    sg[...] = jnp.zeros_like(sg)

    def add_gain(first, value):
        for i in range(width // BLK):
            sg[first + i : first + i + 1, :] += value[:, i * BLK : (i + 1) * BLK]

    @pl.loop(0, SEQ)
    def _(i):
        b = 2 * i + core
        swap_copy(i, gn2_ss, gn2_rs).wait_recv()
        normed = gn[i] + precv[i].astype(F32)
        hidden = hid[i]
        scale = lax.rsqrt(jnp.mean(hidden * hidden, -1, keepdims=True) + EPS)
        add_gain(8, jnp.sum(normed * hidden * scale, 0, keepdims=True))
        scaled = normed * gains[1:2, :]
        inner = jnp.mean(scaled * hidden, -1, keepdims=True)
        result = grads[b].astype(F32) + scale * scaled - hidden * (scale * scale * scale) * inner
        hid[i] = result
        act[tile(b, BLK), 0:width] = result.astype(BF16)
        gat_copy(i).start()

    pool_each("start")
    after("n2")
    for i in range(SEQ):
        gat_copy(i).wait_recv()

    @pl.loop(0, 2)
    def _(i):
        rows = tile(i, middle_q)
        inverse = jnp.concatenate(
            [
                jnp.transpose(
                    jnp.concatenate(
                        [
                            jnp.broadcast_to(gscale[2 * p + h : 2 * p + h + 1, rows], (64, middle_q))
                            for h in range(2)
                        ],
                        axis=0,
                    )
                )
                for p in range(3)
            ],
            axis=1,
        )
        gmix[rows, :] = (contract(act[rows, 0:width], wo[...], 1, 1) * inverse).astype(BF16)

    wo[...] = contract(mixed[...], act[:, 0:width], 0, 0).astype(BF16)
    for i in range(SEQ):
        gat_copy(i).wait_send()
    for qb in range(2):
        fetch(0, qb).start()
    after("op")


    sub = lax.broadcasted_iota(jnp.int32, (16, tokens), 0)
    key_block = lax.div(lax.broadcasted_iota(jnp.int32, (16, tokens), 1), BLK)
    flip[BLK : BLK + 16, :] = (sub == key_block).astype(BF16)
    near[...] = jnp.zeros_like(near)
    far[...] = jnp.zeros_like(far)

    backward_table = {i: [lambda i=i: after(f"u{i}")] for i in range(6)}

    @pl.loop(0, 3)
    def _(pair):
        cols = tile(pair, BLK)
        flip[0:BLK, :] = jnp.transpose(qkv[:, tile(3 * pair + 1, BLK)])
        for qb in range(2):
            rows = pl.ds(qb * middle_q, middle_q)
            upstream = gmix[rows, cols]
            masked = by_head(upstream)
            queries = by_head(qkv[rows, tile(3 * pair, BLK)])
            product = jnp.transpose(upstream.astype(F32) * mixed[rows, cols].astype(F32))
            inner = jnp.concatenate(
                [jnp.sum(product[64 * h : 64 * h + 64, :], 0, keepdims=True) for h in range(2)],
                axis=1,
            )
            fetch(pair, qb).wait()
            raised = slots[qb][...]
            grad_probs = contract(qkv[:, tile(3 * pair + 2, BLK)], masked, 1, 1)
            grad_logits = (raised.astype(F32) * (grad_probs - inner)).astype(BF16)
            grad_values = contract(raised, masked, 1, 0)
            grad_keys = contract(grad_logits, queries, 1, 0)
            if qb == 0:
                dv_acc[...] = grad_values
                dk_acc[...] = grad_keys
            else:
                dv_acc[...] += grad_values
                dk_acc[...] += grad_keys
            result = contract(flip[...], grad_logits, 1, 0)
            dqkv[rows, tile(3 * pair, BLK)] = jnp.transpose(
                jnp.concatenate([result[0:64, 0:middle_q], result[64:BLK, middle_q:]], axis=0)
            ).astype(BF16)
            sums = result[BLK : BLK + 8, :]
            block_row = lax.broadcasted_iota(jnp.int32, sums.shape, 0)
            block_col = lax.rem(
                lax.div(lax.broadcasted_iota(jnp.int32, sums.shape, 1), BLK), middle_q // BLK
            )
            gap = block_row - block_col - qb * (middle_q // BLK)
            far[pair, 0] += jnp.where(gap <= -2, sums, 0.0)
            far[pair, 1] += jnp.where(gap >= 2, sums, 0.0)
            for h in range(2):
                for off in range(3):
                    total = near[(pair * 2 + h) * 3 + off]
                    for i in range(middle_q // BLK):
                        kb = qb * (middle_q // BLK) + i + off - 1
                        if 0 <= kb < tokens // BLK:
                            first = h * middle_q + i * BLK
                            total = total + grad_logits[
                                kb * BLK : (kb + 1) * BLK, first : first + BLK
                            ].astype(F32)
                    near[(pair * 2 + h) * 3 + off] = total

            @pl.when(pair < 2)
            def _():
                fetch(pair + 1, qb).start()

            if qb == 1:
                dqkv[:, tile(3 * pair + 1, BLK)] = dk_acc[...].astype(BF16)
                dqkv[:, tile(3 * pair + 2, BLK)] = dv_acc[...].astype(BF16)
                right = dqkv[:, tile(pair, pair_w)]

                @pl.loop(0, width // middle_w)
                def _(i):
                    gqkv[pair, tile(i, middle_w), :] = contract(
                        nrm1[:, tile(i, middle_w)], right, 0, 0
                    ).astype(BF16)

            serve(2 * pair + qb, backward_table)

    for i in range(SEQ):
        swap_copy(i, gn2_ss, gn2_rs).wait_send()

    swap_out(contract(blocks_of(dqkv, 1 - core), wqkv[...], 1, 1), gn1_ss, gn1_rs)
    diag_row = lax.broadcasted_iota(jnp.int32, (BLK, BLK), 0)
    diag_col = lax.broadcasted_iota(jnp.int32, (BLK, BLK), 1)
    upper = diag_col >= diag_row
    mirror = (diag_row + diag_col == BLK - 1).astype(F32)
    shift = lax.broadcasted_iota(jnp.int32, (1, BLK), 1) + 1
    shift = jnp.where(shift == BLK, 0, shift)
    ids = bucket_of(jnp.concatenate([-shift, BLK - shift], axis=1))
    onehot = (lax.broadcasted_iota(jnp.int32, (BLK, 2 * BLK), 0) == ids).astype(F32)

    def bias_head(h):
        def skew(x):
            return pltpu.roll(exact(mirror, x, 1, 0), 0, 1, stride=1, stride_axis=0)

        def far_of(h, side):
            both = far[lax.div(h, 2), side]
            return jnp.where(lax.rem(h, 2) == 0, both[:, 0:middle_q], both[:, middle_q:])

        tiles = [near[h * 3 + i] for i in range(3)]
        at = [
            jnp.sum(
                skew(jnp.where(upper, tiles[i + 1], 0.0) + jnp.where(upper, 0.0, tiles[i])),
                0,
                keepdims=True,
            )
            for i in range(2)
        ]
        below = full_sum(jnp.where(upper, tiles[0], 0.0)) + full_sum(far_of(h, 0))
        above = full_sum(jnp.where(upper, 0.0, tiles[2])) + full_sum(far_of(h, 1))
        sums = exact(jnp.broadcast_to(jnp.concatenate(at, axis=1), (8, 2 * BLK)), onehot, 1, 1)
        sums = sums[0:1, :] + jnp.where(lane == 15, below, 0.0) + jnp.where(lane == 31, above, 0.0)
        sg[pl.ds(16 + core * 6 + h, 1), :] = sums

    after("sw")

    @pl.loop(0, 3)
    def _(h):
        bias_head(h)

    after("b0")

    @pl.loop(3, 6)
    def _(h):
        bias_head(h)

    after("b1")
    both = contract(blocks_of(dqkv, core), wqkv[...], 1, 1)
    for i in range(SEQ):
        swap_copy(i, gn1_ss, gn1_rs).wait_recv()
        normed = both[i * BLK : (i + 1) * BLK, :] + precv[i].astype(F32)
        source = xown[i].astype(F32)
        scale = lax.rsqrt(jnp.mean(source * source, -1, keepdims=True) + EPS)
        add_gain(0, jnp.sum(normed * source * scale, 0, keepdims=True))
        scaled = normed * gains[0:1, :]
        inner = jnp.mean(scaled * source, -1, keepdims=True)
        result = hid[i] + scale * scaled - source * (scale * scale * scale) * inner
        nrm2[i * BLK : (i + 1) * BLK, :] = result.astype(BF16)

    place = core * SEQ + chip

    def sgp_each(action):
        for step in range(SEQ):
            for cross in range(2):
                if step == 0 and cross == 0:
                    continue
                to_core = lax.rem(core + cross, 2)
                copy = remote(
                    sg,
                    sg_plane.at[place],
                    sgp_ss.at[step * 2 + cross],
                    sgp_rs.at[place],
                    (depth * 2 + to_core, ahead(step)),
                )
                if action == "start":
                    copy.start()
                else:
                    copy.wait_send()

    sgp_each("start")
    pltpu.make_async_copy(sg, sg_plane.at[place], sgp_rs.at[place]).start()
    for copy in pending:
        copy.wait_send()
    spread(inputs, x_slot, x_ss, x_rs, "wait")
    spread(cotangent, c_slot, c_ss, c_rs, "wait")
    for it in qkv_items + down_items:
        it.sent()
    wo_each("wait")
    after("g1")
    after("end")
    for i in range(4):
        await_copy(pool_recv.at[i], pool_rs.at[i])
    for doc in range(2):
        pooled_o[doc : doc + 1, :] = (
            pool_recv[2 * doc, 0:1, :] + pool_recv[2 * doc + 1, 0:1, :]
        ) / own_lengths[:, doc : doc + 1]
    for step in range(1, DEPTH):
        z = lax.rem(depth + DEPTH - step, DEPTH)
        await_copy(sg_depth.at[z], sgz_rs.at[z])
    total = sg_depth[0] + sg_depth[1] + sg_depth[2] + sg_depth[3]
    for which in range(2):
        wide[which : which + 1, :] = jnp.concatenate(
            [total[8 * which + i : 8 * which + i + 1, :] for i in range(width // BLK)], axis=1
        )
    small_o[...] = pltpu.roll(wide[...], lax.rem(width - chip * rows_w, width), 1)[:, : small_o.shape[1]]
    turned[:, 0:16] = jnp.transpose(total[16:32, :])
    table_o[...] = turned[tile(chip, 8), :]

    for i in range(4):
        await_copy(gx_o.at[i // 2, pl.ds((i % 2) * BLK, BLK)], gx_rs.at[i])
    pool_each("wait")
    rso_each("wait")
    sgp_each("wait")
    for i in range(SEQ):
        n1_copy(i).wait_send()
        g_copy(i).wait_send()
        swap_copy(i, gn1_ss, gn1_rs).wait_send()
        gx_each(i, "wait")
    for step in range(1, DEPTH):
        sgz_copy(step).wait_send()
    for chunk in (*d_chunks, *i_chunks, o_chunk, *q_chunks):
        chunk.finish()


def widen_kernel(pooled, small, table, gx, gq, gk, gv, go, gi, gd, *outs):
    pooled_out, one_out, two_out, table_out, *outs = outs
    pooled_out[...] = pooled[...]
    one_out[...] = small[0:1, : one_out.shape[1]]
    two_out[...] = small[1:2, : two_out.shape[1]]
    table_out[...] = table[:, : table_out.shape[1]]
    for value, out in zip((gx, gq, gk, gv, go, gi, gd), outs):
        out[...] = value[...].astype(F32)


def on_device(
    inputs,
    w_query,
    w_key,
    w_value,
    w_out,
    w_ffn_in,
    w_ffn_out,
    attn_gain,
    ffn_gain,
    rel_bias,
    doc_lengths,
    cotangent,
):
    blocks, shard_len, width = inputs.shape
    heads = rel_bias.shape[1]
    head_dim = width // heads
    full_len = shard_len * lax.axis_size("seq")
    total_rows = blocks * shard_len
    gathered = (
        lax.all_gather(w_query, "seq", axis=0, tiled=True),
        lax.all_gather(w_key, "seq", axis=0, tiled=True),
        lax.all_gather(w_value, "seq", axis=0, tiled=True),
        lax.all_gather(w_out, "seq", axis=0, tiled=True),
        lax.all_gather(w_ffn_in, "seq", axis=0, tiled=True),
        lax.all_gather(w_ffn_out, "seq", axis=0, tiled=True),
        lax.all_gather(attn_gain, "seq", axis=0, tiled=True),
        lax.all_gather(ffn_gain, "seq", axis=0, tiled=True),
        lax.all_gather(rel_bias, "seq", axis=0, tiled=True),
    )
    (
        full_query,
        full_key,
        full_value,
        full_out,
        full_in,
        full_down,
        gain_one,
        gain_two,
        bias_table,
    ) = gathered
    gain_one = gain_one.astype(jnp.float32)
    gain_two = gain_two.astype(jnp.float32)
    bucket_range = jnp.arange(bias_table.shape[0], dtype=jnp.int32)
    query_pos = lax.axis_index("seq") * shard_len + jnp.arange(shard_len, dtype=jnp.int32)
    key_pos = jnp.arange(full_len, dtype=jnp.int32)
    onehot = (bucket_ids(query_pos, key_pos)[:, :, None] == bucket_range).astype(jnp.bfloat16)
    bias_heads = jnp.einsum("qkn,nh->hqk", onehot, bias_table, preferred_element_type=jnp.float32)
    key_valid = key_pos[None, :] < doc_lengths[:, None]
    query_valid = (query_pos[None, :] < doc_lengths[:, None]).astype(jnp.float32)
    flat = inputs.astype(jnp.float32).reshape(total_rows, width)
    scale_one = lax.rsqrt(jnp.mean(flat * flat, -1, keepdims=True) + EPS)
    normed_one = (flat * scale_one * gain_one).astype(jnp.bfloat16)
    queries = jnp.dot(normed_one, full_query, preferred_element_type=jnp.float32).astype(
        jnp.bfloat16
    )
    keys_local = jnp.dot(normed_one, full_key, preferred_element_type=jnp.float32).astype(
        jnp.bfloat16
    )
    values_local = jnp.dot(normed_one, full_value, preferred_element_type=jnp.float32).astype(
        jnp.bfloat16
    )
    queries_heads = queries.reshape(blocks, shard_len, heads, head_dim)
    keys_all, values_all = (
        lax.all_gather(keys_local.reshape(blocks, shard_len, width), "seq", axis=1, tiled=True),
        lax.all_gather(values_local.reshape(blocks, shard_len, width), "seq", axis=1, tiled=True),
    )
    scores = jnp.einsum(
        "bqhe,bkhe->bhqk",
        queries_heads,
        keys_all.reshape(blocks, full_len, heads, head_dim),
        preferred_element_type=jnp.float32,
    )
    logits = jnp.where(key_valid[:, None, None, :], scores + bias_heads[None], NEGATIVE)
    highest = jnp.max(logits, -1, keepdims=True)
    log_total = highest + jnp.log(jnp.sum(jnp.exp(logits - highest), -1, keepdims=True))
    probs_low = jnp.exp(logits - log_total).astype(jnp.bfloat16)
    mixed = jnp.einsum(
        "bhqk,bkhe->bqhe",
        probs_low,
        values_all.reshape(blocks, full_len, heads, head_dim),
        preferred_element_type=jnp.float32,
    )
    mixed = mixed.astype(jnp.bfloat16).reshape(total_rows, width)
    hidden = flat + jnp.dot(mixed, full_out, preferred_element_type=jnp.float32)
    scale_two = lax.rsqrt(jnp.mean(hidden * hidden, -1, keepdims=True) + EPS)
    normed_two = (hidden * scale_two * gain_two).astype(jnp.bfloat16)
    pre_act = jnp.dot(normed_two, full_in, preferred_element_type=jnp.float32)
    active = jax.nn.gelu(pre_act, approximate=True).astype(jnp.bfloat16)
    outputs = hidden + jnp.dot(active, full_down, preferred_element_type=jnp.float32)
    partial_pool = jnp.sum(outputs.reshape(blocks, shard_len, width) * query_valid[:, :, None], 1)
    pooled = lax.psum(partial_pool, "seq") / doc_lengths[:, None].astype(jnp.float32)
    regathered = (
        lax.all_gather(w_query, "seq", axis=0, tiled=True),
        lax.all_gather(w_key, "seq", axis=0, tiled=True),
        lax.all_gather(w_value, "seq", axis=0, tiled=True),
        lax.all_gather(w_out, "seq", axis=0, tiled=True),
        lax.all_gather(w_ffn_in, "seq", axis=0, tiled=True),
        lax.all_gather(w_ffn_out, "seq", axis=0, tiled=True),
        lax.all_gather(attn_gain, "seq", axis=0, tiled=True),
        lax.all_gather(ffn_gain, "seq", axis=0, tiled=True),
    )
    full_query, full_key, full_value, full_out, full_in, full_down, gain_back_one, gain_back_two = (
        regathered
    )
    gain_one = gain_back_one.astype(jnp.float32)
    gain_two = gain_back_two.astype(jnp.float32)
    grad_out = (cotangent.astype(jnp.float32) * query_valid[:, :, None]).reshape(total_rows, width)
    grad_branch = grad_out.astype(jnp.bfloat16)
    grad_down = outer_sum(active, grad_branch)
    grad_pre = (back_project(grad_branch, full_down) * gelu_slope(pre_act)).astype(jnp.bfloat16)
    grad_in = outer_sum(normed_two, grad_pre)
    grad_normed_two = back_project(grad_pre, full_in)
    grad_gain_two, grad_hidden_norm = norm_backward(hidden, scale_two, gain_two, grad_normed_two)
    grad_hidden = grad_out + grad_hidden_norm
    grad_attended = grad_hidden.astype(jnp.bfloat16)
    grad_out_proj = outer_sum(mixed, grad_attended)
    grad_mixed = (
        back_project(grad_attended, full_out)
        .astype(jnp.bfloat16)
        .reshape(blocks, shard_len, heads, head_dim)
    )
    keys_back, values_back = (keys_all, values_all)
    probs = jnp.exp(logits - log_total)
    grad_probs = jnp.einsum(
        "bqhe,bkhe->bhqk",
        grad_mixed,
        values_back.reshape(blocks, full_len, heads, head_dim),
        preferred_element_type=jnp.float32,
    )
    inner_term = jnp.sum(probs * grad_probs, -1, keepdims=True)
    grad_logits = (probs * (grad_probs - inner_term)).astype(jnp.bfloat16)
    grad_queries = jnp.einsum(
        "bhqk,bkhe->bqhe",
        grad_logits,
        keys_back.reshape(blocks, full_len, heads, head_dim),
        preferred_element_type=jnp.float32,
    )
    grad_queries = grad_queries.astype(jnp.bfloat16).reshape(total_rows, width)
    grad_table = jnp.einsum("bhqk,qkn->nh", grad_logits, onehot, preferred_element_type=jnp.float32)
    key_terms = jnp.einsum(
        "bhqk,bqhe->bkhe", grad_logits, queries_heads, preferred_element_type=jnp.float32
    ).reshape(blocks, full_len, width)
    value_terms = jnp.einsum(
        "bhqk,bqhe->bkhe", probs_low, grad_mixed, preferred_element_type=jnp.float32
    ).reshape(blocks, full_len, width)
    grad_keys, grad_values = (
        lax.psum_scatter(
            key_terms.astype(jnp.bfloat16), "seq", scatter_dimension=1, tiled=True
        ).astype(jnp.float32),
        lax.psum_scatter(
            value_terms.astype(jnp.bfloat16), "seq", scatter_dimension=1, tiled=True
        ).astype(jnp.float32),
    )
    grad_keys = grad_keys.astype(jnp.bfloat16).reshape(total_rows, width)
    grad_values = grad_values.astype(jnp.bfloat16).reshape(total_rows, width)
    grad_query_w = outer_sum(normed_one, grad_queries)
    grad_key_w = outer_sum(normed_one, grad_keys)
    grad_value_w = outer_sum(normed_one, grad_values)
    grad_normed_one = (
        back_project(grad_queries, full_query)
        + back_project(grad_keys, full_key)
        + back_project(grad_values, full_value)
    )
    grad_gain_one, grad_input_norm = norm_backward(flat, scale_one, gain_one, grad_normed_one)
    grad_input = (grad_hidden + grad_input_norm).reshape(blocks, shard_len, width)
    shards = (
        lax.psum_scatter(
            grad_query_w.astype(jnp.bfloat16), "seq", scatter_dimension=0, tiled=True
        ).astype(jnp.float32),
        lax.psum_scatter(
            grad_key_w.astype(jnp.bfloat16), "seq", scatter_dimension=0, tiled=True
        ).astype(jnp.float32),
        lax.psum_scatter(
            grad_value_w.astype(jnp.bfloat16), "seq", scatter_dimension=0, tiled=True
        ).astype(jnp.float32),
        lax.psum_scatter(
            grad_out_proj.astype(jnp.bfloat16), "seq", scatter_dimension=0, tiled=True
        ).astype(jnp.float32),
        lax.psum_scatter(
            grad_in.astype(jnp.bfloat16), "seq", scatter_dimension=0, tiled=True
        ).astype(jnp.float32),
        lax.psum_scatter(
            grad_down.astype(jnp.bfloat16), "seq", scatter_dimension=0, tiled=True
        ).astype(jnp.float32),
        lax.psum_scatter(
            grad_gain_one.astype(jnp.bfloat16), "seq", scatter_dimension=0, tiled=True
        ).astype(jnp.float32),
        lax.psum_scatter(
            grad_gain_two.astype(jnp.bfloat16), "seq", scatter_dimension=0, tiled=True
        ).astype(jnp.float32),
        lax.psum_scatter(
            grad_table.astype(jnp.bfloat16), "seq", scatter_dimension=0, tiled=True
        ).astype(jnp.float32),
    )
    totals = (
        lax.psum(shards[0].astype(jnp.bfloat16), "dp").astype(jnp.float32),
        lax.psum(shards[1].astype(jnp.bfloat16), "dp").astype(jnp.float32),
        lax.psum(shards[2].astype(jnp.bfloat16), "dp").astype(jnp.float32),
        lax.psum(shards[3].astype(jnp.bfloat16), "dp").astype(jnp.float32),
        lax.psum(shards[4].astype(jnp.bfloat16), "dp").astype(jnp.float32),
        lax.psum(shards[5].astype(jnp.bfloat16), "dp").astype(jnp.float32),
        lax.psum(shards[6].astype(jnp.bfloat16), "dp").astype(jnp.float32),
        lax.psum(shards[7].astype(jnp.bfloat16), "dp").astype(jnp.float32),
        lax.psum(shards[8].astype(jnp.bfloat16), "dp").astype(jnp.float32),
    )
    return (
        pooled,
        grad_input,
        totals[0],
        totals[1],
        totals[2],
        totals[3],
        totals[4],
        totals[5],
        totals[6],
        totals[7],
        totals[8],
    )


def fused_on_device(
    inputs,
    w_query,
    w_key,
    w_value,
    w_out,
    w_ffn_in,
    w_ffn_out,
    attn_gain,
    ffn_gain,
    rel_bias,
    doc_lengths,
    cotangent,
):
    docs, shard_len, width = inputs.shape
    rows_w, hidden_units = w_ffn_in.shape
    tokens = shard_len * SEQ
    half = width // 2
    part = hidden_units // (2 * SEQ)
    blocks = tokens // BLK
    pairs = half // BLK
    parts = part // BLK
    heads = rel_bias.shape[1]
    anywhere = pl.BlockSpec(memory_space=pl.ANY)
    vmem = pl.BlockSpec(memory_space=pltpu.VMEM)
    smem = pl.BlockSpec(memory_space=pltpu.SMEM)
    shape = jax.ShapeDtypeStruct
    narrow = [
        (docs, shard_len, width),
        (rows_w, width),
        (rows_w, width),
        (rows_w, width),
        (rows_w, width),
        (rows_w, hidden_units),
        (2 * part, width),
    ]
    out_shape = (
        shape((docs, width), F32),
        shape((8, 2 * BLK), F32),
        shape((8, BLK), F32),
        *(shape(s, BF16) for s in narrow),
        shape((2 * pairs, tokens, tokens), BF16),
    )
    out_part = rows_w // 2

    def sums(count, size, columns):
        return [((count, size // 2, columns), BF16)] * 2 + [((count, size, columns), BF16)] * 4

    scratch = [
        ((SEQ, BLK, width), BF16),
        ((blocks, BLK, width), BF16),
        ((tokens, width), BF16),
        ((width, 3 * half), BF16),
        ((tokens, 3 * half), BF16),
        ((tokens, half), BF16),
        ((half, width), BF16),
        ((SEQ, BLK, width), BF16),
        ((SEQ, BLK, width), BF16),
        ((SEQ, BLK, width), F32),
        ((tokens, width), BF16),
        ((width, SEQ * part), BF16),
        ((SEQ * part, width), BF16),
        ((tokens, SEQ * part), BF16),
        ((tokens, SEQ * part), BF16),
        ((SEQ, BLK, width), F32),
        ((2 * pairs, 5 * BLK, BLK), F32),
        ((3, 16, 2 * BLK), F32),
        ((tokens, BLK), BF16),
        ((8, tokens), F32),
        ((BLK + 16, tokens), BF16),
        ((tokens, 3 * half), BF16),
        ((tokens, half), BF16),
        ((tokens, BLK), F32),
        ((tokens, BLK), F32),
        ((6 * pairs, BLK, BLK), F32),
        ((pairs, 2, 8, tokens), F32),
        ((pairs, width, 3 * BLK), BF16),
        ((parts, SEQ, BLK, width), BF16),
        *sums(parts, BLK, width),
        *sums(SEQ, rows_w, part),
        *sums(pairs, rows_w, 3 * BLK),
        ((SEQ, out_part, width), BF16),
        ((out_part, width), BF16),
        ((out_part, width), BF16),
        ((SEQ + 1, 48, BLK), F32),
        ((8, width), F32),
        ((8, width), F32),
        ((8, SEQ * part), F32),
        ((8, width), F32),
        ((4, 8, width), F32),
        ((32, BLK), F32),
        ((8, 32, BLK), F32),
        ((4, 32, BLK), F32),
        ((BLK, BLK), F32),
    ]
    chunks = parts + SEQ + pairs + 1
    pair_of = lambda *dims: [pltpu.SemaphoreType.DMA(dims)] * 2
    semaphores = (
        pair_of(5)
        + pair_of(4)
        + pair_of(4)
        + pair_of(8, 8)
        + pair_of(4)
        + pair_of(4) * 8
        + pair_of(chunks, 6)
        + pair_of(4)
        + pair_of(chunks, 6)
        + pair_of(4)
        + pair_of(8)
        + pair_of(4)
        + [pltpu.SemaphoreType.DMA((chunks, 3))]
        + [pltpu.SemaphoreType.DMA((2,))]
    )
    results = pl.pallas_call(
        fused_kernel,
        out_shape=out_shape,
        in_specs=[anywhere] * 8 + [vmem, vmem, vmem, smem],
        out_specs=(vmem, vmem, vmem) + (anywhere,) * 8,
        scratch_shapes=[pltpu.VMEM(*s) for s in scratch] + semaphores,
        compiler_params=pltpu.CompilerParams(
            collective_id=0, has_side_effects=True, vmem_limit_bytes=VMEM_LIMIT
        ),
        name="block",
    )(
        inputs,
        cotangent,
        w_query,
        w_key,
        w_value,
        w_out,
        w_ffn_in,
        w_ffn_out,
        attn_gain,
        ffn_gain,
        rel_bias,
        doc_lengths,
    )

    steps = 2

    def rows_spec(s):
        if len(s) == 3:
            return pl.BlockSpec(
                (1, s[1] * s[0] // steps, s[2]),
                lambda i: (i // (steps // s[0]), i % (steps // s[0]), 0),
            )
        return pl.BlockSpec((s[0] // steps, s[1]), lambda i: (i, 0))

    def whole_spec(s):
        return pl.BlockSpec(s, lambda i: (0,) * len(s))

    tiny = [(docs, width), (1, rows_w), (1, rows_w), (8, heads)]
    pooled, one, two, table, gx, gq, gk, gv, go, gi, gd = pl.pallas_call(
        widen_kernel,
        out_shape=[shape(s, F32) for s in tiny + narrow],
        grid=(steps,),
        in_specs=[whole_spec(r.shape) for r in results[:3]] + [rows_spec(s) for s in narrow],
        out_specs=[whole_spec(s) for s in tiny] + [rows_spec(s) for s in narrow],
        compiler_params=pltpu.CompilerParams(vmem_limit_bytes=VMEM_LIMIT),
        name="widen",
    )(*results[:-1])
    return (pooled, gx, gq, gk, gv, go, gi, gd, one[0], two[0], table)


def fits(mesh):
    return mesh.shape["dp"] == CORES * DEPTH and mesh.shape["seq"] == SEQ


def solution(mesh):
    in_specs = (
        P("dp", "seq", None),
        P("seq", None),
        P("seq", None),
        P("seq", None),
        P("seq", None),
        P("seq", None),
        P("seq", None),
        P("seq"),
        P("seq"),
        P("seq", None),
        P("dp"),
        P("dp", "seq", None),
    )
    out_specs = (
        P("dp", None),
        P("dp", "seq", None),
        P("seq", None),
        P("seq", None),
        P("seq", None),
        P("seq", None),
        P("seq", None),
        P("seq", None),
        P("seq"),
        P("seq"),
        P("seq", None),
    )
    return jax.shard_map(
        fused_on_device if fits(mesh) else on_device, mesh=mesh, in_specs=in_specs, out_specs=out_specs, check_vma=False
    )
```

```python
import math

import jax
import jax.numpy as jnp
from jax import lax
from jax.experimental import pallas as pl
from jax.experimental.pallas import tpu as pltpu
from jax.sharding import PartitionSpec as P

EPS = 1e-06
THRESHOLDS = (12, 16, 23, 32, 46, 64, 91)
NEGATIVE = -1000000000.0
GELU_C = math.sqrt(2.0 / math.pi)
GELU_K = 0.044715


def bucket_ids(query_pos, key_pos):
    offset = key_pos[None, :] - query_pos[:, None]
    distance = jnp.abs(offset)
    upper = jnp.where(offset > 0, 16, 0).astype(jnp.int32)
    beyond = jnp.full(distance.shape, 8, jnp.int32)
    for threshold in THRESHOLDS:
        beyond = beyond + (distance >= threshold).astype(jnp.int32)
    return upper + jnp.where(distance < 8, distance, beyond)


def gelu_slope(value):
    inner = GELU_C * (value + GELU_K * value * value * value)
    tangent = jnp.tanh(inner)
    return 0.5 * (1.0 + tangent) + 0.5 * value * (1.0 - tangent * tangent) * GELU_C * (
        1.0 + 3.0 * GELU_K * value * value
    )


def outer_sum(left, right):
    return lax.dot_general(
        left, right, (((0,), (0,)), ((), ())), preferred_element_type=jnp.float32
    )


def back_project(grad, weight):
    return lax.dot_general(
        grad, weight, (((1,), (1,)), ((), ())), preferred_element_type=jnp.float32
    )


def norm_backward(source, scale, gain, grad_normed):
    grad_gain = jnp.sum(grad_normed * source * scale, 0)
    grad_scaled = grad_normed * gain
    grad_source = scale * grad_scaled - source * scale * scale * scale * jnp.mean(
        grad_scaled * source, -1, keepdims=True
    )
    return (grad_gain, grad_source)


SEQ, CORES, DEPTH = 4, 2, 4
BLK = 128
MESH = pl.DeviceIdType.MESH
F32 = jnp.float32
BF16 = jnp.bfloat16
VMEM_LIMIT = 60 << 20


def contract(left, right, left_dim, right_dim):
    return lax.dot_general(
        left, right, (((left_dim,), (right_dim,)), ((), ())), preferred_element_type=F32
    )


def exact(left, right, left_dim, right_dim):
    return lax.dot_general(
        left,
        right,
        (((left_dim,), (right_dim,)), ((), ())),
        preferred_element_type=F32,
        precision=lax.Precision.HIGHEST,
    )


def await_copy(ref, sem):
    pltpu.make_async_copy(ref, ref, sem).wait()


def tile(index, size):
    return pl.ds(pl.multiple_of(index * size, size), size)


def bucket_of(offset):
    distance = jnp.abs(offset)
    beyond = jnp.full(distance.shape, 8, jnp.int32)
    for threshold in THRESHOLDS:
        beyond = beyond + (distance >= threshold).astype(jnp.int32)
    return jnp.where(offset > 0, 16, 0) + jnp.where(distance < 8, distance, beyond)


STEPS = dict(s="start", m="middle", z1="z_one", z2="z_two", z3="z_three", z4="z_four")
SCHEDULE = {
    "gdn2": [("d2", "s"), ("d1", "s")],
    "wd": [],
    "gact": [("d2", "m"), ("d0", "s")],
    "gn": [("d1", "m")],
    "gin0": [],
    "gin1": [],
    "n2": [("i2", "s")],
    "op": [("d1", "z1"), ("d2", "z1"), ("d0", "m")],
    "u0": [("i3", "s")],
    "u1": [("d1", "z2"), ("i2", "m"), ("d2", "z2"), ("i3", "m"), ("d0", "z1"), ("i0", "s")],
    "u2": [("q0", "s"), ("d1", "z3"), ("d0", "z2"), ("i1", "s")],
    "u3": [("d2", "z3"), ("i3", "z1")],
    "u4": [("i0", "m"), ("d0", "z3"), ("q0", "m"), ("i3", "z2"), ("i2", "z1"), ("i1", "m")],
    "u5": [("i0", "z1"), ("i2", "z2"), ("q2", "s")],
    "sw": [],
    "b0": [("q0", "z1"), ("q1", "s"), ("i3", "z3"), ("i0", "z2"), ("i1", "z1"), ("q2", "m"), ("i2", "z3"), ("q0", "z2"), ("d0", "z4"), ("q1", "m"), ("o", "s")],
    "b1": [("d1", "z4"), ("i0", "z3"), ("i1", "z2"), ("q0", "z3"), ("q2", "z1")],
    "g1": [("i3", "z4"), ("q2", "z2"), ("i1", "z3"), ("q1", "z1"), ("i0", "z4"), ("o", "z1"), ("q0", "z4"), ("q1", "z2"), ("q2", "z3"), ("o", "z2"), ("i2", "z4"), ("q1", "z3"), ("gx", "s"), ("sm", "s"), ("q2", "z4"), ("d2", "z4"), ("q1", "z4"), ("i1", "z4"), ("o", "z3"), ("o", "z4")],
    "end": [],
}


def full_sum(value):
    return jnp.sum(jnp.sum(value, 0, keepdims=True), 1, keepdims=True)


def fused_kernel(
    inputs,
    cotangent,
    w_query,
    w_key,
    w_value,
    w_out,
    w_in,
    w_down,
    gain_one,
    gain_two,
    bias_in,
    lengths_in,
    pooled_o,
    small_o,
    table_o,
    gx_o,
    gq_o,
    gk_o,
    gv_o,
    go_o,
    gi_o,
    gd_o,
    raised_o,
    xown,
    grads,
    nrm1,
    wqkv,
    qkv,
    mixed,
    wo,
    psend,
    precv,
    hid,
    nrm2,
    wi,
    wd,
    act,
    slope,
    gn,
    strip,
    vecs,
    maskc,
    gscale,
    flip,
    dqkv,
    gmix,
    dk_acc,
    dv_acc,
    near,
    far,
    gqkv,
    gdn,
    d_dx,
    d_dy,
    d_rx,
    d_ry,
    d_za,
    d_zb,
    i_dx,
    i_dy,
    i_rx,
    i_ry,
    i_za,
    i_zb,
    q_dx,
    q_dy,
    q_rx,
    q_ry,
    q_za,
    q_zb,
    rs_o,
    o_za,
    o_zb,
    small_all,
    wide,
    gains,
    asum,
    pp,
    pool_recv,
    sg,
    sg_plane,
    sg_depth,
    turned,
    small_ss,
    small_rs,
    x_ss,
    x_rs,
    c_ss,
    c_rs,
    wg_ss,
    wg_rs,
    wo_ss,
    wo_rs,
    n1_ss,
    n1_rs,
    g_ss,
    g_rs,
    part_ss,
    part_rs,
    n2_ss,
    n2_rs,
    gn2_ss,
    gn2_rs,
    gat_ss,
    gat_rs,
    gn1_ss,
    gn1_rs,
    gx_ss,
    gx_rs,
    rs_ss,
    rs_rs,
    rso_ss,
    rso_rs,
    z_ss,
    z_rs,
    pool_ss,
    pool_rs,
    sgp_ss,
    sgp_rs,
    sgz_ss,
    sgz_rs,
    out_s,
    raised_s,
):
    dp = lax.axis_index("dp")
    chip = lax.axis_index("seq")
    depth, core = lax.div(dp, 2), lax.rem(dp, 2)
    row, col = lax.div(chip, 2), lax.rem(chip, 2)
    other = (depth * 2 + 1 - core, chip)
    xn = row * 2 + 1 - col
    yn = (1 - row) * 2 + col
    dn = (1 - row) * 2 + 1 - col
    tokens, width = nrm1.shape
    half = width // 2
    rows_w = w_query.shape[0]
    ff_part = gdn.shape[0] * BLK
    quarter, middle_q = tokens // 4, tokens // 2
    middle_w = width // 2

    def remote(src, dst, send, recv, device):
        return pltpu.make_async_remote_copy(
            src_ref=src,
            dst_ref=dst,
            send_sem=send,
            recv_sem=recv,
            device_id=device,
            device_id_type=MESH,
        )

    def ahead(step):
        return lax.rem(chip + step, SEQ)

    pending = []

    def send_now(*args):
        copy = remote(*args)
        copy.start()
        pending.append(copy)

    lane = lax.broadcasted_iota(jnp.int32, (1, BLK), 1)
    wide[...] = jnp.zeros_like(wide)
    wide[0:1, 0:rows_w] = gain_one[...].astype(F32).reshape(1, rows_w)
    wide[1:2, 0:rows_w] = gain_two[...].astype(F32).reshape(1, rows_w)
    turned_gains = pltpu.roll(wide[...], chip * rows_w, 1)
    small_all[0] = jnp.zeros_like(small_all[0])
    for which in range(2):
        for i in range(width // BLK):
            small_all[0, 8 * which + i : 8 * which + i + 1, :] = turned_gains[
                which : which + 1, i * BLK : (i + 1) * BLK
            ]
    small_all[0, 6:7, :] = jnp.where(
        lane == 0, lengths_in[0].astype(F32), lengths_in[1].astype(F32)
    )
    small_all[0, tile(2 + chip, 8), 0 : bias_in.shape[1]] = bias_in[...].astype(F32)

    barrier = pltpu.get_barrier_semaphore()
    for step in range(SEQ):
        if step:
            pl.semaphore_signal(barrier, inc=1, device_id=(dp, ahead(step)), device_id_type=MESH)
        pl.semaphore_signal(
            barrier, inc=1, device_id=(other[0], ahead(step)), device_id_type=MESH
        )
    for step in range(1, DEPTH):
        pl.semaphore_signal(
            barrier,
            inc=1,
            device_id=(lax.rem(depth + step, DEPTH) * 2 + core, chip),
            device_id_type=MESH,
        )
    pl.semaphore_wait(barrier, 2 * SEQ - 1 + DEPTH - 1)

    mine = small_all.at[0]
    for step in range(1, SEQ):
        send_now(
            mine, small_all.at[step], small_ss.at[step], small_rs.at[step], (dp, ahead(step))
        )
    send_now(mine, small_all.at[SEQ], small_ss.at[SEQ], small_rs.at[SEQ], other)

    def spread(source, dest_of, send, recv, action, halves=(0, 1)):
        for doc in (1 - col, col):
            for to in halves:
                block = source.at[doc, pl.ds(to * BLK, BLK)]
                target = core * 2 + doc
                own = (target == chip) & (core == to)
                copy = remote(
                    block,
                    dest_of(to),
                    send.at[doc * 2 + to],
                    recv.at[chip],
                    (depth * 2 + to, target),
                )
                if action == "start":

                    @pl.when(own)
                    def _():
                        pltpu.make_async_copy(block, dest_of(to), recv.at[chip]).start()

                @pl.when(jnp.logical_not(own))
                def _():
                    if action == "start":
                        copy.start()
                    else:
                        copy.wait_send()

    x_slot = lambda to: xown.at[chip]
    c_slot = lambda to: grads.at[chip * 2 + to]

    class Gather:
        def __init__(self, index, pieces, place):
            self.index, self.pieces, self.place = index, pieces, place
            self.bind()

        def half_of(self, owner, which):
            ref = self.place(owner)
            size = ref.shape[0] // 2
            return ref.at[pl.ds(which * size, size)]

        def bind(self):
            k = self.index
            self.local, self.one, self.two = [], [], []
            for src, cut in self.pieces:
                dst = cut(self.place(chip))
                self.local.append(pltpu.make_async_copy(src, dst, wg_rs.at[k, 0]))
                self.one.append(remote(src, dst, wg_ss.at[k, 0], wg_rs.at[k, 1], (dp, xn)))
                self.one.append(remote(src, dst, wg_ss.at[k, 1], wg_rs.at[k, 2], (dp, yn)))
            via_x, via_y = self.half_of(xn, 1), self.half_of(yn, 0)
            self.two = [
                remote(via_x, via_x, wg_ss.at[k, 2], wg_rs.at[k, 3], (dp, yn)),
                remote(via_y, via_y, wg_ss.at[k, 3], wg_rs.at[k, 4], (dp, xn)),
            ]
            self.from_x, self.from_y = self.place(xn), self.place(yn)
            self.last = [self.half_of(dn, 1), self.half_of(dn, 0)]
            self.own = self.place(chip)

        def first(self):
            for copy in self.local + self.one:
                copy.start()

        def second(self):
            k = self.index
            await_copy(self.from_x, wg_rs.at[k, 1])
            self.two[0].start()
            await_copy(self.from_y, wg_rs.at[k, 2])
            self.two[1].start()

        def done(self):
            k = self.index
            await_copy(self.own, wg_rs.at[k, 0])
            await_copy(self.last[0], wg_rs.at[k, 3])
            await_copy(self.last[1], wg_rs.at[k, 4])

        def sent(self):
            k = self.index
            for copy in self.two:
                copy.wait_send()
            await_copy(self.own, wg_ss.at[k, 0])
            await_copy(self.own, wg_ss.at[k, 1])

    class SharedGather(Gather):
        def part(self, owner, which):
            ref = self.place(owner)
            size = ref.shape[0] // 2
            return ref.at[tile(which, size)]

        def bind(self):
            k = self.index
            mine, theirs = lax.rem(depth, 2), 1 - lax.rem(depth, 2)
            beside = ((depth + theirs - mine) * 2 + core, chip)
            self.local, self.one = [], []
            for src, cut in self.pieces:
                size = src.shape[0] // 2
                self.local.append(
                    pltpu.make_async_copy(src, cut(self.place(chip)), wg_rs.at[k, 0])
                )
                dst = cut(self.part(chip, mine))
                src = src.at[tile(mine, size)]
                self.one.append(remote(src, dst, wg_ss.at[k, 0], wg_rs.at[k, 1], (dp, xn)))
                self.one.append(remote(src, dst, wg_ss.at[k, 1], wg_rs.at[k, 2], (dp, yn)))
            self.from_x, self.from_y = self.part(xn, mine), self.part(yn, mine)
            far = self.part(dn, mine)
            size = far.shape[0] // 2
            cut = lambda ref, which: ref.at[pl.ds(which * size, size)]
            via_x, via_y = cut(self.from_x, 1), cut(self.from_y, 0)
            self.last = [cut(far, 1), cut(far, 0)]
            self.two = [
                remote(via_x, via_x, wg_ss.at[k, 2], wg_rs.at[k, 3], (dp, yn)),
                remote(via_y, via_y, wg_ss.at[k, 3], wg_rs.at[k, 4], (dp, xn)),
            ]
            self.beside = [
                remote(ref, ref, wg_ss.at[k, 4 + n], wg_rs.at[k, 5 + n], beside)
                for n, ref in enumerate((self.from_x, self.from_y, far))
            ]
            self.own = self.place(chip)
            self.half = self.part(chip, mine)

        def second(self):
            super().second()
            self.show()

        def forward(self):
            super().second()

        def show(self):
            for copy in self.beside[:2]:
                copy.start()

        def third(self):
            k = self.index
            await_copy(self.last[0], wg_rs.at[k, 3])
            await_copy(self.last[1], wg_rs.at[k, 4])
            self.beside[2].start()

        def done(self):
            await_copy(self.own, wg_rs.at[self.index, 0])
            for copy in self.beside:
                copy.wait_recv()

        def sent(self):
            k = self.index
            for copy in self.two + self.beside:
                copy.wait_send()
            await_copy(self.half, wg_ss.at[k, 0])
            await_copy(self.half, wg_ss.at[k, 1])

    core_cols = tile(core, half)
    whole = lambda ref: ref
    pair_w = 3 * BLK

    def qkv_item(index, pair):
        return SharedGather(
            index,
            [
                (
                    w.at[:, tile(core * 3 + pair, BLK)],
                    lambda ref, i=i: ref.at[:, pl.ds(i * BLK, BLK)],
                )
                for i, w in enumerate((w_query, w_key, w_value))
            ],
            lambda owner: wqkv.at[tile(owner, rows_w), pl.ds(pair * pair_w, pair_w)],
        )

    def in_item(index, part):
        return SharedGather(
            index,
            [
                (
                    w_in.at[:, tile((2 * part + f) * 2 + core, ff_part)],
                    lambda ref, f=f: ref.at[:, pl.ds(f * ff_part, ff_part)],
                )
                for f in range(2)
            ],
            lambda owner: wi.at[tile(owner, rows_w), pl.ds(part * 2 * ff_part, 2 * ff_part)],
        )

    def down_item(kind, index, first, size):
        unit = ff_part // 4
        at = lambda base: pl.ds(pl.multiple_of(base + first * unit, unit), size * unit)
        return kind(
            index, [(w_down.at[at(core * ff_part)], whole)], lambda owner: wd.at[at(owner * ff_part)]
        )

    qkv_items = [qkv_item(i, i) for i in range(3)]
    in_items = [in_item(3, 0), in_item(4, 1)]
    down_items = [
        down_item(SharedGather, 5, 0, 2),
        down_item(Gather, 6, 2, 1),
        down_item(Gather, 7, 3, 1),
    ]
    for it in qkv_items:
        it.first()
    spread(inputs, x_slot, x_ss, x_rs, "start")

    wo_part = rows_w // 2
    wo_src = w_out.at[tile(core, wo_part)]
    wo_dst = wo.at[tile(col * 2 + core, wo_part)]

    def wo_each(action):
        for to in range(SEQ):
            own = (chip == to) & (core == row)
            copy = remote(
                wo_src, wo_dst, wo_ss.at[to], wo_rs.at[col * 2 + core], (depth * 2 + row, to)
            )
            if action == "start":

                @pl.when(own)
                def _():
                    pltpu.make_async_copy(wo_src, wo_dst, wo_rs.at[col * 2 + core]).start()

            @pl.when(jnp.logical_not(own))
            def _():
                if action == "start":
                    copy.start()
                else:
                    copy.wait_send()

    for step in range(1, SEQ + 1):
        await_copy(small_all.at[step], small_rs.at[step])
    summed = small_all[0] + small_all[1] + small_all[2] + small_all[3]
    for which in range(2):
        gains[which : which + 1, :] = jnp.concatenate(
            [summed[8 * which + i : 8 * which + i + 1, :] for i in range(width // BLK)], axis=1
        )
    length_row = jnp.where(row == core, small_all[0, 6:7, :], small_all[SEQ, 6:7, :])
    length = jnp.where(col == 0, length_row[:, 0:1], length_row[:, 1:2])
    own_lengths = small_all[0, 6:7, 0:2]
    table = summed[16:48, :].astype(BF16)
    lane_two = lax.broadcasted_iota(jnp.int32, (1, 2 * BLK), 1)
    minus = jnp.where(lane_two < BLK, lane_two, lane_two - 2 * BLK)
    for off in (-1, 0, 1):
        ids = bucket_of(off * BLK - minus)
        onehot = (lax.broadcasted_iota(jnp.int32, (32, 2 * BLK), 0) == ids).astype(BF16)
        vecs[off + 1] = contract(table, onehot, 0, 0)[0:24, :]

    @pl.loop(0, 6)
    def _(h):
        values = [vecs[i, pl.ds(core * 6 + h, 1), :] for i in range(3)]
        left = jnp.broadcast_to(values[0][:, BLK - 1 : BLK], (BLK, BLK))
        right = jnp.broadcast_to(values[2][:, BLK + 1 : BLK + 2], (BLK, BLK))
        strip[h, 0:BLK, :] = left
        strip[h, 4 * BLK :, :] = right
        for i in range(3):
            skewed = pltpu.roll(
                jnp.broadcast_to(values[i], (BLK, 2 * BLK)), 0, 1, stride=1, stride_axis=0
            )
            strip[h, (i + 1) * BLK : (i + 2) * BLK, :] = skewed[:, :BLK]

    key_pos = lax.broadcasted_iota(jnp.int32, maskc.shape, 0).astype(F32)
    maskc[...] = jnp.where((key_pos < length) | (lane > 0), 0.0, NEGATIVE).astype(BF16)

    def block_valid(b):
        pos = lax.broadcasted_iota(jnp.int32, (BLK, 1), 0) + b * BLK
        return (pos.astype(F32) < length).astype(F32)

    for it in qkv_items:
        it.second()

    def n1_copy(i):
        block = nrm1.at[tile(2 * i + core, BLK)]
        return remote(block, block, n1_ss.at[i], n1_rs.at[i], other)

    @pl.loop(0, SEQ)
    def _(i):
        await_copy(xown.at[i], x_rs.at[i])
        source = xown[i].astype(F32)
        scale = lax.rsqrt(jnp.mean(source * source, -1, keepdims=True) + EPS)
        nrm1[tile(2 * i + core, BLK), :] = (source * scale * gains[0:1, :]).astype(BF16)
        n1_copy(i).start()

    for it in in_items:
        it.first()
    for it in qkv_items:
        it.third()
    for i in range(SEQ):
        n1_copy(i).wait_recv()
    in_items[0].second()
    spread(cotangent, c_slot, c_ss, c_rs, "start", (0,))

    flip[BLK : BLK + 16, :] = jnp.ones((16, tokens), BF16)
    mine_lanes = [lane < 64, lane >= 64]
    slots = [ref.at[:, pl.ds(0, tokens)] for ref in (act, slope)]

    def by_head(value):
        return jnp.concatenate(
            [jnp.where(lanes, value, jnp.zeros_like(value)) for lanes in mine_lanes], axis=0
        )

    def serve(now, table):
        for when, actions in table.items():

            @pl.when(now == when)
            def _():
                for action in actions:
                    action()

    def keep(pair, qb):
        return pltpu.make_async_copy(slots[qb], raised_o.at[2 * pair + qb], raised_s.at[qb])

    def fetch(pair, qb):
        return pltpu.make_async_copy(raised_o.at[2 * pair + qb], slots[qb], raised_s.at[qb])

    def later_inputs():
        down_items[0].first()
        spread(cotangent, c_slot, c_ss, c_rs, "start", (1,))

    forward_table = {
        0: [in_items[1].second, lambda: wo_each("start")],
        1: [in_items[0].third, later_inputs],
        3: [in_items[1].third],
    }

    @pl.loop(0, 3)
    def _(pair):
        cols = tile(pair, BLK)
        for p in range(3):

            @pl.when(pair == p)
            def _():
                qkv_items[p].done()

        qkv[:, tile(pair, pair_w)] = contract(
            nrm1[...], wqkv[:, tile(pair, pair_w)], 1, 0
        ).astype(BF16)
        flip[0:BLK, :] = jnp.transpose(qkv[:, tile(3 * pair + 2, BLK)])
        keys = jnp.concatenate([qkv[:, tile(3 * pair + 1, BLK)], maskc[...]], axis=1)
        for qb in range(2):
            rows = pl.ds(qb * middle_q, middle_q)
            queries = by_head(qkv[rows, tile(3 * pair, BLK)])
            flag = jnp.broadcast_to(jnp.where(lane == 0, 1.0, 0.0).astype(BF16), queries.shape)
            biases = [
                jnp.concatenate(
                    [
                        strip[
                            pair * 2 + h, pl.ds((min(max(kb - q, -2), 2) + 2) * BLK, BLK), :
                        ]
                        for kb in range(tokens // BLK)
                    ],
                    axis=0,
                )
                for h in range(2)
                for q in range(qb * middle_q // BLK, (qb + 1) * middle_q // BLK)
            ]
            logits = contract(keys, jnp.concatenate([queries, flag], axis=1), 1, 1)
            logits = logits + jnp.concatenate(biases, axis=1)
            highest = jnp.max(logits, 0, keepdims=True)
            raised = jnp.exp(logits - highest).astype(BF16)

            @pl.when(pair > 0)
            def _():
                keep(pair - 1, qb).wait()

            slots[qb][...] = raised
            keep(pair, qb).start()
            result = contract(flip[...], raised, 1, 0)
            inverse = 1.0 / result[BLK : BLK + 1, :]
            scaled = result[0:BLK, :] * inverse
            mixed[rows, cols] = jnp.transpose(
                jnp.concatenate([scaled[0:64, 0:middle_q], scaled[64:BLK, middle_q:]], axis=0)
            ).astype(BF16)
            for h in range(2):
                gscale[pl.ds(2 * pair + h, 1), rows] = inverse[:, h * middle_q : (h + 1) * middle_q]
            serve(2 * pair + qb, forward_table)

    def swap_copy(i, send, recv):
        return remote(psend.at[i], precv.at[i], send.at[i], recv.at[i], other)

    for k in range(4):
        await_copy(wo.at[pl.ds(k * wo_part, wo_part)], wo_rs.at[k])

    def blocks_of(ref, parity):
        return jnp.concatenate(
            [ref[tile(2 * i + parity, BLK), :] for i in range(SEQ)], axis=0
        )

    def swap_out(result, send, recv):
        for i in range(SEQ):
            psend[i] = result[i * BLK : (i + 1) * BLK, :].astype(BF16)
            swap_copy(i, send, recv).start()

    swap_out(contract(blocks_of(mixed, 1 - core), wo[...], 1, 0), part_ss, part_rs)

    def n2_copy(i, send, recv):
        block = nrm2.at[tile(2 * i + core, BLK)]
        return remote(block, block, send.at[i], recv.at[i], other)

    pp[...] = jnp.zeros_like(pp)
    result = contract(blocks_of(mixed, core), wo[...], 1, 0)
    for i in range(SEQ):
        hidden = xown[i].astype(F32) + result[i * BLK : (i + 1) * BLK, :]
        swap_copy(i, part_ss, part_rs).wait_recv()
        hidden = hidden + precv[i].astype(F32)
        hid[i] = hidden
        scale = lax.rsqrt(jnp.mean(hidden * hidden, -1, keepdims=True) + EPS)
        nrm2[tile(2 * i + core, BLK), :] = (hidden * scale * gains[1:2, :]).astype(BF16)
        n2_copy(i, n2_ss, n2_rs).start()
        pp[0:1, :] += jnp.sum(hidden * block_valid(2 * i + core), 0, keepdims=True)
    down_items[0].second()
    for it in down_items[1:]:
        it.first()
    for i in range(SEQ):
        n2_copy(i, n2_ss, n2_rs).wait_recv()
    for qb in range(2):
        keep(2, qb).wait()

    def g_copy(i):
        block = grads.at[2 * i + core]
        return remote(block, block, g_ss.at[i], g_rs.at[i], other)

    def take_cotangent():
        @pl.loop(0, SEQ)
        def _(i):
            b = 2 * i + core
            await_copy(grads.at[b], c_rs.at[i])
            grads[b] = (grads[b].astype(F32) * block_valid(b)).astype(BF16)
            g_copy(i).start()

    asum[...] = jnp.zeros_like(asum)
    wide_part = 2 * ff_part
    for part in range(2):
        part_cols = slice(part * wide_part, (part + 1) * wide_part)
        if part == 1:
            take_cotangent()
            down_items[0].third()
        in_items[part].done()

        @pl.loop(0, 2)
        def _(i):
            rows = tile(i, middle_q)
            value = contract(nrm2[rows, :], wi[:, part_cols], 1, 0)
            square = value * value
            tangent = jnp.tanh(value * (GELU_C + GELU_C * GELU_K * square))
            half_up = 0.5 + 0.5 * tangent
            active = (value * half_up).astype(BF16)
            act[rows, part_cols] = active
            slope[rows, part_cols] = (
                half_up
                + value
                * (1.0 - tangent * tangent)
                * (0.5 * GELU_C + 1.5 * GELU_C * GELU_K * square)
            ).astype(BF16)
            pos = lax.broadcasted_iota(jnp.int32, (8, middle_q), 1) + i * middle_q
            valid = (pos.astype(F32) < length).astype(BF16)
            asum[:, part_cols] += contract(valid, active, 1, 0)


    for i in range(SEQ):
        g_copy(i).wait_recv()
    g_all = lambda: grads[...].reshape(tokens, width)

    class Chunk:
        made = 0

        def __init__(self, src, dx, dy, rx, ry, za, zb, outs):
            self.index = Chunk.made
            Chunk.made += 1
            self.src, self.dx, self.dy, self.rx, self.ry = src, dx, dy, rx, ry
            self.za, self.zb, self.outs = za, zb, outs
            self.bind()

        def bind(self):
            k = self.index
            size = self.dx.shape[0]
            cut = lambda ref, which: ref.at[pl.ds(which * size, size)]
            ss, rs = (lambda i: rs_ss.at[k, i]), (lambda i: rs_rs.at[k, i])
            to_x, to_y = (dp, xn), (dp, yn)
            self.one = [
                remote(cut(self.src(dn), 1), self.dx, ss(0), rs(0), to_x),
                remote(cut(self.src(dn), 0), self.dy, ss(1), rs(1), to_y),
                remote(cut(self.src(xn), 1), cut(self.rx, 1), ss(2), rs(2), to_x),
                remote(cut(self.src(yn), 0), cut(self.ry, 0), ss(3), rs(3), to_y),
            ]
            self.sum_y, self.sum_x = cut(self.src(yn), 1), cut(self.src(xn), 0)
            self.two = [
                remote(self.sum_y, cut(self.ry, 1), ss(4), rs(4), to_y),
                remote(self.sum_x, cut(self.rx, 0), ss(5), rs(5), to_x),
            ]
            self.bind_z(self.rx, self.ry)

        def bind_z(self, reduced, final):
            k = self.index
            self.reduced, self.final = reduced, final
            sem = lambda i: (z_ss.at[k, i], z_rs.at[k, i])
            self.to_inner = remote(reduced, self.za, *sem(0), z_dev(toward))
            self.swap = remote(reduced, self.zb, *sem(1), z_dev(across))
            self.to_end = remote(final, final, *sem(2), z_dev(outward))

        def start(self):
            for copy in self.one:
                copy.start()

        def middle(self):
            for at, sent, sums, copy in (
                (0, self.dx, self.sum_y, self.two[0]),
                (1, self.dy, self.sum_x, self.two[1]),
            ):
                self.one[at].wait_recv()
                sums[...] = (sums[...].astype(F32) + sent[...].astype(F32)).astype(BF16)
                copy.start()

        def total(self):
            for copy in (self.one[2], self.one[3], *self.two):
                copy.wait_recv()
            self.rx[...] = (
                self.src(chip)[...].astype(F32)
                + self.rx[...].astype(F32)
                + self.ry[...].astype(F32)
            ).astype(BF16)

        def z_one(self):
            self.total()

            @pl.when(end_z)
            def _():
                self.to_inner.start()

        def z_two(self):
            @pl.when(inner_z)
            def _():
                self.to_inner.wait_recv()
                self.reduced[...] = (
                    self.reduced[...].astype(F32) + self.za[...].astype(F32)
                ).astype(BF16)
                self.swap.start()

        def z_three(self):
            @pl.when(inner_z)
            def _():
                self.swap.wait_recv()
                self.final[...] = (
                    self.reduced[...].astype(F32) + self.zb[...].astype(F32)
                ).astype(BF16)
                self.to_end.start()

        def each_out(self, act_on):
            k = self.index
            for n, (cols, place) in enumerate(self.outs):
                src = self.final if cols is None else self.final.at[:, cols]
                act_on(
                    remote(src, place(core), z_ss.at[k, 3 + n], z_rs.at[k, 3 + n], other),
                    pltpu.make_async_copy(src, place(core), out_s.at[k, n]),
                )

        def z_four(self):
            @pl.when(end_z)
            def _():
                self.to_end.wait_recv()

            self.each_out(lambda there, here: (there.start(), here.start()))

        def finish(self):
            self.each_out(
                lambda there, here: (there.wait_recv(), there.wait_send(), here.wait())
            )

            @pl.when(end_z)
            def _():
                self.to_inner.wait_send()

            @pl.when(inner_z)
            def _():
                self.swap.wait_send()
                self.to_end.wait_send()

            for copy in self.plane_sends():
                copy.wait_send()

        def plane_sends(self):
            return self.one + self.two

    inner_z = (depth == 1) | (depth == 2)
    end_z = jnp.logical_not(inner_z)
    toward = jnp.where(depth == 0, 1, 2)
    outward = jnp.where(depth == 1, 0, 3)
    across = jnp.where(depth == 1, 2, 1)

    def z_dev(z):
        return (z * 2 + core, chip)

    d_chunks = [
        Chunk(
            lambda owner, i=i: gdn.at[i, owner],
            d_dx.at[i],
            d_dy.at[i],
            d_rx.at[i],
            d_ry.at[i],
            d_za.at[i],
            d_zb.at[i],
            [
                (
                    None,
                    lambda c, i=i: gd_o.at[
                        pl.ds(pl.multiple_of(c * ff_part + i * BLK, BLK), BLK)
                    ],
                )
            ],
        )
        for i in range(ff_part // BLK)
    ]

    i_chunks = [
        Chunk(
            lambda owner, f=f: wi.at[tile(owner, rows_w), pl.ds(f * ff_part, ff_part)],
            i_dx.at[f],
            i_dy.at[f],
            i_rx.at[f],
            i_ry.at[f],
            i_za.at[f],
            i_zb.at[f],
            [(None, lambda c, f=f: gi_o.at[:, tile(2 * f + c, ff_part)])],
        )
        for f in range(SEQ)
    ]
    q_chunks = [
        Chunk(
            lambda owner, p=p: gqkv.at[p, tile(owner, rows_w)],
            q_dx.at[p],
            q_dy.at[p],
            q_rx.at[p],
            q_ry.at[p],
            q_za.at[p],
            q_zb.at[p],
            [
                (
                    pl.ds(j * BLK, BLK),
                    lambda c, p=p, o=o: o.at[:, tile(c * 3 + p, BLK)],
                )
                for j, o in enumerate((gq_o, gk_o, gv_o))
            ],
        )
        for p in range(3)
    ]
    def rso_each(action):
        for k in range(2):
            for to in range(2):
                target = core * 2 + k
                own = (chip == target) & (core == to)
                src = wo.at[pl.ds((2 * k + to) * wo_part, wo_part)]
                dst = rs_o.at[chip]
                copy = remote(
                    src, dst, rso_ss.at[2 * k + to], rso_rs.at[chip], (depth * 2 + to, target)
                )
                if action == "start":

                    @pl.when(own)
                    def _():
                        pltpu.make_async_copy(src, dst, rso_rs.at[chip]).start()

                @pl.when(jnp.logical_not(own))
                def _():
                    if action == "start":
                        copy.start()
                    else:
                        copy.wait_send()

    class OutChunk(Chunk):
        def bind(self):
            self.bind_z(self.src.at[0], self.src.at[1])

        def total(self):
            for i in range(SEQ):
                await_copy(self.src.at[i], rso_rs.at[i])
            value = self.src[0].astype(F32)
            for i in range(1, SEQ):
                value = value + self.src[i].astype(F32)
            self.reduced[...] = value.astype(BF16)

        def plane_sends(self):
            return []

    o_chunk = OutChunk(
        rs_o, None, None, None, None, o_za, o_zb, [(None, lambda c: go_o.at[tile(c, wo_part)])]
    )
    def gx_each(i, action):
        own = (chip == i) & (core == row)
        dst = gx_o.at[col, tile(core, BLK)]
        copy = remote(
            nrm2.at[pl.ds(i * BLK, BLK)], dst, gx_ss.at[i], gx_rs.at[col * 2 + core], (depth * 2 + row, i)
        )
        if action == "start":

            @pl.when(own)
            def _():
                pltpu.make_async_copy(nrm2.at[pl.ds(i * BLK, BLK)], dst, gx_rs.at[col * 2 + core]).start()

        @pl.when(jnp.logical_not(own))
        def _():
            if action == "start":
                copy.start()
            else:
                copy.wait_send()

    def sgz_copy(step):
        return remote(
            sg_depth.at[depth],
            sg_depth.at[depth],
            sgz_ss.at[step],
            sgz_rs.at[depth],
            z_dev(lax.rem(depth + step, DEPTH)),
        )

    def small_along_z():
        for i in range(8):
            await_copy(sg_plane.at[i], sgp_rs.at[i])
        total = sg_plane[0]
        for i in range(1, 8):
            total = total + sg_plane[i]
        sg_depth[depth] = total
        for step in range(1, DEPTH):
            sgz_copy(step).start()

    by_name = dict(
        [(f"d{i}", c) for i, c in enumerate(d_chunks)]
        + [(f"i{i}", c) for i, c in enumerate(i_chunks)]
        + [(f"q{i}", c) for i, c in enumerate(q_chunks)]
        + [("o", o_chunk)]
    )

    def after(block):
        for name, step in SCHEDULE[block]:
            if name == "gx":
                for i in range(SEQ):
                    gx_each(i, "start")
            elif name == "sm":
                small_along_z()
            elif name == "o" and step == "s":
                rso_each("start")
            else:
                getattr(by_name[name], STEPS[step])()

    for it in down_items[1:]:
        it.second()
    for i in range(ff_part // BLK):
        columns = jnp.concatenate(
            [act[:, f * ff_part + i * BLK : f * ff_part + (i + 1) * BLK] for f in range(SEQ)],
            axis=1,
        )
        gdn[i] = contract(columns, g_all(), 0, 0).astype(BF16).reshape(SEQ, BLK, width)
    after("gdn2")
    for it in down_items:
        it.done()
    for it in in_items:
        it.sent()
    after("wd")

    def pooled_part(cols):
        total = asum[0:1, cols]
        high = total.astype(BF16)
        rest = total - high.astype(F32)
        middle = rest.astype(BF16)
        low = (rest - middle.astype(F32)).astype(BF16)
        pieces = jnp.concatenate(
            [jnp.broadcast_to(piece, (16, piece.shape[1])) for piece in (high, middle, low)], axis=0
        )
        result = contract(pieces, wd[cols, :], 1, 0)
        pp[0:1, :] += result[0:1, :] + result[16:17, :] + result[32:33, :]

    for part in range(2):
        part_cols = slice(part * wide_part, (part + 1) * wide_part)

        @pl.loop(0, 2)
        def _(i):
            rows = tile(i, middle_q)
            upstream = grads[pl.ds(4 * i, 4)].reshape(middle_q, width)
            grad = contract(upstream, wd[part_cols, :], 1, 1) * slope[rows, part_cols].astype(F32)
            slope[rows, part_cols] = grad.astype(BF16)

        pooled_part(part_cols)

    after("gact")

    for i in range(SEQ):
        swap_copy(i, part_ss, part_rs).wait_send()
    swap_out(contract(blocks_of(slope, 1 - core), wi[...], 1, 1), gn2_ss, gn2_rs)
    gn[...] = contract(blocks_of(slope, core), wi[...], 1, 1).reshape(SEQ, BLK, width)
    after("gn")
    for part in range(2):
        part_cols = slice(part * wide_part, (part + 1) * wide_part)

        @pl.loop(0, width // (2 * BLK))
        def _(i):
            wi[tile(i, 2 * BLK), part_cols] = contract(
                nrm2[:, tile(i, 2 * BLK)], slope[:, part_cols], 0, 0
            ).astype(BF16)

        after(f"gin{part}")
    def pool_each(action):
        for to in range(SEQ):
            own = (chip == to) & (core == row)
            dst = pool_recv.at[col * 2 + core]
            copy = remote(pp, dst, pool_ss.at[to], pool_rs.at[col * 2 + core], (depth * 2 + row, to))
            if action == "start":

                @pl.when(own)
                def _():
                    pltpu.make_async_copy(pp, dst, pool_rs.at[col * 2 + core]).start()

            @pl.when(jnp.logical_not(own))
            def _():
                if action == "start":
                    copy.start()
                else:
                    copy.wait_send()

    def gat_copy(i):
        block = act.at[tile(2 * i + core, BLK), pl.ds(0, width)]
        return remote(block, block, gat_ss.at[i], gat_rs.at[i], other)

    for i in range(SEQ):
        n2_copy(i, n2_ss, n2_rs).wait_send()
    sg[...] = jnp.zeros_like(sg)

    def add_gain(first, value):
        for i in range(width // BLK):
            sg[first + i : first + i + 1, :] += value[:, i * BLK : (i + 1) * BLK]

    @pl.loop(0, SEQ)
    def _(i):
        b = 2 * i + core
        swap_copy(i, gn2_ss, gn2_rs).wait_recv()
        normed = gn[i] + precv[i].astype(F32)
        hidden = hid[i]
        scale = lax.rsqrt(jnp.mean(hidden * hidden, -1, keepdims=True) + EPS)
        add_gain(8, jnp.sum(normed * hidden * scale, 0, keepdims=True))
        scaled = normed * gains[1:2, :]
        inner = jnp.mean(scaled * hidden, -1, keepdims=True)
        result = grads[b].astype(F32) + scale * scaled - hidden * (scale * scale * scale) * inner
        hid[i] = result
        act[tile(b, BLK), 0:width] = result.astype(BF16)
        gat_copy(i).start()

    pool_each("start")
    after("n2")
    for i in range(SEQ):
        gat_copy(i).wait_recv()

    @pl.loop(0, 2)
    def _(i):
        rows = tile(i, middle_q)
        inverse = jnp.concatenate(
            [
                jnp.transpose(
                    jnp.concatenate(
                        [
                            jnp.broadcast_to(gscale[2 * p + h : 2 * p + h + 1, rows], (64, middle_q))
                            for h in range(2)
                        ],
                        axis=0,
                    )
                )
                for p in range(3)
            ],
            axis=1,
        )
        gmix[rows, :] = (contract(act[rows, 0:width], wo[...], 1, 1) * inverse).astype(BF16)

    wo[...] = contract(mixed[...], act[:, 0:width], 0, 0).astype(BF16)
    for i in range(SEQ):
        gat_copy(i).wait_send()
    for qb in range(2):
        fetch(0, qb).start()
    after("op")


    sub = lax.broadcasted_iota(jnp.int32, (16, tokens), 0)
    key_block = lax.div(lax.broadcasted_iota(jnp.int32, (16, tokens), 1), BLK)
    flip[BLK : BLK + 16, :] = (sub == key_block).astype(BF16)
    near[...] = jnp.zeros_like(near)
    far[...] = jnp.zeros_like(far)

    backward_table = {i: [lambda i=i: after(f"u{i}")] for i in range(6)}

    @pl.loop(0, 3)
    def _(pair):
        cols = tile(pair, BLK)
        flip[0:BLK, :] = jnp.transpose(qkv[:, tile(3 * pair + 1, BLK)])
        for qb in range(2):
            rows = pl.ds(qb * middle_q, middle_q)
            upstream = gmix[rows, cols]
            masked = by_head(upstream)
            queries = by_head(qkv[rows, tile(3 * pair, BLK)])
            product = jnp.transpose(upstream.astype(F32) * mixed[rows, cols].astype(F32))
            inner = jnp.concatenate(
                [jnp.sum(product[64 * h : 64 * h + 64, :], 0, keepdims=True) for h in range(2)],
                axis=1,
            )
            fetch(pair, qb).wait()
            raised = slots[qb][...]
            grad_probs = contract(qkv[:, tile(3 * pair + 2, BLK)], masked, 1, 1)
            grad_logits = (raised.astype(F32) * (grad_probs - inner)).astype(BF16)
            grad_values = contract(raised, masked, 1, 0)
            grad_keys = contract(grad_logits, queries, 1, 0)
            if qb == 0:
                dv_acc[...] = grad_values
                dk_acc[...] = grad_keys
            else:
                dv_acc[...] += grad_values
                dk_acc[...] += grad_keys
            result = contract(flip[...], grad_logits, 1, 0)
            dqkv[rows, tile(3 * pair, BLK)] = jnp.transpose(
                jnp.concatenate([result[0:64, 0:middle_q], result[64:BLK, middle_q:]], axis=0)
            ).astype(BF16)
            sums = result[BLK : BLK + 8, :]
            block_row = lax.broadcasted_iota(jnp.int32, sums.shape, 0)
            block_col = lax.rem(
                lax.div(lax.broadcasted_iota(jnp.int32, sums.shape, 1), BLK), middle_q // BLK
            )
            gap = block_row - block_col - qb * (middle_q // BLK)
            far[pair, 0] += jnp.where(gap <= -2, sums, 0.0)
            far[pair, 1] += jnp.where(gap >= 2, sums, 0.0)
            for h in range(2):
                for off in range(3):
                    total = near[(pair * 2 + h) * 3 + off]
                    for i in range(middle_q // BLK):
                        kb = qb * (middle_q // BLK) + i + off - 1
                        if 0 <= kb < tokens // BLK:
                            first = h * middle_q + i * BLK
                            total = total + grad_logits[
                                kb * BLK : (kb + 1) * BLK, first : first + BLK
                            ].astype(F32)
                    near[(pair * 2 + h) * 3 + off] = total

            @pl.when(pair < 2)
            def _():
                fetch(pair + 1, qb).start()

            if qb == 1:
                dqkv[:, tile(3 * pair + 1, BLK)] = dk_acc[...].astype(BF16)
                dqkv[:, tile(3 * pair + 2, BLK)] = dv_acc[...].astype(BF16)
                right = dqkv[:, tile(pair, pair_w)]

                @pl.loop(0, width // middle_w)
                def _(i):
                    gqkv[pair, tile(i, middle_w), :] = contract(
                        nrm1[:, tile(i, middle_w)], right, 0, 0
                    ).astype(BF16)

            serve(2 * pair + qb, backward_table)

    for i in range(SEQ):
        swap_copy(i, gn2_ss, gn2_rs).wait_send()

    swap_out(contract(blocks_of(dqkv, 1 - core), wqkv[...], 1, 1), gn1_ss, gn1_rs)
    diag_row = lax.broadcasted_iota(jnp.int32, (BLK, BLK), 0)
    diag_col = lax.broadcasted_iota(jnp.int32, (BLK, BLK), 1)
    upper = diag_col >= diag_row
    mirror = (diag_row + diag_col == BLK - 1).astype(F32)
    shift = lax.broadcasted_iota(jnp.int32, (1, BLK), 1) + 1
    shift = jnp.where(shift == BLK, 0, shift)
    ids = bucket_of(jnp.concatenate([-shift, BLK - shift], axis=1))
    onehot = (lax.broadcasted_iota(jnp.int32, (BLK, 2 * BLK), 0) == ids).astype(F32)

    def bias_head(h):
        def skew(x):
            return pltpu.roll(exact(mirror, x, 1, 0), 0, 1, stride=1, stride_axis=0)

        def far_of(h, side):
            both = far[lax.div(h, 2), side]
            return jnp.where(lax.rem(h, 2) == 0, both[:, 0:middle_q], both[:, middle_q:])

        tiles = [near[h * 3 + i] for i in range(3)]
        at = [
            jnp.sum(
                skew(jnp.where(upper, tiles[i + 1], 0.0) + jnp.where(upper, 0.0, tiles[i])),
                0,
                keepdims=True,
            )
            for i in range(2)
        ]
        below = full_sum(jnp.where(upper, tiles[0], 0.0)) + full_sum(far_of(h, 0))
        above = full_sum(jnp.where(upper, 0.0, tiles[2])) + full_sum(far_of(h, 1))
        sums = exact(jnp.broadcast_to(jnp.concatenate(at, axis=1), (8, 2 * BLK)), onehot, 1, 1)
        sums = sums[0:1, :] + jnp.where(lane == 15, below, 0.0) + jnp.where(lane == 31, above, 0.0)
        sg[pl.ds(16 + core * 6 + h, 1), :] = sums

    after("sw")

    @pl.loop(0, 3)
    def _(h):
        bias_head(h)

    after("b0")

    @pl.loop(3, 6)
    def _(h):
        bias_head(h)

    after("b1")
    both = contract(blocks_of(dqkv, core), wqkv[...], 1, 1)
    for i in range(SEQ):
        swap_copy(i, gn1_ss, gn1_rs).wait_recv()
        normed = both[i * BLK : (i + 1) * BLK, :] + precv[i].astype(F32)
        source = xown[i].astype(F32)
        scale = lax.rsqrt(jnp.mean(source * source, -1, keepdims=True) + EPS)
        add_gain(0, jnp.sum(normed * source * scale, 0, keepdims=True))
        scaled = normed * gains[0:1, :]
        inner = jnp.mean(scaled * source, -1, keepdims=True)
        result = hid[i] + scale * scaled - source * (scale * scale * scale) * inner
        nrm2[i * BLK : (i + 1) * BLK, :] = result.astype(BF16)

    place = core * SEQ + chip
    sg_sent = sg.at[pl.ds(0, sg_plane.shape[1])]

    def sgp_each(action):
        for step in range(SEQ):
            for cross in range(2):
                if step == 0 and cross == 0:
                    continue
                to_core = lax.rem(core + cross, 2)
                copy = remote(
                    sg_sent,
                    sg_plane.at[place],
                    sgp_ss.at[step * 2 + cross],
                    sgp_rs.at[place],
                    (depth * 2 + to_core, ahead(step)),
                )
                if action == "start":
                    copy.start()
                else:
                    copy.wait_send()

    sgp_each("start")
    pltpu.make_async_copy(sg_sent, sg_plane.at[place], sgp_rs.at[place]).start()
    for copy in pending:
        copy.wait_send()
    spread(inputs, x_slot, x_ss, x_rs, "wait")
    spread(cotangent, c_slot, c_ss, c_rs, "wait")
    for it in qkv_items + down_items:
        it.sent()
    wo_each("wait")
    after("g1")
    after("end")
    for i in range(4):
        await_copy(pool_recv.at[i], pool_rs.at[i])
    for doc in range(2):
        pooled_o[doc : doc + 1, :] = (
            pool_recv[2 * doc, 0:1, :] + pool_recv[2 * doc + 1, 0:1, :]
        ) / own_lengths[:, doc : doc + 1]
    for step in range(1, DEPTH):
        z = lax.rem(depth + DEPTH - step, DEPTH)
        await_copy(sg_depth.at[z], sgz_rs.at[z])
    total = sg_depth[0] + sg_depth[1] + sg_depth[2] + sg_depth[3]
    for which in range(2):
        wide[which : which + 1, :] = jnp.concatenate(
            [total[8 * which + i : 8 * which + i + 1, :] for i in range(width // BLK)], axis=1
        )
    small_o[...] = pltpu.roll(wide[...], lax.rem(width - chip * rows_w, width), 1)[:, : small_o.shape[1]]
    turned[:, 0:16] = jnp.transpose(total[16:32, :])
    table_o[...] = turned[tile(chip, 8), :]

    for i in range(4):
        await_copy(gx_o.at[i // 2, pl.ds((i % 2) * BLK, BLK)], gx_rs.at[i])
    pool_each("wait")
    rso_each("wait")
    sgp_each("wait")
    for i in range(SEQ):
        n1_copy(i).wait_send()
        g_copy(i).wait_send()
        swap_copy(i, gn1_ss, gn1_rs).wait_send()
        gx_each(i, "wait")
    for step in range(1, DEPTH):
        sgz_copy(step).wait_send()
    for chunk in (*d_chunks, *i_chunks, o_chunk, *q_chunks):
        chunk.finish()


def widen_kernel(pooled, small, table, gx, gq, gk, gv, go, gi, gd, *outs):
    pooled_out, one_out, two_out, table_out, *outs = outs
    pooled_out[...] = pooled[0 : pooled_out.shape[0], :]
    one_out[...] = small[0:1, : one_out.shape[1]]
    two_out[...] = small[1:2, : two_out.shape[1]]
    table_out[...] = table[:, : table_out.shape[1]]
    for value, out in zip((gx, gq, gk, gv, go, gi, gd), outs):
        out[...] = value[...].astype(F32)


def on_device(
    inputs,
    w_query,
    w_key,
    w_value,
    w_out,
    w_ffn_in,
    w_ffn_out,
    attn_gain,
    ffn_gain,
    rel_bias,
    doc_lengths,
    cotangent,
):
    blocks, shard_len, width = inputs.shape
    heads = rel_bias.shape[1]
    head_dim = width // heads
    full_len = shard_len * lax.axis_size("seq")
    total_rows = blocks * shard_len
    gathered = (
        lax.all_gather(w_query, "seq", axis=0, tiled=True),
        lax.all_gather(w_key, "seq", axis=0, tiled=True),
        lax.all_gather(w_value, "seq", axis=0, tiled=True),
        lax.all_gather(w_out, "seq", axis=0, tiled=True),
        lax.all_gather(w_ffn_in, "seq", axis=0, tiled=True),
        lax.all_gather(w_ffn_out, "seq", axis=0, tiled=True),
        lax.all_gather(attn_gain, "seq", axis=0, tiled=True),
        lax.all_gather(ffn_gain, "seq", axis=0, tiled=True),
        lax.all_gather(rel_bias, "seq", axis=0, tiled=True),
    )
    (
        full_query,
        full_key,
        full_value,
        full_out,
        full_in,
        full_down,
        gain_one,
        gain_two,
        bias_table,
    ) = gathered
    gain_one = gain_one.astype(jnp.float32)
    gain_two = gain_two.astype(jnp.float32)
    bucket_range = jnp.arange(bias_table.shape[0], dtype=jnp.int32)
    query_pos = lax.axis_index("seq") * shard_len + jnp.arange(shard_len, dtype=jnp.int32)
    key_pos = jnp.arange(full_len, dtype=jnp.int32)
    onehot = (bucket_ids(query_pos, key_pos)[:, :, None] == bucket_range).astype(jnp.bfloat16)
    bias_heads = jnp.einsum("qkn,nh->hqk", onehot, bias_table, preferred_element_type=jnp.float32)
    key_valid = key_pos[None, :] < doc_lengths[:, None]
    query_valid = (query_pos[None, :] < doc_lengths[:, None]).astype(jnp.float32)
    flat = inputs.astype(jnp.float32).reshape(total_rows, width)
    scale_one = lax.rsqrt(jnp.mean(flat * flat, -1, keepdims=True) + EPS)
    normed_one = (flat * scale_one * gain_one).astype(jnp.bfloat16)
    queries = jnp.dot(normed_one, full_query, preferred_element_type=jnp.float32).astype(
        jnp.bfloat16
    )
    keys_local = jnp.dot(normed_one, full_key, preferred_element_type=jnp.float32).astype(
        jnp.bfloat16
    )
    values_local = jnp.dot(normed_one, full_value, preferred_element_type=jnp.float32).astype(
        jnp.bfloat16
    )
    queries_heads = queries.reshape(blocks, shard_len, heads, head_dim)
    keys_all, values_all = (
        lax.all_gather(keys_local.reshape(blocks, shard_len, width), "seq", axis=1, tiled=True),
        lax.all_gather(values_local.reshape(blocks, shard_len, width), "seq", axis=1, tiled=True),
    )
    scores = jnp.einsum(
        "bqhe,bkhe->bhqk",
        queries_heads,
        keys_all.reshape(blocks, full_len, heads, head_dim),
        preferred_element_type=jnp.float32,
    )
    logits = jnp.where(key_valid[:, None, None, :], scores + bias_heads[None], NEGATIVE)
    highest = jnp.max(logits, -1, keepdims=True)
    log_total = highest + jnp.log(jnp.sum(jnp.exp(logits - highest), -1, keepdims=True))
    probs_low = jnp.exp(logits - log_total).astype(jnp.bfloat16)
    mixed = jnp.einsum(
        "bhqk,bkhe->bqhe",
        probs_low,
        values_all.reshape(blocks, full_len, heads, head_dim),
        preferred_element_type=jnp.float32,
    )
    mixed = mixed.astype(jnp.bfloat16).reshape(total_rows, width)
    hidden = flat + jnp.dot(mixed, full_out, preferred_element_type=jnp.float32)
    scale_two = lax.rsqrt(jnp.mean(hidden * hidden, -1, keepdims=True) + EPS)
    normed_two = (hidden * scale_two * gain_two).astype(jnp.bfloat16)
    pre_act = jnp.dot(normed_two, full_in, preferred_element_type=jnp.float32)
    active = jax.nn.gelu(pre_act, approximate=True).astype(jnp.bfloat16)
    outputs = hidden + jnp.dot(active, full_down, preferred_element_type=jnp.float32)
    partial_pool = jnp.sum(outputs.reshape(blocks, shard_len, width) * query_valid[:, :, None], 1)
    pooled = lax.psum(partial_pool, "seq") / doc_lengths[:, None].astype(jnp.float32)
    regathered = (
        lax.all_gather(w_query, "seq", axis=0, tiled=True),
        lax.all_gather(w_key, "seq", axis=0, tiled=True),
        lax.all_gather(w_value, "seq", axis=0, tiled=True),
        lax.all_gather(w_out, "seq", axis=0, tiled=True),
        lax.all_gather(w_ffn_in, "seq", axis=0, tiled=True),
        lax.all_gather(w_ffn_out, "seq", axis=0, tiled=True),
        lax.all_gather(attn_gain, "seq", axis=0, tiled=True),
        lax.all_gather(ffn_gain, "seq", axis=0, tiled=True),
    )
    full_query, full_key, full_value, full_out, full_in, full_down, gain_back_one, gain_back_two = (
        regathered
    )
    gain_one = gain_back_one.astype(jnp.float32)
    gain_two = gain_back_two.astype(jnp.float32)
    grad_out = (cotangent.astype(jnp.float32) * query_valid[:, :, None]).reshape(total_rows, width)
    grad_branch = grad_out.astype(jnp.bfloat16)
    grad_down = outer_sum(active, grad_branch)
    grad_pre = (back_project(grad_branch, full_down) * gelu_slope(pre_act)).astype(jnp.bfloat16)
    grad_in = outer_sum(normed_two, grad_pre)
    grad_normed_two = back_project(grad_pre, full_in)
    grad_gain_two, grad_hidden_norm = norm_backward(hidden, scale_two, gain_two, grad_normed_two)
    grad_hidden = grad_out + grad_hidden_norm
    grad_attended = grad_hidden.astype(jnp.bfloat16)
    grad_out_proj = outer_sum(mixed, grad_attended)
    grad_mixed = (
        back_project(grad_attended, full_out)
        .astype(jnp.bfloat16)
        .reshape(blocks, shard_len, heads, head_dim)
    )
    keys_back, values_back = (keys_all, values_all)
    probs = jnp.exp(logits - log_total)
    grad_probs = jnp.einsum(
        "bqhe,bkhe->bhqk",
        grad_mixed,
        values_back.reshape(blocks, full_len, heads, head_dim),
        preferred_element_type=jnp.float32,
    )
    inner_term = jnp.sum(probs * grad_probs, -1, keepdims=True)
    grad_logits = (probs * (grad_probs - inner_term)).astype(jnp.bfloat16)
    grad_queries = jnp.einsum(
        "bhqk,bkhe->bqhe",
        grad_logits,
        keys_back.reshape(blocks, full_len, heads, head_dim),
        preferred_element_type=jnp.float32,
    )
    grad_queries = grad_queries.astype(jnp.bfloat16).reshape(total_rows, width)
    grad_table = jnp.einsum("bhqk,qkn->nh", grad_logits, onehot, preferred_element_type=jnp.float32)
    key_terms = jnp.einsum(
        "bhqk,bqhe->bkhe", grad_logits, queries_heads, preferred_element_type=jnp.float32
    ).reshape(blocks, full_len, width)
    value_terms = jnp.einsum(
        "bhqk,bqhe->bkhe", probs_low, grad_mixed, preferred_element_type=jnp.float32
    ).reshape(blocks, full_len, width)
    grad_keys, grad_values = (
        lax.psum_scatter(
            key_terms.astype(jnp.bfloat16), "seq", scatter_dimension=1, tiled=True
        ).astype(jnp.float32),
        lax.psum_scatter(
            value_terms.astype(jnp.bfloat16), "seq", scatter_dimension=1, tiled=True
        ).astype(jnp.float32),
    )
    grad_keys = grad_keys.astype(jnp.bfloat16).reshape(total_rows, width)
    grad_values = grad_values.astype(jnp.bfloat16).reshape(total_rows, width)
    grad_query_w = outer_sum(normed_one, grad_queries)
    grad_key_w = outer_sum(normed_one, grad_keys)
    grad_value_w = outer_sum(normed_one, grad_values)
    grad_normed_one = (
        back_project(grad_queries, full_query)
        + back_project(grad_keys, full_key)
        + back_project(grad_values, full_value)
    )
    grad_gain_one, grad_input_norm = norm_backward(flat, scale_one, gain_one, grad_normed_one)
    grad_input = (grad_hidden + grad_input_norm).reshape(blocks, shard_len, width)
    shards = (
        lax.psum_scatter(
            grad_query_w.astype(jnp.bfloat16), "seq", scatter_dimension=0, tiled=True
        ).astype(jnp.float32),
        lax.psum_scatter(
            grad_key_w.astype(jnp.bfloat16), "seq", scatter_dimension=0, tiled=True
        ).astype(jnp.float32),
        lax.psum_scatter(
            grad_value_w.astype(jnp.bfloat16), "seq", scatter_dimension=0, tiled=True
        ).astype(jnp.float32),
        lax.psum_scatter(
            grad_out_proj.astype(jnp.bfloat16), "seq", scatter_dimension=0, tiled=True
        ).astype(jnp.float32),
        lax.psum_scatter(
            grad_in.astype(jnp.bfloat16), "seq", scatter_dimension=0, tiled=True
        ).astype(jnp.float32),
        lax.psum_scatter(
            grad_down.astype(jnp.bfloat16), "seq", scatter_dimension=0, tiled=True
        ).astype(jnp.float32),
        lax.psum_scatter(
            grad_gain_one.astype(jnp.bfloat16), "seq", scatter_dimension=0, tiled=True
        ).astype(jnp.float32),
        lax.psum_scatter(
            grad_gain_two.astype(jnp.bfloat16), "seq", scatter_dimension=0, tiled=True
        ).astype(jnp.float32),
        lax.psum_scatter(
            grad_table.astype(jnp.bfloat16), "seq", scatter_dimension=0, tiled=True
        ).astype(jnp.float32),
    )
    totals = (
        lax.psum(shards[0].astype(jnp.bfloat16), "dp").astype(jnp.float32),
        lax.psum(shards[1].astype(jnp.bfloat16), "dp").astype(jnp.float32),
        lax.psum(shards[2].astype(jnp.bfloat16), "dp").astype(jnp.float32),
        lax.psum(shards[3].astype(jnp.bfloat16), "dp").astype(jnp.float32),
        lax.psum(shards[4].astype(jnp.bfloat16), "dp").astype(jnp.float32),
        lax.psum(shards[5].astype(jnp.bfloat16), "dp").astype(jnp.float32),
        lax.psum(shards[6].astype(jnp.bfloat16), "dp").astype(jnp.float32),
        lax.psum(shards[7].astype(jnp.bfloat16), "dp").astype(jnp.float32),
        lax.psum(shards[8].astype(jnp.bfloat16), "dp").astype(jnp.float32),
    )
    return (
        pooled,
        grad_input,
        totals[0],
        totals[1],
        totals[2],
        totals[3],
        totals[4],
        totals[5],
        totals[6],
        totals[7],
        totals[8],
    )


def fused_on_device(
    inputs,
    w_query,
    w_key,
    w_value,
    w_out,
    w_ffn_in,
    w_ffn_out,
    attn_gain,
    ffn_gain,
    rel_bias,
    doc_lengths,
    cotangent,
):
    docs, shard_len, width = inputs.shape
    rows_w, hidden_units = w_ffn_in.shape
    tokens = shard_len * SEQ
    half = width // 2
    part = hidden_units // (2 * SEQ)
    blocks = tokens // BLK
    pairs = half // BLK
    parts = part // BLK
    heads = rel_bias.shape[1]
    anywhere = pl.BlockSpec(memory_space=pl.ANY)
    vmem = pl.BlockSpec(memory_space=pltpu.VMEM)
    smem = pl.BlockSpec(memory_space=pltpu.SMEM)
    shape = jax.ShapeDtypeStruct
    narrow = [
        (docs, shard_len, width),
        (rows_w, width),
        (rows_w, width),
        (rows_w, width),
        (rows_w, width),
        (rows_w, hidden_units),
        (2 * part, width),
    ]
    out_shape = (
        shape((8, width), F32),
        shape((8, 2 * BLK), F32),
        shape((8, BLK), F32),
        *(shape(s, BF16) for s in narrow),
        shape((2 * pairs, tokens, tokens), BF16),
    )
    out_part = rows_w // 2

    def sums(count, size, columns):
        return [((count, size // 2, columns), BF16)] * 2 + [((count, size, columns), BF16)] * 4

    scratch = [
        ((SEQ, BLK, width), BF16),
        ((blocks, BLK, width), BF16),
        ((tokens, width), BF16),
        ((width, 3 * half), BF16),
        ((tokens, 3 * half), BF16),
        ((tokens, half), BF16),
        ((half, width), BF16),
        ((SEQ, BLK, width), BF16),
        ((SEQ, BLK, width), BF16),
        ((SEQ, BLK, width), F32),
        ((tokens, width), BF16),
        ((width, SEQ * part), BF16),
        ((SEQ * part, width), BF16),
        ((tokens, SEQ * part), BF16),
        ((tokens, SEQ * part), BF16),
        ((SEQ, BLK, width), F32),
        ((2 * pairs, 5 * BLK, BLK), F32),
        ((3, 24, 2 * BLK), F32),
        ((tokens, BLK), BF16),
        ((16, tokens), F32),
        ((BLK + 16, tokens), BF16),
        ((tokens, 3 * half), BF16),
        ((tokens, half), BF16),
        ((tokens, BLK), F32),
        ((tokens, BLK), F32),
        ((6 * pairs, BLK, BLK), F32),
        ((pairs, 2, 8, tokens), F32),
        ((pairs, width, 3 * BLK), BF16),
        ((parts, SEQ, BLK, width), BF16),
        *sums(parts, BLK, width),
        *sums(SEQ, rows_w, part),
        *sums(pairs, rows_w, 3 * BLK),
        ((SEQ, out_part, width), BF16),
        ((out_part, width), BF16),
        ((out_part, width), BF16),
        ((SEQ + 1, 48, BLK), F32),
        ((8, width), F32),
        ((8, width), F32),
        ((8, SEQ * part), F32),
        ((8, width), F32),
        ((4, 8, width), F32),
        ((40, BLK), F32),
        ((8, 32, BLK), F32),
        ((4, 32, BLK), F32),
        ((BLK, BLK), F32),
    ]
    chunks = parts + SEQ + pairs + 1
    pair_of = lambda *dims: [pltpu.SemaphoreType.DMA(dims)] * 2
    semaphores = (
        pair_of(5)
        + pair_of(4)
        + pair_of(4)
        + pair_of(8, 8)
        + pair_of(4)
        + pair_of(4) * 8
        + pair_of(chunks, 6)
        + pair_of(4)
        + pair_of(chunks, 6)
        + pair_of(4)
        + pair_of(8)
        + pair_of(4)
        + [pltpu.SemaphoreType.DMA((chunks, 3))]
        + [pltpu.SemaphoreType.DMA((2,))]
    )
    results = pl.pallas_call(
        fused_kernel,
        out_shape=out_shape,
        in_specs=[anywhere] * 8 + [vmem, vmem, vmem, smem],
        out_specs=(vmem, vmem, vmem) + (anywhere,) * 8,
        scratch_shapes=[pltpu.VMEM(*s) for s in scratch] + semaphores,
        compiler_params=pltpu.CompilerParams(
            collective_id=0, has_side_effects=True, vmem_limit_bytes=VMEM_LIMIT
        ),
        name="block",
    )(
        inputs,
        cotangent,
        w_query,
        w_key,
        w_value,
        w_out,
        w_ffn_in,
        w_ffn_out,
        attn_gain,
        ffn_gain,
        rel_bias,
        doc_lengths,
    )

    steps = 2

    def rows_spec(s):
        if len(s) == 3:
            return pl.BlockSpec(
                (1, s[1] * s[0] // steps, s[2]),
                lambda i: (i // (steps // s[0]), i % (steps // s[0]), 0),
            )
        return pl.BlockSpec((s[0] // steps, s[1]), lambda i: (i, 0))

    def whole_spec(s):
        return pl.BlockSpec(s, lambda i: (0,) * len(s))

    tiny = [(docs, width), (1, rows_w), (1, rows_w), (8, heads)]
    pooled, one, two, table, gx, gq, gk, gv, go, gi, gd = pl.pallas_call(
        widen_kernel,
        out_shape=[shape(s, F32) for s in tiny + narrow],
        grid=(steps,),
        in_specs=[whole_spec(r.shape) for r in results[:3]] + [rows_spec(s) for s in narrow],
        out_specs=[whole_spec(s) for s in tiny] + [rows_spec(s) for s in narrow],
        compiler_params=pltpu.CompilerParams(vmem_limit_bytes=VMEM_LIMIT),
        name="widen",
    )(*results[:-1])
    return (pooled, gx, gq, gk, gv, go, gi, gd, one[0], two[0], table)


def fits(mesh):
    return mesh.shape["dp"] == CORES * DEPTH and mesh.shape["seq"] == SEQ


def solution(mesh):
    in_specs = (
        P("dp", "seq", None),
        P("seq", None),
        P("seq", None),
        P("seq", None),
        P("seq", None),
        P("seq", None),
        P("seq", None),
        P("seq"),
        P("seq"),
        P("seq", None),
        P("dp"),
        P("dp", "seq", None),
    )
    out_specs = (
        P("dp", None),
        P("dp", "seq", None),
        P("seq", None),
        P("seq", None),
        P("seq", None),
        P("seq", None),
        P("seq", None),
        P("seq", None),
        P("seq"),
        P("seq"),
        P("seq", None),
    )
    return jax.shard_map(
        fused_on_device if fits(mesh) else on_device, mesh=mesh, in_specs=in_specs, out_specs=out_specs, check_vma=False
    )
```

```python
import math

import jax
import jax.numpy as jnp
from jax import lax
from jax.experimental import pallas as pl
from jax.experimental.pallas import tpu as pltpu
from jax.sharding import PartitionSpec as P

EPS = 1e-06
THRESHOLDS = (12, 16, 23, 32, 46, 64, 91)
NEGATIVE = -1000000000.0
GELU_C = math.sqrt(2.0 / math.pi)
GELU_K = 0.044715


def bucket_ids(query_pos, key_pos):
    offset = key_pos[None, :] - query_pos[:, None]
    distance = jnp.abs(offset)
    upper = jnp.where(offset > 0, 16, 0).astype(jnp.int32)
    beyond = jnp.full(distance.shape, 8, jnp.int32)
    for threshold in THRESHOLDS:
        beyond = beyond + (distance >= threshold).astype(jnp.int32)
    return upper + jnp.where(distance < 8, distance, beyond)


def gelu_slope(value):
    inner = GELU_C * (value + GELU_K * value * value * value)
    tangent = jnp.tanh(inner)
    return 0.5 * (1.0 + tangent) + 0.5 * value * (1.0 - tangent * tangent) * GELU_C * (
        1.0 + 3.0 * GELU_K * value * value
    )


def outer_sum(left, right):
    return lax.dot_general(
        left, right, (((0,), (0,)), ((), ())), preferred_element_type=jnp.float32
    )


def back_project(grad, weight):
    return lax.dot_general(
        grad, weight, (((1,), (1,)), ((), ())), preferred_element_type=jnp.float32
    )


def norm_backward(source, scale, gain, grad_normed):
    grad_gain = jnp.sum(grad_normed * source * scale, 0)
    grad_scaled = grad_normed * gain
    grad_source = scale * grad_scaled - source * scale * scale * scale * jnp.mean(
        grad_scaled * source, -1, keepdims=True
    )
    return (grad_gain, grad_source)


SEQ, CORES, DEPTH = 4, 2, 4
BLK = 128
MESH = pl.DeviceIdType.MESH
F32 = jnp.float32
BF16 = jnp.bfloat16
VMEM_LIMIT = 60 << 20


def contract(left, right, left_dim, right_dim):
    return lax.dot_general(
        left, right, (((left_dim,), (right_dim,)), ((), ())), preferred_element_type=F32
    )


def exact(left, right, left_dim, right_dim):
    return lax.dot_general(
        left,
        right,
        (((left_dim,), (right_dim,)), ((), ())),
        preferred_element_type=F32,
        precision=lax.Precision.HIGHEST,
    )


def await_copy(ref, sem):
    pltpu.make_async_copy(ref, ref, sem).wait()


def tile(index, size):
    return pl.ds(pl.multiple_of(index * size, size), size)


def bucket_of(offset):
    distance = jnp.abs(offset)
    beyond = jnp.full(distance.shape, 8, jnp.int32)
    for threshold in THRESHOLDS:
        beyond = beyond + (distance >= threshold).astype(jnp.int32)
    return jnp.where(offset > 0, 16, 0) + jnp.where(distance < 8, distance, beyond)


STEPS = dict(s="start", m="middle", z1="z_one", z2="z_two", z3="z_three", z4="z_four")
SCHEDULE = {
    "gdn2": [("d2", "s"), ("d1", "s")],
    "wd": [],
    "gact": [("d2", "m"), ("d0", "s")],
    "gn": [("d1", "m")],
    "gin0": [],
    "gin1": [],
    "n2": [("i2", "s")],
    "op": [("d1", "z1"), ("d2", "z1"), ("d0", "m")],
    "u0": [("i3", "s")],
    "u1": [("d1", "z2"), ("i2", "m"), ("d2", "z2"), ("i3", "m"), ("d0", "z1"), ("i0", "s")],
    "u2": [("q0", "s"), ("d1", "z3"), ("d0", "z2"), ("i1", "s")],
    "u3": [("d2", "z3"), ("i3", "z1")],
    "u4": [("i0", "m"), ("d0", "z3"), ("q0", "m"), ("i3", "z2"), ("i2", "z1"), ("i1", "m")],
    "u5": [("i0", "z1"), ("i2", "z2"), ("q2", "s")],
    "sw": [],
    "b0": [("q0", "z1"), ("q1", "s"), ("i3", "z3"), ("i0", "z2"), ("i1", "z1"), ("q2", "m"), ("i2", "z3"), ("q0", "z2"), ("d0", "z4"), ("q1", "m"), ("o", "s")],
    "b1": [("d1", "z4"), ("i0", "z3"), ("i1", "z2"), ("q0", "z3"), ("q2", "z1")],
    "g1": [("i3", "z4"), ("q2", "z2"), ("i1", "z3"), ("q1", "z1"), ("i0", "z4"), ("o", "z1"), ("q0", "z4"), ("q1", "z2"), ("q2", "z3"), ("o", "z2"), ("i2", "z4"), ("q1", "z3"), ("gx", "s"), ("sm", "s"), ("q2", "z4"), ("d2", "z4"), ("q1", "z4"), ("i1", "z4"), ("o", "z3"), ("o", "z4")],
    "end": [],
}


def full_sum(value):
    return jnp.sum(jnp.sum(value, 0, keepdims=True), 1, keepdims=True)


def fused_kernel(
    inputs,
    cotangent,
    w_query,
    w_key,
    w_value,
    w_out,
    w_in,
    w_down,
    gain_one,
    gain_two,
    bias_in,
    lengths_in,
    pooled_o,
    small_o,
    table_o,
    gx_o,
    gq_o,
    gk_o,
    gv_o,
    go_o,
    gi_o,
    gd_o,
    raised_o,
    xown,
    grads,
    nrm1,
    wqkv,
    qkv,
    mixed,
    wo,
    psend,
    precv,
    hid,
    nrm2,
    wi,
    wd,
    act,
    slope,
    gn,
    strip,
    vecs,
    maskc,
    gscale,
    flip,
    dqkv,
    gmix,
    dk_acc,
    dv_acc,
    near,
    far,
    gqkv,
    gdn,
    d_dx,
    d_dy,
    d_rx,
    d_ry,
    d_za,
    d_zb,
    i_dx,
    i_dy,
    i_rx,
    i_ry,
    i_za,
    i_zb,
    q_dx,
    q_dy,
    q_rx,
    q_ry,
    q_za,
    q_zb,
    rs_o,
    o_za,
    o_zb,
    small_all,
    wide,
    gains,
    asum,
    pp,
    pool_recv,
    sg,
    sg_plane,
    sg_depth,
    turned,
    small_ss,
    small_rs,
    x_ss,
    x_rs,
    c_ss,
    c_rs,
    wg_ss,
    wg_rs,
    wo_ss,
    wo_rs,
    n1_ss,
    n1_rs,
    g_ss,
    g_rs,
    part_ss,
    part_rs,
    n2_ss,
    n2_rs,
    gn2_ss,
    gn2_rs,
    gat_ss,
    gat_rs,
    gn1_ss,
    gn1_rs,
    gx_ss,
    gx_rs,
    rs_ss,
    rs_rs,
    rso_ss,
    rso_rs,
    z_ss,
    z_rs,
    pool_ss,
    pool_rs,
    sgp_ss,
    sgp_rs,
    sgz_ss,
    sgz_rs,
    out_s,
    raised_s,
):
    dp = lax.axis_index("dp")
    chip = lax.axis_index("seq")
    depth, core = lax.div(dp, 2), lax.rem(dp, 2)
    row, col = lax.div(chip, 2), lax.rem(chip, 2)
    other = (depth * 2 + 1 - core, chip)
    xn = row * 2 + 1 - col
    yn = (1 - row) * 2 + col
    dn = (1 - row) * 2 + 1 - col
    tokens, width = nrm1.shape
    half = width // 2
    rows_w = w_query.shape[0]
    ff_part = gdn.shape[0] * BLK
    quarter, middle_q = tokens // 4, tokens // 2
    middle_w = width // 2

    def remote(src, dst, send, recv, device):
        return pltpu.make_async_remote_copy(
            src_ref=src,
            dst_ref=dst,
            send_sem=send,
            recv_sem=recv,
            device_id=device,
            device_id_type=MESH,
        )

    def ahead(step):
        return lax.rem(chip + step, SEQ)

    pending = []

    def send_now(*args):
        copy = remote(*args)
        copy.start()
        pending.append(copy)

    lane = lax.broadcasted_iota(jnp.int32, (1, BLK), 1)
    wide[...] = jnp.zeros_like(wide)
    wide[0:1, 0:rows_w] = gain_one[...].astype(F32).reshape(1, rows_w)
    wide[1:2, 0:rows_w] = gain_two[...].astype(F32).reshape(1, rows_w)
    turned_gains = pltpu.roll(wide[...], chip * rows_w, 1)
    small_all[0] = jnp.zeros_like(small_all[0])
    for which in range(2):
        for i in range(width // BLK):
            small_all[0, 8 * which + i : 8 * which + i + 1, :] = turned_gains[
                which : which + 1, i * BLK : (i + 1) * BLK
            ]
    small_all[0, 6:7, :] = jnp.where(
        lane == 0, lengths_in[0].astype(F32), lengths_in[1].astype(F32)
    )
    small_all[0, tile(2 + chip, 8), 0 : bias_in.shape[1]] = bias_in[...].astype(F32)

    barrier = pltpu.get_barrier_semaphore()
    for step in range(SEQ):
        if step:
            pl.semaphore_signal(barrier, inc=1, device_id=(dp, ahead(step)), device_id_type=MESH)
        pl.semaphore_signal(
            barrier, inc=1, device_id=(other[0], ahead(step)), device_id_type=MESH
        )
    for step in range(1, DEPTH):
        pl.semaphore_signal(
            barrier,
            inc=1,
            device_id=(lax.rem(depth + step, DEPTH) * 2 + core, chip),
            device_id_type=MESH,
        )
    pl.semaphore_wait(barrier, 2 * SEQ - 1 + DEPTH - 1)

    mine = small_all.at[0]
    for step in range(1, SEQ):
        send_now(
            mine, small_all.at[step], small_ss.at[step], small_rs.at[step], (dp, ahead(step))
        )
    send_now(mine, small_all.at[SEQ], small_ss.at[SEQ], small_rs.at[SEQ], other)

    def spread(source, dest_of, send, recv, action, halves=(0, 1)):
        for doc in (1 - col, col):
            for to in halves:
                block = source.at[doc, pl.ds(to * BLK, BLK)]
                target = core * 2 + doc
                own = (target == chip) & (core == to)
                copy = remote(
                    block,
                    dest_of(to),
                    send.at[doc * 2 + to],
                    recv.at[chip],
                    (depth * 2 + to, target),
                )
                if action == "start":

                    @pl.when(own)
                    def _():
                        pltpu.make_async_copy(block, dest_of(to), recv.at[chip]).start()

                @pl.when(jnp.logical_not(own))
                def _():
                    if action == "start":
                        copy.start()
                    else:
                        copy.wait_send()

    x_slot = lambda to: xown.at[chip]
    c_slot = lambda to: grads.at[chip * 2 + to]

    class Gather:
        def __init__(self, index, pieces, place):
            self.index, self.pieces, self.place = index, pieces, place
            self.bind()

        def half_of(self, owner, which):
            ref = self.place(owner)
            size = ref.shape[0] // 2
            return ref.at[pl.ds(which * size, size)]

        def bind(self):
            k = self.index
            self.local, self.one, self.two = [], [], []
            for src, cut in self.pieces:
                dst = cut(self.place(chip))
                self.local.append(pltpu.make_async_copy(src, dst, wg_rs.at[k, 0]))
                self.one.append(remote(src, dst, wg_ss.at[k, 0], wg_rs.at[k, 1], (dp, xn)))
                self.one.append(remote(src, dst, wg_ss.at[k, 1], wg_rs.at[k, 2], (dp, yn)))
            via_x, via_y = self.half_of(xn, 1), self.half_of(yn, 0)
            self.two = [
                remote(via_x, via_x, wg_ss.at[k, 2], wg_rs.at[k, 3], (dp, yn)),
                remote(via_y, via_y, wg_ss.at[k, 3], wg_rs.at[k, 4], (dp, xn)),
            ]
            self.from_x, self.from_y = self.place(xn), self.place(yn)
            self.last = [self.half_of(dn, 1), self.half_of(dn, 0)]
            self.own = self.place(chip)

        def first(self):
            for copy in self.local + self.one:
                copy.start()

        def second(self):
            k = self.index
            await_copy(self.from_x, wg_rs.at[k, 1])
            self.two[0].start()
            await_copy(self.from_y, wg_rs.at[k, 2])
            self.two[1].start()

        def done(self):
            k = self.index
            await_copy(self.own, wg_rs.at[k, 0])
            await_copy(self.last[0], wg_rs.at[k, 3])
            await_copy(self.last[1], wg_rs.at[k, 4])

        def sent(self):
            k = self.index
            for copy in self.two:
                copy.wait_send()
            await_copy(self.own, wg_ss.at[k, 0])
            await_copy(self.own, wg_ss.at[k, 1])

    class SharedGather(Gather):
        def part(self, owner, which):
            ref = self.place(owner)
            size = ref.shape[0] // 2
            return ref.at[tile(which, size)]

        def bind(self):
            k = self.index
            mine, theirs = lax.rem(depth, 2), 1 - lax.rem(depth, 2)
            beside = ((depth + theirs - mine) * 2 + core, chip)
            self.local, self.one = [], []
            for src, cut in self.pieces:
                size = src.shape[0] // 2
                self.local.append(
                    pltpu.make_async_copy(src, cut(self.place(chip)), wg_rs.at[k, 0])
                )
                dst = cut(self.part(chip, mine))
                src = src.at[tile(mine, size)]
                self.one.append(remote(src, dst, wg_ss.at[k, 0], wg_rs.at[k, 1], (dp, xn)))
                self.one.append(remote(src, dst, wg_ss.at[k, 1], wg_rs.at[k, 2], (dp, yn)))
            self.from_x, self.from_y = self.part(xn, mine), self.part(yn, mine)
            far = self.part(dn, mine)
            size = far.shape[0] // 2
            cut = lambda ref, which: ref.at[pl.ds(which * size, size)]
            via_x, via_y = cut(self.from_x, 1), cut(self.from_y, 0)
            self.last = [cut(far, 1), cut(far, 0)]
            self.two = [
                remote(via_x, via_x, wg_ss.at[k, 2], wg_rs.at[k, 3], (dp, yn)),
                remote(via_y, via_y, wg_ss.at[k, 3], wg_rs.at[k, 4], (dp, xn)),
            ]
            self.beside = [
                remote(ref, ref, wg_ss.at[k, 4 + n], wg_rs.at[k, 5 + n], beside)
                for n, ref in enumerate((self.from_x, self.from_y, far))
            ]
            self.own = self.place(chip)
            self.half = self.part(chip, mine)

        def second(self):
            super().second()
            self.show()

        def forward(self):
            super().second()

        def show(self):
            for copy in self.beside[:2]:
                copy.start()

        def third(self):
            k = self.index
            await_copy(self.last[0], wg_rs.at[k, 3])
            await_copy(self.last[1], wg_rs.at[k, 4])
            self.beside[2].start()

        def done(self):
            await_copy(self.own, wg_rs.at[self.index, 0])
            for copy in self.beside:
                copy.wait_recv()

        def sent(self):
            k = self.index
            for copy in self.two + self.beside:
                copy.wait_send()
            await_copy(self.half, wg_ss.at[k, 0])
            await_copy(self.half, wg_ss.at[k, 1])

    core_cols = tile(core, half)
    whole = lambda ref: ref
    pair_w = 3 * BLK

    def qkv_item(index, pair):
        return SharedGather(
            index,
            [
                (
                    w.at[:, tile(core * 3 + pair, BLK)],
                    lambda ref, i=i: ref.at[:, pl.ds(i * BLK, BLK)],
                )
                for i, w in enumerate((w_query, w_key, w_value))
            ],
            lambda owner: wqkv.at[tile(owner, rows_w), pl.ds(pair * pair_w, pair_w)],
        )

    def in_item(index, part):
        return SharedGather(
            index,
            [
                (
                    w_in.at[:, tile((2 * part + f) * 2 + core, ff_part)],
                    lambda ref, f=f: ref.at[:, pl.ds(f * ff_part, ff_part)],
                )
                for f in range(2)
            ],
            lambda owner: wi.at[tile(owner, rows_w), pl.ds(part * 2 * ff_part, 2 * ff_part)],
        )

    def down_item(kind, index, first, size):
        unit = ff_part // 4
        at = lambda base: pl.ds(pl.multiple_of(base + first * unit, unit), size * unit)
        return kind(
            index, [(w_down.at[at(core * ff_part)], whole)], lambda owner: wd.at[at(owner * ff_part)]
        )

    qkv_items = [qkv_item(i, i) for i in range(3)]
    in_items = [in_item(3, 0), in_item(4, 1)]
    down_items = [
        down_item(SharedGather, 5, 0, 2),
        down_item(Gather, 6, 2, 1),
        down_item(Gather, 7, 3, 1),
    ]
    for it in qkv_items:
        it.first()
    spread(inputs, x_slot, x_ss, x_rs, "start")

    wo_part = rows_w // 2
    wo_src = w_out.at[tile(core, wo_part)]
    wo_dst = wo.at[tile(col * 2 + core, wo_part)]

    def wo_each(action):
        for to in range(SEQ):
            own = (chip == to) & (core == row)
            copy = remote(
                wo_src, wo_dst, wo_ss.at[to], wo_rs.at[col * 2 + core], (depth * 2 + row, to)
            )
            if action == "start":

                @pl.when(own)
                def _():
                    pltpu.make_async_copy(wo_src, wo_dst, wo_rs.at[col * 2 + core]).start()

            @pl.when(jnp.logical_not(own))
            def _():
                if action == "start":
                    copy.start()
                else:
                    copy.wait_send()

    for step in range(1, SEQ + 1):
        await_copy(small_all.at[step], small_rs.at[step])
    summed = small_all[0] + small_all[1] + small_all[2] + small_all[3]
    for which in range(2):
        gains[which : which + 1, :] = jnp.concatenate(
            [summed[8 * which + i : 8 * which + i + 1, :] for i in range(width // BLK)], axis=1
        )
    length_row = jnp.where(row == core, small_all[0, 6:7, :], small_all[SEQ, 6:7, :])
    length = jnp.where(col == 0, length_row[:, 0:1], length_row[:, 1:2])
    own_lengths = small_all[0, 6:7, 0:2]
    table = summed[16:48, :].astype(BF16)
    lane_two = lax.broadcasted_iota(jnp.int32, (1, 2 * BLK), 1)
    minus = jnp.where(lane_two < BLK, lane_two, lane_two - 2 * BLK)
    for off in (-1, 0, 1):
        ids = bucket_of(off * BLK - minus)
        onehot = (lax.broadcasted_iota(jnp.int32, (32, 2 * BLK), 0) == ids).astype(BF16)
        vecs[off + 1] = contract(table, onehot, 0, 0)[0:24, :]

    @pl.loop(0, 6)
    def _(h):
        values = [vecs[i, pl.ds(core * 6 + h, 1), :] for i in range(3)]
        left = jnp.broadcast_to(values[0][:, BLK - 1 : BLK], (BLK, BLK))
        right = jnp.broadcast_to(values[2][:, BLK + 1 : BLK + 2], (BLK, BLK))
        strip[h, 0:BLK, :] = left
        strip[h, 4 * BLK :, :] = right
        for i in range(3):
            skewed = pltpu.roll(
                jnp.broadcast_to(values[i], (BLK, 2 * BLK)), 0, 1, stride=1, stride_axis=0
            )
            strip[h, (i + 1) * BLK : (i + 2) * BLK, :] = skewed[:, :BLK]

    key_pos = lax.broadcasted_iota(jnp.int32, maskc.shape, 0).astype(F32)
    maskc[...] = jnp.where((key_pos < length) | (lane > 0), 0.0, NEGATIVE).astype(BF16)

    def block_valid(b):
        pos = lax.broadcasted_iota(jnp.int32, (BLK, 1), 0) + b * BLK
        return (pos.astype(F32) < length).astype(F32)

    for it in qkv_items:
        it.second()

    def n1_copy(i):
        block = nrm1.at[tile(2 * i + core, BLK)]
        return remote(block, block, n1_ss.at[i], n1_rs.at[i], other)

    @pl.loop(0, SEQ)
    def _(i):
        await_copy(xown.at[i], x_rs.at[i])
        source = xown[i].astype(F32)
        scale = lax.rsqrt(jnp.mean(source * source, -1, keepdims=True) + EPS)
        nrm1[tile(2 * i + core, BLK), :] = (source * scale * gains[0:1, :]).astype(BF16)
        n1_copy(i).start()

    for it in in_items:
        it.first()
    for it in qkv_items:
        it.third()
    for i in range(SEQ):
        n1_copy(i).wait_recv()
    in_items[0].second()
    spread(cotangent, c_slot, c_ss, c_rs, "start", (0,))

    flip[BLK : BLK + 16, :] = jnp.ones((16, tokens), BF16)
    mine_lanes = [lane < 64, lane >= 64]
    slots = [ref.at[:, pl.ds(0, tokens)] for ref in (act, slope)]

    def by_head(value):
        return jnp.concatenate(
            [jnp.where(lanes, value, jnp.zeros_like(value)) for lanes in mine_lanes], axis=0
        )

    def serve(now, table):
        for when, actions in table.items():

            @pl.when(now == when)
            def _():
                for action in actions:
                    action()

    def keep(pair, qb):
        return pltpu.make_async_copy(slots[qb], raised_o.at[2 * pair + qb], raised_s.at[qb])

    def fetch(pair, qb):
        return pltpu.make_async_copy(raised_o.at[2 * pair + qb], slots[qb], raised_s.at[qb])

    def later_inputs():
        down_items[0].first()
        spread(cotangent, c_slot, c_ss, c_rs, "start", (1,))

    forward_table = {
        0: [in_items[1].second, lambda: wo_each("start")],
        1: [in_items[0].third, later_inputs],
        3: [in_items[1].third],
    }

    @pl.loop(0, 3)
    def _(pair):
        cols = tile(pair, BLK)
        for p in range(3):

            @pl.when(pair == p)
            def _():
                qkv_items[p].done()

        qkv[:, tile(pair, pair_w)] = contract(
            nrm1[...], wqkv[:, tile(pair, pair_w)], 1, 0
        ).astype(BF16)
        flip[0:BLK, :] = jnp.transpose(qkv[:, tile(3 * pair + 2, BLK)])
        keys = jnp.concatenate([qkv[:, tile(3 * pair + 1, BLK)], maskc[...]], axis=1)
        for qb in range(2):
            rows = pl.ds(qb * middle_q, middle_q)
            queries = by_head(qkv[rows, tile(3 * pair, BLK)])
            flag = jnp.broadcast_to(jnp.where(lane == 0, 1.0, 0.0).astype(BF16), queries.shape)
            biases = [
                jnp.concatenate(
                    [
                        strip[
                            pair * 2 + h, pl.ds((min(max(kb - q, -2), 2) + 2) * BLK, BLK), :
                        ]
                        for kb in range(tokens // BLK)
                    ],
                    axis=0,
                )
                for h in range(2)
                for q in range(qb * middle_q // BLK, (qb + 1) * middle_q // BLK)
            ]
            logits = contract(keys, jnp.concatenate([queries, flag], axis=1), 1, 1)
            logits = logits + jnp.concatenate(biases, axis=1)
            highest = jnp.max(logits, 0, keepdims=True)
            raised = jnp.exp(logits - highest).astype(BF16)

            @pl.when(pair > 0)
            def _():
                keep(pair - 1, qb).wait()

            slots[qb][...] = raised
            keep(pair, qb).start()
            result = contract(flip[...], raised, 1, 0)
            inverse = 1.0 / result[BLK : BLK + 1, :]
            scaled = result[0:BLK, :] * inverse
            mixed[rows, cols] = jnp.transpose(
                jnp.concatenate([scaled[0:64, 0:middle_q], scaled[64:BLK, middle_q:]], axis=0)
            ).astype(BF16)
            for h in range(2):
                gscale[pl.ds(2 * pair + h, 1), rows] = inverse[:, h * middle_q : (h + 1) * middle_q]
            serve(2 * pair + qb, forward_table)

    def swap_copy(i, send, recv):
        return remote(psend.at[i], precv.at[i], send.at[i], recv.at[i], other)

    for k in range(4):
        await_copy(wo.at[pl.ds(k * wo_part, wo_part)], wo_rs.at[k])

    def blocks_of(ref, parity):
        return jnp.concatenate(
            [ref[tile(2 * i + parity, BLK), :] for i in range(SEQ)], axis=0
        )

    def swap_out(result, send, recv):
        for i in range(SEQ):
            psend[i] = result[i * BLK : (i + 1) * BLK, :].astype(BF16)
            swap_copy(i, send, recv).start()

    swap_out(contract(blocks_of(mixed, 1 - core), wo[...], 1, 0), part_ss, part_rs)

    def n2_copy(i, send, recv):
        block = nrm2.at[tile(2 * i + core, BLK)]
        return remote(block, block, send.at[i], recv.at[i], other)

    pp[...] = jnp.zeros_like(pp)
    result = contract(blocks_of(mixed, core), wo[...], 1, 0)
    for i in range(SEQ):
        hidden = xown[i].astype(F32) + result[i * BLK : (i + 1) * BLK, :]
        swap_copy(i, part_ss, part_rs).wait_recv()
        hidden = hidden + precv[i].astype(F32)
        hid[i] = hidden
        scale = lax.rsqrt(jnp.mean(hidden * hidden, -1, keepdims=True) + EPS)
        nrm2[tile(2 * i + core, BLK), :] = (hidden * scale * gains[1:2, :]).astype(BF16)
        n2_copy(i, n2_ss, n2_rs).start()
        pp[0:1, :] += jnp.sum(hidden * block_valid(2 * i + core), 0, keepdims=True)
    down_items[0].second()
    for it in down_items[1:]:
        it.first()
    for i in range(SEQ):
        n2_copy(i, n2_ss, n2_rs).wait_recv()
    for qb in range(2):
        keep(2, qb).wait()

    def g_copy(i):
        block = grads.at[2 * i + core]
        return remote(block, block, g_ss.at[i], g_rs.at[i], other)

    def take_cotangent():
        @pl.loop(0, SEQ)
        def _(i):
            b = 2 * i + core
            await_copy(grads.at[b], c_rs.at[i])
            grads[b] = (grads[b].astype(F32) * block_valid(b)).astype(BF16)
            g_copy(i).start()

    asum[...] = jnp.zeros_like(asum)
    wide_part = 2 * ff_part
    for part in range(2):
        part_cols = slice(part * wide_part, (part + 1) * wide_part)
        if part == 1:
            take_cotangent()
            down_items[0].third()
        in_items[part].done()

        @pl.loop(0, 2)
        def _(i):
            rows = tile(i, middle_q)
            value = contract(nrm2[rows, :], wi[:, part_cols], 1, 0)
            square = value * value
            tangent = jnp.tanh(value * (GELU_C + GELU_C * GELU_K * square))
            half_up = 0.5 + 0.5 * tangent
            active = (value * half_up).astype(BF16)
            act[rows, part_cols] = active
            slope[rows, part_cols] = (
                half_up
                + value
                * (1.0 - tangent * tangent)
                * (0.5 * GELU_C + 1.5 * GELU_C * GELU_K * square)
            ).astype(BF16)
            pos = lax.broadcasted_iota(jnp.int32, (8, middle_q), 1) + i * middle_q
            valid = (pos.astype(F32) < length).astype(BF16)
            asum[:, part_cols] += contract(valid, active, 1, 0)


    for i in range(SEQ):
        g_copy(i).wait_recv()
    g_all = lambda: grads[...].reshape(tokens, width)

    class Chunk:
        made = 0

        def __init__(self, src, dx, dy, rx, ry, za, zb, outs):
            self.index = Chunk.made
            Chunk.made += 1
            self.src, self.dx, self.dy, self.rx, self.ry = src, dx, dy, rx, ry
            self.za, self.zb, self.outs = za, zb, outs
            self.bind()

        def bind(self):
            k = self.index
            size = self.dx.shape[0]
            cut = lambda ref, which: ref.at[pl.ds(which * size, size)]
            ss, rs = (lambda i: rs_ss.at[k, i]), (lambda i: rs_rs.at[k, i])
            to_x, to_y = (dp, xn), (dp, yn)
            self.one = [
                remote(cut(self.src(dn), 1), self.dx, ss(0), rs(0), to_x),
                remote(cut(self.src(dn), 0), self.dy, ss(1), rs(1), to_y),
                remote(cut(self.src(xn), 1), cut(self.rx, 1), ss(2), rs(2), to_x),
                remote(cut(self.src(yn), 0), cut(self.ry, 0), ss(3), rs(3), to_y),
            ]
            self.sum_y, self.sum_x = cut(self.src(yn), 1), cut(self.src(xn), 0)
            self.two = [
                remote(self.sum_y, cut(self.ry, 1), ss(4), rs(4), to_y),
                remote(self.sum_x, cut(self.rx, 0), ss(5), rs(5), to_x),
            ]
            self.bind_z(self.rx, self.ry)

        def bind_z(self, reduced, final):
            k = self.index
            self.reduced, self.final = reduced, final
            sem = lambda i: (z_ss.at[k, i], z_rs.at[k, i])
            self.to_inner = remote(reduced, self.za, *sem(0), z_dev(toward))
            self.swap = remote(reduced, self.zb, *sem(1), z_dev(across))
            self.to_end = remote(final, final, *sem(2), z_dev(outward))

        def start(self):
            for copy in self.one:
                copy.start()

        def middle(self):
            for at, sent, sums, copy in (
                (0, self.dx, self.sum_y, self.two[0]),
                (1, self.dy, self.sum_x, self.two[1]),
            ):
                self.one[at].wait_recv()
                sums[...] = (sums[...].astype(F32) + sent[...].astype(F32)).astype(BF16)
                copy.start()

        def total(self):
            for copy in (self.one[2], self.one[3], *self.two):
                copy.wait_recv()
            self.rx[...] = (
                self.src(chip)[...].astype(F32)
                + self.rx[...].astype(F32)
                + self.ry[...].astype(F32)
            ).astype(BF16)

        def z_one(self):
            self.total()

            @pl.when(end_z)
            def _():
                self.to_inner.start()

        def z_two(self):
            @pl.when(inner_z)
            def _():
                self.to_inner.wait_recv()
                self.reduced[...] = (
                    self.reduced[...].astype(F32) + self.za[...].astype(F32)
                ).astype(BF16)
                self.swap.start()

        def z_three(self):
            @pl.when(inner_z)
            def _():
                self.swap.wait_recv()
                self.final[...] = (
                    self.reduced[...].astype(F32) + self.zb[...].astype(F32)
                ).astype(BF16)
                self.to_end.start()

        def each_out(self, act_on):
            k = self.index
            for n, (cols, place) in enumerate(self.outs):
                src = self.final if cols is None else self.final.at[:, cols]
                act_on(
                    remote(src, place(core), z_ss.at[k, 3 + n], z_rs.at[k, 3 + n], other),
                    pltpu.make_async_copy(src, place(core), out_s.at[k, n]),
                )

        def z_four(self):
            @pl.when(end_z)
            def _():
                self.to_end.wait_recv()

            self.each_out(lambda there, here: (there.start(), here.start()))

        def finish(self):
            self.each_out(
                lambda there, here: (there.wait_recv(), there.wait_send(), here.wait())
            )

            @pl.when(end_z)
            def _():
                self.to_inner.wait_send()

            @pl.when(inner_z)
            def _():
                self.swap.wait_send()
                self.to_end.wait_send()

            for copy in self.plane_sends():
                copy.wait_send()

        def plane_sends(self):
            return self.one + self.two

    inner_z = (depth == 1) | (depth == 2)
    end_z = jnp.logical_not(inner_z)
    toward = jnp.where(depth == 0, 1, 2)
    outward = jnp.where(depth == 1, 0, 3)
    across = jnp.where(depth == 1, 2, 1)

    def z_dev(z):
        return (z * 2 + core, chip)

    d_chunks = [
        Chunk(
            lambda owner, i=i: gdn.at[i, owner],
            d_dx.at[i],
            d_dy.at[i],
            d_rx.at[i],
            d_ry.at[i],
            d_za.at[i],
            d_zb.at[i],
            [
                (
                    None,
                    lambda c, i=i: gd_o.at[
                        pl.ds(pl.multiple_of(c * ff_part + i * BLK, BLK), BLK)
                    ],
                )
            ],
        )
        for i in range(ff_part // BLK)
    ]

    i_chunks = [
        Chunk(
            lambda owner, f=f: wi.at[tile(owner, rows_w), pl.ds(f * ff_part, ff_part)],
            i_dx.at[f],
            i_dy.at[f],
            i_rx.at[f],
            i_ry.at[f],
            i_za.at[f],
            i_zb.at[f],
            [(None, lambda c, f=f: gi_o.at[:, tile(2 * f + c, ff_part)])],
        )
        for f in range(SEQ)
    ]
    q_chunks = [
        Chunk(
            lambda owner, p=p: gqkv.at[p, tile(owner, rows_w)],
            q_dx.at[p],
            q_dy.at[p],
            q_rx.at[p],
            q_ry.at[p],
            q_za.at[p],
            q_zb.at[p],
            [
                (
                    pl.ds(j * BLK, BLK),
                    lambda c, p=p, o=o: o.at[:, tile(c * 3 + p, BLK)],
                )
                for j, o in enumerate((gq_o, gk_o, gv_o))
            ],
        )
        for p in range(3)
    ]
    def rso_each(action):
        for k in range(2):
            for to in range(2):
                target = core * 2 + k
                own = (chip == target) & (core == to)
                src = wo.at[pl.ds((2 * k + to) * wo_part, wo_part)]
                dst = rs_o.at[chip]
                copy = remote(
                    src, dst, rso_ss.at[2 * k + to], rso_rs.at[chip], (depth * 2 + to, target)
                )
                if action == "start":

                    @pl.when(own)
                    def _():
                        pltpu.make_async_copy(src, dst, rso_rs.at[chip]).start()

                @pl.when(jnp.logical_not(own))
                def _():
                    if action == "start":
                        copy.start()
                    else:
                        copy.wait_send()

    class OutChunk(Chunk):
        def bind(self):
            self.bind_z(self.src.at[0], self.src.at[1])

        def total(self):
            for i in range(SEQ):
                await_copy(self.src.at[i], rso_rs.at[i])
            value = self.src[0].astype(F32)
            for i in range(1, SEQ):
                value = value + self.src[i].astype(F32)
            self.reduced[...] = value.astype(BF16)

        def plane_sends(self):
            return []

    o_chunk = OutChunk(
        rs_o, None, None, None, None, o_za, o_zb, [(None, lambda c: go_o.at[tile(c, wo_part)])]
    )
    def gx_each(i, action):
        own = (chip == i) & (core == row)
        dst = gx_o.at[col, tile(core, BLK)]
        copy = remote(
            nrm2.at[pl.ds(i * BLK, BLK)], dst, gx_ss.at[i], gx_rs.at[col * 2 + core], (depth * 2 + row, i)
        )
        if action == "start":

            @pl.when(own)
            def _():
                pltpu.make_async_copy(nrm2.at[pl.ds(i * BLK, BLK)], dst, gx_rs.at[col * 2 + core]).start()

        @pl.when(jnp.logical_not(own))
        def _():
            if action == "start":
                copy.start()
            else:
                copy.wait_send()

    def sgz_copy(step):
        return remote(
            sg_depth.at[depth],
            sg_depth.at[depth],
            sgz_ss.at[step],
            sgz_rs.at[depth],
            z_dev(lax.rem(depth + step, DEPTH)),
        )

    def small_along_z():
        for i in range(8):
            await_copy(sg_plane.at[i], sgp_rs.at[i])
        total = sg_plane[0]
        for i in range(1, 8):
            total = total + sg_plane[i]
        sg_depth[depth] = total
        for step in range(1, DEPTH):
            sgz_copy(step).start()

    by_name = dict(
        [(f"d{i}", c) for i, c in enumerate(d_chunks)]
        + [(f"i{i}", c) for i, c in enumerate(i_chunks)]
        + [(f"q{i}", c) for i, c in enumerate(q_chunks)]
        + [("o", o_chunk)]
    )

    def after(block):
        for name, step in SCHEDULE[block]:
            if name == "gx":
                for i in range(SEQ):
                    gx_each(i, "start")
            elif name == "sm":
                small_along_z()
            elif name == "o" and step == "s":
                rso_each("start")
            else:
                getattr(by_name[name], STEPS[step])()

    for it in down_items[1:]:
        it.second()
    for i in range(ff_part // BLK):
        columns = jnp.concatenate(
            [act[:, f * ff_part + i * BLK : f * ff_part + (i + 1) * BLK] for f in range(SEQ)],
            axis=1,
        )
        gdn[i] = contract(columns, g_all(), 0, 0).astype(BF16).reshape(SEQ, BLK, width)
    after("gdn2")
    for it in down_items:
        it.done()
    for it in in_items:
        it.sent()
    after("wd")

    def pooled_part(cols):
        total = asum[0:1, cols]
        high = total.astype(BF16)
        rest = total - high.astype(F32)
        middle = rest.astype(BF16)
        low = (rest - middle.astype(F32)).astype(BF16)
        pieces = jnp.concatenate(
            [jnp.broadcast_to(piece, (16, piece.shape[1])) for piece in (high, middle, low)], axis=0
        )
        result = contract(pieces, wd[cols, :], 1, 0)
        pp[0:1, :] += result[0:1, :] + result[16:17, :] + result[32:33, :]

    for part in range(2):
        part_cols = slice(part * wide_part, (part + 1) * wide_part)

        @pl.loop(0, 2)
        def _(i):
            rows = tile(i, middle_q)
            upstream = grads[pl.ds(4 * i, 4)].reshape(middle_q, width)
            grad = contract(upstream, wd[part_cols, :], 1, 1) * slope[rows, part_cols].astype(F32)
            slope[rows, part_cols] = grad.astype(BF16)

        pooled_part(part_cols)

    after("gact")

    for i in range(SEQ):
        swap_copy(i, part_ss, part_rs).wait_send()
    swap_out(contract(blocks_of(slope, 1 - core), wi[...], 1, 1), gn2_ss, gn2_rs)
    gn[...] = contract(blocks_of(slope, core), wi[...], 1, 1).reshape(SEQ, BLK, width)
    after("gn")
    for part in range(2):
        part_cols = slice(part * wide_part, (part + 1) * wide_part)

        @pl.loop(0, width // (2 * BLK))
        def _(i):
            wi[tile(i, 2 * BLK), part_cols] = contract(
                nrm2[:, tile(i, 2 * BLK)], slope[:, part_cols], 0, 0
            ).astype(BF16)

        after(f"gin{part}")
    def pool_each(action):
        for to in range(SEQ):
            own = (chip == to) & (core == row)
            dst = pool_recv.at[col * 2 + core]
            copy = remote(pp, dst, pool_ss.at[to], pool_rs.at[col * 2 + core], (depth * 2 + row, to))
            if action == "start":

                @pl.when(own)
                def _():
                    pltpu.make_async_copy(pp, dst, pool_rs.at[col * 2 + core]).start()

            @pl.when(jnp.logical_not(own))
            def _():
                if action == "start":
                    copy.start()
                else:
                    copy.wait_send()

    def gat_copy(i):
        block = act.at[tile(2 * i + core, BLK), pl.ds(0, width)]
        return remote(block, block, gat_ss.at[i], gat_rs.at[i], other)

    for i in range(SEQ):
        n2_copy(i, n2_ss, n2_rs).wait_send()
    sg[...] = jnp.zeros_like(sg)

    def add_gain(first, value):
        for i in range(width // BLK):
            sg[first + i : first + i + 1, :] += value[:, i * BLK : (i + 1) * BLK]

    @pl.loop(0, SEQ)
    def _(i):
        b = 2 * i + core
        swap_copy(i, gn2_ss, gn2_rs).wait_recv()
        normed = gn[i] + precv[i].astype(F32)
        hidden = hid[i]
        scale = lax.rsqrt(jnp.mean(hidden * hidden, -1, keepdims=True) + EPS)
        add_gain(8, jnp.sum(normed * hidden * scale, 0, keepdims=True))
        scaled = normed * gains[1:2, :]
        inner = jnp.mean(scaled * hidden, -1, keepdims=True)
        result = grads[b].astype(F32) + scale * scaled - hidden * (scale * scale * scale) * inner
        hid[i] = result
        act[tile(b, BLK), 0:width] = result.astype(BF16)
        gat_copy(i).start()

    pool_each("start")
    after("n2")
    for i in range(SEQ):
        gat_copy(i).wait_recv()

    @pl.loop(0, 2)
    def _(i):
        rows = tile(i, middle_q)
        inverse = jnp.concatenate(
            [
                jnp.transpose(
                    jnp.concatenate(
                        [
                            jnp.broadcast_to(gscale[2 * p + h : 2 * p + h + 1, rows], (64, middle_q))
                            for h in range(2)
                        ],
                        axis=0,
                    )
                )
                for p in range(3)
            ],
            axis=1,
        )
        gmix[rows, :] = (contract(act[rows, 0:width], wo[...], 1, 1) * inverse).astype(BF16)

    wo[...] = contract(mixed[...], act[:, 0:width], 0, 0).astype(BF16)
    for i in range(SEQ):
        gat_copy(i).wait_send()
    for qb in range(2):
        fetch(0, qb).start()
    after("op")


    sub = lax.broadcasted_iota(jnp.int32, (16, tokens), 0)
    key_block = lax.div(lax.broadcasted_iota(jnp.int32, (16, tokens), 1), BLK)
    flip[BLK : BLK + 16, :] = (sub == key_block).astype(BF16)
    near[...] = jnp.zeros_like(near)
    far[...] = jnp.zeros_like(far)

    backward_table = {i: [lambda i=i: after(f"u{i}")] for i in range(6)}

    @pl.loop(0, 3)
    def _(pair):
        cols = tile(pair, BLK)
        flip[0:BLK, :] = jnp.transpose(qkv[:, tile(3 * pair + 1, BLK)])
        for qb in range(2):
            rows = pl.ds(qb * middle_q, middle_q)
            upstream = gmix[rows, cols]
            masked = by_head(upstream)
            queries = by_head(qkv[rows, tile(3 * pair, BLK)])
            product = jnp.transpose(upstream.astype(F32) * mixed[rows, cols].astype(F32))
            inner = jnp.concatenate(
                [jnp.sum(product[64 * h : 64 * h + 64, :], 0, keepdims=True) for h in range(2)],
                axis=1,
            )
            fetch(pair, qb).wait()
            raised = slots[qb][...]
            grad_probs = contract(qkv[:, tile(3 * pair + 2, BLK)], masked, 1, 1)
            grad_logits = (raised.astype(F32) * (grad_probs - inner)).astype(BF16)
            grad_values = contract(raised, masked, 1, 0)
            grad_keys = contract(grad_logits, queries, 1, 0)
            if qb == 0:
                dv_acc[...] = grad_values
                dk_acc[...] = grad_keys
            else:
                dv_acc[...] += grad_values
                dk_acc[...] += grad_keys
            result = contract(flip[...], grad_logits, 1, 0)
            dqkv[rows, tile(3 * pair, BLK)] = jnp.transpose(
                jnp.concatenate([result[0:64, 0:middle_q], result[64:BLK, middle_q:]], axis=0)
            ).astype(BF16)
            sums = result[BLK : BLK + 8, :]
            block_row = lax.broadcasted_iota(jnp.int32, sums.shape, 0)
            block_col = lax.rem(
                lax.div(lax.broadcasted_iota(jnp.int32, sums.shape, 1), BLK), middle_q // BLK
            )
            gap = block_row - block_col - qb * (middle_q // BLK)
            far[pair, 0] += jnp.where(gap <= -2, sums, 0.0)
            far[pair, 1] += jnp.where(gap >= 2, sums, 0.0)
            for h in range(2):
                for off in range(3):
                    total = near[(pair * 2 + h) * 3 + off]
                    for i in range(middle_q // BLK):
                        kb = qb * (middle_q // BLK) + i + off - 1
                        if 0 <= kb < tokens // BLK:
                            first = h * middle_q + i * BLK
                            total = total + grad_logits[
                                kb * BLK : (kb + 1) * BLK, first : first + BLK
                            ].astype(F32)
                    near[(pair * 2 + h) * 3 + off] = total

            @pl.when(pair < 2)
            def _():
                fetch(pair + 1, qb).start()

            if qb == 1:
                dqkv[:, tile(3 * pair + 1, BLK)] = dk_acc[...].astype(BF16)
                dqkv[:, tile(3 * pair + 2, BLK)] = dv_acc[...].astype(BF16)
                right = dqkv[:, tile(pair, pair_w)]

                @pl.loop(0, width // middle_w)
                def _(i):
                    gqkv[pair, tile(i, middle_w), :] = contract(
                        nrm1[:, tile(i, middle_w)], right, 0, 0
                    ).astype(BF16)

            serve(2 * pair + qb, backward_table)

    for i in range(SEQ):
        swap_copy(i, gn2_ss, gn2_rs).wait_send()

    swap_out(contract(blocks_of(dqkv, 1 - core), wqkv[...], 1, 1), gn1_ss, gn1_rs)
    diag_row = lax.broadcasted_iota(jnp.int32, (BLK, BLK), 0)
    diag_col = lax.broadcasted_iota(jnp.int32, (BLK, BLK), 1)
    upper = diag_col >= diag_row
    mirror = (diag_row + diag_col == BLK - 1).astype(F32)
    shift = lax.broadcasted_iota(jnp.int32, (1, BLK), 1) + 1
    shift = jnp.where(shift == BLK, 0, shift)
    ids = bucket_of(jnp.concatenate([-shift, BLK - shift], axis=1))
    onehot = (lax.broadcasted_iota(jnp.int32, (BLK, 2 * BLK), 0) == ids).astype(F32)

    def bias_head(h):
        def skew(x):
            return pltpu.roll(exact(mirror, x, 1, 0), 0, 1, stride=1, stride_axis=0)

        def far_of(h, side):
            both = far[lax.div(h, 2), side]
            return jnp.where(lax.rem(h, 2) == 0, both[:, 0:middle_q], both[:, middle_q:])

        tiles = [near[h * 3 + i] for i in range(3)]
        at = [
            jnp.sum(
                skew(jnp.where(upper, tiles[i + 1], 0.0) + jnp.where(upper, 0.0, tiles[i])),
                0,
                keepdims=True,
            )
            for i in range(2)
        ]
        below = full_sum(jnp.where(upper, tiles[0], 0.0)) + full_sum(far_of(h, 0))
        above = full_sum(jnp.where(upper, 0.0, tiles[2])) + full_sum(far_of(h, 1))
        sums = exact(jnp.broadcast_to(jnp.concatenate(at, axis=1), (8, 2 * BLK)), onehot, 1, 1)
        sums = sums[0:1, :] + jnp.where(lane == 15, below, 0.0) + jnp.where(lane == 31, above, 0.0)
        sg[pl.ds(16 + core * 6 + h, 1), :] = sums

    after("sw")

    @pl.loop(0, 3)
    def _(h):
        bias_head(h)

    after("b0")

    @pl.loop(3, 6)
    def _(h):
        bias_head(h)

    after("b1")
    both = contract(blocks_of(dqkv, core), wqkv[...], 1, 1)
    for i in range(SEQ):
        swap_copy(i, gn1_ss, gn1_rs).wait_recv()
        normed = both[i * BLK : (i + 1) * BLK, :] + precv[i].astype(F32)
        source = xown[i].astype(F32)
        scale = lax.rsqrt(jnp.mean(source * source, -1, keepdims=True) + EPS)
        add_gain(0, jnp.sum(normed * source * scale, 0, keepdims=True))
        scaled = normed * gains[0:1, :]
        inner = jnp.mean(scaled * source, -1, keepdims=True)
        result = hid[i] + scale * scaled - source * (scale * scale * scale) * inner
        nrm2[i * BLK : (i + 1) * BLK, :] = result.astype(BF16)

    place = core * SEQ + chip
    sg_sent = sg.at[pl.ds(0, sg_plane.shape[1])]

    def sgp_each(action):
        for step in range(SEQ):
            for cross in range(2):
                if step == 0 and cross == 0:
                    continue
                to_core = lax.rem(core + cross, 2)
                copy = remote(
                    sg_sent,
                    sg_plane.at[place],
                    sgp_ss.at[step * 2 + cross],
                    sgp_rs.at[place],
                    (depth * 2 + to_core, ahead(step)),
                )
                if action == "start":
                    copy.start()
                else:
                    copy.wait_send()

    sgp_each("start")
    pltpu.make_async_copy(sg_sent, sg_plane.at[place], sgp_rs.at[place]).start()
    for copy in pending:
        copy.wait_send()
    spread(inputs, x_slot, x_ss, x_rs, "wait")
    spread(cotangent, c_slot, c_ss, c_rs, "wait")
    for it in qkv_items + down_items:
        it.sent()
    wo_each("wait")
    after("g1")
    after("end")
    for i in range(4):
        await_copy(pool_recv.at[i], pool_rs.at[i])
    for doc in range(2):
        pooled_o[doc : doc + 1, :] = (
            pool_recv[2 * doc, 0:1, :] + pool_recv[2 * doc + 1, 0:1, :]
        ) / own_lengths[:, doc : doc + 1]
    for step in range(1, DEPTH):
        z = lax.rem(depth + DEPTH - step, DEPTH)
        await_copy(sg_depth.at[z], sgz_rs.at[z])
    total = sg_depth[0] + sg_depth[1] + sg_depth[2] + sg_depth[3]
    for which in range(2):
        wide[which : which + 1, :] = jnp.concatenate(
            [total[8 * which + i : 8 * which + i + 1, :] for i in range(width // BLK)], axis=1
        )
    small_o[...] = pltpu.roll(wide[...], lax.rem(width - chip * rows_w, width), 1)[:, : small_o.shape[1]]
    turned[:, 0:16] = jnp.transpose(total[16:32, :])
    table_o[...] = turned[tile(chip, 8), :]

    for i in range(4):
        await_copy(gx_o.at[i // 2, pl.ds((i % 2) * BLK, BLK)], gx_rs.at[i])
    pool_each("wait")
    rso_each("wait")
    sgp_each("wait")
    for i in range(SEQ):
        n1_copy(i).wait_send()
        g_copy(i).wait_send()
        swap_copy(i, gn1_ss, gn1_rs).wait_send()
        gx_each(i, "wait")
    for step in range(1, DEPTH):
        sgz_copy(step).wait_send()
    for chunk in (*d_chunks, *i_chunks, o_chunk, *q_chunks):
        chunk.finish()


def widen_kernel(pooled, small, table, gx, gq, gk, gv, go, gi, gd, *outs):
    pooled_out, one_out, two_out, table_out, *outs = outs
    pooled_out[...] = pooled[0 : pooled_out.shape[0], :]
    one_out[...] = small[0:1, : one_out.shape[1]]
    two_out[...] = small[1:2, : two_out.shape[1]]
    table_out[...] = table[:, : table_out.shape[1]]
    for value, out in zip((gx, gq, gk, gv, go, gi, gd), outs):
        out[...] = value[...].astype(F32)


def on_device(
    inputs,
    w_query,
    w_key,
    w_value,
    w_out,
    w_ffn_in,
    w_ffn_out,
    attn_gain,
    ffn_gain,
    rel_bias,
    doc_lengths,
    cotangent,
):
    blocks, shard_len, width = inputs.shape
    heads = rel_bias.shape[1]
    head_dim = width // heads
    full_len = shard_len * lax.axis_size("seq")
    total_rows = blocks * shard_len
    gathered = (
        lax.all_gather(w_query, "seq", axis=0, tiled=True),
        lax.all_gather(w_key, "seq", axis=0, tiled=True),
        lax.all_gather(w_value, "seq", axis=0, tiled=True),
        lax.all_gather(w_out, "seq", axis=0, tiled=True),
        lax.all_gather(w_ffn_in, "seq", axis=0, tiled=True),
        lax.all_gather(w_ffn_out, "seq", axis=0, tiled=True),
        lax.all_gather(attn_gain, "seq", axis=0, tiled=True),
        lax.all_gather(ffn_gain, "seq", axis=0, tiled=True),
        lax.all_gather(rel_bias, "seq", axis=0, tiled=True),
    )
    (
        full_query,
        full_key,
        full_value,
        full_out,
        full_in,
        full_down,
        gain_one,
        gain_two,
        bias_table,
    ) = gathered
    gain_one = gain_one.astype(jnp.float32)
    gain_two = gain_two.astype(jnp.float32)
    bucket_range = jnp.arange(bias_table.shape[0], dtype=jnp.int32)
    query_pos = lax.axis_index("seq") * shard_len + jnp.arange(shard_len, dtype=jnp.int32)
    key_pos = jnp.arange(full_len, dtype=jnp.int32)
    onehot = (bucket_ids(query_pos, key_pos)[:, :, None] == bucket_range).astype(jnp.bfloat16)
    bias_heads = jnp.einsum("qkn,nh->hqk", onehot, bias_table, preferred_element_type=jnp.float32)
    key_valid = key_pos[None, :] < doc_lengths[:, None]
    query_valid = (query_pos[None, :] < doc_lengths[:, None]).astype(jnp.float32)
    flat = inputs.astype(jnp.float32).reshape(total_rows, width)
    scale_one = lax.rsqrt(jnp.mean(flat * flat, -1, keepdims=True) + EPS)
    normed_one = (flat * scale_one * gain_one).astype(jnp.bfloat16)
    queries = jnp.dot(normed_one, full_query, preferred_element_type=jnp.float32).astype(
        jnp.bfloat16
    )
    keys_local = jnp.dot(normed_one, full_key, preferred_element_type=jnp.float32).astype(
        jnp.bfloat16
    )
    values_local = jnp.dot(normed_one, full_value, preferred_element_type=jnp.float32).astype(
        jnp.bfloat16
    )
    queries_heads = queries.reshape(blocks, shard_len, heads, head_dim)
    keys_all, values_all = (
        lax.all_gather(keys_local.reshape(blocks, shard_len, width), "seq", axis=1, tiled=True),
        lax.all_gather(values_local.reshape(blocks, shard_len, width), "seq", axis=1, tiled=True),
    )
    scores = jnp.einsum(
        "bqhe,bkhe->bhqk",
        queries_heads,
        keys_all.reshape(blocks, full_len, heads, head_dim),
        preferred_element_type=jnp.float32,
    )
    logits = jnp.where(key_valid[:, None, None, :], scores + bias_heads[None], NEGATIVE)
    highest = jnp.max(logits, -1, keepdims=True)
    log_total = highest + jnp.log(jnp.sum(jnp.exp(logits - highest), -1, keepdims=True))
    probs_low = jnp.exp(logits - log_total).astype(jnp.bfloat16)
    mixed = jnp.einsum(
        "bhqk,bkhe->bqhe",
        probs_low,
        values_all.reshape(blocks, full_len, heads, head_dim),
        preferred_element_type=jnp.float32,
    )
    mixed = mixed.astype(jnp.bfloat16).reshape(total_rows, width)
    hidden = flat + jnp.dot(mixed, full_out, preferred_element_type=jnp.float32)
    scale_two = lax.rsqrt(jnp.mean(hidden * hidden, -1, keepdims=True) + EPS)
    normed_two = (hidden * scale_two * gain_two).astype(jnp.bfloat16)
    pre_act = jnp.dot(normed_two, full_in, preferred_element_type=jnp.float32)
    active = jax.nn.gelu(pre_act, approximate=True).astype(jnp.bfloat16)
    outputs = hidden + jnp.dot(active, full_down, preferred_element_type=jnp.float32)
    partial_pool = jnp.sum(outputs.reshape(blocks, shard_len, width) * query_valid[:, :, None], 1)
    pooled = lax.psum(partial_pool, "seq") / doc_lengths[:, None].astype(jnp.float32)
    regathered = (
        lax.all_gather(w_query, "seq", axis=0, tiled=True),
        lax.all_gather(w_key, "seq", axis=0, tiled=True),
        lax.all_gather(w_value, "seq", axis=0, tiled=True),
        lax.all_gather(w_out, "seq", axis=0, tiled=True),
        lax.all_gather(w_ffn_in, "seq", axis=0, tiled=True),
        lax.all_gather(w_ffn_out, "seq", axis=0, tiled=True),
        lax.all_gather(attn_gain, "seq", axis=0, tiled=True),
        lax.all_gather(ffn_gain, "seq", axis=0, tiled=True),
    )
    full_query, full_key, full_value, full_out, full_in, full_down, gain_back_one, gain_back_two = (
        regathered
    )
    gain_one = gain_back_one.astype(jnp.float32)
    gain_two = gain_back_two.astype(jnp.float32)
    grad_out = (cotangent.astype(jnp.float32) * query_valid[:, :, None]).reshape(total_rows, width)
    grad_branch = grad_out.astype(jnp.bfloat16)
    grad_down = outer_sum(active, grad_branch)
    grad_pre = (back_project(grad_branch, full_down) * gelu_slope(pre_act)).astype(jnp.bfloat16)
    grad_in = outer_sum(normed_two, grad_pre)
    grad_normed_two = back_project(grad_pre, full_in)
    grad_gain_two, grad_hidden_norm = norm_backward(hidden, scale_two, gain_two, grad_normed_two)
    grad_hidden = grad_out + grad_hidden_norm
    grad_attended = grad_hidden.astype(jnp.bfloat16)
    grad_out_proj = outer_sum(mixed, grad_attended)
    grad_mixed = (
        back_project(grad_attended, full_out)
        .astype(jnp.bfloat16)
        .reshape(blocks, shard_len, heads, head_dim)
    )
    keys_back, values_back = (keys_all, values_all)
    probs = jnp.exp(logits - log_total)
    grad_probs = jnp.einsum(
        "bqhe,bkhe->bhqk",
        grad_mixed,
        values_back.reshape(blocks, full_len, heads, head_dim),
        preferred_element_type=jnp.float32,
    )
    inner_term = jnp.sum(probs * grad_probs, -1, keepdims=True)
    grad_logits = (probs * (grad_probs - inner_term)).astype(jnp.bfloat16)
    grad_queries = jnp.einsum(
        "bhqk,bkhe->bqhe",
        grad_logits,
        keys_back.reshape(blocks, full_len, heads, head_dim),
        preferred_element_type=jnp.float32,
    )
    grad_queries = grad_queries.astype(jnp.bfloat16).reshape(total_rows, width)
    grad_table = jnp.einsum("bhqk,qkn->nh", grad_logits, onehot, preferred_element_type=jnp.float32)
    key_terms = jnp.einsum(
        "bhqk,bqhe->bkhe", grad_logits, queries_heads, preferred_element_type=jnp.float32
    ).reshape(blocks, full_len, width)
    value_terms = jnp.einsum(
        "bhqk,bqhe->bkhe", probs_low, grad_mixed, preferred_element_type=jnp.float32
    ).reshape(blocks, full_len, width)
    grad_keys, grad_values = (
        lax.psum_scatter(
            key_terms.astype(jnp.bfloat16), "seq", scatter_dimension=1, tiled=True
        ).astype(jnp.float32),
        lax.psum_scatter(
            value_terms.astype(jnp.bfloat16), "seq", scatter_dimension=1, tiled=True
        ).astype(jnp.float32),
    )
    grad_keys = grad_keys.astype(jnp.bfloat16).reshape(total_rows, width)
    grad_values = grad_values.astype(jnp.bfloat16).reshape(total_rows, width)
    grad_query_w = outer_sum(normed_one, grad_queries)
    grad_key_w = outer_sum(normed_one, grad_keys)
    grad_value_w = outer_sum(normed_one, grad_values)
    grad_normed_one = (
        back_project(grad_queries, full_query)
        + back_project(grad_keys, full_key)
        + back_project(grad_values, full_value)
    )
    grad_gain_one, grad_input_norm = norm_backward(flat, scale_one, gain_one, grad_normed_one)
    grad_input = (grad_hidden + grad_input_norm).reshape(blocks, shard_len, width)
    shards = (
        lax.psum_scatter(
            grad_query_w.astype(jnp.bfloat16), "seq", scatter_dimension=0, tiled=True
        ).astype(jnp.float32),
        lax.psum_scatter(
            grad_key_w.astype(jnp.bfloat16), "seq", scatter_dimension=0, tiled=True
        ).astype(jnp.float32),
        lax.psum_scatter(
            grad_value_w.astype(jnp.bfloat16), "seq", scatter_dimension=0, tiled=True
        ).astype(jnp.float32),
        lax.psum_scatter(
            grad_out_proj.astype(jnp.bfloat16), "seq", scatter_dimension=0, tiled=True
        ).astype(jnp.float32),
        lax.psum_scatter(
            grad_in.astype(jnp.bfloat16), "seq", scatter_dimension=0, tiled=True
        ).astype(jnp.float32),
        lax.psum_scatter(
            grad_down.astype(jnp.bfloat16), "seq", scatter_dimension=0, tiled=True
        ).astype(jnp.float32),
        lax.psum_scatter(
            grad_gain_one.astype(jnp.bfloat16), "seq", scatter_dimension=0, tiled=True
        ).astype(jnp.float32),
        lax.psum_scatter(
            grad_gain_two.astype(jnp.bfloat16), "seq", scatter_dimension=0, tiled=True
        ).astype(jnp.float32),
        lax.psum_scatter(
            grad_table.astype(jnp.bfloat16), "seq", scatter_dimension=0, tiled=True
        ).astype(jnp.float32),
    )
    totals = (
        lax.psum(shards[0].astype(jnp.bfloat16), "dp").astype(jnp.float32),
        lax.psum(shards[1].astype(jnp.bfloat16), "dp").astype(jnp.float32),
        lax.psum(shards[2].astype(jnp.bfloat16), "dp").astype(jnp.float32),
        lax.psum(shards[3].astype(jnp.bfloat16), "dp").astype(jnp.float32),
        lax.psum(shards[4].astype(jnp.bfloat16), "dp").astype(jnp.float32),
        lax.psum(shards[5].astype(jnp.bfloat16), "dp").astype(jnp.float32),
        lax.psum(shards[6].astype(jnp.bfloat16), "dp").astype(jnp.float32),
        lax.psum(shards[7].astype(jnp.bfloat16), "dp").astype(jnp.float32),
        lax.psum(shards[8].astype(jnp.bfloat16), "dp").astype(jnp.float32),
    )
    return (
        pooled,
        grad_input,
        totals[0],
        totals[1],
        totals[2],
        totals[3],
        totals[4],
        totals[5],
        totals[6],
        totals[7],
        totals[8],
    )


def fused_on_device(
    inputs,
    w_query,
    w_key,
    w_value,
    w_out,
    w_ffn_in,
    w_ffn_out,
    attn_gain,
    ffn_gain,
    rel_bias,
    doc_lengths,
    cotangent,
):
    docs, shard_len, width = inputs.shape
    rows_w, hidden_units = w_ffn_in.shape
    tokens = shard_len * SEQ
    half = width // 2
    part = hidden_units // (2 * SEQ)
    blocks = tokens // BLK
    pairs = half // BLK
    parts = part // BLK
    heads = rel_bias.shape[1]
    anywhere = pl.BlockSpec(memory_space=pl.ANY)
    vmem = pl.BlockSpec(memory_space=pltpu.VMEM)
    smem = pl.BlockSpec(memory_space=pltpu.SMEM)
    shape = jax.ShapeDtypeStruct
    narrow = [
        (docs, shard_len, width),
        (rows_w, width),
        (rows_w, width),
        (rows_w, width),
        (rows_w, width),
        (rows_w, hidden_units),
        (2 * part, width),
    ]
    out_shape = (
        shape((8, width), F32),
        shape((8, 2 * BLK), F32),
        shape((8, BLK), F32),
        *(shape(s, BF16) for s in narrow),
        shape((2 * pairs, tokens, tokens), BF16),
    )
    out_part = rows_w // 2

    def sums(count, size, columns):
        return [((count, size // 2, columns), BF16)] * 2 + [((count, size, columns), BF16)] * 4

    scratch = [
        ((SEQ, BLK, width), BF16),
        ((blocks, BLK, width), BF16),
        ((tokens, width), BF16),
        ((width, 3 * half), BF16),
        ((tokens, 3 * half), BF16),
        ((tokens, half), BF16),
        ((half, width), BF16),
        ((SEQ, BLK, width), BF16),
        ((SEQ, BLK, width), BF16),
        ((SEQ, BLK, width), F32),
        ((tokens, width), BF16),
        ((width, SEQ * part), BF16),
        ((SEQ * part, width), BF16),
        ((tokens, SEQ * part), BF16),
        ((tokens, SEQ * part), BF16),
        ((SEQ, BLK, width), F32),
        ((2 * pairs, 5 * BLK, BLK), F32),
        ((3, 24, 2 * BLK), F32),
        ((tokens, BLK), BF16),
        ((16, tokens), F32),
        ((BLK + 16, tokens), BF16),
        ((tokens, 3 * half), BF16),
        ((tokens, half), BF16),
        ((tokens, BLK), F32),
        ((tokens, BLK), F32),
        ((6 * pairs, BLK, BLK), F32),
        ((pairs, 2, 8, tokens), F32),
        ((pairs, width, 3 * BLK), BF16),
        ((parts, SEQ, BLK, width), BF16),
        *sums(parts, BLK, width),
        *sums(SEQ, rows_w, part),
        *sums(pairs, rows_w, 3 * BLK),
        ((SEQ, out_part, width), BF16),
        ((out_part, width), BF16),
        ((out_part, width), BF16),
        ((SEQ + 1, 48, BLK), F32),
        ((8, width), F32),
        ((8, width), F32),
        ((8, SEQ * part), F32),
        ((8, width), F32),
        ((4, 8, width), F32),
        ((40, BLK), F32),
        ((8, 32, BLK), F32),
        ((4, 32, BLK), F32),
        ((BLK, BLK), F32),
    ]
    chunks = parts + SEQ + pairs + 1
    pair_of = lambda *dims: [pltpu.SemaphoreType.DMA(dims)] * 2
    semaphores = (
        pair_of(5)
        + pair_of(4)
        + pair_of(4)
        + pair_of(8, 8)
        + pair_of(4)
        + pair_of(4) * 8
        + pair_of(chunks, 6)
        + pair_of(4)
        + pair_of(chunks, 6)
        + pair_of(4)
        + pair_of(8)
        + pair_of(4)
        + [pltpu.SemaphoreType.DMA((chunks, 3))]
        + [pltpu.SemaphoreType.DMA((2,))]
    )
    results = pl.pallas_call(
        fused_kernel,
        out_shape=out_shape,
        in_specs=[anywhere] * 8 + [vmem, vmem, vmem, smem],
        out_specs=(vmem, vmem, vmem) + (anywhere,) * 8,
        scratch_shapes=[pltpu.VMEM(*s) for s in scratch] + semaphores,
        compiler_params=pltpu.CompilerParams(
            collective_id=0, has_side_effects=True, vmem_limit_bytes=VMEM_LIMIT
        ),
        name="block",
    )(
        inputs,
        cotangent,
        w_query,
        w_key,
        w_value,
        w_out,
        w_ffn_in,
        w_ffn_out,
        attn_gain,
        ffn_gain,
        rel_bias,
        doc_lengths,
    )

    steps = 1

    def whole_spec(s):
        return pl.BlockSpec(s, lambda i: (0,) * len(s))

    tiny = [(docs, width), (1, rows_w), (1, rows_w), (8, heads)]
    pooled, one, two, table, gx, gq, gk, gv, go, gi, gd = pl.pallas_call(
        widen_kernel,
        out_shape=[shape(s, F32) for s in tiny + narrow],
        grid=(steps,),
        in_specs=[whole_spec(r.shape) for r in results[:3]] + [whole_spec(s) for s in narrow],
        out_specs=[whole_spec(s) for s in tiny] + [whole_spec(s) for s in narrow],
        compiler_params=pltpu.CompilerParams(vmem_limit_bytes=VMEM_LIMIT),
        name="widen",
    )(*results[:-1])
    return (pooled, gx, gq, gk, gv, go, gi, gd, one[0], two[0], table)


def fits(mesh):
    return mesh.shape["dp"] == CORES * DEPTH and mesh.shape["seq"] == SEQ


def solution(mesh):
    in_specs = (
        P("dp", "seq", None),
        P("seq", None),
        P("seq", None),
        P("seq", None),
        P("seq", None),
        P("seq", None),
        P("seq", None),
        P("seq"),
        P("seq"),
        P("seq", None),
        P("dp"),
        P("dp", "seq", None),
    )
    out_specs = (
        P("dp", None),
        P("dp", "seq", None),
        P("seq", None),
        P("seq", None),
        P("seq", None),
        P("seq", None),
        P("seq", None),
        P("seq", None),
        P("seq"),
        P("seq"),
        P("seq", None),
    )
    return jax.shard_map(
        fused_on_device if fits(mesh) else on_device, mesh=mesh, in_specs=in_specs, out_specs=out_specs, check_vma=False
    )
```
